32 devices in a mesh: seq: 8 (over y, x, core), img: 4 (over z).
Axes of the slice: x: 2, y: 2, z: 4, core: 2. Of those that a mesh axis runs over, the one named last changes fastest.
Arguments:
- images: bfloat16 [8, 3072, 1024], P('img', 'seq'), may hold values from -6 to 6
- cotangent: bfloat16 [8, 3072, 1024], P('img', 'seq'), may hold values from -6 to 6
- attention_weight: float32 [4, 1024, 1024], P(None, ('seq', 'img')), as said below
- feedforward_weight: float32 [2, 1024, 4096], P(None, ('seq', 'img')), as said below
- norm_vectors: float32 [4, 1024], P(None, ('seq', 'img')), as said below
- attention_moment: float32 [4, 1024, 1024], P(None, ('seq', 'img')), may hold values from -0.00018310547 to 0.00018310547
- feedforward_moment: float32 [2, 1024, 4096], P(None, ('seq', 'img')), may hold values from -0.00018310547 to 0.00018310547
- norm_moment: float32 [4, 1024], P(None, ('seq', 'img')), may hold values from -0.00048828125 to 0.00048828125
- attention_second: float32 [4, 1024, 1024], P(None, ('seq', 'img')), may hold values from 2.38341e-09 to 3.17788e-08
- feedforward_second: float32 [2, 1024, 4096], P(None, ('seq', 'img')), may hold values from 2.38341e-09 to 3.17788e-08
- norm_second: float32 [4, 1024], P(None, ('seq', 'img')), may hold values from 2.145069e-08 to 2.860092e-07
- attention_average: float32 [4, 1024, 1024], P(None, ('seq', 'img')), may hold values from -0.1875 to 0.1875
- feedforward_average: float32 [2, 1024, 4096], P(None, ('seq', 'img')), may hold values from -0.1875 to 0.1875
- norm_average: float32 [4, 1024], P(None, ('seq', 'img')), may hold values from 0.5 to 1.5
Outputs:
- output: bfloat16 [8, 3072, 1024], P('img', 'seq')
- input_grad: bfloat16 [8, 3072, 1024], P('img', 'seq')
- grad_norm: float32 [], replicated
- new_attention: float32 [4, 1024, 1024], P(None, ('seq', 'img'))
- new_attention_moment: float32 [4, 1024, 1024], P(None, ('seq', 'img'))
- new_attention_second: float32 [4, 1024, 1024], P(None, ('seq', 'img'))
- new_attention_average: float32 [4, 1024, 1024], P(None, ('seq', 'img'))
- new_feedforward: float32 [2, 1024, 4096], P(None, ('seq', 'img'))
- new_feedforward_moment: float32 [2, 1024, 4096], P(None, ('seq', 'img'))
- new_feedforward_second: float32 [2, 1024, 4096], P(None, ('seq', 'img'))
- new_feedforward_average: float32 [2, 1024, 4096], P(None, ('seq', 'img'))
- new_norm: float32 [4, 1024], P(None, ('seq', 'img'))
- new_norm_moment: float32 [4, 1024], P(None, ('seq', 'img'))
- new_norm_second: float32 [4, 1024], P(None, ('seq', 'img'))
- new_norm_average: float32 [4, 1024], P(None, ('seq', 'img'))
The draws below stay inside these ranges and needn't reach their ends.
Inputs may be any that keep to these rules, and one draw needn't show every extreme that they name: `attention_weight`: float32 master weights. `feedforward_weight`: float32 master weights. `norm_vectors`: gains are positive.
All inputs are finite; a program needn't handle non-finite values.
Results may differ from the reference program's by a relative error of at most 0.009.
Values may be sent and summed in bfloat16 or wider, within the bound.
No kernel may reach another device: no remote copies, remote signals or barrier semaphores. Data moves between devices by JAX's collectives and lax.ppermute only.
A program may use at most 256 MiB of HBM per device.

```python
import math
import jax
import jax.numpy as jnp
from jax import lax

D = 1024
HEADS = 16
HEAD_DIM = 64
FF = 4096
IMG_DEV = 2
LEN = 3072
STEP = 10
SPAN = 384
IMAGES = 8


def draw_attention_weight(key, part):
    key = jax.random.fold_in(key, 11)
    values = jnp.clip(jax.random.normal(key, (4, D, D), jnp.float32), -4.0, 4.0)
    scaling = jnp.array([1.0, 1.0, 1.0, 4.0], jnp.float32)[:, None, None]
    return values * scaling * D ** (-0.5)


def draw_feedforward_weight(key, part):
    key = jax.random.fold_in(key, 12)
    values = jnp.clip(jax.random.normal(key, (2, D, FF), jnp.float32), -4.0, 4.0)
    scaling = jnp.array([D ** (-0.5), FF ** (-0.5)], jnp.float32)[:, None, None]
    return values * scaling


def draw_norm_vectors(key, part):
    key = jax.random.fold_in(key, 13)
    subkeys = jax.random.split(key, 2)
    seq_ways = LEN // SPAN
    img_ways = IMAGES // IMG_DEV
    owner_index = jnp.arange(D) // (D // (seq_ways * img_ways))
    seq_place = (owner_index // img_ways).astype(jnp.float32) / max(seq_ways - 1, 1)
    img_place = (owner_index % img_ways).astype(jnp.float32) / max(img_ways - 1, 1)
    rising = 3.0
    jitter = jnp.exp(jax.random.uniform(subkeys[0], (2, D), jnp.float32, -0.22, 0.22))
    shifts = 0.3 * jax.random.normal(subkeys[1], (2, D), jnp.float32)
    gain_rows = 0.55 * rising ** (0.5 * (seq_place + img_place)) * jitter
    return jnp.stack([gain_rows[0], shifts[0], gain_rows[1], shifts[1]])


def level_of(own_key, dims, cuts, least, largest):
    factor_of = 1.0
    for position, blocks in cuts:
        steps = jax.random.uniform(jax.random.fold_in(jax.random.fold_in(own_key, 6), position), (blocks,), jnp.float32, least / len(cuts), largest / len(cuts))
        factor_of = factor_of * jnp.repeat(jnp.exp(steps), dims[position] // blocks).reshape((-1,) + (1,) * (len(dims) - 1 - position))
    return factor_of


def bell_draw(stream_key, dims, scale, most, shards=(), held_as=jnp.bfloat16):
    entries = scale * jax.random.normal(stream_key, dims, jnp.float32)
    if shards:
        entries = entries * level_of(stream_key, dims, shards, -0.22, 0.18)
    return jnp.clip(entries, -most, most).astype(held_as)


def setup_inputs(seed: int = 0) -> dict:
    keys = jax.random.split(jax.random.key(seed), 15)
    images = bell_draw(keys[0], (IMAGES, LEN, D), 1.0, 6.0, ((0, 4), (1, 8)))
    cotangent = bell_draw(keys[1], (IMAGES, LEN, D), 1.0, 6.0, ((0, 4), (1, 8)))
    attention_weight = draw_attention_weight(jax.random.fold_in(keys[14], 71), 0)
    feedforward_weight = draw_feedforward_weight(jax.random.fold_in(keys[14], 71), 0)
    norm_vectors = draw_norm_vectors(jax.random.fold_in(keys[14], 71), 0)
    attention_moment = bell_draw(keys[5], (4, D, D), (0.11 * (4 * D * D + 2 * D * FF + 4 * D) ** -0.5), 0.00018310547, ((1, 32),), jnp.float32)
    feedforward_moment = bell_draw(keys[6], (2, D, FF), (0.11 * (4 * D * D + 2 * D * FF + 4 * D) ** -0.5), 0.00018310547, ((1, 32),), jnp.float32)
    norm_moment = bell_draw(keys[7], (4, D), (0.33 * (4 * D * D + 2 * D * FF + 4 * D) ** -0.5), 0.00048828125, ((1, 32),), jnp.float32)
    attention_second = jnp.clip(jnp.exp(math.log(3.1778800035908716e-08) - 2.5902672 * jax.random.uniform(keys[8], (4, D, D), jnp.float32) ** level_of(keys[8], (4, D, D), ((1, 32),), -0.2, 0.2)), 2.3834099138753118e-09, 3.1778800035908716e-08)
    feedforward_second = jnp.clip(jnp.exp(math.log(3.1778800035908716e-08) - 2.5902672 * jax.random.uniform(keys[9], (2, D, FF), jnp.float32) ** level_of(keys[9], (2, D, FF), ((1, 32),), -0.2, 0.2)), 2.3834099138753118e-09, 3.1778800035908716e-08)
    norm_second = jnp.clip(jnp.exp(math.log(2.8600919677046477e-07) - 2.5902671 * jax.random.uniform(keys[10], (4, D), jnp.float32) ** level_of(keys[10], (4, D), ((1, 32),), -0.2, 0.2)), 2.1450690113056226e-08, 2.8600919677046477e-07)
    attention_average = bell_draw(keys[11], (4, D, D), D ** -0.5, 0.1875, ((1, 32),), jnp.float32)
    feedforward_average = bell_draw(keys[12], (2, D, FF), D ** -0.5, 0.1875, ((1, 32),), jnp.float32)
    norm_average = jnp.clip(1.0 + 0.1 * jax.random.normal(keys[13], (4, D), jnp.float32), 0.5, 1.5)
    return dict(images=images, cotangent=cotangent, attention_weight=attention_weight, feedforward_weight=feedforward_weight, norm_vectors=norm_vectors, attention_moment=attention_moment, feedforward_moment=feedforward_moment, norm_moment=norm_moment, attention_second=attention_second, feedforward_second=feedforward_second, norm_second=norm_second, attention_average=attention_average, feedforward_average=feedforward_average, norm_average=norm_average)


highest = lax.Precision.HIGHEST
beta_first = 0.9
beta_second = 0.95
learn_rate = 0.02
norm_rate = 0.2
weight_decay = 0.1
average_decay = 0.75
clip_bound = 1.0
eps_norm = 1e-05
eps_adam = 1e-08

@jax.custom_vjp
def low(v):
    return lax.optimization_barrier(v.astype(jnp.bfloat16)).astype(jnp.float32)

@jax.custom_vjp
def low_back(v):
    return v

def low_keep(v):
    return (low(v), None)

def low_pass(kept, grad):
    return (grad,)

def back_keep(v):
    return (v, None)

def back_low(kept, grad):
    return (low(grad),)
low.defvjp(low_keep, low_pass)
low_back.defvjp(back_keep, back_low)

def layer_norm(values, gain_row, shift_row):
    centre = lax.optimization_barrier(jnp.mean(values, axis=-1, keepdims=True))
    centred = values - centre
    spread = lax.optimization_barrier(jnp.mean(centred * centred, axis=-1, keepdims=True))
    return centred * lax.rsqrt(spread + eps_norm) * gain_row + shift_row

def feature(values):
    return jax.nn.elu(values) + 1.0

def attend(query_feat, key_feat, value_heads):
    block_len = 512 if LEN % 512 == 0 else LEN
    blocks = LEN // block_len
    causal = (jnp.arange(block_len)[:, None] >= jnp.arange(block_len)[None, :]).astype(jnp.float32)

    def one_block(carry, pieces):
        state, key_total = carry
        block_query, block_key, block_value = pieces
        scores = low(low_back(jnp.einsum('ihe,jhe->hij', block_query, block_key, precision=highest) * causal))
        numerator = jnp.einsum('hij,jhe->ihe', scores, block_value, precision=highest)
        numerator = numerator + jnp.einsum('ihe,hef->ihf', block_query, state, precision=highest)
        numerator = low_back(numerator)
        denominator = lax.optimization_barrier(jnp.sum(scores, axis=-1)).T + jnp.einsum('ihe,he->ih', block_query, key_total, precision=highest)
        state = state + jnp.einsum('jhe,jhf->hef', block_key, block_value, precision=highest)
        key_total = key_total + lax.optimization_barrier(jnp.sum(block_key, axis=0))
        return ((state, key_total), numerator / denominator[:, :, None])
    initial = (jnp.zeros((HEADS, HEAD_DIM, HEAD_DIM), jnp.float32), jnp.zeros((HEADS, HEAD_DIM), jnp.float32))
    pieces = tuple((member.reshape(blocks, block_len, HEADS, HEAD_DIM) for member in (query_feat, key_feat, value_heads)))
    final_state, mixed = lax.scan(jax.checkpoint(one_block), initial, pieces)
    return mixed.reshape(LEN, HEADS * HEAD_DIM)

def forward(seq_in, attention_weight, feedforward_weight, norm_vectors):
    attn_work = low(attention_weight)
    feed_work = low(feedforward_weight)
    vector_work = low(norm_vectors)
    normed = low(layer_norm(seq_in, vector_work[0], vector_work[1]))
    query_feat = low(feature(low_back(jnp.dot(normed, attn_work[0], precision=highest))))
    key_feat = low(feature(low_back(jnp.dot(normed, attn_work[1], precision=highest))))
    value_rows = low(low_back(jnp.dot(normed, attn_work[2], precision=highest)))
    head_shape = (LEN, HEADS, HEAD_DIM)
    mixed = low(low_back(attend(query_feat.reshape(head_shape), key_feat.reshape(head_shape), value_rows.reshape(head_shape))))
    residual = seq_in + low_back(jnp.dot(mixed, attn_work[3], precision=highest))
    normed_second = low(layer_norm(residual, vector_work[2], vector_work[3]))
    hidden = low(jax.nn.gelu(low_back(jnp.dot(normed_second, feed_work[0], precision=highest))))
    return residual + low_back(jnp.dot(hidden, feed_work[1].T, precision=highest))

def adam_update(master, moment, second, average, gradient, factor, rate):
    clipped = gradient * factor
    moment = beta_first * moment + (1.0 - beta_first) * clipped
    second = beta_second * second + (1.0 - beta_second) * clipped * clipped
    first_hat = moment / (1.0 - beta_first ** STEP)
    second_hat = second / (1.0 - beta_second ** STEP)
    master = master - rate * (first_hat / (jnp.sqrt(second_hat) + eps_adam) + weight_decay * master)
    average = average_decay * average + (1.0 - average_decay) * master
    return (master, moment, second, average)

def reference(images, cotangent, attention_weight, feedforward_weight, norm_vectors, attention_moment, feedforward_moment, norm_moment, attention_second, feedforward_second, norm_second, attention_average, feedforward_average, norm_average):
    inputs = images.astype(jnp.float32)
    incoming = cotangent.astype(jnp.float32)

    def one_image(totals, pieces):
        seq_in, seq_cot = pieces
        result, pull_back = jax.vjp(forward, seq_in, attention_weight, feedforward_weight, norm_vectors)
        gradients = pull_back(seq_cot)
        totals = tuple((running + addition for running, addition in zip(totals, gradients[1:])))
        return (totals, (result, gradients[0]))
    zeros_start = (jnp.zeros_like(attention_weight), jnp.zeros_like(feedforward_weight), jnp.zeros_like(norm_vectors))
    totals, (results, input_grads) = lax.scan(one_image, zeros_start, (inputs, incoming))
    squares = jnp.sum(totals[0] * totals[0]) + jnp.sum(totals[1] * totals[1]) + jnp.sum(totals[2] * totals[2])
    grad_norm = jnp.sqrt(squares)
    factor = clip_bound / jnp.maximum(grad_norm, clip_bound)
    attn_new, attn_moment_new, attn_second_new, attn_average_new = adam_update(attention_weight, attention_moment, attention_second, attention_average, totals[0], factor, learn_rate)
    feed_new, feed_moment_new, feed_second_new, feed_average_new = adam_update(feedforward_weight, feedforward_moment, feedforward_second, feedforward_average, totals[1], factor, learn_rate)
    norm_new, norm_moment_new, norm_second_new, norm_average_new = adam_update(norm_vectors, norm_moment, norm_second, norm_average, totals[2], factor, norm_rate)
    return (results.astype(jnp.bfloat16), input_grads.astype(jnp.bfloat16), grad_norm, attn_new, attn_moment_new, attn_second_new, attn_average_new, feed_new, feed_moment_new, feed_second_new, feed_average_new, norm_new, norm_moment_new, norm_second_new, norm_average_new)
```

```python
import jax
import jax.numpy as jnp
from jax import lax
from jax.sharding import PartitionSpec as P

HEADS = 16
HEAD_DIM = 64
STEP = 10


highest = lax.Precision.HIGHEST
beta_first = 0.9
beta_second = 0.95
learn_rate = 0.02
norm_rate = 0.2
weight_decay = 0.1
average_decay = 0.75
clip_bound = 1.0
eps_norm = 1e-05
eps_adam = 1e-08


def entering(array, axis, join, neutral, backward):
    count = lax.axis_size(axis)
    place = lax.axis_index(axis)
    ahead = count - 1 - place if backward else place
    gathered = jax.tree.map(
        lambda a, kind: lax.all_gather(a.astype(kind), axis), array, (jnp.bfloat16, jnp.bfloat16)
    )
    state = jax.tree.map(lambda a, e: jnp.zeros_like(a) + jnp.asarray(e, a.dtype), array, neutral)

    def one(lap, state):
        source = count - 1 - lap if backward else lap
        return join(
            state,
            jax.tree.map(
                lambda a, own: lax.dynamic_index_in_dim(a, source, 0, False).astype(own.dtype),
                gathered,
                array,
            ),
        )

    return lax.fori_loop(0, ahead, one, state)


def layer_norm(values, gain_row, shift_row):
    centre = jnp.mean(values, axis=-1, keepdims=True)
    centred = values - centre
    spread = jnp.mean(centred * centred, axis=-1, keepdims=True)
    return centred * lax.rsqrt(spread + eps_norm) * gain_row + shift_row


def feature(values):
    return jax.nn.elu(values) + 1.0


def add_pair(earlier, later):
    return (earlier[0] + later[0], earlier[1] + later[1])


def adam_update(master, moment, second, average, gradient, factor, rate):
    clipped = gradient * factor
    moment = beta_first * moment + (1.0 - beta_first) * clipped
    second = beta_second * second + (1.0 - beta_second) * clipped * clipped
    first_hat = moment / (1.0 - beta_first**STEP)
    second_hat = second / (1.0 - beta_second**STEP)
    master = master - rate * (first_hat / (jnp.sqrt(second_hat) + eps_adam) + weight_decay * master)
    average = average_decay * average + (1.0 - average_decay) * master
    return (master, moment, second, average)


def contract_rows(left, right):
    return lax.dot_general(
        left, right, (((0,), (0,)), ((), ())), preferred_element_type=jnp.float32
    )


def contract_last(left, right):
    return lax.dot_general(
        left, right, (((1,), (1,)), ((), ())), preferred_element_type=jnp.float32
    )


def flip_pairs(count, bit):
    return [(i, i ^ bit) for i in range(count)]


def block_order(count, bits):
    order = [0]
    for bit in reversed(bits):
        order = [j | bit for j in order] + order
    return order


def powers(count):
    return [1 << k for k in range(count.bit_length() - 1)]


def relative_columns(array, axis, bits):
    count = lax.axis_size(axis)
    place = lax.axis_index(axis)
    width = array.shape[-1] // count
    return jnp.concatenate(
        [
            lax.dynamic_slice_in_dim(array, (place ^ j) * width, width, array.ndim - 1)
            for j in block_order(count, bits)
        ],
        axis=-1,
    )


def reduce_rows(rest, axis, bits):
    count = lax.axis_size(axis)
    for bit in bits:
        half = rest.shape[0] // 2
        sent = rest[:half].astype(jnp.bfloat16)
        came = lax.ppermute(sent, axis, flip_pairs(count, bit))
        rest = rest[half:].astype(jnp.float32) + came.astype(jnp.float32)
    return rest


def relative_rows(array, axis, bits):
    count = lax.axis_size(axis)
    place = lax.axis_index(axis)
    width = array.shape[0] // count
    return jnp.concatenate(
        [
            lax.dynamic_slice_in_dim(array, (place ^ j) * width, width, 0)
            for j in block_order(count, bits)
        ],
        axis=0,
    )


def scatter_product(left, right, bits):
    count = lax.axis_size("seq")
    half = left.shape[1] // 2
    sent = contract_rows(left[:, :half], right).astype(jnp.bfloat16)
    came = lax.ppermute(sent, "seq", flip_pairs(count, bits[0]))
    rest = contract_rows(left[:, half:], right) + came.astype(jnp.float32)
    return scatter_rest(rest, bits[1:])


def scatter_rest(rest, bits):
    rest = reduce_rows(rest, "seq", bits)
    ways = powers(lax.axis_size("img"))
    return reduce_rows(relative_rows(rest, "img", ways), "img", ways)


def body(
    images,
    cotangent,
    attention_weight,
    feedforward_weight,
    norm_vectors,
    attention_moment,
    feedforward_moment,
    norm_moment,
    attention_second,
    feedforward_second,
    norm_second,
    attention_average,
    feedforward_average,
    norm_average,
):
    work_attention, work_feed, work_vectors = (
        lax.all_gather(attention_weight.astype(jnp.bfloat16), ("seq", "img"), axis=1, tiled=True),
        lax.all_gather(feedforward_weight.astype(jnp.bfloat16), ("seq", "img"), axis=1, tiled=True),
        lax.all_gather(norm_vectors.astype(jnp.bfloat16), ("seq", "img"), axis=1, tiled=True),
    )
    norm_rows = work_vectors.astype(jnp.float32)
    count_images, span_rows, width_all = images.shape
    token_rows = count_images * span_rows
    head_shape = (count_images, span_rows, HEADS, HEAD_DIM)
    owner_rows = attention_weight.shape[1]
    hidden_width = feedforward_weight.shape[2]
    inputs = images.astype(jnp.float32).reshape(token_rows, width_all)
    normed_raw, first_pull = jax.vjp(layer_norm, inputs, norm_rows[0], norm_rows[1])
    normed = normed_raw.astype(jnp.bfloat16)
    projected = jnp.einsum(
        "td,kde->kte", normed, work_attention[:3], preferred_element_type=jnp.float32
    )
    query_raw, query_pull = jax.vjp(feature, projected[0])
    key_raw, key_pull = jax.vjp(feature, projected[1])
    query_feat = query_raw.astype(jnp.bfloat16).reshape(head_shape)
    key_feat = key_raw.astype(jnp.bfloat16).reshape(head_shape)
    value_heads = projected[2].astype(jnp.bfloat16).reshape(head_shape)
    key_state = jnp.einsum(
        "bjhe,bjhf->bhef", key_feat, value_heads, preferred_element_type=jnp.float32
    )
    key_total = jnp.sum(key_feat.astype(jnp.float32), axis=1)
    zero_state = jnp.zeros_like(key_state)
    zero_total = jnp.zeros_like(key_total)
    prior_state, prior_total = entering(
        (key_state, key_total), "seq", add_pair, (zero_state, zero_total), False
    )
    causal = (jnp.arange(span_rows)[:, None] >= jnp.arange(span_rows)[None, :]).astype(jnp.float32)
    query_wide = query_feat.astype(jnp.float32)
    key_wide = key_feat.astype(jnp.float32)
    value_wide = value_heads.astype(jnp.float32)
    score_low = (
        jnp.einsum("bihe,bjhe->bhij", query_feat, key_feat, preferred_element_type=jnp.float32)
        * causal
    ).astype(jnp.bfloat16)
    numerator = jnp.einsum(
        "bhij,bjhe->bihe", score_low, value_heads, preferred_element_type=jnp.float32
    )
    numerator = numerator + jnp.einsum(
        "bihe,bhef->bihf", query_wide, prior_state, precision=highest
    )
    score_sums = jnp.sum(score_low.astype(jnp.float32), axis=-1)
    denominator = jnp.swapaxes(score_sums, 1, 2) + jnp.einsum(
        "bihe,bhe->bih", query_wide, prior_total, precision=highest
    )
    mixed_raw = numerator / denominator[..., None]
    mixed = mixed_raw.reshape(token_rows, width_all).astype(jnp.bfloat16)
    residual = inputs + jnp.dot(mixed, work_attention[3], preferred_element_type=jnp.float32)
    second_raw, second_pull = jax.vjp(layer_norm, residual, norm_rows[2], norm_rows[3])
    normed_second = second_raw.astype(jnp.bfloat16)
    pre_gelu = jnp.dot(normed_second, work_feed[0], preferred_element_type=jnp.float32)
    hidden_raw, gelu_pull = jax.vjp(jax.nn.gelu, pre_gelu)
    hidden = hidden_raw.astype(jnp.bfloat16)
    down_rows = contract_last(hidden, work_feed[1])
    output = (residual + down_rows).astype(jnp.bfloat16).reshape(count_images, span_rows, width_all)
    incoming = cotangent.reshape(token_rows, width_all)
    grad_hidden = jnp.dot(incoming, work_feed[1], preferred_element_type=jnp.float32)
    grad_pre = gelu_pull(grad_hidden)[0].astype(jnp.bfloat16)
    grad_normed_second = contract_last(grad_pre, work_feed[0])
    grad_resid_norm, grad_gain_second, grad_shift_second = second_pull(grad_normed_second)
    grad_residual = incoming.astype(jnp.float32) + grad_resid_norm
    branch = grad_residual.astype(jnp.bfloat16)
    grad_mixed = contract_last(branch, work_attention[3])
    grad_mixed = (
        lax.optimization_barrier(grad_mixed.astype(jnp.bfloat16))
        .astype(jnp.float32)
        .reshape(head_shape)
    )
    grad_numer = (grad_mixed / denominator[..., None]).astype(jnp.bfloat16)
    grad_numer_wide = grad_numer.astype(jnp.float32)
    grad_denom = -jnp.sum(grad_mixed * mixed_raw, axis=-1) / denominator
    grad_scores = jnp.einsum(
        "bihe,bjhe->bhij", grad_numer, value_heads, preferred_element_type=jnp.float32
    )
    grad_score_low = ((grad_scores + jnp.swapaxes(grad_denom, 1, 2)[..., None]) * causal).astype(
        jnp.bfloat16
    )
    grad_query = jnp.einsum(
        "bhij,bjhe->bihe", grad_score_low, key_feat, preferred_element_type=jnp.float32
    )
    grad_query = grad_query + jnp.einsum(
        "bihf,bhef->bihe", grad_numer_wide, prior_state, precision=highest
    )
    grad_query = grad_query + grad_denom[..., None] * prior_total[:, None, :, :]
    grad_prior = jnp.einsum(
        "bihe,bihf->bhef", query_feat, grad_numer, preferred_element_type=jnp.float32
    )
    grad_prior_total = jnp.einsum("bihe,bih->bhe", query_wide, grad_denom, precision=highest)
    later_state, later_total = entering(
        (grad_prior, grad_prior_total), "seq", add_pair, (zero_state, zero_total), True
    )
    grad_key = jnp.einsum(
        "bhij,bihe->bjhe", grad_score_low, query_feat, preferred_element_type=jnp.float32
    )
    grad_key = grad_key + jnp.einsum("bjhf,bhef->bjhe", value_wide, later_state, precision=highest)
    grad_key = grad_key + later_total[:, None, :, :]
    grad_value = jnp.einsum(
        "bhij,bihe->bjhe", score_low, grad_numer, preferred_element_type=jnp.float32
    )
    grad_value = grad_value + jnp.einsum(
        "bjhe,bhef->bjhf", key_wide, later_state, precision=highest
    )
    grad_query_raw = query_pull(grad_query.reshape(token_rows, width_all))[0].astype(jnp.bfloat16)
    grad_key_raw = key_pull(grad_key.reshape(token_rows, width_all))[0].astype(jnp.bfloat16)
    grad_value_raw = grad_value.reshape(token_rows, width_all).astype(jnp.bfloat16)
    stacked_grads = jnp.stack([grad_query_raw, grad_key_raw, grad_value_raw])
    grad_normed = jnp.einsum(
        "kte,kde->td", stacked_grads, work_attention[:3], preferred_element_type=jnp.float32
    )
    grad_input_norm, grad_gain_first, grad_shift_first = first_pull(grad_normed)
    input_grad = (
        (grad_residual + grad_input_norm)
        .astype(jnp.bfloat16)
        .reshape(count_images, span_rows, width_all)
    )
    vector_grad = jnp.stack(
        [grad_gain_first, grad_shift_first, grad_gain_second, grad_shift_second]
    )
    first_bits = powers(lax.axis_size("seq"))
    other_bits = first_bits[:1] + first_bits[1:][::-1]
    down_shard = scatter_product(
        relative_columns(incoming, "seq", first_bits), hidden, first_bits
    )
    up_shard = scatter_product(
        relative_columns(normed_second, "seq", other_bits), grad_pre, other_bits
    )
    out_shard = scatter_product(
        relative_columns(mixed, "seq", first_bits), branch, first_bits
    )
    normed_relative = relative_columns(normed, "seq", first_bits)
    inner_shards = [
        scatter_product(normed_relative, member, first_bits)
        for member in (grad_query_raw, grad_key_raw, grad_value_raw)
    ]
    vector_rows = relative_rows(vector_grad.T, "seq", first_bits)
    vector_shard = scatter_rest(vector_rows, first_bits).T
    attn_shard = jnp.stack(inner_shards + [out_shard])
    feed_shard = jnp.stack([up_shard, down_shard])
    local_squares = (
        jnp.sum(attn_shard * attn_shard)
        + jnp.sum(feed_shard * feed_shard)
        + jnp.sum(vector_shard * vector_shard)
    )
    grad_norm = jnp.sqrt(lax.psum(local_squares, ("seq", "img")))
    factor = clip_bound / jnp.maximum(grad_norm, clip_bound)
    attn_new, attn_moment_new, attn_second_new, attn_average_new = adam_update(
        attention_weight,
        attention_moment,
        attention_second,
        attention_average,
        attn_shard,
        factor,
        learn_rate,
    )
    feed_new, feed_moment_new, feed_second_new, feed_average_new = adam_update(
        feedforward_weight,
        feedforward_moment,
        feedforward_second,
        feedforward_average,
        feed_shard,
        factor,
        learn_rate,
    )
    norm_new, norm_moment_new, norm_second_new, norm_average_new = adam_update(
        norm_vectors, norm_moment, norm_second, norm_average, vector_shard, factor, norm_rate
    )
    return (
        output,
        input_grad,
        grad_norm,
        attn_new,
        attn_moment_new,
        attn_second_new,
        attn_average_new,
        feed_new,
        feed_moment_new,
        feed_second_new,
        feed_average_new,
        norm_new,
        norm_moment_new,
        norm_second_new,
        norm_average_new,
    )


def solution(mesh):
    return jax.shard_map(
        body,
        mesh=mesh,
        in_specs=(
            P("img", "seq", None),
            P("img", "seq", None),
            P(None, ("seq", "img"), None),
            P(None, ("seq", "img"), None),
            P(None, ("seq", "img")),
            P(None, ("seq", "img"), None),
            P(None, ("seq", "img"), None),
            P(None, ("seq", "img")),
            P(None, ("seq", "img"), None),
            P(None, ("seq", "img"), None),
            P(None, ("seq", "img")),
            P(None, ("seq", "img"), None),
            P(None, ("seq", "img"), None),
            P(None, ("seq", "img")),
        ),
        out_specs=(
            P("img", "seq", None),
            P("img", "seq", None),
            P(),
            P(None, ("seq", "img"), None),
            P(None, ("seq", "img"), None),
            P(None, ("seq", "img"), None),
            P(None, ("seq", "img"), None),
            P(None, ("seq", "img"), None),
            P(None, ("seq", "img"), None),
            P(None, ("seq", "img"), None),
            P(None, ("seq", "img"), None),
            P(None, ("seq", "img")),
            P(None, ("seq", "img")),
            P(None, ("seq", "img")),
            P(None, ("seq", "img")),
        ),
        check_vma=False,
    )
```

```python
import functools

import jax
import jax.numpy as jnp
from jax import lax
from jax.experimental import pallas as pl
from jax.experimental.pallas import tpu as pltpu
from jax.sharding import Mesh
from jax.sharding import PartitionSpec as P

HEADS = 16
HEAD_DIM = 64
STEP = 10

beta_first = 0.9
beta_second = 0.95
learn_rate = 0.02
norm_rate = 0.2
weight_decay = 0.1
average_decay = 0.75
clip_bound = 1.0
eps_norm = 1e-05
eps_adam = 1e-08

PAIR = 2 * HEAD_DIM
STATE_ROWS = HEAD_DIM + 16
SLAB = 1024
TILE = 512
GROUP = 256
VMEM_BYTES = 56 * 1024 * 1024

low = jnp.bfloat16
wide = jnp.float32


def params():
    return pltpu.CompilerParams(vmem_limit_bytes=VMEM_BYTES)


def shaped(shape, kind):
    return jax.ShapeDtypeStruct(shape, kind)


def whole(shape):
    return pl.BlockSpec(shape, lambda *_: (0,) * len(shape))


def mm(left, right):
    return lax.dot_general(left, right, (((1,), (0,)), ((), ())), preferred_element_type=wide)


def mt(left, right):
    return lax.dot_general(left, right, (((1,), (1,)), ((), ())), preferred_element_type=wide)


def tm(left, right):
    return lax.dot_general(left, right, (((0,), (0,)), ((), ())), preferred_element_type=wide)


def first_head(rows):
    return lax.broadcasted_iota(jnp.int32, (rows, PAIR), 1) < HEAD_DIM


def fold_state(product):
    return jnp.where(first_head(HEAD_DIM), product[:HEAD_DIM], product[HEAD_DIM:])


def unfold_state(folded):
    own = first_head(HEAD_DIM)
    zero = jnp.zeros_like(folded)
    return jnp.concatenate([jnp.where(own, folded, zero), jnp.where(own, zero, folded)], axis=0)


def unfold_total(row):
    tall = jnp.broadcast_to(row, (PAIR, PAIR))
    lanes = lax.broadcasted_iota(jnp.int32, (PAIR, PAIR), 1) < HEAD_DIM
    rows = lax.broadcasted_iota(jnp.int32, (PAIR, PAIR), 0) < HEAD_DIM
    return jnp.where(lanes == rows, tall, jnp.zeros_like(tall))


def split_low(values):
    high = values.astype(low)
    return high, (values - high.astype(wide)).astype(low)


def normalised(values):
    centre = jnp.mean(values, axis=-1, keepdims=True)
    centred = values - centre
    spread = jnp.mean(centred * centred, axis=-1, keepdims=True)
    scale = lax.rsqrt(spread + eps_norm)
    return centred * scale, scale


def project_kernel(images, span, x_ref, vec_ref, mine_ref, other_ref, fq_ref, fk_ref, v_ref, a_ref, at_ref, state_ref):
    half = mine_ref.shape[1]

    @pl.when(pl.program_id(0) == 0)
    def _():
        gain, shift = vec_ref[0:1, :], vec_ref[1:2, :]
        step = span // 3
        for start in range(0, images * span, step):
            rows = slice(start, start + step)
            unit, _ = normalised(x_ref[rows, :].astype(wide))
            a_ref[rows, :] = (unit * gain + shift).astype(low)
        at_ref[...] = a_ref[...].T

    normed = a_ref[...]
    left, right = normed[:, :half], normed[:, half:]

    def project(k):
        return mm(left, mine_ref[k]) + mm(right, other_ref[k])

    def feature(raw):
        return jnp.where(raw > 0, raw + 1.0, jnp.exp(jnp.minimum(raw, 0.0))).astype(low)

    fk_ref[...] = feature(project(1))
    v_ref[...] = project(2).astype(low)
    fq_ref[...] = feature(project(0))
    ones = jnp.ones((16, span), low)
    for image in range(images):
        rows = slice(image * span, (image + 1) * span)
        for pair in range(GROUP // PAIR):
            lanes = slice(pair * PAIR, (pair + 1) * PAIR)
            key, value = fk_ref[rows, lanes], v_ref[rows, lanes]
            state_ref[image, pair, :HEAD_DIM, :] = fold_state(tm(value, key))
            state_ref[image, pair, HEAD_DIM:, :] = mm(ones, key)


def project(x, vec, mine, other, images, span):
    tokens, width = x.shape
    half = mine.shape[1]
    groups = width // GROUP
    pairs = GROUP // PAIR
    weight = pl.BlockSpec((3, half, GROUP), lambda g: (0, 0, g))
    column = pl.BlockSpec((tokens, GROUP), lambda g: (0, g))
    return pl.pallas_call(
        functools.partial(project_kernel, images, span),
        grid=(groups,),
        in_specs=[whole((tokens, width)), whole(vec.shape), weight, weight],
        out_specs=[
            column,
            column,
            column,
            whole((tokens, width)),
            whole((width, tokens)),
            pl.BlockSpec((images, pairs, STATE_ROWS, PAIR), lambda g: (0, g, 0, 0)),
        ],
        out_shape=[
            shaped((tokens, width), low),
            shaped((tokens, width), low),
            shaped((tokens, width), low),
            shaped((tokens, width), low),
            shaped((width, tokens), low),
            shaped((images, width // PAIR, STATE_ROWS, PAIR), wide),
        ],
        compiler_params=params(),
        name="project",
    )(x, vec, mine, other)


def attend_kernel(span, fq_ref, fk_ref, v_ref, num_ref, den_ref):
    query, key, value = fq_ref[...], fk_ref[...], v_ref[...]
    own = first_head(span)
    zero = jnp.zeros_like(query)
    causal = lax.broadcasted_iota(jnp.int32, (span, span), 0) >= lax.broadcasted_iota(jnp.int32, (span, span), 1)
    total = None
    for head in range(2):
        mask = own if head == 0 else jnp.logical_not(own)
        scores = mt(jnp.where(mask, query, zero), key)
        scores = jnp.where(causal, scores, 0.0).astype(low)
        ones = jnp.where(mask, jnp.ones_like(value), zero)
        part = mm(scores, jnp.concatenate([jnp.where(mask, value, zero), ones], axis=1))
        total = part if total is None else total + part
    num_ref[...] = total[:, :PAIR]
    den_ref[...] = total[:, PAIR:]


def attend(fq, fk, v, images, span):
    tokens, width = fq.shape
    block = pl.BlockSpec((span, PAIR), lambda b, p: (b, p))
    return pl.pallas_call(
        functools.partial(attend_kernel, span),
        grid=(images, width // PAIR),
        in_specs=[block] * 3,
        out_specs=[block] * 2,
        out_shape=[shaped((tokens, width), wide)] * 2,
        compiler_params=params(),
        name="attend",
    )(fq, fk, v)


def mix_kernel(x_ref, vec_ref, wo_ref, fq_ref, num_ref, den_ref, prior_ref, mixed_ref, rden_ref, resid_ref, a_ref, at_ref):
    width = x_ref.shape[1]
    for pair in range(width // PAIR):
        lanes = slice(pair * PAIR, (pair + 1) * PAIR)
        folded = prior_ref[0, pair]
        matrix = jnp.concatenate(
            [unfold_state(folded[:HEAD_DIM]), unfold_total(folded[HEAD_DIM : HEAD_DIM + 1])], axis=0
        )
        high, rest = split_low(matrix)
        query = fq_ref[:, lanes]
        both = mt(jnp.concatenate([query, query], axis=1), jnp.concatenate([high, rest], axis=1))
        scale = 1.0 / (den_ref[:, lanes] + both[:, PAIR:])
        rden_ref[:, lanes] = scale
        mixed_ref[:, lanes] = ((num_ref[:, lanes] + both[:, :PAIR]) * scale).astype(low)
    resid = x_ref[...].astype(wide) + mm(mixed_ref[...], wo_ref[...])
    resid_ref[...] = resid
    unit, _ = normalised(resid)
    normed = (unit * vec_ref[2:3, :] + vec_ref[3:4, :]).astype(low)
    a_ref[...] = normed
    at_ref[...] = normed.T


def mix(x, vec, wo, fq, num, den, prior, images, span):
    tokens, width = x.shape
    rows = pl.BlockSpec((span, width), lambda b: (b, 0))
    return pl.pallas_call(
        mix_kernel,
        grid=(images,),
        in_specs=[
            rows,
            whole(vec.shape),
            whole(wo.shape),
            rows,
            rows,
            rows,
            pl.BlockSpec((1,) + prior.shape[1:], lambda b: (b, 0, 0, 0)),
        ],
        out_specs=[rows, rows, rows, rows, pl.BlockSpec((None, width, span), lambda b: (b, 0, 0))],
        out_shape=[
            shaped((tokens, width), low),
            shaped((tokens, width), wide),
            shaped((tokens, width), wide),
            shaped((tokens, width), low),
            shaped((images, width, span), low),
        ],
        compiler_params=params(),
        name="mix",
    )(x, vec, wo, fq, num, den, prior)


def turn_kernel(x_ref, out_ref):
    out_ref[...] = x_ref[...].T


def turn(x, images, span):
    tokens, width = x.shape
    return pl.pallas_call(
        turn_kernel,
        grid=(images,),
        in_specs=[pl.BlockSpec((span, width), lambda b: (b, 0))],
        out_specs=pl.BlockSpec((None, width, span), lambda b: (b, 0, 0)),
        out_shape=shaped((images, width, span), low),
        compiler_params=params(),
        name="turn",
    )(x)


gelu_scale = 0.7978845608028654
gelu_cubic = 0.044715


def feed_kernel(fresh, images, span, *refs):
    a_ref, at_ref, e_ref, et_ref, um_ref, uo_ref, dm_ref, do_ref = refs[:8]
    out_ref, da_ref, gum_ref, guo_ref, gdm_ref, gdo_ref = refs[-6:]
    half = um_ref.shape[1]

    @pl.when(pl.program_id(0) == 0)
    def _():
        if fresh:
            out_ref[...] = jnp.zeros_like(out_ref)
            da_ref[...] = jnp.zeros_like(da_ref)
        else:
            out_ref[...] = refs[8][...]
            da_ref[...] = refs[9][...]

    um, uo, dm, do = um_ref[0], uo_ref[0], dm_ref[0], do_ref[0]
    for image in range(images):
        rows = slice(image * span, (image + 1) * span)
        upper = mm(a_ref[rows, :half], um) + mm(a_ref[rows, half:], uo)
        grad = mm(e_ref[rows, :half], dm) + mm(e_ref[rows, half:], do)
        square = upper * upper
        bend = jnp.tanh(gelu_scale * upper * (1.0 + gelu_cubic * square))
        gate = 0.5 + 0.5 * bend
        hidden = (upper * gate).astype(low)
        slope = gate + 0.5 * upper * (1.0 - bend * bend) * (gelu_scale * (1.0 + 3.0 * gelu_cubic * square))
        dupper = (grad * slope).astype(low)
        out_ref[rows, :half] += mt(hidden, dm)
        out_ref[rows, half:] += mt(hidden, do)
        da_ref[rows, :half] += mt(dupper, um)
        da_ref[rows, half:] += mt(dupper, uo)
        parts = [
            (gdm_ref, mm(et_ref[image, :half, :], hidden)),
            (gdo_ref, mm(et_ref[image, half:, :], hidden)),
            (gum_ref, mm(at_ref[image, :half, :], dupper)),
            (guo_ref, mm(at_ref[image, half:, :], dupper)),
        ]
        if image == 0:
            sums = [part for _, part in parts]
        else:
            sums = [total + part for total, (_, part) in zip(sums, parts)]
    for (ref, _), total in zip(parts, sums):
        ref[...] = total.astype(ref.dtype)


def feed(a, at, e, et, mine, other, first, chunks, carried, images, span):
    tokens, width = a.shape
    half = mine.shape[1]
    tiles = SLAB // TILE
    up = pl.BlockSpec((1, half, TILE), lambda g: (first + 2 * (g // tiles), 0, g % tiles))
    down = pl.BlockSpec((1, half, TILE), lambda g: (first + 1 + 2 * (g // tiles), 0, g % tiles))
    grads = pl.BlockSpec((half, TILE), lambda g: (0, g))
    full = whole((tokens, width))
    turned = whole((images, width, span))
    fresh = carried is None
    return pl.pallas_call(
        functools.partial(feed_kernel, fresh, images, span),
        grid=(chunks * tiles,),
        in_specs=[full, turned, full, turned, up, up, down, down] + ([] if fresh else [full, full]),
        out_specs=[full, full] + [grads] * 4,
        out_shape=[shaped((tokens, width), wide)] * 2 + [shaped((half, chunks * SLAB), low)] * 4,
        compiler_params=params(),
        name="feed",
    )(a, at, e, et, mine, other, mine, other, *(() if fresh else carried))


def turn_back_kernel(x_out_ref, da_ref, resid_ref, e_ref, vec_ref, wo_ref, mixed_ref, rden_ref, fq_ref,
                     out_ref, dres_ref, branch_ref, dn_ref, w_ref, state_ref, sums_ref):
    width = da_ref.shape[1]
    resid = resid_ref[...]
    out_ref[...] = (resid + x_out_ref[...]).astype(low)
    unit, scale = normalised(resid)
    da = da_ref[...]

    @pl.when(pl.program_id(0) == 0)
    def _():
        sums_ref[...] = jnp.zeros_like(sums_ref)

    sums_ref[0:1, :] += jnp.sum(da * unit, axis=0, keepdims=True)
    sums_ref[1:2, :] += jnp.sum(da, axis=0, keepdims=True)
    p = da * vec_ref[2:3, :]
    back = p - jnp.mean(p, axis=-1, keepdims=True) - unit * jnp.mean(p * unit, axis=-1, keepdims=True)
    dres = e_ref[...].astype(wide) + scale * back
    dres_ref[...] = dres
    branch = dres.astype(low)
    branch_ref[...] = branch
    dmixed = mt(branch, wo_ref[...]).astype(low).astype(wide)
    dnumer = dmixed * rden_ref[...]
    dn_ref[...] = dnumer.astype(low)
    w_ref[...] = (-dnumer * mixed_ref[...].astype(wide)).astype(low)
    for pair in range(width // PAIR):
        lanes = slice(pair * PAIR, (pair + 1) * PAIR)
        query = fq_ref[:, lanes]
        state_ref[0, pair, :HEAD_DIM, :] = fold_state(tm(dn_ref[:, lanes], query))
        total = jnp.sum(fold_state(tm(w_ref[:, lanes], query)), axis=0, keepdims=True)
        state_ref[0, pair, HEAD_DIM:, :] = jnp.broadcast_to(total, (STATE_ROWS - HEAD_DIM, PAIR))


def turn_back(x_out, da, resid, e, vec, wo, mixed, rden, fq, images, span):
    tokens, width = da.shape
    rows = pl.BlockSpec((span, width), lambda b: (b, 0))
    state = (images, width // PAIR, STATE_ROWS, PAIR)
    return pl.pallas_call(
        turn_back_kernel,
        grid=(images,),
        in_specs=[rows, rows, rows, rows, whole(vec.shape), whole(wo.shape), rows, rows, rows],
        out_specs=[rows] * 5 + [pl.BlockSpec((1,) + state[1:], lambda b: (b, 0, 0, 0)), whole((8, width))],
        out_shape=[
            shaped((tokens, width), low),
            shaped((tokens, width), wide),
            shaped((tokens, width), low),
            shaped((tokens, width), low),
            shaped((tokens, width), low),
            shaped(state, wide),
            shaped((8, width), wide),
        ],
        compiler_params=params(),
        name="turn_back",
    )(x_out, da, resid, e, vec, wo, mixed, rden, fq)


def attend_back_kernel(span, fq_ref, fk_ref, v_ref, dn_ref, w_ref, prior_ref, dq_ref, dfk_ref, dv_ref):
    query, key, value = fq_ref[...], fk_ref[...], v_ref[...]
    grads = jnp.concatenate([dn_ref[...], w_ref[...]], axis=1)
    ones = jnp.ones_like(value)
    extended = jnp.concatenate([value, ones], axis=1)
    own = first_head(span)
    own_twice = jnp.concatenate([own, own], axis=1)
    zero = jnp.zeros_like(query)
    rows = lax.broadcasted_iota(jnp.int32, (span, span), 0)
    columns = lax.broadcasted_iota(jnp.int32, (span, span), 1)
    folded = prior_ref[0, 0]
    matrix = jnp.concatenate(
        [unfold_state(folded[:HEAD_DIM]), unfold_total(folded[HEAD_DIM : HEAD_DIM + 1])], axis=0
    )
    high, rest = split_low(matrix)
    dfq = mm(grads, high) + mm(grads, rest)
    dfk = jnp.zeros((span, PAIR), wide)
    dv = jnp.zeros((span, PAIR), wide)
    for head in range(2):
        mask = own if head == 0 else jnp.logical_not(own)
        both = own_twice if head == 0 else jnp.logical_not(own_twice)
        head_grads = jnp.where(both, grads, jnp.zeros_like(grads))
        head_query = jnp.where(mask, query, zero)
        head_key = jnp.where(mask, key, zero)
        dscore = jnp.where(rows >= columns, mt(head_grads, extended), 0.0).astype(low)
        dfq += mm(dscore, head_key)
        dscore_t = jnp.where(rows <= columns, mt(extended, head_grads), 0.0).astype(low)
        dfk += mm(dscore_t, head_query)
        score_t = jnp.where(rows <= columns, mt(head_key, query), 0.0).astype(low)
        dv += mm(score_t, head_grads[:, :PAIR])
    dq_ref[...] = (dfq * jnp.minimum(query.astype(wide), 1.0)).astype(low)
    dfk_ref[...] = dfk
    dv_ref[...] = dv


def attend_back(fq, fk, v, dn, w, prior, images, span):
    tokens, width = fq.shape
    block = pl.BlockSpec((span, PAIR), lambda b, p: (b, p))
    return pl.pallas_call(
        functools.partial(attend_back_kernel, span),
        grid=(images, width // PAIR),
        in_specs=[block] * 5 + [pl.BlockSpec((1, 1) + prior.shape[2:], lambda b, p: (b, p, 0, 0))],
        out_specs=[block] * 3,
        out_shape=[shaped((tokens, width), low), shaped((tokens, width), wide), shaped((tokens, width), wide)],
        compiler_params=params(),
        name="attend_back",
    )(fq, fk, v, dn, w, prior)


def finish_kernel(images, span, dq_ref, dfk_ref, dvl_ref, fk_ref, v_ref, later_ref, at_ref,
                  dk_ref, dv_ref, gm_ref, go_ref):
    half = gm_ref.shape[1]
    for image in range(images):
        rows = slice(image * span, (image + 1) * span)
        for pair in range(GROUP // PAIR):
            lanes = slice(pair * PAIR, (pair + 1) * PAIR)
            folded = later_ref[image, pair]
            high, rest = split_low(unfold_state(folded[:HEAD_DIM]))
            key, value = fk_ref[rows, lanes], v_ref[rows, lanes]
            dfk = dfk_ref[rows, lanes] + folded[HEAD_DIM : HEAD_DIM + 1]
            dfk = dfk + mm(jnp.concatenate([value, value], axis=1), jnp.concatenate([high, rest], axis=0))
            dv = dvl_ref[rows, lanes] + mt(
                jnp.concatenate([key, key], axis=1), jnp.concatenate([high, rest], axis=1)
            )
            dk_ref[rows, lanes] = (dfk * jnp.minimum(key.astype(wide), 1.0)).astype(low)
            dv_ref[rows, lanes] = dv.astype(low)
    for k, ref in enumerate((dq_ref, dk_ref, dv_ref)):
        gm_ref[k] = mm(at_ref[:half, :], ref[...]).astype(gm_ref.dtype)
        go_ref[k] = mm(at_ref[half:, :], ref[...]).astype(go_ref.dtype)


def finish(dq, dfk, dv, fk, v, later, at, images, span):
    tokens, width = dq.shape
    half = width // 2
    column = pl.BlockSpec((tokens, GROUP), lambda g: (0, g))
    grads = pl.BlockSpec((3, half, GROUP), lambda g: (0, 0, g))
    return pl.pallas_call(
        functools.partial(finish_kernel, images, span),
        grid=(width // GROUP,),
        in_specs=[column] * 5
        + [pl.BlockSpec((images, GROUP // PAIR) + later.shape[2:], lambda g: (0, g, 0, 0)), whole(at.shape)],
        out_specs=[column, column, grads, grads],
        out_shape=[shaped((tokens, width), low)] * 2 + [shaped((3, half, width), low)] * 2,
        compiler_params=params(),
        name="finish",
    )(dq, dfk, dv, fk, v, later, at)


def enter_kernel(dq_ref, dk_ref, dv_ref, mine_ref, other_ref, x_ref, dres_ref, vec_ref, grad_ref, sums_ref):
    width = x_ref.shape[1]
    parts = []
    for weight in (mine_ref, other_ref):
        parts.append(
            mt(dq_ref[...], weight[0, :, :width])
            + mt(dk_ref[...], weight[1, :, :width])
            + mt(dv_ref[...], weight[2, :, :width])
        )
    da = jnp.concatenate(parts, axis=1)
    unit, scale = normalised(x_ref[...].astype(wide))

    @pl.when(pl.program_id(0) == 0)
    def _():
        sums_ref[...] = jnp.zeros_like(sums_ref)

    sums_ref[0:1, :] += jnp.sum(da * unit, axis=0, keepdims=True)
    sums_ref[1:2, :] += jnp.sum(da, axis=0, keepdims=True)
    p = da * vec_ref[0:1, :]
    back = p - jnp.mean(p, axis=-1, keepdims=True) - unit * jnp.mean(p * unit, axis=-1, keepdims=True)
    grad_ref[...] = (dres_ref[...] + scale * back).astype(low)


def enter(dq, dk, dv, mine, other, x, dres, vec, images, span):
    tokens, width = x.shape
    rows = pl.BlockSpec((span, width), lambda b: (b, 0))
    return pl.pallas_call(
        enter_kernel,
        grid=(images,),
        in_specs=[rows, rows, rows, whole(mine.shape), whole(other.shape), rows, rows, whole(vec.shape)],
        out_specs=[rows, whole((8, width))],
        out_shape=[shaped((tokens, width), low), shaped((8, width), wide)],
        compiler_params=params(),
        name="enter",
    )(dq, dk, dv, mine, other, x, dres, vec)


def adam_update(master, moment, second, average, gradient, factor, rate):
    clipped = gradient * factor
    moment = beta_first * moment + (1.0 - beta_first) * clipped
    second = beta_second * second + (1.0 - beta_second) * clipped * clipped
    first_hat = moment / (1.0 - beta_first**STEP)
    second_hat = second / (1.0 - beta_second**STEP)
    master = master - rate * (first_hat / (jnp.sqrt(second_hat) + eps_adam) + weight_decay * master)
    average = average_decay * average + (1.0 - average_decay) * master
    return (master, moment, second, average)


def flip_pairs(count, bit):
    return [(i, i ^ bit) for i in range(count)]


def powers(count):
    return [1 << k for k in range(count.bit_length() - 1)]


def flip(array, axis, bit=1):
    return lax.ppermute(array, axis, flip_pairs(lax.axis_size(axis), bit))


def scatter_axis(array, axis, bits):
    count = lax.axis_size(axis)
    place = lax.axis_index(axis)
    left = powers(count)[::-1]
    array = array.reshape((2,) * len(left) + array.shape[1:])
    for bit in bits:
        dim = left.index(bit)
        own = (place // bit) % 2
        came = flip(lax.dynamic_index_in_dim(array, 1 - own, dim, False).astype(low), axis, bit)
        array = lax.dynamic_index_in_dim(array, own, dim, False) + came.astype(wide)
        left.remove(bit)
    return array


def scatter_rows(kept, sent, order):
    spots, slices = lax.axis_size("pos"), lax.axis_size("img")
    came = flip(sent.astype(low), "core")
    rest = kept.astype(wide) + came.astype(wide)
    bits = powers(spots)[::order]
    rest = scatter_axis(rest.reshape((spots, -1) + rest.shape[1:]), "pos", bits)
    return scatter_axis(rest.reshape((slices, -1) + rest.shape[1:]), "img", powers(slices))


def passing(own, backward):
    total = own
    outside = jnp.zeros_like(own)
    for axis in ("core", "pos"):
        for bit in powers(lax.axis_size(axis)):
            came = flip(total.astype(low), axis, bit).astype(wide)
            upper = (lax.axis_index(axis) // bit) % 2
            counts = upper == (0 if backward else 1)
            outside = outside + jnp.where(counts, came, 0.0)
            total = total + came
    return outside


def body(
    images,
    cotangent,
    attention_weight,
    feedforward_weight,
    norm_vectors,
    attention_moment,
    feedforward_moment,
    norm_moment,
    attention_second,
    feedforward_second,
    norm_second,
    attention_average,
    feedforward_average,
    norm_average,
):
    count, span, width = images.shape
    tokens = count * span
    spots = lax.axis_size("pos")
    slices = lax.axis_size("img")
    core = lax.axis_index("core")
    owned = attention_weight.shape[1]
    hidden_width = feedforward_weight.shape[2]
    slabs = hidden_width // SLAB

    def gather(array):
        mine = lax.all_gather(array, ("pos", "img"), axis=1, tiled=True)
        return mine, flip(mine, "core")

    def to_mine_first(array):
        parts = array.reshape(array.shape[:-1] + (spots, 2, -1))
        straight = jnp.swapaxes(parts, -3, -2).reshape(array.shape)
        turned = jnp.swapaxes(parts[..., ::-1, :], -3, -2).reshape(array.shape)
        return jnp.where(core == 0, straight, turned)

    def from_mine_first(array):
        parts = array.reshape(array.shape[:-1] + (2, spots, -1))
        straight = jnp.swapaxes(parts, -3, -2).reshape(array.shape)
        turned = jnp.swapaxes(parts[..., ::-1, :, :], -3, -2).reshape(array.shape)
        return jnp.where(core == 0, straight, turned)

    vectors = jnp.pad(norm_vectors.astype(low).T[None], ((0, 2), (0, 0), (0, 124)))
    first = jnp.concatenate([attention_weight[:3].astype(low), vectors], axis=2)
    feed_low = feedforward_weight.astype(low).reshape(2, owned, slabs, SLAB)
    feed_low = jnp.transpose(feed_low, (2, 0, 1, 3)).reshape(2 * slabs, owned, SLAB)
    second = jnp.concatenate([attention_weight[3:].astype(low), feed_low[:slabs]], axis=0)
    third = feed_low[slabs:]
    first_mine, first_other = gather(first)
    second_mine, second_other = gather(second)
    third_mine, third_other = gather(third)

    x = to_mine_first(images.reshape(tokens, width))
    e = to_mine_first(cotangent.reshape(tokens, width))
    et = turn(e, count, span)
    vec = jnp.concatenate([first_mine[0, :, width : width + 4], first_other[0, :, width : width + 4]], axis=0)
    vec = vec.astype(wide).T

    fq, fk, v, a1, a1t, state = project(x, vec, first_mine, first_other, count, span)
    prior = passing(state, False)
    num, den = attend(fq, fk, v, count, span)
    wo = jnp.stack([second_mine[0].reshape(spots, -1, width), second_other[0].reshape(spots, -1, width)], axis=1)
    wo = jnp.where(core == 0, wo, wo[:, ::-1]).reshape(width, width)
    wo = to_mine_first(wo)
    mixed, rden, resid, a2, a2t = mix(x, vec, wo, fq, num, den, prior, count, span)

    early = feed(a2, a2t, e, et, second_mine, second_other, 1, slabs // 2, None, count, span)
    late = feed(a2, a2t, e, et, third_mine, third_other, 0, slabs - slabs // 2, early[:2], count, span)
    feed_shards = []
    for group in (early, late):
        up_mine, up_other, down_mine, down_other = group[2:]
        feed_shards.append((scatter_rows(up_mine, up_other, 1), scatter_rows(down_mine, down_other, -1)))
    output, dres, branch, dn, w, dstate, sums_second = turn_back(
        late[0], late[1], resid, e, vec, wo, mixed, rden, fq, count, span
    )
    later = passing(dstate, True)
    grad_out = tm(mixed, branch).reshape(spots, 2, -1, width)
    out_other = lax.dynamic_index_in_dim(grad_out, 1 - core, 1, False).reshape(-1, width).astype(low)
    out_mine = lax.dynamic_index_in_dim(grad_out, core, 1, False).reshape(-1, width)
    out_other = jnp.roll(out_other, width // 2, axis=1)
    dq, dfk, dvl = attend_back(fq, fk, v, dn, w, prior, count, span)
    dk, dv, inner_mine, inner_other = finish(dq, dfk, dvl, fk, v, later, a1t, count, span)
    inner_shards = [scatter_rows(inner_mine[k], inner_other[k], 1 if k % 2 else -1) for k in range(3)]
    input_grad, sums_first = enter(dq, dk, dv, first_mine, first_other, x, dres, vec, count, span)
    out_shard = from_mine_first(scatter_rows(out_mine, out_other, 1))
    vector_grad = jnp.concatenate([sums_first[:2], sums_second[:2]], axis=0).T
    vector_shard = scatter_rows(vector_grad[: width // 2], vector_grad[width // 2 :], 1).T

    attn_shard = jnp.stack(inner_shards + [out_shard])
    feed_shard = jnp.stack([jnp.concatenate([pair[k] for pair in feed_shards], axis=1) for k in range(2)])

    local_squares = (
        jnp.sum(attn_shard * attn_shard) + jnp.sum(feed_shard * feed_shard) + jnp.sum(vector_shard * vector_shard)
    )
    grad_norm = jnp.sqrt(lax.psum(local_squares, ("pos", "core", "img")))
    factor = clip_bound / jnp.maximum(grad_norm, clip_bound)
    attn_new = adam_update(
        attention_weight, attention_moment, attention_second, attention_average, attn_shard, factor, learn_rate
    )
    feed_new = adam_update(
        feedforward_weight, feedforward_moment, feedforward_second, feedforward_average, feed_shard, factor, learn_rate
    )
    norm_new = adam_update(norm_vectors, norm_moment, norm_second, norm_average, vector_shard, factor, norm_rate)
    output = from_mine_first(output).reshape(images.shape)
    input_grad = from_mine_first(input_grad).reshape(images.shape)
    return (output, input_grad, grad_norm) + attn_new + feed_new + norm_new


def solution(mesh):
    seq, img = mesh.devices.shape
    inner = Mesh(mesh.devices.reshape(seq // 2, 2, img), ("pos", "core", "img"))
    tokens = P("img", ("pos", "core"), None)
    rows = P(None, ("pos", "core", "img"), None)
    vectors = P(None, ("pos", "core", "img"))
    group = (rows, rows, vectors)
    return jax.shard_map(
        body,
        mesh=inner,
        in_specs=(tokens, tokens) + group * 4,
        out_specs=(tokens, tokens, P()) + (rows,) * 8 + (vectors,) * 4,
        check_vma=False,
    )
```

```python
import functools

import jax
import jax.numpy as jnp
from jax import lax
from jax.experimental import pallas as pl
from jax.experimental.pallas import tpu as pltpu
from jax.sharding import Mesh
from jax.sharding import PartitionSpec as P

HEADS = 16
HEAD_DIM = 64
STEP = 10

beta_first = 0.9
beta_second = 0.95
learn_rate = 0.02
norm_rate = 0.2
weight_decay = 0.1
average_decay = 0.75
clip_bound = 1.0
eps_norm = 1e-05
eps_adam = 1e-08

PAIR = 2 * HEAD_DIM
STATE_ROWS = HEAD_DIM + 16
SLAB = 1024
TILE = 512
GROUP = 256
VMEM_BYTES = 56 * 1024 * 1024

low = jnp.bfloat16
wide = jnp.float32


def params():
    return pltpu.CompilerParams(vmem_limit_bytes=VMEM_BYTES)


def cost(products, elements):
    return pl.CostEstimate(flops=2 * products, bytes_accessed=elements, transcendentals=0)


def launch(kernel, tokens, in_specs, **keys):
    known, extra = len(in_specs), len(tokens)

    def run(*refs):
        kernel(*refs[:known], *refs[known + extra :])

    call = pl.pallas_call(
        run, in_specs=list(in_specs) + [pl.BlockSpec(memory_space=pl.ANY)] * extra, compiler_params=params(), **keys
    )
    return lambda *args: call(*args, *tokens)


def shaped(shape, kind):
    return jax.ShapeDtypeStruct(shape, kind)


def whole(shape):
    return pl.BlockSpec(shape, lambda *_: (0,) * len(shape))


def mm(left, right):
    return lax.dot_general(left, right, (((1,), (0,)), ((), ())), preferred_element_type=wide)


def mt(left, right):
    return lax.dot_general(left, right, (((1,), (1,)), ((), ())), preferred_element_type=wide)


def tm(left, right):
    return lax.dot_general(left, right, (((0,), (0,)), ((), ())), preferred_element_type=wide)


def first_head(rows):
    return lax.broadcasted_iota(jnp.int32, (rows, PAIR), 1) < HEAD_DIM


def fold_state(product):
    return jnp.where(first_head(HEAD_DIM), product[:HEAD_DIM], product[HEAD_DIM:])


def unfold_state(folded):
    own = first_head(HEAD_DIM)
    zero = jnp.zeros_like(folded)
    return jnp.concatenate([jnp.where(own, folded, zero), jnp.where(own, zero, folded)], axis=0)


def unfold_total(row):
    tall = jnp.broadcast_to(row, (PAIR, PAIR))
    lanes = lax.broadcasted_iota(jnp.int32, (PAIR, PAIR), 1) < HEAD_DIM
    rows = lax.broadcasted_iota(jnp.int32, (PAIR, PAIR), 0) < HEAD_DIM
    return jnp.where(lanes == rows, tall, jnp.zeros_like(tall))


def split_low(values):
    high = values.astype(low)
    return high, (values - high.astype(wide)).astype(low)


def normalised(values):
    centre = jnp.mean(values, axis=-1, keepdims=True)
    centred = values - centre
    spread = jnp.mean(centred * centred, axis=-1, keepdims=True)
    scale = lax.rsqrt(spread + eps_norm)
    return centred * scale, scale


def project_kernel(images, span, x_ref, vec_ref, am_ref, ao_ref, bm_ref, bo_ref, fq_ref, fk_ref, v_ref, a_ref, at_ref, state_ref):
    half = am_ref.shape[1]
    early = pl.program_id(0) < pl.num_programs(0) // 2

    @pl.when(pl.program_id(0) == 0)
    def _():
        gain, shift = vec_ref[0:1, :], vec_ref[1:2, :]
        step = span // 3
        for start in range(0, images * span, step):
            rows = slice(start, start + step)
            unit, _ = normalised(x_ref[rows, :].astype(wide))
            a_ref[rows, :] = (unit * gain + shift).astype(low)
        at_ref[...] = a_ref[...].T

    normed = a_ref[...]
    left, right = normed[:, :half], normed[:, half:]

    def product(k):
        mine = jnp.where(early, am_ref[k], bm_ref[k])
        other = jnp.where(early, ao_ref[k], bo_ref[k])
        return mm(left, mine) + mm(right, other)

    def feature(raw):
        return jnp.where(raw > 0, raw + 1.0, jnp.exp(jnp.minimum(raw, 0.0))).astype(low)

    fk_ref[...] = feature(product(1))
    v_ref[...] = product(2).astype(low)
    fq_ref[...] = feature(product(0))
    ones = jnp.ones((16, span), low)
    for image in range(images):
        rows = slice(image * span, (image + 1) * span)
        for pair in range(GROUP // PAIR):
            lanes = slice(pair * PAIR, (pair + 1) * PAIR)
            key, value = fk_ref[rows, lanes], v_ref[rows, lanes]
            state_ref[image, pair, :HEAD_DIM, :] = fold_state(tm(value, key))
            state_ref[image, pair, HEAD_DIM:, :] = mm(ones, key)


def project(x, vec, first, second, images, span, tokens=()):
    rows_, width = x.shape
    half = first[0].shape[1]
    groups = width // GROUP
    pairs = GROUP // PAIR
    weight = pl.BlockSpec((3, half, GROUP), lambda g: (0, 0, jnp.minimum(g, groups // 2 - 1)))
    later = pl.BlockSpec((3, half, GROUP), lambda g: (0, 0, jnp.maximum(g - groups // 2, 0)))
    column = pl.BlockSpec((rows_, GROUP), lambda g: (0, g))
    return launch(
        functools.partial(project_kernel, images, span),
        tokens,
        grid=(groups,),
        in_specs=[whole((rows_, width)), whole(vec.shape), weight, weight, later, later],
        out_specs=[
            column,
            column,
            column,
            whole((rows_, width)),
            whole((width, rows_)),
            pl.BlockSpec((images, pairs, STATE_ROWS, PAIR), lambda g: (0, g, 0, 0)),
        ],
        out_shape=[
            shaped((rows_, width), low),
            shaped((rows_, width), low),
            shaped((rows_, width), low),
            shaped((rows_, width), low),
            shaped((width, rows_), low),
            shaped((images, width // PAIR, STATE_ROWS, PAIR), wide),
        ],
        cost_estimate=cost(3 * rows_ * width * width, 8 * width * width + 12 * rows_ * width),
        name="project",
    )(x, vec, *first, *second)


def attend_kernel(span, fq_ref, fk_ref, v_ref, num_ref, den_ref):
    own = first_head(span)
    causal = lax.broadcasted_iota(jnp.int32, (span, span), 0) >= lax.broadcasted_iota(jnp.int32, (span, span), 1)
    for pair in range(GROUP // PAIR):
        lanes = slice(pair * PAIR, (pair + 1) * PAIR)
        query, key, value = fq_ref[:, lanes], fk_ref[:, lanes], v_ref[:, lanes]
        zero = jnp.zeros_like(query)
        total = None
        for head in range(2):
            mask = own if head == 0 else jnp.logical_not(own)
            scores = mt(jnp.where(mask, query, zero), key)
            scores = jnp.where(causal, scores, 0.0).astype(low)
            ones = jnp.where(mask, jnp.ones_like(value), zero)
            part = mm(scores, jnp.concatenate([jnp.where(mask, value, zero), ones], axis=1))
            total = part if total is None else total + part
        num_ref[:, lanes] = total[:, :PAIR]
        den_ref[:, lanes] = total[:, PAIR:]


def attend(fq, fk, v, images, span, tokens=()):
    rows, width = fq.shape
    block = pl.BlockSpec((span, GROUP), lambda b, p: (b, p))
    return launch(
        functools.partial(attend_kernel, span),
        tokens,
        grid=(images, width // GROUP),
        in_specs=[block] * 3,
        out_specs=[block] * 2,
        out_shape=[shaped((rows, width), wide)] * 2,
        cost_estimate=cost(16 * rows * span * width, 14 * rows * width),
        name="attend",
    )(fq, fk, v)


def mix_kernel(x_ref, vec_ref, wo_ref, fq_ref, num_ref, den_ref, prior_ref, mixed_ref, rden_ref, resid_ref, a_ref, at_ref):
    width = x_ref.shape[1]
    for pair in range(width // PAIR):
        lanes = slice(pair * PAIR, (pair + 1) * PAIR)
        folded = prior_ref[0, pair]
        matrix = jnp.concatenate(
            [unfold_state(folded[:HEAD_DIM]), unfold_total(folded[HEAD_DIM : HEAD_DIM + 1])], axis=0
        )
        high, rest = split_low(matrix)
        query = fq_ref[:, lanes]
        both = mt(jnp.concatenate([query, query], axis=1), jnp.concatenate([high, rest], axis=1))
        scale = 1.0 / (den_ref[:, lanes] + both[:, PAIR:])
        rden_ref[:, lanes] = scale
        mixed_ref[:, lanes] = ((num_ref[:, lanes] + both[:, :PAIR]) * scale).astype(low)
    resid = x_ref[...].astype(wide) + mm(mixed_ref[...], wo_ref[...])
    resid_ref[...] = resid
    unit, _ = normalised(resid)
    normed = (unit * vec_ref[2:3, :] + vec_ref[3:4, :]).astype(low)
    a_ref[...] = normed
    at_ref[...] = normed.T


def mix(x, vec, wo, fq, num, den, prior, images, span, tokens=()):
    rows_, width = x.shape
    rows = pl.BlockSpec((span, width), lambda b: (b, 0))
    return launch(
        mix_kernel,
        tokens,
        grid=(images,),
        in_specs=[
            rows,
            whole(vec.shape),
            whole(wo.shape),
            rows,
            rows,
            rows,
            pl.BlockSpec((1,) + prior.shape[1:], lambda b: (b, 0, 0, 0)),
        ],
        out_specs=[rows, rows, rows, rows, pl.BlockSpec((None, width, span), lambda b: (b, 0, 0))],
        out_shape=[
            shaped((rows_, width), low),
            shaped((rows_, width), wide),
            shaped((rows_, width), wide),
            shaped((rows_, width), low),
            shaped((images, width, span), low),
        ],
        cost_estimate=cost(4 * rows_ * width * width, 24 * rows_ * width + 2 * width * width),
        name="mix",
    )(x, vec, wo, fq, num, den, prior)


def turn_kernel(x_ref, out_ref):
    out_ref[...] = x_ref[...].T


def turn(x, images, span, tokens=()):
    rows_, width = x.shape
    return launch(
        turn_kernel,
        tokens,
        grid=(images,),
        in_specs=[pl.BlockSpec((span, width), lambda b: (b, 0))],
        out_specs=pl.BlockSpec((None, width, span), lambda b: (b, 0, 0)),
        out_shape=shaped((images, width, span), low),
        cost_estimate=cost(1, 8 * rows_ * width),
        name="turn",
    )(x)


gelu_scale = 0.7978845608028654
gelu_cubic = 0.044715


def feed_kernel(fresh, images, span, *refs):
    a_ref, at_ref, e_ref, et_ref, um_ref, uo_ref, dm_ref, do_ref = refs[:8]
    out_ref, da_ref, gum_ref, guo_ref, gdm_ref, gdo_ref = refs[-6:]
    half = um_ref.shape[1]

    @pl.when(pl.program_id(0) == 0)
    def _():
        if fresh:
            out_ref[...] = jnp.zeros_like(out_ref)
            da_ref[...] = jnp.zeros_like(da_ref)
        else:
            out_ref[...] = refs[8][...]
            da_ref[...] = refs[9][...]

    um, uo, dm, do = um_ref[0], uo_ref[0], dm_ref[0], do_ref[0]
    for image in range(images):
        rows = slice(image * span, (image + 1) * span)
        upper = mm(a_ref[rows, :half], um) + mm(a_ref[rows, half:], uo)
        grad = mm(e_ref[rows, :half], dm) + mm(e_ref[rows, half:], do)
        square = upper * upper
        bend = jnp.tanh(gelu_scale * upper * (1.0 + gelu_cubic * square))
        gate = 0.5 + 0.5 * bend
        hidden = (upper * gate).astype(low)
        slope = gate + 0.5 * upper * (1.0 - bend * bend) * (gelu_scale * (1.0 + 3.0 * gelu_cubic * square))
        dupper = (grad * slope).astype(low)
        out_ref[rows, :half] += mt(hidden, dm)
        out_ref[rows, half:] += mt(hidden, do)
        da_ref[rows, :half] += mt(dupper, um)
        da_ref[rows, half:] += mt(dupper, uo)
        parts = [
            (gdm_ref, mm(et_ref[image, :half, :], hidden)),
            (gdo_ref, mm(et_ref[image, half:, :], hidden)),
            (gum_ref, mm(at_ref[image, :half, :], dupper)),
            (guo_ref, mm(at_ref[image, half:, :], dupper)),
        ]
        if image == 0:
            sums = [part for _, part in parts]
        else:
            sums = [total + part for total, (_, part) in zip(sums, parts)]
    for (ref, _), total in zip(parts, sums):
        ref[...] = total.astype(ref.dtype)


def feed(a, at, e, et, up, down, skipped, carried, images, span, tokens=()):
    rows, width = a.shape
    half = up[0].shape[1]
    chunks = down[0].shape[0]
    tiles = SLAB // TILE
    above = pl.BlockSpec((1, half, TILE), lambda g: (skipped + g // tiles, 0, g % tiles))
    below = pl.BlockSpec((1, half, TILE), lambda g: (g // tiles, 0, g % tiles))
    grads = pl.BlockSpec((half, TILE), lambda g: (0, g))
    full = whole((rows, width))
    turned = whole((images, width, span))
    fresh = carried is None
    return launch(
        functools.partial(feed_kernel, fresh, images, span),
        tokens,
        grid=(chunks * tiles,),
        in_specs=[full, turned, full, turned, above, above, below, below] + ([] if fresh else [full, full]),
        out_specs=[full, full] + [grads] * 4,
        out_shape=[shaped((rows, width), wide)] * 2 + [shaped((half, chunks * SLAB), low)] * 4,
        cost_estimate=cost(6 * rows * width * chunks * SLAB, 8 * width * chunks * SLAB + 20 * rows * width),
        name="feed",
    )(a, at, e, et, *up, *down, *(() if fresh else carried))


def turn_back_kernel(x_out_ref, da_ref, resid_ref, e_ref, vec_ref, wo_ref, mixed_ref, rden_ref, fq_ref,
                     out_ref, dres_ref, branch_ref, dn_ref, w_ref, state_ref, sums_ref):
    width = da_ref.shape[1]
    resid = resid_ref[...]
    out_ref[...] = (resid + x_out_ref[...]).astype(low)
    unit, scale = normalised(resid)
    da = da_ref[...]

    @pl.when(pl.program_id(0) == 0)
    def _():
        sums_ref[...] = jnp.zeros_like(sums_ref)

    sums_ref[0:1, :] += jnp.sum(da * unit, axis=0, keepdims=True)
    sums_ref[1:2, :] += jnp.sum(da, axis=0, keepdims=True)
    p = da * vec_ref[2:3, :]
    back = p - jnp.mean(p, axis=-1, keepdims=True) - unit * jnp.mean(p * unit, axis=-1, keepdims=True)
    dres = e_ref[...].astype(wide) + scale * back
    dres_ref[...] = dres
    branch = dres.astype(low)
    branch_ref[...] = branch
    dmixed = mt(branch, wo_ref[...]).astype(low).astype(wide)
    dnumer = dmixed * rden_ref[...]
    dn_ref[...] = dnumer.astype(low)
    w_ref[...] = (-dnumer * mixed_ref[...].astype(wide)).astype(low)
    for pair in range(width // PAIR):
        lanes = slice(pair * PAIR, (pair + 1) * PAIR)
        query = fq_ref[:, lanes]
        state_ref[0, pair, :HEAD_DIM, :] = fold_state(tm(dn_ref[:, lanes], query))
        total = jnp.sum(fold_state(tm(w_ref[:, lanes], query)), axis=0, keepdims=True)
        state_ref[0, pair, HEAD_DIM:, :] = jnp.broadcast_to(total, (STATE_ROWS - HEAD_DIM, PAIR))


def turn_back(x_out, da, resid, e, vec, wo, mixed, rden, fq, images, span, tokens=()):
    rows_, width = da.shape
    rows = pl.BlockSpec((span, width), lambda b: (b, 0))
    state = (images, width // PAIR, STATE_ROWS, PAIR)
    return launch(
        turn_back_kernel,
        tokens,
        grid=(images,),
        in_specs=[rows, rows, rows, rows, whole(vec.shape), whole(wo.shape), rows, rows, rows],
        out_specs=[rows] * 5 + [pl.BlockSpec((1,) + state[1:], lambda b: (b, 0, 0, 0)), whole((8, width))],
        out_shape=[
            shaped((rows_, width), low),
            shaped((rows_, width), wide),
            shaped((rows_, width), low),
            shaped((rows_, width), low),
            shaped((rows_, width), low),
            shaped(state, wide),
            shaped((8, width), wide),
        ],
        cost_estimate=cost(5 * rows_ * width * width, 30 * rows_ * width),
        name="turn_back",
    )(x_out, da, resid, e, vec, wo, mixed, rden, fq)


def attend_back_kernel(span, fq_ref, fk_ref, v_ref, dn_ref, w_ref, prior_ref, dq_ref, dfk_ref, dv_ref):
    own = first_head(span)
    own_twice = jnp.concatenate([own, own], axis=1)
    rows = lax.broadcasted_iota(jnp.int32, (span, span), 0)
    columns = lax.broadcasted_iota(jnp.int32, (span, span), 1)
    for pair in range(GROUP // PAIR):
        lanes = slice(pair * PAIR, (pair + 1) * PAIR)
        query, key, value = fq_ref[:, lanes], fk_ref[:, lanes], v_ref[:, lanes]
        grads = jnp.concatenate([dn_ref[:, lanes], w_ref[:, lanes]], axis=1)
        extended = jnp.concatenate([value, jnp.ones_like(value)], axis=1)
        zero = jnp.zeros_like(query)
        folded = prior_ref[0, pair]
        matrix = jnp.concatenate(
            [unfold_state(folded[:HEAD_DIM]), unfold_total(folded[HEAD_DIM : HEAD_DIM + 1])], axis=0
        )
        high, rest = split_low(matrix)
        dfq = mm(grads, high) + mm(grads, rest)
        dfk = jnp.zeros((span, PAIR), wide)
        dv = jnp.zeros((span, PAIR), wide)
        for head in range(2):
            mask = own if head == 0 else jnp.logical_not(own)
            both = own_twice if head == 0 else jnp.logical_not(own_twice)
            head_grads = jnp.where(both, grads, jnp.zeros_like(grads))
            head_query = jnp.where(mask, query, zero)
            head_key = jnp.where(mask, key, zero)
            dscore = jnp.where(rows >= columns, mt(head_grads, extended), 0.0).astype(low)
            dfq += mm(dscore, head_key)
            dscore_t = jnp.where(rows <= columns, mt(extended, head_grads), 0.0).astype(low)
            dfk += mm(dscore_t, head_query)
            score_t = jnp.where(rows <= columns, mt(head_key, query), 0.0).astype(low)
            dv += mm(score_t, head_grads[:, :PAIR])
        dq_ref[:, lanes] = (dfq * jnp.minimum(query.astype(wide), 1.0)).astype(low)
        dfk_ref[:, lanes] = dfk
        dv_ref[:, lanes] = dv


def attend_back(image, fq, fk, v, dn, w, prior, span, tokens=()):
    width = fq.shape[1]
    block = pl.BlockSpec((span, GROUP), lambda p: (image, p))
    column = pl.BlockSpec((span, GROUP), lambda p: (0, p))
    return launch(
        functools.partial(attend_back_kernel, span),
        tokens,
        grid=(width // GROUP,),
        in_specs=[block] * 5 + [pl.BlockSpec((1, GROUP // PAIR) + prior.shape[2:], lambda p: (image, p, 0, 0))],
        out_specs=[column] * 3,
        out_shape=[shaped((span, width), low), shaped((span, width), wide), shaped((span, width), wide)],
        cost_estimate=cost(32 * span * span * width, 24 * span * width),
        name="attend_back",
    )(fq, fk, v, dn, w, prior)


def finish_kernel(images, span, *refs):
    locals_ = [refs[3 * image : 3 * image + 3] for image in range(images)]
    fk_ref, v_ref, later_ref, at_ref, dq_ref, dk_ref, dv_ref, mine_ref, other_ref = refs[3 * images :]
    half = mine_ref.shape[1]
    for image in range(images):
        rows = slice(image * span, (image + 1) * span)
        dqi_ref, dfk_ref, dvl_ref = locals_[image]
        dq_ref[rows, :] = dqi_ref[...]
        for pair in range(GROUP // PAIR):
            lanes = slice(pair * PAIR, (pair + 1) * PAIR)
            folded = later_ref[image, pair]
            high, rest = split_low(unfold_state(folded[:HEAD_DIM]))
            key, value = fk_ref[rows, lanes], v_ref[rows, lanes]
            dfk = dfk_ref[:, lanes] + folded[HEAD_DIM : HEAD_DIM + 1]
            dfk = dfk + mm(jnp.concatenate([value, value], axis=1), jnp.concatenate([high, rest], axis=0))
            dv = dvl_ref[:, lanes] + mt(
                jnp.concatenate([key, key], axis=1), jnp.concatenate([high, rest], axis=1)
            )
            dk_ref[rows, lanes] = (dfk * jnp.minimum(key.astype(wide), 1.0)).astype(low)
            dv_ref[rows, lanes] = dv.astype(low)
    for k, ref in enumerate((dq_ref, dk_ref, dv_ref)):
        mine_ref[k] = mm(at_ref[:half, :], ref[...]).astype(low)
        other_ref[k] = mm(at_ref[half:, :], ref[...]).astype(low)


def finish(side, parts, fk, v, later, at, images, span, tokens=()):
    rows, width = fk.shape
    half = width // 2
    groups = half // GROUP
    column = pl.BlockSpec((rows, GROUP), lambda g: (0, side * groups + g))
    part = pl.BlockSpec((span, GROUP), lambda g: (0, side * groups + g))
    result = pl.BlockSpec((rows, GROUP), lambda g: (0, g))
    grads = pl.BlockSpec((3, half, GROUP), lambda g: (0, 0, g))
    state = pl.BlockSpec((images, GROUP // PAIR) + later.shape[2:], lambda g: (0, side * groups + g, 0, 0))
    return launch(
        functools.partial(finish_kernel, images, span),
        tokens,
        grid=(groups,),
        in_specs=[part] * (3 * images) + [column] * 2 + [state, whole(at.shape)],
        out_specs=[result] * 3 + [grads, grads],
        out_shape=[shaped((rows, half), low)] * 3 + [shaped((3, half, half), low)] * 2,
        cost_estimate=cost(2 * rows * width * width, 15 * rows * width),
        name="finish",
    )(*[array for image in parts for array in image], fk, v, later, at)


def enter_kernel(*refs):
    grad_refs, (am_ref, ao_ref, bm_ref, bo_ref) = (refs[:3], refs[3:6]), refs[6:10]
    x_ref, dres_ref, vec_ref, grad_ref, sums_ref = refs[10:]
    half = x_ref.shape[1] // 2
    parts = []
    for weights in ((am_ref, bm_ref), (ao_ref, bo_ref)):
        total = None
        for side, weight in zip(grad_refs, weights):
            for k, ref in enumerate(side):
                part = mt(ref[...], weight[k, :, :half])
                total = part if total is None else total + part
        parts.append(total)
    da = jnp.concatenate(parts, axis=1)
    unit, scale = normalised(x_ref[...].astype(wide))

    @pl.when(pl.program_id(0) == 0)
    def _():
        sums_ref[...] = jnp.zeros_like(sums_ref)

    sums_ref[0:1, :] += jnp.sum(da * unit, axis=0, keepdims=True)
    sums_ref[1:2, :] += jnp.sum(da, axis=0, keepdims=True)
    p = da * vec_ref[0:1, :]
    back = p - jnp.mean(p, axis=-1, keepdims=True) - unit * jnp.mean(p * unit, axis=-1, keepdims=True)
    grad_ref[...] = (dres_ref[...] + scale * back).astype(low)


def enter(left, right, first, second, x, dres, vec, images, span, tokens=()):
    rows_, width = x.shape
    rows = pl.BlockSpec((span, width), lambda b: (b, 0))
    half = pl.BlockSpec((span, width // 2), lambda b: (b, 0))
    return launch(
        enter_kernel,
        tokens,
        grid=(images,),
        in_specs=[half] * 6 + [whole(part.shape) for part in (*first, *second)] + [rows, rows, whole(vec.shape)],
        out_specs=[rows, whole((8, width))],
        out_shape=[shaped((rows_, width), low), shaped((8, width), wide)],
        cost_estimate=cost(5 * rows_ * width * width, 30 * rows_ * width),
        name="enter",
    )(*left, *right, *first, *second, x, dres, vec)


def adam_update(master, moment, second, average, gradient, factor, rate):
    clipped = gradient * factor
    moment = beta_first * moment + (1.0 - beta_first) * clipped
    second = beta_second * second + (1.0 - beta_second) * clipped * clipped
    first_hat = moment / (1.0 - beta_first**STEP)
    second_hat = second / (1.0 - beta_second**STEP)
    master = master - rate * (first_hat / (jnp.sqrt(second_hat) + eps_adam) + weight_decay * master)
    average = average_decay * average + (1.0 - average_decay) * master
    return (master, moment, second, average)


def flip_pairs(count, bit):
    return [(i, i ^ bit) for i in range(count)]


def powers(count):
    return [1 << k for k in range(count.bit_length() - 1)]


def flip(array, axis, bit=1):
    return lax.ppermute(array, axis, flip_pairs(lax.axis_size(axis), bit))


class Scatter:
    def __init__(self, kept, sent, order):
        self.kept, self.sent, self.axis, self.bit = kept, sent, "core", 1
        self.order = order
        self.left = None

    def start(self):
        self.came = flip(self.sent.astype(low), self.axis, self.bit)

    def finish(self):
        rest = self.kept.astype(wide) + self.came.astype(wide)
        if self.axis == "core":
            self.open(rest, "pos", self.order)
        elif self.left:
            self.choose(rest)
        elif self.axis == "pos":
            self.open(rest, "img", 1)
        else:
            self.result = rest
            return []
        return [self.sent]

    def open(self, rest, axis, order):
        count = lax.axis_size(axis)
        self.axis, self.left, self.bits = axis, powers(count)[::-1], powers(count)[::order]
        at = rest.ndim - 2
        rest = rest.reshape(rest.shape[:at] + (2,) * len(self.left) + (-1,) + rest.shape[-1:])
        self.choose(rest)

    def choose(self, rest):
        self.bit = next(bit for bit in self.bits if bit in self.left)
        dim = rest.ndim - 2 - len(self.left) + self.left.index(self.bit)
        own = (lax.axis_index(self.axis) // self.bit) % 2
        self.sent = lax.dynamic_index_in_dim(rest, 1 - own, dim, False).astype(low)
        self.kept = lax.dynamic_index_in_dim(rest, own, dim, False)
        self.left.remove(self.bit)

    def step(self):
        self.start()
        return self.finish()

    def drain(self):
        while not hasattr(self, "result"):
            self.step()
        return self.result


def assemble_kernel(plan, spot_ref, *refs):
    outs = sorted({out for _, _, out, _ in plan})
    count = len(refs) - 1 - len(outs)
    sems = refs[-1]
    copies = []
    for k, (piece, cut, out, where) in enumerate(plan):
        source = refs[piece].at[cut] if cut is not None else refs[piece]
        target = refs[count + out].at[where(spot_ref)]
        copies.append(pltpu.make_async_copy(source, target, sems.at[k]))
    for copy in copies:
        copy.start()
    for copy in copies:
        copy.wait()


def assemble(plan, spots, pieces, shapes, tokens=()):
    anywhere = pl.BlockSpec(memory_space=pl.ANY)
    return launch(
        functools.partial(assemble_kernel, plan),
        tokens,
        in_specs=[pl.BlockSpec(memory_space=pltpu.SMEM)] + [anywhere] * len(pieces),
        out_specs=[anywhere] * len(shapes),
        out_shape=[shaped(shape, low) for shape in shapes],
        scratch_shapes=[pltpu.SemaphoreType.DMA((len(plan),))],
        cost_estimate=cost(1, 2 * sum(2 * piece.size for piece in pieces)),
        name="assemble",
    )(jnp.stack(spots).astype(jnp.int32), *pieces)


class Gather:
    def __init__(self, packed, cuts, shapes, order):
        self.packed, self.cuts, self.shapes = packed, cuts, shapes
        self.orders = [order, -order]

    def start_slices(self):
        self.pieces = [self.packed] + [flip(self.packed, "img", j) for j in range(1, lax.axis_size("img"))]

    def finish_slices(self, tokens=()):
        slices = len(self.pieces)
        plan = [
            (j, cut, out, lambda spot, j=j: (slice(None), spot[0] ^ j))
            for j in range(slices)
            for out, cut in enumerate(self.cuts)
        ]
        shapes = [(k, slices, r, c) for k, r, c in self.shapes]
        parts = assemble(plan, [lax.axis_index("img")], self.pieces, shapes, tokens)
        self.parts = [part.reshape(k, slices * r, c) for part, (k, r, c) in zip(parts, self.shapes)]
        self.dims = [[], []]
        return self.parts

    def start_pos(self):
        self.bits = [powers(lax.axis_size("pos"))[::order][len(dims)] for order, dims in zip(self.orders, self.dims)]
        self.came = [flip(part, "pos", bit) for part, bit in zip(self.parts, self.bits)]

    def finish_pos(self, tokens=()):
        plan, shapes, places = [], [], []
        for out, (part, bit, dims) in enumerate(zip(self.parts, self.bits, self.dims)):
            place = 1 + sum(other > bit for other in dims)
            places.append(place)
            shapes.append(part.shape[:place] + (2,) + part.shape[place:])
            ahead = (slice(None),) * place
            plan.append((2 * out, None, out, lambda spot, ahead=ahead, out=out: ahead + (spot[out],)))
            plan.append((2 * out + 1, None, out, lambda spot, ahead=ahead, out=out: ahead + (1 - spot[out],)))
            dims.append(bit)
        spots = [(lax.axis_index("pos") // bit) % 2 for bit in self.bits]
        pieces = [array for pair in zip(self.parts, self.came) for array in pair]
        self.parts = assemble(plan, spots, pieces, shapes, tokens)
        return self.parts

    def start_core(self):
        self.mine = [part.reshape(part.shape[0], -1, part.shape[-1]) for part in self.parts]
        self.other = [flip(part, "core") for part in self.mine]
        return list(zip(self.mine, self.other))


def narrow_kernel(count, attention_ref, feed_ref, out_ref):
    slabs, at = out_ref.shape[0], 0
    which, first = count
    if which is not None:
        out_ref[0] = attention_ref[which].astype(low)
        at = 1
    half = (slabs - at) // 2
    for k in range(2):
        for n in range(half):
            columns = slice((first + n) * SLAB, (first + n + 1) * SLAB)
            out_ref[at + k * half + n] = feed_ref[k, :, columns].astype(low)


def narrow(attention, feed_weight, which, first, slabs, tokens=()):
    owned = attention.shape[1]
    return launch(
        functools.partial(narrow_kernel, (which, first)),
        tokens,
        in_specs=[pl.BlockSpec(memory_space=pltpu.VMEM)] * 2,
        out_specs=pl.BlockSpec(memory_space=pltpu.VMEM),
        out_shape=shaped((slabs, owned, SLAB), low),
        cost_estimate=cost(1, 6 * slabs * owned * SLAB),
        name="narrow",
    )(attention, feed_weight)


def passing(own, backward):
    total = own
    outside = jnp.zeros_like(own)
    for axis in ("core", "pos"):
        for bit in powers(lax.axis_size(axis)):
            came = flip(total.astype(low), axis, bit).astype(wide)
            upper = (lax.axis_index(axis) // bit) % 2
            counts = upper == (0 if backward else 1)
            outside = outside + jnp.where(counts, came, 0.0)
            total = total + came
    return outside


def body(
    images,
    cotangent,
    attention_weight,
    feedforward_weight,
    norm_vectors,
    attention_moment,
    feedforward_moment,
    norm_moment,
    attention_second,
    feedforward_second,
    norm_second,
    attention_average,
    feedforward_average,
    norm_average,
):
    count, span, width = images.shape
    tokens = count * span
    spots = lax.axis_size("pos")
    slices = lax.axis_size("img")
    core = lax.axis_index("core")
    owned = attention_weight.shape[1]
    hidden_width = feedforward_weight.shape[2]
    slabs = hidden_width // SLAB

    def to_mine_first(array):
        parts = array.reshape(array.shape[:-1] + (spots, 2, -1))
        even, odd = (parts[..., k, :].reshape(array.shape[:-1] + (-1,)) for k in range(2))
        return jnp.concatenate([jnp.where(core == 0, even, odd), jnp.where(core == 0, odd, even)], axis=-1)

    def from_mine_first(array):
        half = array.shape[-1] // 2
        mine, other = (part.reshape(array.shape[:-1] + (spots, 1, -1)) for part in (array[..., :half], array[..., half:]))
        parts = [jnp.where(core == 0, mine, other), jnp.where(core == 0, other, mine)]
        return jnp.concatenate(parts, axis=-2).reshape(array.shape)

    vectors = jnp.pad(norm_vectors.astype(low).T[None], ((0, 2), (0, 0), (0, 124)))
    first = jnp.concatenate([attention_weight[:3].astype(low), vectors], axis=2)
    middle = width // 2
    every = slice(None)
    cuts = [(every, every, slice(0, middle)), (every, every, slice(middle, width + 128))]
    one = Gather(first, cuts, [(3, owned, middle), (3, owned, middle + 128)], 1)
    one.start_slices()
    tokens_one = one.finish_slices()
    one.start_pos()

    half = slabs // 2
    packed = narrow(attention_weight, feedforward_weight, 3, 0, 1 + 2 * half, tokens_one)
    two = Gather(
        packed, [slice(0, 1 + half), slice(1 + half, 1 + 2 * half)], [(1 + half, owned, SLAB), (half, owned, SLAB)], 1
    )
    two.start_slices()
    while len(one.dims[0]) < len(powers(spots)):
        tokens_one = one.finish_pos()
        if len(one.dims[0]) < len(powers(spots)):
            one.start_pos()
    first_a, first_b = one.start_core()
    tokens_two = two.finish_slices(tokens_one)
    two.start_pos()
    packed = narrow(attention_weight, feedforward_weight, None, half, 2 * half, tokens_one)
    three = Gather(packed, [slice(0, half), slice(half, 2 * half)], [(half, owned, SLAB)] * 2, -1)
    three.start_slices()
    while len(two.dims[0]) < len(powers(spots)):
        tokens_two = two.finish_pos(tokens_one)
        if len(two.dims[0]) < len(powers(spots)):
            two.start_pos()
    second_a, second_b = two.start_core()
    three.finish_slices(tokens_two)
    three.start_pos()
    while len(three.dims[0]) < len(powers(spots)):
        three.finish_pos()
        if len(three.dims[0]) < len(powers(spots)):
            three.start_pos()
    third_a, third_b = three.start_core()

    x = to_mine_first(images.reshape(tokens, width))
    e = to_mine_first(cotangent.reshape(tokens, width))
    et = turn(e, count, span)
    vec = jnp.concatenate([part[0, :, width // 2 : width // 2 + 4] for part in first_b], axis=0)
    vec = vec.astype(wide).T

    fq, fk, v, a1, a1t, state = project(x, vec, first_a, first_b, count, span)
    prior = passing(state, False)
    num, den = attend(fq, fk, v, count, span)
    outer = [part[0].reshape(spots, 1, -1, width) for part in second_a]
    wo = jnp.where(core == 0, jnp.concatenate(outer, axis=1), jnp.concatenate(outer[::-1], axis=1))
    wo = to_mine_first(wo.reshape(width, width))
    mixed, rden, resid, a2, a2t = mix(x, vec, wo, fq, num, den, prior, count, span)

    early = feed(a2, a2t, e, et, second_a, second_b, 1, None, count, span)
    early_parts = [Scatter(early[2], early[3], 1), Scatter(early[4], early[5], -1)]
    for part in early_parts:
        part.start()
    late = feed(a2, a2t, e, et, third_a, third_b, 0, early[:2], count, span)
    late_parts = [Scatter(late[2], late[3], 1), Scatter(late[4], late[5], -1)]

    def advance(parts):
        marks = []
        for part in parts:
            marks += part.finish()
        for part in parts:
            if not hasattr(part, "result"):
                part.start()
        return marks

    marks = advance(early_parts)
    output, dres, branch, dn, w, dstate, sums_second = turn_back(
        late[0], late[1], resid, e, vec, wo, mixed, rden, fq, count, span, marks
    )
    for part in late_parts:
        part.start()
    later = passing(dstate, True)
    grad_out = tm(mixed, branch).reshape(spots, 2, -1, width)
    out_other = lax.dynamic_index_in_dim(grad_out, 1 - core, 1, False).reshape(-1, width).astype(low)
    out_other = jnp.concatenate([out_other[:, width // 2 :], out_other[:, : width // 2]], axis=1)
    out_mine = lax.dynamic_index_in_dim(grad_out, core, 1, False).reshape(-1, width)
    out_part = [Scatter(out_mine, out_other, 1)]
    marks = advance(late_parts)
    parts = []
    for image in range(count):
        parts.append(attend_back(image, fq, fk, v, dn, w, prior, span, marks))
        if image == 0:
            out_part[0].start()
            marks = advance(early_parts)
    marks = advance(late_parts) + advance(out_part)
    left = finish(0, parts, fk, v, later, a1t, count, span, marks)
    inner_parts = [Scatter(left[3], left[4], 1)]
    inner_parts[0].start()
    marks = advance(early_parts)
    right = finish(1, parts, fk, v, later, a1t, count, span, marks)
    inner_parts.append(Scatter(right[3], right[4], -1))
    inner_parts[1].start()
    marks = advance(out_part) + advance(inner_parts[:1])
    input_grad, sums_first = enter(left[:3], right[:3], first_a, first_b, x, dres, vec, count, span, marks)
    vector_grad = jnp.concatenate([sums_first[:2], sums_second[:2]], axis=0).T
    vector_shard = Scatter(vector_grad[: width // 2], vector_grad[width // 2 :], 1).drain().T
    inner_shards = [part.drain() for part in inner_parts]
    early_shards = [part.drain() for part in early_parts]
    late_shards = [part.drain() for part in late_parts]
    out_shard = from_mine_first(out_part[0].drain())
    inner_shard = jnp.concatenate(inner_shards, axis=2)
    feed_shards = [(early_shards[k], late_shards[k]) for k in range(2)]

    attn_shard = jnp.concatenate([inner_shard, out_shard[None]], axis=0)
    feed_shard = jnp.stack([jnp.concatenate(pair, axis=1) for pair in feed_shards])

    local_squares = (
        jnp.sum(attn_shard * attn_shard) + jnp.sum(feed_shard * feed_shard) + jnp.sum(vector_shard * vector_shard)
    )
    squares = lax.all_gather(jnp.full((1, 128), local_squares), ("pos", "core", "img"), axis=0, tiled=True)
    grad_norm = jnp.sqrt(jnp.sum(squares[:, 0]))
    factor = clip_bound / jnp.maximum(grad_norm, clip_bound)
    attn_new = adam_update(
        attention_weight, attention_moment, attention_second, attention_average, attn_shard, factor, learn_rate
    )
    feed_new = adam_update(
        feedforward_weight, feedforward_moment, feedforward_second, feedforward_average, feed_shard, factor, learn_rate
    )
    norm_new = adam_update(norm_vectors, norm_moment, norm_second, norm_average, vector_shard, factor, norm_rate)
    output = from_mine_first(output).reshape(images.shape)
    input_grad = from_mine_first(input_grad).reshape(images.shape)
    return (output, input_grad, grad_norm) + attn_new + feed_new + norm_new


def solution(mesh):
    seq, img = mesh.devices.shape
    inner = Mesh(mesh.devices.reshape(seq // 2, 2, img), ("pos", "core", "img"))
    tokens = P("img", ("pos", "core"), None)
    rows = P(None, ("pos", "core", "img"), None)
    vectors = P(None, ("pos", "core", "img"))
    group = (rows, rows, vectors)
    return jax.shard_map(
        body,
        mesh=inner,
        in_specs=(tokens, tokens) + group * 4,
        out_specs=(tokens, tokens, P()) + (rows,) * 8 + (vectors,) * 4,
        check_vma=False,
    )
```

```python
import functools

import jax
import jax.numpy as jnp
from jax import lax
from jax.experimental import pallas as pl
from jax.experimental.pallas import tpu as pltpu
from jax.sharding import Mesh
from jax.sharding import PartitionSpec as P

HEADS = 16
HEAD_DIM = 64
STEP = 10

beta_first = 0.9
beta_second = 0.95
learn_rate = 0.02
norm_rate = 0.2
weight_decay = 0.1
average_decay = 0.75
clip_bound = 1.0
eps_norm = 1e-05
eps_adam = 1e-08

PAIR = 2 * HEAD_DIM
STATE_ROWS = HEAD_DIM + 16
SLAB = 1024
TILE = 512
GROUP = 256
VMEM_BYTES = 56 * 1024 * 1024

low = jnp.bfloat16
wide = jnp.float32


def params():
    return pltpu.CompilerParams(vmem_limit_bytes=VMEM_BYTES)


def cost(products, elements):
    return pl.CostEstimate(flops=products // 4, bytes_accessed=elements // 8, transcendentals=0)


def launch(kernel, tokens, in_specs, **keys):
    known, extra = len(in_specs), len(tokens)

    def run(*refs):
        kernel(*refs[:known], *refs[known + extra :])

    call = pl.pallas_call(
        run, in_specs=list(in_specs) + [pl.BlockSpec(memory_space=pl.ANY)] * extra, compiler_params=params(), **keys
    )
    return lambda *args: call(*args, *tokens)


def shaped(shape, kind):
    return jax.ShapeDtypeStruct(shape, kind)


def whole(shape):
    return pl.BlockSpec(shape, lambda *_: (0,) * len(shape))


def mm(left, right):
    return lax.dot_general(left, right, (((1,), (0,)), ((), ())), preferred_element_type=wide)


def mt(left, right):
    return lax.dot_general(left, right, (((1,), (1,)), ((), ())), preferred_element_type=wide)


def tm(left, right):
    return lax.dot_general(left, right, (((0,), (0,)), ((), ())), preferred_element_type=wide)


def first_head(rows):
    return lax.broadcasted_iota(jnp.int32, (rows, PAIR), 1) < HEAD_DIM


def fold_state(product):
    return jnp.where(first_head(HEAD_DIM), product[:HEAD_DIM], product[HEAD_DIM:])


def unfold_state(folded):
    own = first_head(HEAD_DIM)
    zero = jnp.zeros_like(folded)
    return jnp.concatenate([jnp.where(own, folded, zero), jnp.where(own, zero, folded)], axis=0)


def unfold_total(row):
    tall = jnp.broadcast_to(row, (PAIR, PAIR))
    lanes = lax.broadcasted_iota(jnp.int32, (PAIR, PAIR), 1) < HEAD_DIM
    rows = lax.broadcasted_iota(jnp.int32, (PAIR, PAIR), 0) < HEAD_DIM
    return jnp.where(lanes == rows, tall, jnp.zeros_like(tall))


def split_low(values):
    high = values.astype(low)
    return high, (values - high.astype(wide)).astype(low)


def normalised(values):
    centre = jnp.mean(values, axis=-1, keepdims=True)
    centred = values - centre
    spread = jnp.mean(centred * centred, axis=-1, keepdims=True)
    scale = lax.rsqrt(spread + eps_norm)
    return centred * scale, scale


def feature(raw):
    return jnp.where(raw > 0, raw + 1.0, jnp.exp(jnp.minimum(raw, 0.0))).astype(low)


def project_kernel(images, span, x_ref, vec_ref, km_ref, ko_ref, vm_ref, vo_ref, fk_ref, v_ref, a_ref, at_ref, state_ref):
    half = km_ref.shape[1]

    @pl.when(pl.program_id(0) == 0)
    def _():
        gain, shift = vec_ref[0:1, :], vec_ref[1:2, :]
        step = span // 3
        for start in range(0, images * span, step):
            rows = slice(start, start + step)
            unit, _ = normalised(x_ref[rows, :].astype(wide))
            a_ref[rows, :] = (unit * gain + shift).astype(low)
        at_ref[...] = a_ref[...].T

    left, right = a_ref[:, :half], a_ref[:, half:]
    fk_ref[...] = feature(mm(left, km_ref[0]) + mm(right, ko_ref[0]))
    v_ref[...] = (mm(left, vm_ref[0]) + mm(right, vo_ref[0])).astype(low)
    ones = jnp.ones((16, span), low)
    for image in range(images):
        rows = slice(image * span, (image + 1) * span)
        for pair in range(GROUP // PAIR):
            lanes = slice(pair * PAIR, (pair + 1) * PAIR)
            key, value = fk_ref[rows, lanes], v_ref[rows, lanes]
            state_ref[image, pair, :HEAD_DIM, :] = fold_state(tm(value, key))
            state_ref[image, pair, HEAD_DIM:, :] = mm(ones, key)


def project(x, vec, keys, values, images, span, tokens=()):
    count, width = x.shape
    half = keys[0].shape[1]
    pairs = GROUP // PAIR
    weight = pl.BlockSpec((1, half, GROUP), lambda g: (0, 0, g))
    column = pl.BlockSpec((count, GROUP), lambda g: (0, g))
    return launch(
        functools.partial(project_kernel, images, span),
        tokens,
        grid=(width // GROUP,),
        in_specs=[whole((count, width)), whole(vec.shape)] + [weight] * 4,
        out_specs=[
            column,
            column,
            whole((count, width)),
            whole((width, count)),
            pl.BlockSpec((images, pairs, STATE_ROWS, PAIR), lambda g: (0, g, 0, 0)),
        ],
        out_shape=[
            shaped((count, width), low),
            shaped((count, width), low),
            shaped((count, width), low),
            shaped((width, count), low),
            shaped((images, width // PAIR, STATE_ROWS, PAIR), wide),
        ],
        cost_estimate=cost(2 * count * width * width, 8 * width * width + 12 * count * width),
        name="project",
    )(x, vec, *keys, *values)


def query_kernel(a_ref, qm_ref, qo_ref, fq_ref):
    half = qm_ref.shape[1]
    fq_ref[...] = feature(mm(a_ref[:, :half], qm_ref[0]) + mm(a_ref[:, half:], qo_ref[0]))


def query(a, queries, tokens=()):
    count, width = a.shape
    half = queries[0].shape[1]
    weight = pl.BlockSpec((1, half, GROUP), lambda g: (0, 0, g))
    return launch(
        query_kernel,
        tokens,
        grid=(width // GROUP,),
        in_specs=[whole((count, width))] + [weight] * 2,
        out_specs=pl.BlockSpec((count, GROUP), lambda g: (0, g)),
        out_shape=shaped((count, width), low),
        cost_estimate=cost(count * width * width, 3 * width * width + 4 * count * width),
        name="query",
    )(a, *queries)


def swap_blocks(array, core, spots, inverse):
    if inverse:
        half = array.shape[-1] // 2
        mine, other = (part.reshape(array.shape[:-1] + (spots, 1, -1)) for part in (array[..., :half], array[..., half:]))
        parts = [jnp.where(core == 0, mine, other), jnp.where(core == 0, other, mine)]
        return jnp.concatenate(parts, axis=-2).reshape(array.shape)
    parts = array.reshape(array.shape[:-1] + (spots, 2, -1))
    even, odd = (parts[..., k, :].reshape(array.shape[:-1] + (-1,)) for k in range(2))
    return jnp.concatenate([jnp.where(core == 0, even, odd), jnp.where(core == 0, odd, even)], axis=-1)


def block_of(spot, core, block):
    return pl.ds(pl.multiple_of((2 * spot + core) * block, block), block)


def prepare_kernel(spots, core_ref, x_ref, e_ref, xo_ref, eo_ref, et_ref):
    width = x_ref.shape[1]
    block = width // (2 * spots)
    for side in range(2):
        core = core_ref[0] if side == 0 else 1 - core_ref[0]
        for spot in range(spots):
            target = slice((side * spots + spot) * block, (side * spots + spot + 1) * block)
            source = block_of(spot, core, block)
            xo_ref[:, target] = x_ref[:, source]
            eo_ref[:, target] = e_ref[:, source]
    et_ref[...] = eo_ref[...].T


def turn_kernel(x_ref, out_ref):
    out_ref[...] = x_ref[...].T


def prepare(x, e, core, spots, images, span, tokens=()):
    count, width = x.shape
    rows = pl.BlockSpec((span, width), lambda b: (b, 0))
    turned = pl.BlockSpec((None, width, span), lambda b: (b, 0, 0))
    turned_shape = shaped((images, width, span), low)
    if (width // (2 * spots)) % 128:
        x, e = swap_blocks(x, core, spots, False), swap_blocks(e, core, spots, False)
        et = launch(
            turn_kernel, tokens, grid=(images,), in_specs=[rows], out_specs=turned, out_shape=turned_shape, name="turn"
        )(e)
        return x, e, et
    return launch(
        functools.partial(prepare_kernel, spots),
        tokens,
        grid=(images,),
        in_specs=[pl.BlockSpec(memory_space=pltpu.SMEM), rows, rows],
        out_specs=[rows, rows, turned],
        out_shape=[shaped((count, width), low)] * 2 + [turned_shape],
        cost_estimate=cost(1, 12 * count * width),
        name="prepare",
    )(core.reshape(1), x, e)


def arrange_kernel(spots, core_ref, mine_ref, other_ref, out_ref):
    width = out_ref.shape[0]
    block = width // (2 * spots)
    for side, ref in enumerate((mine_ref, other_ref)):
        core = core_ref[0] if side == 0 else 1 - core_ref[0]
        for row in range(spots):
            rows = block_of(row, core, block)
            for half in range(2):
                origin = core_ref[0] if half == 0 else 1 - core_ref[0]
                for spot in range(spots):
                    target = slice((half * spots + spot) * block, (half * spots + spot + 1) * block)
                    out_ref[rows, target] = ref[0, row * block : (row + 1) * block, block_of(spot, origin, block)]


def arrange(parts, core, spots, tokens=()):
    mine, other = parts
    width = mine.shape[2]
    if (width // (2 * spots)) % 128:
        parts = [part.reshape(spots, 1, -1, width) for part in parts]
        wo = jnp.where(core == 0, jnp.concatenate(parts, axis=1), jnp.concatenate(parts[::-1], axis=1))
        return swap_blocks(wo.reshape(width, width), core, spots, False)
    inside = pl.BlockSpec(memory_space=pltpu.VMEM)
    return launch(
        functools.partial(arrange_kernel, spots),
        tokens,
        in_specs=[pl.BlockSpec(memory_space=pltpu.SMEM), inside, inside],
        out_specs=inside,
        out_shape=shaped((width, width), low),
        cost_estimate=cost(1, 4 * width * width),
        name="arrange",
    )(core.reshape(1), mine, other)


def put_natural(ref, value, core_ref, spots):
    width = value.shape[1]
    block = width // (2 * spots)
    if block % 128:
        ref[...] = value
        return
    for side in range(2):
        core = core_ref[0] if side == 0 else 1 - core_ref[0]
        for spot in range(spots):
            at = (side * spots + spot) * block
            ref[:, block_of(spot, core, block)] = value[:, at : at + block]


def attend_kernel(span, fq_ref, fk_ref, v_ref, num_ref, den_ref):
    own = first_head(span)
    causal = lax.broadcasted_iota(jnp.int32, (span, span), 0) >= lax.broadcasted_iota(jnp.int32, (span, span), 1)
    for pair in range(GROUP // PAIR):
        lanes = slice(pair * PAIR, (pair + 1) * PAIR)
        query, key, value = fq_ref[:, lanes], fk_ref[:, lanes], v_ref[:, lanes]
        zero = jnp.zeros_like(query)
        total = None
        for head in range(2):
            mask = own if head == 0 else jnp.logical_not(own)
            scores = mt(jnp.where(mask, query, zero), key)
            scores = jnp.where(causal, scores, 0.0).astype(low)
            ones = jnp.where(mask, jnp.ones_like(value), zero)
            part = mm(scores, jnp.concatenate([jnp.where(mask, value, zero), ones], axis=1))
            total = part if total is None else total + part
        num_ref[:, lanes] = total[:, :PAIR]
        den_ref[:, lanes] = total[:, PAIR:]


def attend(fq, fk, v, images, span, tokens=()):
    rows, width = fq.shape
    block = pl.BlockSpec((span, GROUP), lambda b, p: (b, p))
    return launch(
        functools.partial(attend_kernel, span),
        tokens,
        grid=(images, width // GROUP),
        in_specs=[block] * 3,
        out_specs=[block] * 2,
        out_shape=[shaped((rows, width), wide)] * 2,
        cost_estimate=cost(16 * rows * span * width, 14 * rows * width),
        name="attend",
    )(fq, fk, v)


def mix_kernel(x_ref, vec_ref, wo_ref, fq_ref, num_ref, den_ref, prior_ref, mixed_ref, rden_ref, resid_ref, a_ref, at_ref):
    width = x_ref.shape[1]
    for pair in range(width // PAIR):
        lanes = slice(pair * PAIR, (pair + 1) * PAIR)
        folded = prior_ref[0, pair]
        matrix = jnp.concatenate(
            [unfold_state(folded[:HEAD_DIM]), unfold_total(folded[HEAD_DIM : HEAD_DIM + 1])], axis=0
        )
        high, rest = split_low(matrix)
        query = fq_ref[:, lanes]
        both = mt(jnp.concatenate([query, query], axis=1), jnp.concatenate([high, rest], axis=1))
        scale = 1.0 / (den_ref[:, lanes] + both[:, PAIR:])
        rden_ref[:, lanes] = scale
        mixed_ref[:, lanes] = ((num_ref[:, lanes] + both[:, :PAIR]) * scale).astype(low)
    resid = x_ref[...].astype(wide) + mm(mixed_ref[...], wo_ref[...])
    resid_ref[...] = resid
    unit, _ = normalised(resid)
    normed = (unit * vec_ref[2:3, :] + vec_ref[3:4, :]).astype(low)
    a_ref[...] = normed
    at_ref[...] = normed.T


def mix(x, vec, wo, fq, num, den, prior, images, span, tokens=()):
    rows_, width = x.shape
    rows = pl.BlockSpec((span, width), lambda b: (b, 0))
    return launch(
        mix_kernel,
        tokens,
        grid=(images,),
        in_specs=[
            rows,
            whole(vec.shape),
            whole(wo.shape),
            rows,
            rows,
            rows,
            pl.BlockSpec((1,) + prior.shape[1:], lambda b: (b, 0, 0, 0)),
        ],
        out_specs=[rows, rows, rows, rows, pl.BlockSpec((None, width, span), lambda b: (b, 0, 0))],
        out_shape=[
            shaped((rows_, width), low),
            shaped((rows_, width), wide),
            shaped((rows_, width), wide),
            shaped((rows_, width), low),
            shaped((images, width, span), low),
        ],
        cost_estimate=cost(4 * rows_ * width * width, 24 * rows_ * width + 2 * width * width),
        name="mix",
    )(x, vec, wo, fq, num, den, prior)


gelu_scale = 0.7978845608028654
gelu_cubic = 0.044715


def feed_kernel(fresh, images, span, *refs):
    a_ref, at_ref, e_ref, et_ref, um_ref, uo_ref, dm_ref, do_ref = refs[:8]
    out_ref, da_ref, gum_ref, guo_ref, gdm_ref, gdo_ref = refs[-6:]
    half = um_ref.shape[1]

    @pl.when(pl.program_id(0) == 0)
    def _():
        if fresh:
            out_ref[...] = jnp.zeros_like(out_ref)
            da_ref[...] = jnp.zeros_like(da_ref)
        else:
            out_ref[...] = refs[8][...]
            da_ref[...] = refs[9][...]

    um, uo, dm, do = um_ref[0], uo_ref[0], dm_ref[0], do_ref[0]
    for image in range(images):
        rows = slice(image * span, (image + 1) * span)
        upper = mm(a_ref[rows, :half], um) + mm(a_ref[rows, half:], uo)
        grad = mm(e_ref[rows, :half], dm) + mm(e_ref[rows, half:], do)
        square = upper * upper
        bend = jnp.tanh(gelu_scale * upper * (1.0 + gelu_cubic * square))
        gate = 0.5 + 0.5 * bend
        hidden = (upper * gate).astype(low)
        slope = gate + 0.5 * upper * (1.0 - bend * bend) * (gelu_scale * (1.0 + 3.0 * gelu_cubic * square))
        dupper = (grad * slope).astype(low)
        out_ref[rows, :half] += mt(hidden, dm)
        out_ref[rows, half:] += mt(hidden, do)
        da_ref[rows, :half] += mt(dupper, um)
        da_ref[rows, half:] += mt(dupper, uo)
        parts = [
            (gdm_ref, mm(et_ref[image, :half, :], hidden)),
            (gdo_ref, mm(et_ref[image, half:, :], hidden)),
            (gum_ref, mm(at_ref[image, :half, :], dupper)),
            (guo_ref, mm(at_ref[image, half:, :], dupper)),
        ]
        if image == 0:
            sums = [part for _, part in parts]
        else:
            sums = [total + part for total, (_, part) in zip(sums, parts)]
    for (ref, _), total in zip(parts, sums):
        ref[...] = total.astype(ref.dtype)


def feed(a, at, e, et, up, down, skipped, carried, images, span, tokens=()):
    rows, width = a.shape
    half = up[0].shape[1]
    chunks = down[0].shape[0]
    tiles = SLAB // TILE
    above = pl.BlockSpec((1, half, TILE), lambda g: (skipped + g // tiles, 0, g % tiles))
    below = pl.BlockSpec((1, half, TILE), lambda g: (g // tiles, 0, g % tiles))
    grads = pl.BlockSpec((half, TILE), lambda g: (0, g))
    full = whole((rows, width))
    turned = whole((images, width, span))
    fresh = carried is None
    return launch(
        functools.partial(feed_kernel, fresh, images, span),
        tokens,
        grid=(chunks * tiles,),
        in_specs=[full, turned, full, turned, above, above, below, below] + ([] if fresh else [full, full]),
        out_specs=[full, full] + [grads] * 4,
        out_shape=[shaped((rows, width), wide)] * 2 + [shaped((half, chunks * SLAB), low)] * 4,
        cost_estimate=cost(6 * rows * width * chunks * SLAB, 8 * width * chunks * SLAB + 20 * rows * width),
        name="feed",
    )(a, at, e, et, *up, *down, *(() if fresh else carried))


def turn_back_kernel(spots, core_ref, x_out_ref, da_ref, resid_ref, e_ref, vec_ref, wo_ref, mixed_ref, rden_ref, fq_ref,
                     out_ref, dres_ref, branch_ref, dn_ref, w_ref, state_ref, sums_ref):
    width = da_ref.shape[1]
    resid = resid_ref[...]
    put_natural(out_ref, (resid + x_out_ref[...]).astype(low), core_ref, spots)
    unit, scale = normalised(resid)
    da = da_ref[...]

    @pl.when(pl.program_id(0) == 0)
    def _():
        sums_ref[...] = jnp.zeros_like(sums_ref)

    sums_ref[0:1, :] += jnp.sum(da * unit, axis=0, keepdims=True)
    sums_ref[1:2, :] += jnp.sum(da, axis=0, keepdims=True)
    p = da * vec_ref[2:3, :]
    back = p - jnp.mean(p, axis=-1, keepdims=True) - unit * jnp.mean(p * unit, axis=-1, keepdims=True)
    dres = e_ref[...].astype(wide) + scale * back
    dres_ref[...] = dres
    branch = dres.astype(low)
    branch_ref[...] = branch
    dmixed = mt(branch, wo_ref[...]).astype(low).astype(wide)
    dnumer = dmixed * rden_ref[...]
    dn_ref[...] = dnumer.astype(low)
    w_ref[...] = (-dnumer * mixed_ref[...].astype(wide)).astype(low)
    for pair in range(width // PAIR):
        lanes = slice(pair * PAIR, (pair + 1) * PAIR)
        query = fq_ref[:, lanes]
        state_ref[0, pair, :HEAD_DIM, :] = fold_state(tm(dn_ref[:, lanes], query))
        total = jnp.sum(fold_state(tm(w_ref[:, lanes], query)), axis=0, keepdims=True)
        state_ref[0, pair, HEAD_DIM:, :] = jnp.broadcast_to(total, (STATE_ROWS - HEAD_DIM, PAIR))


def turn_back(core, spots, x_out, da, resid, e, vec, wo, mixed, rden, fq, images, span, tokens=()):
    rows_, width = da.shape
    rows = pl.BlockSpec((span, width), lambda b: (b, 0))
    state = (images, width // PAIR, STATE_ROWS, PAIR)
    return launch(
        functools.partial(turn_back_kernel, spots),
        tokens,
        grid=(images,),
        in_specs=[pl.BlockSpec(memory_space=pltpu.SMEM)]
        + [rows, rows, rows, rows, whole(vec.shape), whole(wo.shape), rows, rows, rows],
        out_specs=[rows] * 5 + [pl.BlockSpec((1,) + state[1:], lambda b: (b, 0, 0, 0)), whole((8, width))],
        out_shape=[
            shaped((rows_, width), low),
            shaped((rows_, width), wide),
            shaped((rows_, width), low),
            shaped((rows_, width), low),
            shaped((rows_, width), low),
            shaped(state, wide),
            shaped((8, width), wide),
        ],
        cost_estimate=cost(5 * rows_ * width * width, 30 * rows_ * width),
        name="turn_back",
    )(core.reshape(1), x_out, da, resid, e, vec, wo, mixed, rden, fq)


def attend_back_kernel(span, fq_ref, fk_ref, v_ref, dn_ref, w_ref, prior_ref, dq_ref, dfk_ref, dv_ref):
    own = first_head(span)
    own_twice = jnp.concatenate([own, own], axis=1)
    rows = lax.broadcasted_iota(jnp.int32, (span, span), 0)
    columns = lax.broadcasted_iota(jnp.int32, (span, span), 1)
    for pair in range(GROUP // PAIR):
        lanes = slice(pair * PAIR, (pair + 1) * PAIR)
        query, key, value = fq_ref[:, lanes], fk_ref[:, lanes], v_ref[:, lanes]
        grads = jnp.concatenate([dn_ref[:, lanes], w_ref[:, lanes]], axis=1)
        extended = jnp.concatenate([value, jnp.ones_like(value)], axis=1)
        zero = jnp.zeros_like(query)
        folded = prior_ref[0, pair]
        matrix = jnp.concatenate(
            [unfold_state(folded[:HEAD_DIM]), unfold_total(folded[HEAD_DIM : HEAD_DIM + 1])], axis=0
        )
        high, rest = split_low(matrix)
        dfq = mm(grads, high) + mm(grads, rest)
        dfk = jnp.zeros((span, PAIR), wide)
        dv = jnp.zeros((span, PAIR), wide)
        for head in range(2):
            mask = own if head == 0 else jnp.logical_not(own)
            both = own_twice if head == 0 else jnp.logical_not(own_twice)
            head_grads = jnp.where(both, grads, jnp.zeros_like(grads))
            head_query = jnp.where(mask, query, zero)
            head_key = jnp.where(mask, key, zero)
            dscore = jnp.where(rows >= columns, mt(head_grads, extended), 0.0).astype(low)
            dfq += mm(dscore, head_key)
            dscore_t = jnp.where(rows <= columns, mt(extended, head_grads), 0.0).astype(low)
            dfk += mm(dscore_t, head_query)
            score_t = jnp.where(rows <= columns, mt(head_key, query), 0.0).astype(low)
            dv += mm(score_t, head_grads[:, :PAIR])
        dq_ref[:, lanes] = (dfq * jnp.minimum(query.astype(wide), 1.0)).astype(low)
        dfk_ref[:, lanes] = dfk
        dv_ref[:, lanes] = dv


def attend_back(image, fq, fk, v, dn, w, prior, span, tokens=()):
    width = fq.shape[1]
    block = pl.BlockSpec((span, GROUP), lambda p: (image, p))
    column = pl.BlockSpec((span, GROUP), lambda p: (0, p))
    return launch(
        functools.partial(attend_back_kernel, span),
        tokens,
        grid=(width // GROUP,),
        in_specs=[block] * 5 + [pl.BlockSpec((1, GROUP // PAIR) + prior.shape[2:], lambda p: (image, p, 0, 0))],
        out_specs=[column] * 3,
        out_shape=[shaped((span, width), low), shaped((span, width), wide), shaped((span, width), wide)],
        cost_estimate=cost(32 * span * span * width, 24 * span * width),
        name="attend_back",
    )(fq, fk, v, dn, w, prior)


def finish_kernel(images, span, *refs):
    locals_ = [refs[3 * image : 3 * image + 3] for image in range(images)]
    fk_ref, v_ref, later_ref, at_ref, dq_ref, dk_ref, dv_ref, mine_ref, other_ref = refs[3 * images :]
    half = mine_ref.shape[1]
    for image in range(images):
        rows = slice(image * span, (image + 1) * span)
        dqi_ref, dfk_ref, dvl_ref = locals_[image]
        dq_ref[rows, :] = dqi_ref[...]
        for pair in range(GROUP // PAIR):
            lanes = slice(pair * PAIR, (pair + 1) * PAIR)
            folded = later_ref[image, pair]
            high, rest = split_low(unfold_state(folded[:HEAD_DIM]))
            key, value = fk_ref[rows, lanes], v_ref[rows, lanes]
            dfk = dfk_ref[:, lanes] + folded[HEAD_DIM : HEAD_DIM + 1]
            dfk = dfk + mm(jnp.concatenate([value, value], axis=1), jnp.concatenate([high, rest], axis=0))
            dv = dvl_ref[:, lanes] + mt(
                jnp.concatenate([key, key], axis=1), jnp.concatenate([high, rest], axis=1)
            )
            dk_ref[rows, lanes] = (dfk * jnp.minimum(key.astype(wide), 1.0)).astype(low)
            dv_ref[rows, lanes] = dv.astype(low)
    for k, ref in enumerate((dq_ref, dk_ref, dv_ref)):
        mine_ref[k] = mm(at_ref[:half, :], ref[...]).astype(low)
        other_ref[k] = mm(at_ref[half:, :], ref[...]).astype(low)


def finish(side, parts, fk, v, later, at, images, span, tokens=()):
    rows, width = fk.shape
    half = width // 2
    groups = half // GROUP
    column = pl.BlockSpec((rows, GROUP), lambda g: (0, side * groups + g))
    part = pl.BlockSpec((span, GROUP), lambda g: (0, side * groups + g))
    result = pl.BlockSpec((rows, GROUP), lambda g: (0, g))
    grads = pl.BlockSpec((3, half, GROUP), lambda g: (0, 0, g))
    state = pl.BlockSpec((images, GROUP // PAIR) + later.shape[2:], lambda g: (0, side * groups + g, 0, 0))
    return launch(
        functools.partial(finish_kernel, images, span),
        tokens,
        grid=(groups,),
        in_specs=[part] * (3 * images) + [column] * 2 + [state, whole(at.shape)],
        out_specs=[result] * 3 + [grads, grads],
        out_shape=[shaped((rows, half), low)] * 3 + [shaped((3, half, half), low)] * 2,
        cost_estimate=cost(2 * rows * width * width, 15 * rows * width),
        name="finish",
    )(*[array for image in parts for array in image], fk, v, later, at)


def enter_kernel(spots, core_ref, *refs):
    lefts, rights, weights = refs[:3], refs[3:6], refs[6:12]
    x_ref, dres_ref, vec_ref, grad_ref, sums_ref = refs[12:]
    half = x_ref.shape[1] // 2
    parts = []
    for side in range(2):
        total = None
        for k in range(3):
            weight = weights[2 * k + side]
            part = mt(lefts[k][...], weight[0, :, :half]) + mt(rights[k][...], weight[0, :, half : 2 * half])
            total = part if total is None else total + part
        parts.append(total)
    da = jnp.concatenate(parts, axis=1)
    unit, scale = normalised(x_ref[...].astype(wide))
    sums_ref[0:1, :] = jnp.sum(da * unit, axis=0, keepdims=True)
    sums_ref[1:2, :] = jnp.sum(da, axis=0, keepdims=True)
    sums_ref[2:, :] = jnp.zeros_like(sums_ref[2:, :])
    p = da * vec_ref[0:1, :]
    back = p - jnp.mean(p, axis=-1, keepdims=True) - unit * jnp.mean(p * unit, axis=-1, keepdims=True)
    put_natural(grad_ref, (dres_ref[...] + scale * back).astype(low), core_ref, spots)


def enter(image, core, spots, left, right, weights, x, dres, vec, span, tokens=()):
    width = x.shape[1]
    half = width // 2
    rows = pl.BlockSpec((span, width), lambda g: (image, 0))
    part = pl.BlockSpec((span, half), lambda g: (image, 0))
    weights = [array for pair in weights for array in pair]
    return launch(
        functools.partial(enter_kernel, spots),
        tokens,
        grid=(1,),
        in_specs=[pl.BlockSpec(memory_space=pltpu.SMEM)]
        + [part] * 6
        + [pl.BlockSpec((1, half, width), lambda g: (0, 0, 0))] * 6
        + [rows, rows, whole(vec.shape)],
        out_specs=[whole((span, width)), whole((8, width))],
        out_shape=[shaped((span, width), low), shaped((8, width), wide)],
        cost_estimate=cost(3 * span * width * width, 14 * span * width + 6 * width * width),
        name="enter",
    )(core.reshape(1), *left, *right, *weights, x, dres, vec)


def adam_update(master, moment, second, average, gradient, factor, rate):
    clipped = gradient * factor
    moment = beta_first * moment + (1.0 - beta_first) * clipped
    second = beta_second * second + (1.0 - beta_second) * clipped * clipped
    first_hat = moment / (1.0 - beta_first**STEP)
    second_hat = second / (1.0 - beta_second**STEP)
    master = master - rate * (first_hat / (jnp.sqrt(second_hat) + eps_adam) + weight_decay * master)
    average = average_decay * average + (1.0 - average_decay) * master
    return (master, moment, second, average)


def flip_pairs(count, bit):
    return [(i, i ^ bit) for i in range(count)]


def powers(count):
    return [1 << k for k in range(count.bit_length() - 1)]


def flip(array, axis, bit=1):
    return lax.ppermute(array, axis, flip_pairs(lax.axis_size(axis), bit))


def fold_kernel(counts, spot_ref, *refs):
    total = sum(counts)
    ins, outs = refs[: 2 * total], refs[2 * total :]
    for k in range(total):
        value = ins[2 * k][...].astype(wide) + ins[2 * k + 1][...].astype(wide)
        outs[k][...] = value.astype(outs[k].dtype)


def fold(chains, tokens=()):
    steps = 2
    in_specs, out_specs, out_shape, arrays, counts, spots, moved = [], [], [], [], [], [], 0
    for k, (kept, came, pre, ways, own) in enumerate(chains):
        columns = kept.shape[-1]
        rows = kept.size // (columns * pre * ways)
        kept, came = (array.reshape(pre, ways, rows, columns) for array in (kept, came))
        counts.append(ways)
        spots.append(own)
        moved += 8 * kept.size
        for j in range(ways):
            block = (pre, 1, rows, columns // steps)
            spec = pl.BlockSpec(block, lambda c, spot, k=k, j=j: (0, spot[k] ^ j, 0, c))
            in_specs += [spec, spec]
            arrays += [kept, came]
            out_specs.append(pl.BlockSpec(block, lambda c, spot: (0, 0, 0, c)))
            out_shape.append(shaped((pre, 1, rows, columns), low if j else wide))
    total, extra = len(in_specs), len(tokens)

    def run(spot_ref, *refs):
        fold_kernel(counts, spot_ref, *refs[:total], *refs[total + extra :])

    results = pl.pallas_call(
        run,
        grid_spec=pltpu.PrefetchScalarGridSpec(
            num_scalar_prefetch=1,
            grid=(steps,),
            in_specs=in_specs + [pl.BlockSpec(memory_space=pl.ANY)] * extra,
            out_specs=out_specs,
        ),
        out_shape=out_shape,
        compiler_params=params(),
        cost_estimate=cost(1, moved),
        name="fold",
    )(jnp.stack(spots).astype(jnp.int32), *arrays, *tokens)
    groups = []
    for ways in counts:
        groups.append([part.reshape(part.shape[0], part.shape[2], part.shape[3]) for part in results[:ways]])
        results = results[ways:]
    return groups


class Chain:
    def __init__(self, kept, sent, order):
        self.lead = kept.shape[0] if kept.ndim == 3 else 1
        self.kept = kept
        self.sends = [sent]
        self.hops = [("core", 1)]
        self.bits = powers(lax.axis_size("pos"))[::order]
        self.left = powers(lax.axis_size("pos"))[::-1]

    def start(self):
        self.came = [flip(array, axis, bit) for array, (axis, bit) in zip(self.sends, self.hops)]

    def cut(self):
        bit = next(bit for bit in self.bits if bit in self.left)
        pre = self.lead << self.left.index(bit)
        self.left.remove(bit)
        self.hops = [("pos", bit)]
        return (self.kept, self.came[0], pre, 2, (lax.axis_index("pos") // bit) % 2)

    def take(self, parts):
        self.kept, self.sends = parts[0], list(parts[1:])


def advance(chains, tokens=()):
    groups = fold([chain.cut() for chain in chains], tokens)
    for chain, parts in zip(chains, groups):
        chain.take(parts)
        chain.start()
    return [array for chain in chains for array in chain.sends]


def last_kernel(ways, lead, pieces, spot_ref, *refs):
    ins, outs = refs[: 2 * pieces], refs[2 * pieces :]
    at = 0
    for k in range(pieces):
        columns = ins[2 * k].shape[-1]
        for j in range(ways):
            place = spot_ref[0] ^ j
            for n in range(lead):
                value = ins[2 * k][n, place].astype(wide) + ins[2 * k + 1][n, place].astype(wide)
                outs[j][n, :, at : at + columns] = value.astype(outs[j].dtype)
        at += columns


class Last:
    def __init__(self, chains, tokens=()):
        ways = lax.axis_size("img")
        lead = chains[0].lead
        arrays = []
        for chain in chains:
            for array in (chain.kept, chain.came[0]):
                arrays.append(array.reshape(lead, ways, -1, array.shape[-1]))
        self.widths = [array.shape[-1] for array in arrays[::2]]
        rows = arrays[0].shape[2]
        inside = pl.BlockSpec(memory_space=pltpu.VMEM)
        parts = launch(
            functools.partial(last_kernel, ways, lead, len(chains)),
            tokens,
            in_specs=[pl.BlockSpec(memory_space=pltpu.SMEM)] + [inside] * len(arrays),
            out_specs=[inside] * ways,
            out_shape=[shaped((lead, rows, sum(self.widths)), low if j else wide) for j in range(ways)],
            cost_estimate=cost(1, 4 * sum(array.size for array in arrays)),
            name="last",
        )(lax.axis_index("img").reshape(1), *arrays)
        self.kept, self.sends = parts[0], list(parts[1:])
        self.came = [flip(array, "img", j + 1) for j, array in enumerate(self.sends)]

    def result(self):
        total = self.kept
        for came in self.came:
            total = total + came.astype(wide)
        self.total = total
        return total

    def pieces(self):
        at, found = 0, []
        for columns in self.widths:
            found.append(self.total[..., at : at + columns])
            at += columns
        return found


def sum_slowly(array):
    for axis in ("core", "pos", "img"):
        for bit in powers(lax.axis_size(axis)):
            array = array + flip(array, axis, bit)
    return array


def sum_all(array):
    for axis in ("img", "pos", "core"):
        came = [flip(array, axis, j) for j in range(1, lax.axis_size(axis))]
        for other in came:
            array = array + other
    return array


def assemble_kernel(plan, spot_ref, *refs):
    outs = sorted({out for _, _, out, _ in plan})
    count = len(refs) - 1 - len(outs)
    sems = refs[-1]
    copies = []
    for k, (piece, cut, out, where) in enumerate(plan):
        source = refs[piece].at[cut] if cut is not None else refs[piece]
        target = refs[count + out].at[where(spot_ref)]
        copies.append(pltpu.make_async_copy(source, target, sems.at[k]))
    for copy in copies:
        copy.start()
    for copy in copies:
        copy.wait()


def assemble(plan, spots, pieces, shapes, tokens=()):
    anywhere = pl.BlockSpec(memory_space=pl.ANY)
    return launch(
        functools.partial(assemble_kernel, plan),
        tokens,
        in_specs=[pl.BlockSpec(memory_space=pltpu.SMEM)] + [anywhere] * len(pieces),
        out_specs=[pl.BlockSpec(memory_space=pltpu.VMEM)] * len(shapes),
        out_shape=[shaped(shape, low) for shape in shapes],
        scratch_shapes=[pltpu.SemaphoreType.DMA((len(plan),))],
        cost_estimate=cost(1, 2 * sum(2 * piece.size for piece in pieces)),
        name="assemble",
    )(jnp.stack(spots).astype(jnp.int32), *pieces)


class Gather:
    def __init__(self, packed, cuts, shapes, order):
        self.packed, self.cuts, self.shapes = packed, cuts, shapes
        self.orders = [order, -order]

    def start_slices(self):
        self.pieces = [self.packed] + [flip(self.packed, "img", j) for j in range(1, lax.axis_size("img"))]

    def finish_slices(self, tokens=()):
        slices = len(self.pieces)
        plan = [
            (j, cut, out, lambda spot, j=j: (slice(None), spot[0] ^ j))
            for j in range(slices)
            for out, cut in enumerate(self.cuts)
        ]
        shapes = [(k, slices, r, c) for k, r, c in self.shapes]
        parts = assemble(plan, [lax.axis_index("img")], self.pieces, shapes, tokens)
        self.parts = [part.reshape(k, slices * r, c) for part, (k, r, c) in zip(parts, self.shapes)]
        self.dims = [[], []]
        return self.parts

    def start_pos(self):
        self.bits = [powers(lax.axis_size("pos"))[::order][len(dims)] for order, dims in zip(self.orders, self.dims)]
        self.came = [flip(part, "pos", bit) for part, bit in zip(self.parts, self.bits)]

    def finish_pos(self, tokens=()):
        plan, shapes, places = [], [], []
        for out, (part, bit, dims) in enumerate(zip(self.parts, self.bits, self.dims)):
            place = 1 + sum(other > bit for other in dims)
            places.append(place)
            shapes.append(part.shape[:place] + (2,) + part.shape[place:])
            ahead = (slice(None),) * place
            plan.append((2 * out, None, out, lambda spot, ahead=ahead, out=out: ahead + (spot[out],)))
            plan.append((2 * out + 1, None, out, lambda spot, ahead=ahead, out=out: ahead + (1 - spot[out],)))
            dims.append(bit)
        spots = [(lax.axis_index("pos") // bit) % 2 for bit in self.bits]
        pieces = [array for pair in zip(self.parts, self.came) for array in pair]
        self.parts = assemble(plan, spots, pieces, shapes, tokens)
        return self.parts

    def start_core(self):
        self.mine = [part.reshape(part.shape[0], -1, part.shape[-1]) for part in self.parts]
        self.other = [flip(part, "core") for part in self.mine]
        return list(zip(self.mine, self.other))


def narrow_kernel(plan, *refs):
    out_ref = refs[-1]
    for k, (ref, member, columns) in enumerate(plan):
        out_ref[k] = refs[ref][member, :, columns].astype(low)


def narrow(plan, weights, tokens=()):
    owned = weights[0].shape[1]
    inside = pl.BlockSpec(memory_space=pltpu.VMEM)
    return launch(
        functools.partial(narrow_kernel, plan),
        tokens,
        in_specs=[inside] * len(weights),
        out_specs=inside,
        out_shape=shaped((len(plan), owned, SLAB), low),
        cost_estimate=cost(1, 6 * len(plan) * owned * SLAB),
        name="narrow",
    )(*weights)


def passing(own, backward):
    total = own
    outside = jnp.zeros_like(own)
    for axis in ("core", "pos"):
        for bit in powers(lax.axis_size(axis)):
            came = flip(total.astype(low), axis, bit).astype(wide)
            upper = (lax.axis_index(axis) // bit) % 2
            counts = upper == (0 if backward else 1)
            outside = outside + jnp.where(counts, came, 0.0)
            total = total + came
    return outside


def body(
    images,
    cotangent,
    attention_weight,
    feedforward_weight,
    norm_vectors,
    attention_moment,
    feedforward_moment,
    norm_moment,
    attention_second,
    feedforward_second,
    norm_second,
    attention_average,
    feedforward_average,
    norm_average,
):
    count, span, width = images.shape
    tokens = count * span
    spots = lax.axis_size("pos")
    slices = lax.axis_size("img")
    core = lax.axis_index("core")
    owned = attention_weight.shape[1]
    hidden_width = feedforward_weight.shape[2]
    slabs = hidden_width // SLAB

    weights = (attention_weight, feedforward_weight)
    steps = len(powers(spots))
    half = slabs // 2
    every = slice(None)

    def stretch(k):
        return slice(k * SLAB, (k + 1) * SLAB)

    vectors = jnp.pad(norm_vectors.astype(low).T[None], ((1, 0), (0, 0), (0, 124)))
    packed = jnp.concatenate([attention_weight[1:3].astype(low), vectors], axis=2)
    cuts = [(slice(0, 1), every, slice(0, width)), (slice(1, 2), every, every)]
    one = Gather(packed, cuts, [(1, owned, width), (1, owned, width + 128)], 1)
    packed = narrow([(0, 0, every), (0, 3, every)], weights)
    two = Gather(packed, [slice(0, 1), slice(1, 2)], [(1, owned, width)] * 2, -1)

    def feed_group(first, order, tokens):
        plan = [(1, k, stretch(first + n)) for k in range(2) for n in range(half)]
        packed = narrow(plan, weights, tokens)
        return Gather(packed, [slice(0, half), slice(half, 2 * half)], [(half, owned, SLAB)] * 2, order)

    one.start_slices()
    x, e, et = prepare(images.reshape(tokens, width), cotangent.reshape(tokens, width), core, spots, count, span)
    one.finish_slices([et, two.packed])
    one.start_pos()
    two.start_slices()
    for step in range(steps - 1):
        marks = one.finish_pos()
        one.start_pos()
    marks = two.finish_slices(marks)
    two.start_pos()
    marks = one.finish_pos(marks)
    keys, values = one.start_core()
    for step in range(steps - 1):
        marks = two.finish_pos(marks)
        two.start_pos()
    three = feed_group(0, 1, marks)
    three.start_slices()
    vec = jnp.concatenate([part[0, :, width : width + 4] for part in values], axis=0).astype(wide).T

    fk, v, a1, a1t, state = project(x, vec, keys, values, count, span, marks)
    marks = two.finish_pos([state])
    queries, outer = two.start_core()
    marks = three.finish_slices(marks)
    three.start_pos()
    four = feed_group(half, -1, marks)
    four.start_slices()
    prior = passing(state, False)
    fq = query(a1, queries, marks)
    for step in range(steps - 1):
        marks = three.finish_pos([fq])
        three.start_pos()
    num, den = attend(fq, fk, v, count, span, marks)
    marks = four.finish_slices([num])
    four.start_pos()
    wo = arrange(outer, core, spots, marks)
    mixed, rden, resid, a2, a2t = mix(x, vec, wo, fq, num, den, prior, count, span)
    marks = three.finish_pos([resid])
    third_a, third_b = three.start_core()
    for step in range(steps - 1):
        marks = four.finish_pos(marks)
        four.start_pos()

    early = feed(a2, a2t, e, et, third_a, third_b, 0, None, count, span, marks)
    firsts = [Chain(early[2], early[3], 1), Chain(early[4], early[5], -1)]
    for chain in firsts:
        chain.start()
    four.finish_pos([early[0]])
    fourth_a, fourth_b = four.start_core()
    late = feed(a2, a2t, e, et, fourth_a, fourth_b, 0, early[:2], count, span)
    seconds = [Chain(late[2], late[3], 1), Chain(late[4], late[5], -1)]
    for chain in seconds:
        chain.start()
    marks = advance(firsts)
    output, dres, branch, dn, w, dstate, sums_second = turn_back(
        core, spots, late[0], late[1], resid, e, vec, wo, mixed, rden, fq, count, span, marks
    )
    later = passing(dstate, True)
    grad_out = tm(mixed, branch).reshape(spots, 2, -1, width)
    out_other = lax.dynamic_index_in_dim(grad_out, 1 - core, 1, False).reshape(-1, width).astype(low)
    out_other = jnp.concatenate([out_other[:, width // 2 :], out_other[:, : width // 2]], axis=1)
    out_mine = lax.dynamic_index_in_dim(grad_out, core, 1, False).reshape(-1, width)
    outs = [Chain(out_mine, out_other, 1)]
    marks = advance(seconds)
    parts = []
    for image in range(count):
        parts.append(attend_back(image, fq, fk, v, dn, w, prior, span, marks))
        if image == 0:
            outs[0].start()
            marks = advance(firsts, [parts[0][0]])
    for step in range(steps - 2):
        advance(firsts)
        advance(seconds)
    marks = advance(seconds) + advance(outs)
    firsts_last = Last(firsts)
    left = finish(0, parts, fk, v, later, a1t, count, span, marks + firsts_last.sends)
    inner = [Chain(left[3], left[4], 1)]
    inner[0].start()
    for step in range(steps - 1):
        marks = advance(outs, [left[0]])
    right = finish(1, parts, fk, v, later, a1t, count, span, marks)
    inner.append(Chain(right[3], right[4], -1))
    inner[1].start()
    firsts_last.result()
    marks = advance(inner[:1], [right[0]])
    projections = (queries, keys, values)
    grads_in = []
    for image in range(count):
        grads_in.append(
            enter(image, core, spots, left[:3], right[:3], projections, x, dres, vec, span, marks + [firsts_last.total])
        )
        if image == 0:
            marks = advance(inner[1:], [grads_in[0][1]])
            seconds_last = Last(seconds + outs, [grads_in[0][1]])
            marks = marks + seconds_last.sends
    input_grad = jnp.stack([part[0] for part in grads_in])
    sums_first = sum(part[1] for part in grads_in)
    vector_grad = jnp.concatenate([swap_blocks(part[:2], core, spots, True) for part in (sums_first, sums_second)], axis=0)
    vector_grad = sum_slowly(vector_grad)
    device = (lax.axis_index("pos") * 2 + core) * slices + lax.axis_index("img")
    vector_shard = lax.dynamic_slice_in_dim(vector_grad, device * norm_vectors.shape[1], norm_vectors.shape[1], 1)
    seconds_last.result()
    while inner[0].left:
        advance(inner)
    inner_shard = Last(inner).result()
    up_late, down_late, out_shard = seconds_last.pieces()
    up_early, down_early = firsts_last.pieces()
    out_shard = swap_blocks(out_shard, core, spots, True)
    attn_shard = jnp.concatenate([inner_shard, out_shard], axis=0)
    feed_shard = jnp.concatenate(
        [jnp.concatenate([up_early, up_late], axis=2), jnp.concatenate([down_early, down_late], axis=2)], axis=0
    )
    if (width // (2 * spots)) % 128:
        output = swap_blocks(output, core, spots, True)
        input_grad = swap_blocks(input_grad, core, spots, True)

    local_squares = (
        jnp.sum(attn_shard * attn_shard) + jnp.sum(feed_shard * feed_shard) + jnp.sum(vector_shard * vector_shard)
    )
    grad_norm = jnp.sqrt(sum_all(jnp.full((8, 128), local_squares))[0, 0])
    factor = clip_bound / jnp.maximum(grad_norm, clip_bound)
    attn_new = adam_update(
        attention_weight, attention_moment, attention_second, attention_average, attn_shard, factor, learn_rate
    )
    feed_new = adam_update(
        feedforward_weight, feedforward_moment, feedforward_second, feedforward_average, feed_shard, factor, learn_rate
    )
    norm_new = adam_update(norm_vectors, norm_moment, norm_second, norm_average, vector_shard, factor, norm_rate)
    output = output.reshape(images.shape)
    input_grad = input_grad.reshape(images.shape)
    return (output, input_grad, grad_norm) + attn_new + feed_new + norm_new


def solution(mesh):
    seq, img = mesh.devices.shape
    inner = Mesh(mesh.devices.reshape(seq // 2, 2, img), ("pos", "core", "img"))
    tokens = P("img", ("pos", "core"), None)
    rows = P(None, ("pos", "core", "img"), None)
    vectors = P(None, ("pos", "core", "img"))
    group = (rows, rows, vectors)
    return jax.shard_map(
        body,
        mesh=inner,
        in_specs=(tokens, tokens) + group * 4,
        out_specs=(tokens, tokens, P()) + (rows,) * 8 + (vectors,) * 4,
        check_vma=False,
    )
```

```python
import functools

import jax
import jax.numpy as jnp
from jax import lax
from jax.experimental import pallas as pl
from jax.experimental.pallas import tpu as pltpu
from jax.sharding import Mesh
from jax.sharding import PartitionSpec as P

HEADS = 16
HEAD_DIM = 64
STEP = 10

beta_first = 0.9
beta_second = 0.95
learn_rate = 0.02
norm_rate = 0.2
weight_decay = 0.1
average_decay = 0.75
clip_bound = 1.0
eps_norm = 1e-05
eps_adam = 1e-08

PAIR = 2 * HEAD_DIM
STATE_ROWS = HEAD_DIM + 16
SLAB = 1024
TILE = 512
GROUP = 256
VMEM_BYTES = 56 * 1024 * 1024

low = jnp.bfloat16
wide = jnp.float32


def params():
    return pltpu.CompilerParams(vmem_limit_bytes=VMEM_BYTES)


def cost(products, elements):
    return pl.CostEstimate(flops=products // 4, bytes_accessed=elements // 8, transcendentals=0)


def launch(kernel, tokens, in_specs, **keys):
    known, extra = len(in_specs), len(tokens)

    def run(*refs):
        kernel(*refs[:known], *refs[known + extra :])

    call = pl.pallas_call(
        run, in_specs=list(in_specs) + [pl.BlockSpec(memory_space=pl.ANY)] * extra, compiler_params=params(), **keys
    )
    return lambda *args: call(*args, *tokens)


def shaped(shape, kind):
    return jax.ShapeDtypeStruct(shape, kind)


def whole(shape):
    return pl.BlockSpec(shape, lambda *_: (0,) * len(shape))


def mm(left, right):
    return lax.dot_general(left, right, (((1,), (0,)), ((), ())), preferred_element_type=wide)


def mt(left, right):
    return lax.dot_general(left, right, (((1,), (1,)), ((), ())), preferred_element_type=wide)


def tm(left, right):
    return lax.dot_general(left, right, (((0,), (0,)), ((), ())), preferred_element_type=wide)


def pair_mm(first, second):
    if first[0].shape[1] % 128:
        return mm(*first) + mm(*second)
    return mm(jnp.concatenate([first[0], second[0]], axis=1), jnp.concatenate([first[1], second[1]], axis=0))


def causal_mask(span, below):
    rows = lax.broadcasted_iota(jnp.int32, (span, span), 0)
    columns = lax.broadcasted_iota(jnp.int32, (span, span), 1)
    return (rows >= columns if below else rows <= columns).astype(wide).astype(low)


def first_head(rows):
    return lax.broadcasted_iota(jnp.int32, (rows, PAIR), 1) < HEAD_DIM


def fold_state(product):
    return jnp.where(first_head(HEAD_DIM), product[:HEAD_DIM], product[HEAD_DIM:])


def unfold_state(folded):
    own = first_head(HEAD_DIM)
    zero = jnp.zeros_like(folded)
    return jnp.concatenate([jnp.where(own, folded, zero), jnp.where(own, zero, folded)], axis=0)


def unfold_total(row):
    tall = jnp.broadcast_to(row, (PAIR, PAIR))
    lanes = lax.broadcasted_iota(jnp.int32, (PAIR, PAIR), 1) < HEAD_DIM
    rows = lax.broadcasted_iota(jnp.int32, (PAIR, PAIR), 0) < HEAD_DIM
    return jnp.where(lanes == rows, tall, jnp.zeros_like(tall))


def split_low(values):
    high = values.astype(low)
    return high, (values - high.astype(wide)).astype(low)


def normalised(values):
    centre = jnp.mean(values, axis=-1, keepdims=True)
    centred = values - centre
    spread = jnp.mean(centred * centred, axis=-1, keepdims=True)
    scale = lax.rsqrt(spread + eps_norm)
    return centred * scale, scale


def feature(raw):
    return jnp.where(raw > 0, raw + 1.0, jnp.exp(jnp.minimum(raw, 0.0))).astype(low)


def project_kernel(images, span, x_ref, vec_ref, km_ref, ko_ref, vm_ref, vo_ref, fk_ref, v_ref, a_ref, at_ref, state_ref):
    half = km_ref.shape[1]

    @pl.when(pl.program_id(0) == 0)
    def _():
        gain, shift = vec_ref[0:1, :], vec_ref[1:2, :]
        step = span // 3
        for start in range(0, images * span, step):
            rows = slice(start, start + step)
            unit, _ = normalised(x_ref[rows, :].astype(wide))
            a_ref[rows, :] = (unit * gain + shift).astype(low)
        at_ref[...] = a_ref[...].T

    left, right = a_ref[:, :half], a_ref[:, half:]
    fk_ref[...] = feature(mm(left, km_ref[0]) + mm(right, ko_ref[0]))
    v_ref[...] = (mm(left, vm_ref[0]) + mm(right, vo_ref[0])).astype(low)
    ones = jnp.ones((16, span), low)
    for image in range(images):
        rows = slice(image * span, (image + 1) * span)
        for pair in range(GROUP // PAIR):
            lanes = slice(pair * PAIR, (pair + 1) * PAIR)
            key, value = fk_ref[rows, lanes], v_ref[rows, lanes]
            state_ref[image, pair, :HEAD_DIM, :] = fold_state(tm(value, key))
            state_ref[image, pair, HEAD_DIM:, :] = mm(ones, key)


def project(x, vec, keys, values, images, span, tokens=()):
    count, width = x.shape
    half = keys[0].shape[1]
    pairs = GROUP // PAIR
    weight = pl.BlockSpec((1, half, GROUP), lambda g: (0, 0, g))
    column = pl.BlockSpec((count, GROUP), lambda g: (0, g))
    return launch(
        functools.partial(project_kernel, images, span),
        tokens,
        grid=(width // GROUP,),
        in_specs=[whole((count, width)), whole(vec.shape)] + [weight] * 4,
        out_specs=[
            column,
            column,
            whole((count, width)),
            whole((width, count)),
            pl.BlockSpec((images, pairs, STATE_ROWS, PAIR), lambda g: (0, g, 0, 0)),
        ],
        out_shape=[
            shaped((count, width), low),
            shaped((count, width), low),
            shaped((count, width), low),
            shaped((width, count), low),
            shaped((images, width // PAIR, STATE_ROWS, PAIR), wide),
        ],
        cost_estimate=cost(2 * count * width * width, 8 * width * width + 12 * count * width),
        name="project",
    )(x, vec, *keys, *values)


def query_kernel(a_ref, qm_ref, qo_ref, fq_ref):
    half = qm_ref.shape[1]
    fq_ref[...] = feature(mm(a_ref[:, :half], qm_ref[0]) + mm(a_ref[:, half:], qo_ref[0]))


def query(a, queries, tokens=()):
    count, width = a.shape
    half = queries[0].shape[1]
    weight = pl.BlockSpec((1, half, GROUP), lambda g: (0, 0, g))
    return launch(
        query_kernel,
        tokens,
        grid=(width // GROUP,),
        in_specs=[whole((count, width))] + [weight] * 2,
        out_specs=pl.BlockSpec((count, GROUP), lambda g: (0, g)),
        out_shape=shaped((count, width), low),
        cost_estimate=cost(count * width * width, 3 * width * width + 4 * count * width),
        name="query",
    )(a, *queries)


def swap_blocks(array, core, spots, inverse):
    if inverse:
        half = array.shape[-1] // 2
        mine, other = (part.reshape(array.shape[:-1] + (spots, 1, -1)) for part in (array[..., :half], array[..., half:]))
        parts = [jnp.where(core == 0, mine, other), jnp.where(core == 0, other, mine)]
        return jnp.concatenate(parts, axis=-2).reshape(array.shape)
    parts = array.reshape(array.shape[:-1] + (spots, 2, -1))
    even, odd = (parts[..., k, :].reshape(array.shape[:-1] + (-1,)) for k in range(2))
    return jnp.concatenate([jnp.where(core == 0, even, odd), jnp.where(core == 0, odd, even)], axis=-1)


def block_of(spot, core, block):
    return pl.ds(pl.multiple_of((2 * spot + core) * block, block), block)


def prepare_kernel(spots, core_ref, x_ref, e_ref, xo_ref, eo_ref, et_ref):
    width = x_ref.shape[1]
    block = width // (2 * spots)
    for side in range(2):
        core = core_ref[0] if side == 0 else 1 - core_ref[0]
        for spot in range(spots):
            target = slice((side * spots + spot) * block, (side * spots + spot + 1) * block)
            source = block_of(spot, core, block)
            xo_ref[:, target] = x_ref[:, source]
            eo_ref[:, target] = e_ref[:, source]
    et_ref[...] = eo_ref[...].T


def turn_kernel(x_ref, out_ref):
    out_ref[...] = x_ref[...].T


def prepare(x, e, core, spots, images, span, tokens=()):
    count, width = x.shape
    rows = pl.BlockSpec((span, width), lambda b: (b, 0))
    turned = turned_block(width, span)
    if (width // (2 * spots)) % 128:
        x, e = swap_blocks(x, core, spots, False), swap_blocks(e, core, spots, False)
        et = launch(
            turn_kernel, tokens, grid=(images,), in_specs=[rows], out_specs=turned, out_shape=turned_shape(images, width, span), name="turn"
        )(e)
        return x, e, et
    return launch(
        functools.partial(prepare_kernel, spots),
        tokens,
        grid=(images,),
        in_specs=[pl.BlockSpec(memory_space=pltpu.SMEM), rows, rows],
        out_specs=[rows, rows, turned],
        out_shape=[shaped((count, width), low)] * 2 + [turned_shape(images, width, span)],
        cost_estimate=cost(1, 12 * count * width),
        name="prepare",
    )(core.reshape(1), x, e)


def arrange_kernel(spots, core_ref, mine_ref, other_ref, out_ref):
    width = out_ref.shape[0]
    block = width // (2 * spots)
    for side, ref in enumerate((mine_ref, other_ref)):
        core = core_ref[0] if side == 0 else 1 - core_ref[0]
        for row in range(spots):
            rows = block_of(row, core, block)
            for half in range(2):
                origin = core_ref[0] if half == 0 else 1 - core_ref[0]
                for spot in range(spots):
                    target = slice((half * spots + spot) * block, (half * spots + spot + 1) * block)
                    out_ref[rows, target] = ref[0, row * block : (row + 1) * block, block_of(spot, origin, block)]


def arrange(parts, core, spots, tokens=()):
    mine, other = parts
    width = mine.shape[2]
    if (width // (2 * spots)) % 128:
        parts = [part.reshape(spots, 1, -1, width) for part in parts]
        wo = jnp.where(core == 0, jnp.concatenate(parts, axis=1), jnp.concatenate(parts[::-1], axis=1))
        return swap_blocks(wo.reshape(width, width), core, spots, False)
    inside = pl.BlockSpec(memory_space=pltpu.VMEM)
    return launch(
        functools.partial(arrange_kernel, spots),
        tokens,
        in_specs=[pl.BlockSpec(memory_space=pltpu.SMEM), inside, inside],
        out_specs=inside,
        out_shape=shaped((width, width), low),
        cost_estimate=cost(1, 4 * width * width),
        name="arrange",
    )(core.reshape(1), mine, other)


def put_natural(ref, value, core_ref, spots):
    width = value.shape[1]
    block = width // (2 * spots)
    if block % 128:
        ref[...] = value
        return
    for side in range(2):
        core = core_ref[0] if side == 0 else 1 - core_ref[0]
        for spot in range(spots):
            at = (side * spots + spot) * block
            ref[:, block_of(spot, core, block)] = value[:, at : at + block]


def attend_kernel(span, fq_ref, fk_ref, v_ref, num_ref, den_ref):
    own = first_head(span)
    causal = causal_mask(span, True)
    one = jnp.ones((span, PAIR), low)
    zero = jnp.zeros((span, PAIR), low)
    for pair in range(GROUP // PAIR):
        lanes = slice(pair * PAIR, (pair + 1) * PAIR)
        query, key, value = fq_ref[:, lanes], fk_ref[:, lanes], v_ref[:, lanes]
        products = []
        for mask in (own, jnp.logical_not(own)):
            scores = mt(jnp.where(mask, query, zero), key).astype(low) * causal
            right = jnp.concatenate([jnp.where(mask, value, zero), jnp.where(mask, one, zero)], axis=1)
            products.append((scores, right))
        total = pair_mm(*products)
        num_ref[:, lanes] = total[:, :PAIR]
        den_ref[:, lanes] = total[:, PAIR:]


def attend(fq, fk, v, images, span, tokens=()):
    rows, width = fq.shape
    block = pl.BlockSpec((span, GROUP), lambda b, p: (b, p))
    return launch(
        functools.partial(attend_kernel, span),
        tokens,
        grid=(images, width // GROUP),
        in_specs=[block] * 3,
        out_specs=[block] * 2,
        out_shape=[shaped((rows, width), wide)] * 2,
        cost_estimate=cost(16 * rows * span * width, 14 * rows * width),
        name="attend",
    )(fq, fk, v)


def turned_block(width, span):
    if span % 128:
        return pl.BlockSpec((None, width, span), lambda b: (b, 0, 0))
    return pl.BlockSpec((width, span), lambda b: (0, b))


def turned_shape(images, width, span):
    return shaped((images, width, span) if span % 128 else (width, images * span), low)


def turned_whole(array):
    if array.ndim == 2:
        return array
    return jnp.swapaxes(array, 0, 1).reshape(array.shape[1], -1)


def mix_kernel(x_ref, vec_ref, wo_ref, fq_ref, num_ref, den_ref, prior_ref, mixed_ref, rden_ref, resid_ref, a_ref, at_ref):
    width = x_ref.shape[1]
    for pair in range(width // PAIR):
        lanes = slice(pair * PAIR, (pair + 1) * PAIR)
        folded = prior_ref[0, pair]
        matrix = jnp.concatenate(
            [unfold_state(folded[:HEAD_DIM]), unfold_total(folded[HEAD_DIM : HEAD_DIM + 1])], axis=0
        )
        high, rest = split_low(matrix)
        query = fq_ref[:, lanes]
        both = mt(jnp.concatenate([query, query], axis=1), jnp.concatenate([high, rest], axis=1))
        scale = 1.0 / (den_ref[:, lanes] + both[:, PAIR:])
        rden_ref[:, lanes] = scale
        mixed_ref[:, lanes] = ((num_ref[:, lanes] + both[:, :PAIR]) * scale).astype(low)
    resid = x_ref[...].astype(wide) + mm(mixed_ref[...], wo_ref[...])
    resid_ref[...] = resid
    unit, _ = normalised(resid)
    normed = (unit * vec_ref[2:3, :] + vec_ref[3:4, :]).astype(low)
    a_ref[...] = normed
    at_ref[...] = normed.T


def mix(x, vec, wo, fq, num, den, prior, images, span, tokens=()):
    rows_, width = x.shape
    rows = pl.BlockSpec((span, width), lambda b: (b, 0))
    return launch(
        mix_kernel,
        tokens,
        grid=(images,),
        in_specs=[
            rows,
            whole(vec.shape),
            whole(wo.shape),
            rows,
            rows,
            rows,
            pl.BlockSpec((1,) + prior.shape[1:], lambda b: (b, 0, 0, 0)),
        ],
        out_specs=[rows, rows, rows, rows, turned_block(width, span)],
        out_shape=[
            shaped((rows_, width), low),
            shaped((rows_, width), wide),
            shaped((rows_, width), wide),
            shaped((rows_, width), low),
            turned_shape(images, width, span),
        ],
        cost_estimate=cost(4 * rows_ * width * width, 24 * rows_ * width + 2 * width * width),
        name="mix",
    )(x, vec, wo, fq, num, den, prior)


gelu_scale = 0.7978845608028654
gelu_cubic = 0.044715


def feed_kernel(fresh, core_ref, *refs):
    a_ref, at_ref, e_ref, et_ref, um_ref, uo_ref, dm_ref, do_ref = refs[:8]
    out_ref, da_ref, gum_ref, guo_ref, gdm_ref, gdo_ref = refs[-6:]

    @pl.when(pl.program_id(0) == 0)
    def _():
        if fresh:
            out_ref[...] = jnp.zeros_like(out_ref)
            da_ref[...] = jnp.zeros_like(da_ref)
        else:
            out_ref[...] = refs[8][...]
            da_ref[...] = refs[9][...]

    um, uo, dm, do = (ref[...].reshape(-1, ref.shape[-1]) for ref in (um_ref, uo_ref, dm_ref, do_ref))
    half = um.shape[0]
    upper = mm(a_ref[:, :half], um) + mm(a_ref[:, half:], uo)
    grad = mm(e_ref[:, :half], dm) + mm(e_ref[:, half:], do)
    square = upper * upper
    bend = jnp.tanh(gelu_scale * upper * (1.0 + gelu_cubic * square))
    gate = 0.5 + 0.5 * bend
    hidden = (upper * gate).astype(low)
    slope = gate + 0.5 * upper * (1.0 - bend * bend) * (gelu_scale * (1.0 + 3.0 * gelu_cubic * square))
    dupper = (grad * slope).astype(low)
    out_ref[:, :half] += mt(hidden, dm)
    out_ref[:, half:] += mt(hidden, do)
    da_ref[:, :half] += mt(dupper, um)
    da_ref[:, half:] += mt(dupper, uo)
    gdm_ref[...] = mm(et_ref[:half, :], hidden).astype(low)
    gdo_ref[...] = mm(et_ref[half:, :], hidden).astype(low)
    gum_ref[...] = mm(at_ref[:half, :], dupper).astype(low)
    guo_ref[...] = mm(at_ref[half:, :], dupper).astype(low)


def feed(core, weights, part, parts, a, at, e, et, carried, tokens=()):
    rows, width = a.shape
    half = width // 2
    hidden = weights.shape[-1] // parts
    steps = hidden // TILE

    def weight(which, flipped):
        block = (None, weights.shape[1], None, weights.shape[3], TILE)
        return pl.BlockSpec(block, lambda g, core: (which, 0, core[0] ^ flipped, 0, part * steps + g))

    grads = pl.BlockSpec((half, TILE), lambda g, core: (0, g))
    full = whole((rows, width))
    turned = whole((width, rows))
    fresh = carried is None
    in_specs = [full, turned, full, turned] + [weight(which, flipped) for which in range(2) for flipped in range(2)]
    if not fresh:
        in_specs += [full, full]
    known, extra = len(in_specs), len(tokens)

    def run(core_ref, *refs):
        feed_kernel(fresh, core_ref, *refs[:known], *refs[known + extra :])

    return pl.pallas_call(
        run,
        grid_spec=pltpu.PrefetchScalarGridSpec(
            num_scalar_prefetch=1,
            grid=(steps,),
            in_specs=in_specs + [pl.BlockSpec(memory_space=pl.ANY)] * extra,
            out_specs=[full, full] + [grads] * 4,
        ),
        out_shape=[shaped((rows, width), wide)] * 2 + [shaped((half, hidden), low)] * 4,
        compiler_params=params(),
        cost_estimate=cost(6 * rows * width * hidden, 8 * width * hidden + 20 * rows * width),
        name="feed",
    )(core.reshape(1), a, at, e, et, *[weights] * 4, *(() if fresh else carried), *tokens)


def outer_kernel(core_ref, mixed_ref, branch_ref, out_ref):
    product = tm(mixed_ref[...], branch_ref[...]).astype(low)
    half = product.shape[1] // 2
    swap = pl.program_id(0) == 1
    out_ref[:, :half] = jnp.where(swap, product[:, half:], product[:, :half])
    out_ref[:, half:] = jnp.where(swap, product[:, :half], product[:, half:])


def outer(core, spots, mixed, branch, tokens=()):
    rows, width = mixed.shape
    block = width // (2 * spots)
    if block % 128:
        product = tm(mixed, branch).astype(low).reshape(spots, 2, -1, width)
        mine = lax.dynamic_index_in_dim(product, core, 1, False).reshape(-1, width)
        other = lax.dynamic_index_in_dim(product, 1 - core, 1, False).reshape(-1, width)
        return mine, jnp.concatenate([other[:, width // 2 :], other[:, : width // 2]], axis=1)
    known, extra = 2, len(tokens)

    def run(core_ref, *refs):
        outer_kernel(core_ref, *refs[:known], *refs[known + extra :])

    result = pl.pallas_call(
        run,
        grid_spec=pltpu.PrefetchScalarGridSpec(
            num_scalar_prefetch=1,
            grid=(2, spots),
            in_specs=[
                pl.BlockSpec((rows, block), lambda side, spot, core: (0, 2 * spot + (core[0] ^ side))),
                whole((rows, width)),
            ]
            + [pl.BlockSpec(memory_space=pl.ANY)] * extra,
            out_specs=pl.BlockSpec((None, block, width), lambda side, spot, core: (side, spot, 0)),
        ),
        out_shape=shaped((2, width // 2, width), low),
        compiler_params=params(),
        cost_estimate=cost(rows * width * width, 4 * rows * width + 2 * width * width),
        name="outer",
    )(core.reshape(1), mixed, branch, *tokens)
    return result[0], result[1]


def turn_back_kernel(spots, core_ref, x_out_ref, da_ref, resid_ref, e_ref, vec_ref, wo_ref, mixed_ref, rden_ref, fq_ref,
                     out_ref, dres_ref, branch_ref, dn_ref, w_ref, state_ref, sums_ref):
    width = da_ref.shape[1]
    resid = resid_ref[...]
    put_natural(out_ref, (resid + x_out_ref[...]).astype(low), core_ref, spots)
    unit, scale = normalised(resid)
    da = da_ref[...]

    @pl.when(pl.program_id(0) == 0)
    def _():
        sums_ref[...] = jnp.zeros_like(sums_ref)

    sums_ref[0:1, :] += jnp.sum(da * unit, axis=0, keepdims=True)
    sums_ref[1:2, :] += jnp.sum(da, axis=0, keepdims=True)
    p = da * vec_ref[2:3, :]
    back = p - jnp.mean(p, axis=-1, keepdims=True) - unit * jnp.mean(p * unit, axis=-1, keepdims=True)
    dres = e_ref[...].astype(wide) + scale * back
    dres_ref[...] = dres
    branch = dres.astype(low)
    branch_ref[...] = branch
    dmixed = mt(branch, wo_ref[...]).astype(low).astype(wide)
    dnumer = dmixed * rden_ref[...]
    dn_ref[...] = dnumer.astype(low)
    w_ref[...] = (-dnumer * mixed_ref[...].astype(wide)).astype(low)
    for pair in range(width // PAIR):
        lanes = slice(pair * PAIR, (pair + 1) * PAIR)
        query = fq_ref[:, lanes]
        state_ref[0, pair, :HEAD_DIM, :] = fold_state(tm(dn_ref[:, lanes], query))
        total = jnp.sum(fold_state(tm(w_ref[:, lanes], query)), axis=0, keepdims=True)
        state_ref[0, pair, HEAD_DIM:, :] = jnp.broadcast_to(total, (STATE_ROWS - HEAD_DIM, PAIR))


def turn_back(core, spots, x_out, da, resid, e, vec, wo, mixed, rden, fq, images, span, tokens=()):
    rows_, width = da.shape
    rows = pl.BlockSpec((span, width), lambda b: (b, 0))
    state = (images, width // PAIR, STATE_ROWS, PAIR)
    return launch(
        functools.partial(turn_back_kernel, spots),
        tokens,
        grid=(images,),
        in_specs=[pl.BlockSpec(memory_space=pltpu.SMEM)]
        + [rows, rows, rows, rows, whole(vec.shape), whole(wo.shape), rows, rows, rows],
        out_specs=[rows] * 5 + [pl.BlockSpec((1,) + state[1:], lambda b: (b, 0, 0, 0)), whole((8, width))],
        out_shape=[
            shaped((rows_, width), low),
            shaped((rows_, width), wide),
            shaped((rows_, width), low),
            shaped((rows_, width), low),
            shaped((rows_, width), low),
            shaped(state, wide),
            shaped((8, width), wide),
        ],
        cost_estimate=cost(5 * rows_ * width * width, 30 * rows_ * width),
        name="turn_back",
    )(core.reshape(1), x_out, da, resid, e, vec, wo, mixed, rden, fq)


def attend_back_kernel(span, fq_ref, fk_ref, v_ref, dn_ref, w_ref, prior_ref, dq_ref, dfk_ref, dv_ref):
    own = first_head(span)
    own_twice = jnp.concatenate([own, own], axis=1)
    below, above = causal_mask(span, True), causal_mask(span, False)
    one = jnp.ones((span, PAIR), low)
    zero = jnp.zeros((span, PAIR), low)
    zero_twice = jnp.zeros((span, 2 * PAIR), low)
    for pair in range(GROUP // PAIR):
        lanes = slice(pair * PAIR, (pair + 1) * PAIR)
        query, key, value = fq_ref[:, lanes], fk_ref[:, lanes], v_ref[:, lanes]
        grads = jnp.concatenate([dn_ref[:, lanes], w_ref[:, lanes]], axis=1)
        extended = jnp.concatenate([value, one], axis=1)
        folded = prior_ref[0, pair]
        matrix = jnp.concatenate(
            [unfold_state(folded[:HEAD_DIM]), unfold_total(folded[HEAD_DIM : HEAD_DIM + 1])], axis=0
        )
        high, rest = split_low(matrix)
        dfq = mm(jnp.concatenate([grads, grads], axis=1), jnp.concatenate([high, rest], axis=0))
        to_query, to_key, to_value = [], [], []
        for mask, both in ((own, own_twice), (jnp.logical_not(own), jnp.logical_not(own_twice))):
            head_grads = jnp.where(both, grads, zero_twice)
            head_query = jnp.where(mask, query, zero)
            head_key = jnp.where(mask, key, zero)
            to_query.append((mt(head_grads, extended).astype(low) * below, head_key))
            to_key.append((mt(extended, head_grads).astype(low) * above, head_query))
            to_value.append((mt(head_key, query).astype(low) * above, head_grads[:, :PAIR]))
        dfq = dfq + pair_mm(*to_query)
        dq_ref[:, lanes] = (dfq * jnp.minimum(query.astype(wide), 1.0)).astype(low)
        dfk_ref[:, lanes] = pair_mm(*to_key)
        dv_ref[:, lanes] = pair_mm(*to_value)


def attend_back(image, fq, fk, v, dn, w, prior, span, tokens=()):
    width = fq.shape[1]
    block = pl.BlockSpec((span, GROUP), lambda p: (image, p))
    column = pl.BlockSpec((span, GROUP), lambda p: (0, p))
    return launch(
        functools.partial(attend_back_kernel, span),
        tokens,
        grid=(width // GROUP,),
        in_specs=[block] * 5 + [pl.BlockSpec((1, GROUP // PAIR) + prior.shape[2:], lambda p: (image, p, 0, 0))],
        out_specs=[column] * 3,
        out_shape=[shaped((span, width), low), shaped((span, width), wide), shaped((span, width), wide)],
        cost_estimate=cost(32 * span * span * width, 24 * span * width),
        name="attend_back",
    )(fq, fk, v, dn, w, prior)


def finish_kernel(images, span, *refs):
    locals_ = [refs[3 * image : 3 * image + 3] for image in range(images)]
    fk_ref, v_ref, later_ref, at_ref, dq_ref, dk_ref, dv_ref, mine_ref, other_ref = refs[3 * images :]
    half = mine_ref.shape[1]
    for image in range(images):
        rows = slice(image * span, (image + 1) * span)
        dqi_ref, dfk_ref, dvl_ref = locals_[image]
        dq_ref[rows, :] = dqi_ref[...]
        for pair in range(GROUP // PAIR):
            lanes = slice(pair * PAIR, (pair + 1) * PAIR)
            folded = later_ref[image, pair]
            high, rest = split_low(unfold_state(folded[:HEAD_DIM]))
            key, value = fk_ref[rows, lanes], v_ref[rows, lanes]
            dfk = dfk_ref[:, lanes] + folded[HEAD_DIM : HEAD_DIM + 1]
            dfk = dfk + mm(jnp.concatenate([value, value], axis=1), jnp.concatenate([high, rest], axis=0))
            dv = dvl_ref[:, lanes] + mt(
                jnp.concatenate([key, key], axis=1), jnp.concatenate([high, rest], axis=1)
            )
            dk_ref[rows, lanes] = (dfk * jnp.minimum(key.astype(wide), 1.0)).astype(low)
            dv_ref[rows, lanes] = dv.astype(low)
    for k, ref in enumerate((dq_ref, dk_ref, dv_ref)):
        mine_ref[k] = mm(at_ref[:half, :], ref[...]).astype(low)
        other_ref[k] = mm(at_ref[half:, :], ref[...]).astype(low)


def finish(side, parts, fk, v, later, at, images, span, tokens=()):
    rows, width = fk.shape
    half = width // 2
    groups = half // GROUP
    column = pl.BlockSpec((rows, GROUP), lambda g: (0, side * groups + g))
    part = pl.BlockSpec((span, GROUP), lambda g: (0, side * groups + g))
    result = pl.BlockSpec((rows, GROUP), lambda g: (0, g))
    grads = pl.BlockSpec((3, half, GROUP), lambda g: (0, 0, g))
    state = pl.BlockSpec((images, GROUP // PAIR) + later.shape[2:], lambda g: (0, side * groups + g, 0, 0))
    return launch(
        functools.partial(finish_kernel, images, span),
        tokens,
        grid=(groups,),
        in_specs=[part] * (3 * images) + [column] * 2 + [state, whole(at.shape)],
        out_specs=[result] * 3 + [grads, grads],
        out_shape=[shaped((rows, half), low)] * 3 + [shaped((3, half, half), low)] * 2,
        cost_estimate=cost(2 * rows * width * width, 15 * rows * width),
        name="finish",
    )(*[array for image in parts for array in image], fk, v, later, at)


def enter_kernel(spots, core_ref, *refs):
    lefts, rights, weights = refs[:3], refs[3:6], refs[6:12]
    x_ref, dres_ref, vec_ref, grad_ref, sums_ref = refs[12:]
    half = x_ref.shape[1] // 2
    parts = []
    for side in range(2):
        total = None
        for k in range(3):
            weight = weights[2 * k + side]
            part = mt(lefts[k][...], weight[0, :, :half]) + mt(rights[k][...], weight[0, :, half : 2 * half])
            total = part if total is None else total + part
        parts.append(total)
    da = jnp.concatenate(parts, axis=1)
    unit, scale = normalised(x_ref[...].astype(wide))
    sums_ref[0:1, :] = jnp.sum(da * unit, axis=0, keepdims=True)
    sums_ref[1:2, :] = jnp.sum(da, axis=0, keepdims=True)
    sums_ref[2:, :] = jnp.zeros_like(sums_ref[2:, :])
    p = da * vec_ref[0:1, :]
    back = p - jnp.mean(p, axis=-1, keepdims=True) - unit * jnp.mean(p * unit, axis=-1, keepdims=True)
    put_natural(grad_ref, (dres_ref[...] + scale * back).astype(low), core_ref, spots)


def enter(image, core, spots, left, right, weights, x, dres, vec, span, tokens=()):
    width = x.shape[1]
    half = width // 2
    rows = pl.BlockSpec((span, width), lambda g: (image, 0))
    part = pl.BlockSpec((span, half), lambda g: (image, 0))
    weights = [array for pair in weights for array in pair]
    return launch(
        functools.partial(enter_kernel, spots),
        tokens,
        grid=(1,),
        in_specs=[pl.BlockSpec(memory_space=pltpu.SMEM)]
        + [part] * 6
        + [pl.BlockSpec((1, half, width), lambda g: (0, 0, 0))] * 6
        + [rows, rows, whole(vec.shape)],
        out_specs=[whole((span, width)), whole((8, width))],
        out_shape=[shaped((span, width), low), shaped((8, width), wide)],
        cost_estimate=cost(3 * span * width * width, 14 * span * width + 6 * width * width),
        name="enter",
    )(core.reshape(1), *left, *right, *weights, x, dres, vec)


def adam_update(master, moment, second, average, gradient, factor, rate):
    clipped = gradient * factor
    moment = beta_first * moment + (1.0 - beta_first) * clipped
    second = beta_second * second + (1.0 - beta_second) * clipped * clipped
    first_hat = moment / (1.0 - beta_first**STEP)
    second_hat = second / (1.0 - beta_second**STEP)
    master = master - rate * (first_hat / (jnp.sqrt(second_hat) + eps_adam) + weight_decay * master)
    average = average_decay * average + (1.0 - average_decay) * master
    return (master, moment, second, average)


def flip_pairs(count, bit):
    return [(i, i ^ bit) for i in range(count)]


def powers(count):
    return [1 << k for k in range(count.bit_length() - 1)]


def flip(array, axis, bit=1):
    return lax.ppermute(array, axis, flip_pairs(lax.axis_size(axis), bit))


def fold_kernel(counts, spot_ref, *refs):
    total = sum(counts)
    ins, outs = refs[: 2 * total], refs[2 * total :]
    for k in range(total):
        value = ins[2 * k][...].astype(wide) + ins[2 * k + 1][...].astype(wide)
        outs[k][...] = value.astype(outs[k].dtype)


def fold(chains, tokens=()):
    steps = 4
    in_specs, out_specs, out_shape, arrays, counts, spots, moved = [], [], [], [], [], [], 0
    for k, (kept, came, pre, ways, own) in enumerate(chains):
        columns = kept.shape[-1]
        first = kept.dtype == low
        rows = kept.size // (columns * pre * ways)
        kept, came = (array.reshape(pre, ways, rows, columns) for array in (kept, came))
        counts.append(ways)
        spots.append(own)
        moved += 8 * kept.size
        for j in range(ways):
            block = (pre, 1, rows, columns // steps)
            spec = pl.BlockSpec(block, lambda c, spot, k=k, j=j: (0, spot[k] ^ j, 0, c))
            in_specs += [spec, spec]
            arrays += [kept, came]
            out_specs.append(pl.BlockSpec(block, lambda c, spot: (0, 0, 0, c)))
            out_shape.append(shaped((pre, 1, rows, columns), low if j or first else wide))
    total, extra = len(in_specs), len(tokens)

    def run(spot_ref, *refs):
        fold_kernel(counts, spot_ref, *refs[:total], *refs[total + extra :])

    results = pl.pallas_call(
        run,
        grid_spec=pltpu.PrefetchScalarGridSpec(
            num_scalar_prefetch=1,
            grid=(steps,),
            in_specs=in_specs + [pl.BlockSpec(memory_space=pl.ANY)] * extra,
            out_specs=out_specs,
        ),
        out_shape=out_shape,
        compiler_params=params(),
        cost_estimate=cost(1, moved),
        name="fold",
    )(jnp.stack(spots).astype(jnp.int32), *arrays, *tokens)
    groups = []
    for ways in counts:
        groups.append([part.reshape(part.shape[0], part.shape[2], part.shape[3]) for part in results[:ways]])
        results = results[ways:]
    return groups


class Chain:
    def __init__(self, kept, sent, order):
        self.lead = kept.shape[0] if kept.ndim == 3 else 1
        self.kept = kept
        self.sends = [sent]
        self.hops = [("core", 1)]
        self.axis = "pos"
        self.bits = powers(lax.axis_size("pos"))[::order]
        self.left = powers(lax.axis_size("pos"))[::-1]

    def start(self):
        self.came = [flip(array, axis, bit) for array, (axis, bit) in zip(self.sends, self.hops)]

    def cut(self):
        bit = next(bit for bit in self.bits if bit in self.left)
        pre = self.lead << self.left.index(bit)
        self.left.remove(bit)
        self.hops = [(self.axis, bit)]
        return (self.kept, self.came[0], pre, 2, (lax.axis_index(self.axis) // bit) % 2)

    def take(self, parts):
        self.kept, self.sends = parts[0], list(parts[1:])


def advance(chains, tokens=()):
    groups = fold([chain.cut() for chain in chains], tokens)
    for chain, parts in zip(chains, groups):
        chain.take(parts)
        chain.start()
    return [array for chain in chains for array in chain.sends]


def last_kernel(ways, lead, pieces, spot_ref, *refs):
    ins, outs = refs[: 2 * pieces], refs[2 * pieces :]
    at = 0
    for k in range(pieces):
        columns = ins[2 * k].shape[-1]
        for j in range(ways):
            place = spot_ref[0] ^ j
            for n in range(lead):
                value = ins[2 * k][n, place].astype(wide) + ins[2 * k + 1][n, place].astype(wide)
                outs[j][n, :, at : at + columns] = value.astype(outs[j].dtype)
        at += columns


class Last:
    def __init__(self, chains, tokens=(), slowly=False):
        ways = 2 if slowly else lax.axis_size("img")
        lead = chains[0].lead
        pre = lead * lax.axis_size("img") // ways
        arrays = []
        for chain in chains:
            for array in (chain.kept, chain.came[0]):
                arrays.append(array.reshape(pre, ways, -1, array.shape[-1]))
        self.widths = [array.shape[-1] for array in arrays[::2]]
        rows = chains[0].kept.size // (chains[0].kept.shape[-1] * pre * ways)
        inside = pl.BlockSpec(memory_space=pltpu.VMEM)
        parts = launch(
            functools.partial(last_kernel, ways, pre, len(chains)),
            tokens,
            in_specs=[pl.BlockSpec(memory_space=pltpu.SMEM)] + [inside] * len(arrays),
            out_specs=[inside] * ways,
            out_shape=[shaped((pre, rows, sum(self.widths)), low if j else wide) for j in range(ways)],
            cost_estimate=cost(1, 4 * sum(array.size for array in arrays)),
            name="last",
        )((lax.axis_index("img") % ways).reshape(1), *arrays)
        self.lead = lead
        self.kept, self.sends = parts[0], list(parts[1:])
        self.axis = "img"
        self.hops = [("img", j + 1) for j in range(ways - 1)]
        self.bits = powers(lax.axis_size("img"))[1:] if slowly else []
        self.left = self.bits[::-1]
        self.start()

    start, cut, take = Chain.start, Chain.cut, Chain.take

    def result(self):
        while self.left:
            advance([self])
        total = self.kept
        for came in self.came:
            total = total + came.astype(wide)
        self.total = total
        return total

    def pieces(self):
        at, found = 0, []
        for columns in self.widths:
            found.append(self.total[..., at : at + columns])
            at += columns
        return found


def sum_slowly(array):
    for axis in ("core", "pos", "img"):
        for bit in powers(lax.axis_size(axis)):
            array = array + flip(array, axis, bit)
    return array


def sum_all(array):
    for axis in ("img", "pos", "core"):
        came = [flip(array, axis, j) for j in range(1, lax.axis_size(axis))]
        for other in came:
            array = array + other
    return array


def assemble_kernel(plan, spot_ref, *refs):
    outs = sorted({out for _, _, out, _ in plan})
    count = len(refs) - 1 - len(outs)
    sems = refs[-1]
    copies = []
    for k, (piece, cut, out, where) in enumerate(plan):
        source = refs[piece].at[cut] if cut is not None else refs[piece]
        target = refs[count + out].at[where(spot_ref)]
        copies.append(pltpu.make_async_copy(source, target, sems.at[k]))
    for copy in copies:
        copy.start()
    for copy in copies:
        copy.wait()


def assemble(plan, spots, pieces, shapes, tokens=()):
    anywhere = pl.BlockSpec(memory_space=pl.ANY)
    return launch(
        functools.partial(assemble_kernel, plan),
        tokens,
        in_specs=[pl.BlockSpec(memory_space=pltpu.SMEM)] + [anywhere] * len(pieces),
        out_specs=[pl.BlockSpec(memory_space=pltpu.VMEM)] * len(shapes),
        out_shape=[shaped(shape, low) for shape in shapes],
        scratch_shapes=[pltpu.SemaphoreType.DMA((len(plan),))],
        cost_estimate=cost(1, 2 * sum(2 * piece.size for piece in pieces)),
        name="assemble",
    )(jnp.stack(spots).astype(jnp.int32), *pieces)


class Gather:
    def __init__(self, packed, cuts, shapes, order):
        self.packed, self.cuts, self.shapes = packed, cuts, shapes
        self.orders = [order, -order]

    def start_slices(self):
        self.pieces = [self.packed] + [flip(self.packed, "img", j) for j in range(1, lax.axis_size("img"))]

    def finish_slices(self, tokens=()):
        slices = len(self.pieces)
        plan = [
            (j, cut, out, lambda spot, j=j: (slice(None), spot[0] ^ j))
            for j in range(slices)
            for out, cut in enumerate(self.cuts)
        ]
        shapes = [(k, slices, r, c) for k, r, c in self.shapes]
        parts = assemble(plan, [lax.axis_index("img")], self.pieces, shapes, tokens)
        self.parts = [part.reshape(k, slices * r, c) for part, (k, r, c) in zip(parts, self.shapes)]
        self.dims = [[], []]
        return self.parts

    def start_pos(self):
        self.bits = [powers(lax.axis_size("pos"))[::order][len(dims)] for order, dims in zip(self.orders, self.dims)]
        self.came = [flip(part, "pos", bit) for part, bit in zip(self.parts, self.bits)]

    def finish_pos(self, tokens=()):
        plan, shapes, places = [], [], []
        for out, (part, bit, dims) in enumerate(zip(self.parts, self.bits, self.dims)):
            place = 1 + sum(other > bit for other in dims)
            places.append(place)
            shapes.append(part.shape[:place] + (2,) + part.shape[place:])
            ahead = (slice(None),) * place
            plan.append((2 * out, None, out, lambda spot, ahead=ahead, out=out: ahead + (spot[out],)))
            plan.append((2 * out + 1, None, out, lambda spot, ahead=ahead, out=out: ahead + (1 - spot[out],)))
            dims.append(bit)
        spots = [(lax.axis_index("pos") // bit) % 2 for bit in self.bits]
        pieces = [array for pair in zip(self.parts, self.came) for array in pair]
        self.parts = assemble(plan, spots, pieces, shapes, tokens)
        return self.parts

    def start_core(self):
        self.mine = [part.reshape(part.shape[0], -1, part.shape[-1]) for part in self.parts]
        self.other = [flip(part, "core") for part in self.mine]
        return list(zip(self.mine, self.other))


def narrow_kernel(plan, *refs):
    out_ref = refs[-1]
    for k, (ref, member, columns) in enumerate(plan):
        out_ref[k] = refs[ref][member, :, columns].astype(low)


def narrow(plan, weights, tokens=()):
    owned = weights[0].shape[1]
    inside = pl.BlockSpec(memory_space=pltpu.VMEM)
    return launch(
        functools.partial(narrow_kernel, plan),
        tokens,
        in_specs=[inside] * len(weights),
        out_specs=inside,
        out_shape=shaped((len(plan), owned, SLAB), low),
        cost_estimate=cost(1, 6 * len(plan) * owned * SLAB),
        name="narrow",
    )(*weights)


def passing(own, backward):
    total = own
    outside = jnp.zeros_like(own)
    for axis in ("core", "pos"):
        for bit in powers(lax.axis_size(axis)):
            came = flip(total.astype(low), axis, bit).astype(wide)
            upper = (lax.axis_index(axis) // bit) % 2
            counts = upper == (0 if backward else 1)
            outside = outside + jnp.where(counts, came, 0.0)
            total = total + came
    return outside


def body(
    images,
    cotangent,
    attention_weight,
    feedforward_weight,
    norm_vectors,
    attention_moment,
    feedforward_moment,
    norm_moment,
    attention_second,
    feedforward_second,
    norm_second,
    attention_average,
    feedforward_average,
    norm_average,
):
    count, span, width = images.shape
    tokens = count * span
    spots = lax.axis_size("pos")
    slices = lax.axis_size("img")
    core = lax.axis_index("core")
    owned = attention_weight.shape[1]
    hidden_width = feedforward_weight.shape[2]
    slabs = hidden_width // SLAB

    weights = (attention_weight, feedforward_weight)
    steps = len(powers(spots))
    half = slabs // 2
    every = slice(None)

    def stretch(k):
        return slice(k * SLAB, (k + 1) * SLAB)

    vectors = jnp.pad(norm_vectors.astype(low).T[None], ((1, 0), (0, 0), (0, 124)))
    packed = jnp.concatenate([attention_weight[1:3].astype(low), vectors], axis=2)
    cuts = [(slice(0, 1), every, slice(0, width)), (slice(1, 2), every, every)]
    one = Gather(packed, cuts, [(1, owned, width), (1, owned, width + 128)], 1)
    packed = narrow([(0, 0, every), (0, 3, every)], weights)
    two = Gather(packed, [slice(0, 1), slice(1, 2)], [(1, owned, width)] * 2, -1)

    one.start_slices()
    feeds = lax.all_gather(feedforward_weight.astype(low), ("pos", "core", "img"), axis=1, tiled=True)
    feeds = feeds.reshape(2, spots, 2, -1, hidden_width)
    x, e, et = prepare(images.reshape(tokens, width), cotangent.reshape(tokens, width), core, spots, count, span)
    et = turned_whole(et)
    one.finish_slices([et, two.packed])
    one.start_pos()
    two.start_slices()
    for step in range(steps - 1):
        marks = one.finish_pos()
        one.start_pos()
    marks = two.finish_slices(marks)
    two.start_pos()
    marks = one.finish_pos(marks)
    keys, values = one.start_core()
    for step in range(steps - 1):
        marks = two.finish_pos(marks)
        two.start_pos()
    vec = jnp.concatenate([part[0, :, width : width + 4] for part in values], axis=0).astype(wide).T

    fk, v, a1, a1t, state = project(x, vec, keys, values, count, span, marks)
    marks = two.finish_pos([state])
    queries, outer_weight = two.start_core()
    prior = passing(state, False)
    fq = query(a1, queries)
    num, den = attend(fq, fk, v, count, span)
    wo = arrange(outer_weight, core, spots)
    mixed, rden, resid, a2, a2t = mix(x, vec, wo, fq, num, den, prior, count, span)
    a2t = turned_whole(a2t)

    early = feed(core, feeds, 0, 2, a2, a2t, e, et, None)
    firsts = [Chain(early[2], early[3], 1), Chain(early[4], early[5], -1)]
    for chain in firsts:
        chain.start()
    late = feed(core, feeds, 1, 2, a2, a2t, e, et, early[:2])
    seconds = [Chain(late[2], late[3], 1), Chain(late[4], late[5], -1)]
    for chain in seconds:
        chain.start()
    marks = advance(firsts)
    output, dres, branch, dn, w, dstate, sums_second = turn_back(
        core, spots, late[0], late[1], resid, e, vec, wo, mixed, rden, fq, count, span, marks
    )
    later = passing(dstate, True)
    outs = [Chain(*outer(core, spots, mixed, branch), 1)]
    marks = advance(seconds) + advance(firsts)
    parts = []
    for image in range(count):
        parts.append(attend_back(image, fq, fk, v, dn, w, prior, span, marks))
        if image == 0:
            outs[0].start()
            marks = advance(outs, [parts[0][0]])
            for step in range(steps - 2):
                advance(firsts)
            firsts_last = Last(firsts, [parts[0][0]], True)
            marks = marks + firsts_last.sends
    for step in range(steps - 2):
        advance(seconds)
        advance(outs)
    marks = advance(seconds + outs, [parts[-1][0]])
    if firsts_last.left:
        marks = marks + advance([firsts_last], [parts[-1][0]])
    left = finish(0, parts, fk, v, later, a1t, count, span, marks)
    inner = [Chain(left[3], left[4], 1)]
    inner[0].start()
    firsts_last.result()
    seconds_last = Last(seconds + outs, [left[0]], True)
    marks = seconds_last.sends + [firsts_last.total]
    right = finish(1, parts, fk, v, later, a1t, count, span, marks)
    inner.append(Chain(right[3], right[4], -1))
    inner[1].start()
    marks = advance(inner[:1], [right[0]])
    if seconds_last.left:
        marks = marks + advance([seconds_last], [right[0]])
    projections = (queries, keys, values)
    grads_in = []
    for image in range(count):
        grads_in.append(
            enter(image, core, spots, left[:3], right[:3], projections, x, dres, vec, span, marks)
        )
        if image == 0:
            seconds_last.result()
            marks = advance(inner[1:], [grads_in[0][1]]) + [seconds_last.total]
    input_grad = jnp.stack([part[0] for part in grads_in])
    sums_first = sum(part[1] for part in grads_in)
    vector_grad = jnp.concatenate([swap_blocks(part[:2], core, spots, True) for part in (sums_first, sums_second)], axis=0)
    vector_grad = sum_slowly(vector_grad)
    device = (lax.axis_index("pos") * 2 + core) * slices + lax.axis_index("img")
    vector_shard = lax.dynamic_slice_in_dim(vector_grad, device * norm_vectors.shape[1], norm_vectors.shape[1], 1)
    advance(inner)
    while inner[0].left:
        advance(inner)
    inner_last = Last(inner, [vector_shard])
    inner_shard = inner_last.result()
    up_late, down_late, out_shard = seconds_last.pieces()
    up_early, down_early = firsts_last.pieces()
    out_shard = swap_blocks(out_shard, core, spots, True)
    attn_shard = jnp.concatenate([inner_shard, out_shard], axis=0)
    feed_shard = jnp.concatenate(
        [jnp.concatenate([up_early, up_late], axis=2), jnp.concatenate([down_early, down_late], axis=2)], axis=0
    )
    if (width // (2 * spots)) % 128:
        output = swap_blocks(output, core, spots, True)
        input_grad = swap_blocks(input_grad, core, spots, True)

    local_squares = (
        jnp.sum(attn_shard * attn_shard) + jnp.sum(feed_shard * feed_shard) + jnp.sum(vector_shard * vector_shard)
    )
    grad_norm = jnp.sqrt(sum_all(jnp.full((8, 128), local_squares))[0, 0])
    factor = clip_bound / jnp.maximum(grad_norm, clip_bound)
    attn_new = adam_update(
        attention_weight, attention_moment, attention_second, attention_average, attn_shard, factor, learn_rate
    )
    feed_new = adam_update(
        feedforward_weight, feedforward_moment, feedforward_second, feedforward_average, feed_shard, factor, learn_rate
    )
    norm_new = adam_update(norm_vectors, norm_moment, norm_second, norm_average, vector_shard, factor, norm_rate)
    output = output.reshape(images.shape)
    input_grad = input_grad.reshape(images.shape)
    return (output, input_grad, grad_norm) + attn_new + feed_new + norm_new


def solution(mesh):
    seq, img = mesh.devices.shape
    inner = Mesh(mesh.devices.reshape(seq // 2, 2, img), ("pos", "core", "img"))
    tokens = P("img", ("pos", "core"), None)
    rows = P(None, ("pos", "core", "img"), None)
    vectors = P(None, ("pos", "core", "img"))
    group = (rows, rows, vectors)
    return jax.shard_map(
        body,
        mesh=inner,
        in_specs=(tokens, tokens) + group * 4,
        out_specs=(tokens, tokens, P()) + (rows,) * 8 + (vectors,) * 4,
        check_vma=False,
    )
```

```python
import functools

import jax
import jax.numpy as jnp
from jax import lax
from jax.experimental import pallas as pl
from jax.experimental.pallas import tpu as pltpu
from jax.sharding import Mesh
from jax.sharding import PartitionSpec as P

HEADS = 16
HEAD_DIM = 64
STEP = 10

beta_first = 0.9
beta_second = 0.95
learn_rate = 0.02
norm_rate = 0.2
weight_decay = 0.1
average_decay = 0.75
clip_bound = 1.0
eps_norm = 1e-05
eps_adam = 1e-08

PAIR = 2 * HEAD_DIM
STATE_ROWS = HEAD_DIM + 16
SLAB = 1024
TILE = 512
GROUP = 256

low = jnp.bfloat16
wide = jnp.float32


def params(megabytes=56):
    return pltpu.CompilerParams(vmem_limit_bytes=megabytes * 1024 * 1024)


def cost(products, elements):
    return pl.CostEstimate(flops=products // 4, bytes_accessed=elements // 8, transcendentals=0)


def launch(kernel, tokens, in_specs, megabytes=56, **keys):
    known, extra = len(in_specs), len(tokens)

    def run(*refs):
        kernel(*refs[:known], *refs[known + extra :])

    call = pl.pallas_call(
        run, in_specs=list(in_specs) + [pl.BlockSpec(memory_space=pl.ANY)] * extra, compiler_params=params(megabytes), **keys
    )
    return lambda *args: call(*args, *tokens)


def launch_at(kernel, spot, tokens, grid, in_specs, out_specs, megabytes=56, **keys):
    known, extra = len(in_specs), len(tokens)

    def run(spot_ref, *refs):
        kernel(spot_ref, *refs[:known], *refs[known + extra :])

    call = pl.pallas_call(
        run,
        grid_spec=pltpu.PrefetchScalarGridSpec(
            num_scalar_prefetch=1,
            grid=grid,
            in_specs=list(in_specs) + [pl.BlockSpec(memory_space=pl.ANY)] * extra,
            out_specs=out_specs,
        ),
        compiler_params=params(megabytes),
        **keys,
    )
    return lambda *args: call(spot.reshape(-1).astype(jnp.int32), *args, *tokens)


def owned_block(weights, which, flipped, columns, place):
    block = (None, weights.shape[1], None, weights.shape[3], columns)
    return pl.BlockSpec(block, lambda *g: (which, 0, g[-1][0] ^ flipped, 0, place(*g[:-1])))


def flat(ref):
    return ref[...].reshape(-1, ref.shape[-1])


def shaped(shape, kind):
    return jax.ShapeDtypeStruct(shape, kind)


def whole(shape):
    return pl.BlockSpec(shape, lambda *_: (0,) * len(shape))


def mm(left, right):
    return lax.dot_general(left, right, (((1,), (0,)), ((), ())), preferred_element_type=wide)


def mt(left, right):
    return lax.dot_general(left, right, (((1,), (1,)), ((), ())), preferred_element_type=wide)


def tm(left, right):
    return lax.dot_general(left, right, (((0,), (0,)), ((), ())), preferred_element_type=wide)


def pair_mm(first, second):
    if first[0].shape[1] % 128:
        return mm(*first) + mm(*second)
    return mm(jnp.concatenate([first[0], second[0]], axis=1), jnp.concatenate([first[1], second[1]], axis=0))


def causal_mask(span, below):
    rows = lax.broadcasted_iota(jnp.int32, (span, span), 0)
    columns = lax.broadcasted_iota(jnp.int32, (span, span), 1)
    return (rows >= columns if below else rows <= columns).astype(wide).astype(low)


def first_head(rows):
    return lax.broadcasted_iota(jnp.int32, (rows, PAIR), 1) < HEAD_DIM


def fold_state(product):
    return jnp.where(first_head(HEAD_DIM), product[:HEAD_DIM], product[HEAD_DIM:])


def unfold_state(folded):
    own = first_head(HEAD_DIM)
    zero = jnp.zeros_like(folded)
    return jnp.concatenate([jnp.where(own, folded, zero), jnp.where(own, zero, folded)], axis=0)


def unfold_total(row):
    tall = jnp.broadcast_to(row, (PAIR, PAIR))
    lanes = lax.broadcasted_iota(jnp.int32, (PAIR, PAIR), 1) < HEAD_DIM
    rows = lax.broadcasted_iota(jnp.int32, (PAIR, PAIR), 0) < HEAD_DIM
    return jnp.where(lanes == rows, tall, jnp.zeros_like(tall))


def split_low(values):
    high = values.astype(low)
    return high, (values - high.astype(wide)).astype(low)


def normalised(values):
    centre = jnp.mean(values, axis=-1, keepdims=True)
    centred = values - centre
    spread = jnp.mean(centred * centred, axis=-1, keepdims=True)
    scale = lax.rsqrt(spread + eps_norm)
    return centred * scale, scale


def feature(raw):
    return jnp.where(raw > 0, raw + 1.0, jnp.exp(jnp.minimum(raw, 0.0))).astype(low)


def project_kernel(images, span, core_ref, x_ref, vec_ref, km_ref, ko_ref, vm_ref, vo_ref, fk_ref, v_ref, a_ref, at_ref, state_ref):
    half = x_ref.shape[1] // 2

    @pl.when(pl.program_id(0) == 0)
    def _():
        gain, shift = vec_ref[0:1, :], vec_ref[1:2, :]
        step = span // 3
        for start in range(0, images * span, step):
            rows = slice(start, start + step)
            unit, _ = normalised(x_ref[rows, :].astype(wide))
            a_ref[rows, :] = (unit * gain + shift).astype(low)
        at_ref[...] = a_ref[...].T

    left, right = a_ref[:, :half], a_ref[:, half:]
    fk_ref[...] = feature(mm(left, flat(km_ref)) + mm(right, flat(ko_ref)))
    v_ref[...] = (mm(left, flat(vm_ref)) + mm(right, flat(vo_ref))).astype(low)
    ones = jnp.ones((16, span), low)
    for image in range(images):
        rows = slice(image * span, (image + 1) * span)
        for pair in range(GROUP // PAIR):
            lanes = slice(pair * PAIR, (pair + 1) * PAIR)
            key, value = fk_ref[rows, lanes], v_ref[rows, lanes]
            state_ref[image, pair, :HEAD_DIM, :] = fold_state(tm(value, key))
            state_ref[image, pair, HEAD_DIM:, :] = mm(ones, key)


def project(core, x, vec, weights, images, span, tokens=()):
    count, width = x.shape
    pairs = GROUP // PAIR
    blocks = [owned_block(weights, which, flipped, GROUP, lambda g: g) for which in range(2) for flipped in range(2)]
    column = pl.BlockSpec((count, GROUP), lambda g, core: (0, g))
    return launch_at(
        functools.partial(project_kernel, images, span),
        core,
        tokens,
        grid=(width // GROUP,),
        in_specs=[whole((count, width)), whole(vec.shape)] + blocks,
        out_specs=[
            column,
            column,
            whole((count, width)),
            whole((width, count)),
            pl.BlockSpec((images, pairs, STATE_ROWS, PAIR), lambda g, core: (0, g, 0, 0)),
        ],
        out_shape=[
            shaped((count, width), low),
            shaped((count, width), low),
            shaped((count, width), low),
            shaped((width, count), low),
            shaped((images, width // PAIR, STATE_ROWS, PAIR), wide),
        ],
        cost_estimate=cost(2 * count * width * width, 8 * width * width + 12 * count * width),
        megabytes=40,
        name="project",
    )(x, vec, *[weights] * 4)


def query_kernel(core_ref, a_ref, qm_ref, qo_ref, fq_ref):
    half = a_ref.shape[1] // 2
    fq_ref[...] = feature(mm(a_ref[:, :half], flat(qm_ref)) + mm(a_ref[:, half:], flat(qo_ref)))


def query(core, a, weights, tokens=()):
    count, width = a.shape
    return launch_at(
        query_kernel,
        core,
        tokens,
        grid=(width // GROUP,),
        in_specs=[whole((count, width))] + [owned_block(weights, 0, flipped, GROUP, lambda g: g) for flipped in range(2)],
        out_specs=pl.BlockSpec((count, GROUP), lambda g, core: (0, g)),
        out_shape=shaped((count, width), low),
        cost_estimate=cost(count * width * width, 3 * width * width + 4 * count * width),
        megabytes=20,
        name="query",
    )(a, *[weights] * 2)


def swap_blocks(array, core, spots, inverse):
    if inverse:
        half = array.shape[-1] // 2
        mine, other = (part.reshape(array.shape[:-1] + (spots, 1, -1)) for part in (array[..., :half], array[..., half:]))
        parts = [jnp.where(core == 0, mine, other), jnp.where(core == 0, other, mine)]
        return jnp.concatenate(parts, axis=-2).reshape(array.shape)
    parts = array.reshape(array.shape[:-1] + (spots, 2, -1))
    even, odd = (parts[..., k, :].reshape(array.shape[:-1] + (-1,)) for k in range(2))
    return jnp.concatenate([jnp.where(core == 0, even, odd), jnp.where(core == 0, odd, even)], axis=-1)


def block_of(spot, core, block):
    return pl.ds(pl.multiple_of((2 * spot + core) * block, block), block)


def prepare_kernel(spots, core_ref, x_ref, e_ref, xo_ref, eo_ref, et_ref):
    width = x_ref.shape[1]
    block = width // (2 * spots)
    for side in range(2):
        core = core_ref[0] if side == 0 else 1 - core_ref[0]
        for spot in range(spots):
            target = slice((side * spots + spot) * block, (side * spots + spot + 1) * block)
            source = block_of(spot, core, block)
            xo_ref[:, target] = x_ref[:, source]
            eo_ref[:, target] = e_ref[:, source]
    et_ref[...] = eo_ref[...].T


def turn_kernel(x_ref, out_ref):
    out_ref[...] = x_ref[...].T


def prepare(x, e, core, spots, images, span, tokens=()):
    count, width = x.shape
    rows = pl.BlockSpec((span, width), lambda b: (b, 0))
    turned = turned_block(width, span)
    if (width // (2 * spots)) % 128:
        x, e = swap_blocks(x, core, spots, False), swap_blocks(e, core, spots, False)
        et = launch(
            turn_kernel, tokens, grid=(images,), in_specs=[rows], out_specs=turned, out_shape=turned_shape(images, width, span), name="turn"
        )(e)
        return x, e, et
    return launch(
        functools.partial(prepare_kernel, spots),
        tokens,
        grid=(images,),
        in_specs=[pl.BlockSpec(memory_space=pltpu.SMEM), rows, rows],
        out_specs=[rows, rows, turned],
        out_shape=[shaped((count, width), low)] * 2 + [turned_shape(images, width, span)],
        cost_estimate=cost(1, 12 * count * width),
        megabytes=16,
        name="prepare",
    )(core.reshape(1), x, e)


def arrange_kernel(spots, core_ref, weight_ref, out_ref):
    width = out_ref.shape[1]
    block = width // (2 * spots)
    for half in range(2):
        origin = core_ref[0] if half == 0 else 1 - core_ref[0]
        for spot in range(spots):
            at = (half * spots + spot) * block
            out_ref[:, at : at + block] = weight_ref[:, block_of(spot, origin, block)]


def arrange(weights, core, spots, tokens=()):
    width = weights.shape[2]
    if (width // (2 * spots)) % 128:
        return swap_blocks(weights[1], core, spots, False)
    return launch(
        functools.partial(arrange_kernel, spots),
        tokens,
        grid=(2,),
        in_specs=[
            pl.BlockSpec(memory_space=pltpu.SMEM),
            pl.BlockSpec((None, width // 2, width), lambda g: (1, g, 0)),
        ],
        out_specs=pl.BlockSpec((width // 2, width), lambda g: (g, 0)),
        out_shape=shaped((width, width), low),
        cost_estimate=cost(1, 4 * width * width),
        megabytes=16,
        name="arrange",
    )(core.reshape(1), weights)


def put_natural(ref, value, core_ref, spots):
    width = value.shape[1]
    block = width // (2 * spots)
    if block % 128:
        ref[...] = value
        return
    for side in range(2):
        core = core_ref[0] if side == 0 else 1 - core_ref[0]
        for spot in range(spots):
            at = (side * spots + spot) * block
            ref[:, block_of(spot, core, block)] = value[:, at : at + block]


def attend_kernel(span, fq_ref, fk_ref, v_ref, num_ref, den_ref):
    own = first_head(span)
    causal = causal_mask(span, True)
    one = jnp.ones((span, PAIR), low)
    zero = jnp.zeros((span, PAIR), low)
    for pair in range(GROUP // PAIR):
        lanes = slice(pair * PAIR, (pair + 1) * PAIR)
        query, key, value = fq_ref[:, lanes], fk_ref[:, lanes], v_ref[:, lanes]
        products = []
        for mask in (own, jnp.logical_not(own)):
            scores = mt(jnp.where(mask, query, zero), key).astype(low) * causal
            right = jnp.concatenate([jnp.where(mask, value, zero), jnp.where(mask, one, zero)], axis=1)
            products.append((scores, right))
        total = pair_mm(*products)
        num_ref[:, lanes] = total[:, :PAIR]
        den_ref[:, lanes] = total[:, PAIR:]


def attend(fq, fk, v, images, span, tokens=()):
    rows, width = fq.shape
    block = pl.BlockSpec((span, GROUP), lambda b, p: (b, p))
    return launch(
        functools.partial(attend_kernel, span),
        tokens,
        grid=(images, width // GROUP),
        in_specs=[block] * 3,
        out_specs=[block] * 2,
        out_shape=[shaped((rows, width), wide)] * 2,
        cost_estimate=cost(16 * rows * span * width, 14 * rows * width),
        megabytes=16,
        name="attend",
    )(fq, fk, v)


def turned_block(width, span):
    if span % 128:
        return pl.BlockSpec((None, width, span), lambda b: (b, 0, 0))
    return pl.BlockSpec((width, span), lambda b: (0, b))


def turned_shape(images, width, span):
    return shaped((images, width, span) if span % 128 else (width, images * span), low)


def turned_whole(array):
    if array.ndim == 2:
        return array
    return jnp.swapaxes(array, 0, 1).reshape(array.shape[1], -1)


def mix_kernel(x_ref, vec_ref, wo_ref, fq_ref, num_ref, den_ref, prior_ref, mixed_ref, rden_ref, resid_ref, a_ref, at_ref):
    width = x_ref.shape[1]
    for pair in range(width // PAIR):
        lanes = slice(pair * PAIR, (pair + 1) * PAIR)
        folded = prior_ref[0, pair]
        matrix = jnp.concatenate(
            [unfold_state(folded[:HEAD_DIM]), unfold_total(folded[HEAD_DIM : HEAD_DIM + 1])], axis=0
        )
        high, rest = split_low(matrix)
        query = fq_ref[:, lanes]
        both = mt(jnp.concatenate([query, query], axis=1), jnp.concatenate([high, rest], axis=1))
        scale = 1.0 / (den_ref[:, lanes] + both[:, PAIR:])
        rden_ref[:, lanes] = scale
        mixed_ref[:, lanes] = ((num_ref[:, lanes] + both[:, :PAIR]) * scale).astype(low)
    resid = x_ref[...].astype(wide) + mm(mixed_ref[...], wo_ref[...])
    resid_ref[...] = resid
    unit, _ = normalised(resid)
    normed = (unit * vec_ref[2:3, :] + vec_ref[3:4, :]).astype(low)
    a_ref[...] = normed
    at_ref[...] = normed.T


def mix(x, vec, wo, fq, num, den, prior, images, span, tokens=()):
    rows_, width = x.shape
    rows = pl.BlockSpec((span, width), lambda b: (b, 0))
    return launch(
        mix_kernel,
        tokens,
        grid=(images,),
        in_specs=[
            rows,
            whole(vec.shape),
            whole(wo.shape),
            rows,
            rows,
            rows,
            pl.BlockSpec((1,) + prior.shape[1:], lambda b: (b, 0, 0, 0)),
        ],
        out_specs=[rows, rows, rows, rows, turned_block(width, span)],
        out_shape=[
            shaped((rows_, width), low),
            shaped((rows_, width), wide),
            shaped((rows_, width), wide),
            shaped((rows_, width), low),
            turned_shape(images, width, span),
        ],
        cost_estimate=cost(4 * rows_ * width * width, 24 * rows_ * width + 2 * width * width),
        megabytes=36,
        name="mix",
    )(x, vec, wo, fq, num, den, prior)


gelu_scale = 0.7978845608028654
gelu_cubic = 0.044715


def feed_kernel(fresh, *refs):
    a_ref, at_ref, e_ref, et_ref, um_ref, uo_ref, dm_ref, do_ref = refs[:8]
    out_ref, da_ref, gum_ref, guo_ref, gdm_ref, gdo_ref = refs[-6:]

    @pl.when(pl.program_id(0) == 0)
    def _():
        if fresh:
            out_ref[...] = jnp.zeros_like(out_ref)
            da_ref[...] = jnp.zeros_like(da_ref)
        else:
            out_ref[...] = refs[8][...]
            da_ref[...] = refs[9][...]

    um, uo, dm, do = um_ref[...], uo_ref[...], dm_ref[...], do_ref[...]
    half = um.shape[0]
    upper = mm(a_ref[:, :half], um) + mm(a_ref[:, half:], uo)
    grad = mm(e_ref[:, :half], dm) + mm(e_ref[:, half:], do)
    square = upper * upper
    bend = jnp.tanh(gelu_scale * upper * (1.0 + gelu_cubic * square))
    gate = 0.5 + 0.5 * bend
    hidden = (upper * gate).astype(low)
    slope = gate + 0.5 * upper * (1.0 - bend * bend) * (gelu_scale * (1.0 + 3.0 * gelu_cubic * square))
    dupper = (grad * slope).astype(low)
    out_ref[:, :half] += mt(hidden, dm)
    out_ref[:, half:] += mt(hidden, do)
    da_ref[:, :half] += mt(dupper, um)
    da_ref[:, half:] += mt(dupper, uo)
    gdm_ref[...] = mm(et_ref[:half, :], hidden).astype(low)
    gdo_ref[...] = mm(et_ref[half:, :], hidden).astype(low)
    gum_ref[...] = mm(at_ref[:half, :], dupper).astype(low)
    guo_ref[...] = mm(at_ref[half:, :], dupper).astype(low)


def feed(up, down, a, at, e, et, carried, tokens=()):
    rows, width = a.shape
    slabs, half = up[0].shape[:2]
    tiles = SLAB // TILE
    weight = pl.BlockSpec((None, half, TILE), lambda g: (g // tiles, 0, g % tiles))
    grads = pl.BlockSpec((half, TILE), lambda g: (0, g))
    full = whole((rows, width))
    turned = whole((width, rows))
    fresh = carried is None
    return launch(
        functools.partial(feed_kernel, fresh),
        tokens,
        grid=(slabs * tiles,),
        in_specs=[full, turned, full, turned] + [weight] * 4 + ([] if fresh else [full, full]),
        out_specs=[full, full] + [grads] * 4,
        out_shape=[shaped((rows, width), wide)] * 2 + [shaped((half, slabs * SLAB), low)] * 4,
        cost_estimate=cost(6 * rows * width * slabs * SLAB, 8 * width * slabs * SLAB + 20 * rows * width),
        name="feed",
    )(a, at, e, et, *up, *down, *(() if fresh else carried))


def outer_kernel(core_ref, mixed_ref, branch_ref, out_ref):
    product = tm(mixed_ref[...], branch_ref[...]).astype(low)
    half = product.shape[1] // 2
    swap = pl.program_id(0) == 1
    out_ref[:, :half] = jnp.where(swap, product[:, half:], product[:, :half])
    out_ref[:, half:] = jnp.where(swap, product[:, :half], product[:, half:])


def outer(core, spots, mixed, branch, tokens=()):
    rows, width = mixed.shape
    block = width // (2 * spots)
    if block % 128:
        product = tm(mixed, branch).astype(low).reshape(spots, 2, -1, width)
        mine = lax.dynamic_index_in_dim(product, core, 1, False).reshape(-1, width)
        other = lax.dynamic_index_in_dim(product, 1 - core, 1, False).reshape(-1, width)
        return mine, jnp.concatenate([other[:, width // 2 :], other[:, : width // 2]], axis=1)
    known, extra = 2, len(tokens)

    def run(core_ref, *refs):
        outer_kernel(core_ref, *refs[:known], *refs[known + extra :])

    result = pl.pallas_call(
        run,
        grid_spec=pltpu.PrefetchScalarGridSpec(
            num_scalar_prefetch=1,
            grid=(2, spots),
            in_specs=[
                pl.BlockSpec((rows, block), lambda side, spot, core: (0, 2 * spot + (core[0] ^ side))),
                whole((rows, width)),
            ]
            + [pl.BlockSpec(memory_space=pl.ANY)] * extra,
            out_specs=pl.BlockSpec((None, block, width), lambda side, spot, core: (side, spot, 0)),
        ),
        out_shape=shaped((2, width // 2, width), low),
        compiler_params=params(20),
        cost_estimate=cost(rows * width * width, 4 * rows * width + 2 * width * width),
        name="outer",
    )(core.reshape(1), mixed, branch, *tokens)
    return result[0], result[1]


def turn_back_kernel(spots, core_ref, x_out_ref, da_ref, resid_ref, e_ref, vec_ref, wo_ref, mixed_ref, rden_ref, fq_ref,
                     out_ref, dres_ref, branch_ref, dn_ref, w_ref, state_ref, sums_ref):
    width = da_ref.shape[1]
    resid = resid_ref[...]
    put_natural(out_ref, (resid + x_out_ref[...]).astype(low), core_ref, spots)
    unit, scale = normalised(resid)
    da = da_ref[...]

    @pl.when(pl.program_id(0) == 0)
    def _():
        sums_ref[...] = jnp.zeros_like(sums_ref)

    sums_ref[0:1, :] += jnp.sum(da * unit, axis=0, keepdims=True)
    sums_ref[1:2, :] += jnp.sum(da, axis=0, keepdims=True)
    p = da * vec_ref[2:3, :]
    back = p - jnp.mean(p, axis=-1, keepdims=True) - unit * jnp.mean(p * unit, axis=-1, keepdims=True)
    dres = e_ref[...].astype(wide) + scale * back
    dres_ref[...] = dres
    branch = dres.astype(low)
    branch_ref[...] = branch
    dmixed = mt(branch, wo_ref[...]).astype(low).astype(wide)
    dnumer = dmixed * rden_ref[...]
    dn_ref[...] = dnumer.astype(low)
    w_ref[...] = (-dnumer * mixed_ref[...].astype(wide)).astype(low)
    for pair in range(width // PAIR):
        lanes = slice(pair * PAIR, (pair + 1) * PAIR)
        query = fq_ref[:, lanes]
        state_ref[0, pair, :HEAD_DIM, :] = fold_state(tm(dn_ref[:, lanes], query))
        total = jnp.sum(fold_state(tm(w_ref[:, lanes], query)), axis=0, keepdims=True)
        state_ref[0, pair, HEAD_DIM:, :] = jnp.broadcast_to(total, (STATE_ROWS - HEAD_DIM, PAIR))


def turn_back(core, spots, x_out, da, resid, e, vec, wo, mixed, rden, fq, images, span, tokens=()):
    rows_, width = da.shape
    rows = pl.BlockSpec((span, width), lambda b: (b, 0))
    state = (images, width // PAIR, STATE_ROWS, PAIR)
    return launch(
        functools.partial(turn_back_kernel, spots),
        tokens,
        grid=(images,),
        in_specs=[pl.BlockSpec(memory_space=pltpu.SMEM)]
        + [rows, rows, rows, rows, whole(vec.shape), whole(wo.shape), rows, rows, rows],
        out_specs=[rows] * 5 + [pl.BlockSpec((1,) + state[1:], lambda b: (b, 0, 0, 0)), whole((8, width))],
        out_shape=[
            shaped((rows_, width), low),
            shaped((rows_, width), wide),
            shaped((rows_, width), low),
            shaped((rows_, width), low),
            shaped((rows_, width), low),
            shaped(state, wide),
            shaped((8, width), wide),
        ],
        cost_estimate=cost(5 * rows_ * width * width, 30 * rows_ * width),
        megabytes=44,
        name="turn_back",
    )(core.reshape(1), x_out, da, resid, e, vec, wo, mixed, rden, fq)


def attend_back_kernel(span, fq_ref, fk_ref, v_ref, dn_ref, w_ref, prior_ref, dq_ref, dfk_ref, dv_ref):
    own = first_head(span)
    own_twice = jnp.concatenate([own, own], axis=1)
    below, above = causal_mask(span, True), causal_mask(span, False)
    one = jnp.ones((span, PAIR), low)
    zero = jnp.zeros((span, PAIR), low)
    zero_twice = jnp.zeros((span, 2 * PAIR), low)
    for pair in range(GROUP // PAIR):
        lanes = slice(pair * PAIR, (pair + 1) * PAIR)
        query, key, value = fq_ref[:, lanes], fk_ref[:, lanes], v_ref[:, lanes]
        grads = jnp.concatenate([dn_ref[:, lanes], w_ref[:, lanes]], axis=1)
        extended = jnp.concatenate([value, one], axis=1)
        folded = prior_ref[0, pair]
        matrix = jnp.concatenate(
            [unfold_state(folded[:HEAD_DIM]), unfold_total(folded[HEAD_DIM : HEAD_DIM + 1])], axis=0
        )
        high, rest = split_low(matrix)
        dfq = mm(jnp.concatenate([grads, grads], axis=1), jnp.concatenate([high, rest], axis=0))
        to_query, to_key, to_value = [], [], []
        for mask, both in ((own, own_twice), (jnp.logical_not(own), jnp.logical_not(own_twice))):
            head_grads = jnp.where(both, grads, zero_twice)
            head_query = jnp.where(mask, query, zero)
            head_key = jnp.where(mask, key, zero)
            to_query.append((mt(head_grads, extended).astype(low) * below, head_key))
            to_key.append((mt(extended, head_grads).astype(low) * above, head_query))
            to_value.append((mt(head_key, query).astype(low) * above, head_grads[:, :PAIR]))
        dfq = dfq + pair_mm(*to_query)
        dq_ref[:, lanes] = (dfq * jnp.minimum(query.astype(wide), 1.0)).astype(low)
        dfk_ref[:, lanes] = pair_mm(*to_key)
        dv_ref[:, lanes] = pair_mm(*to_value)


def attend_back(image, fq, fk, v, dn, w, prior, span, tokens=()):
    width = fq.shape[1]
    block = pl.BlockSpec((span, GROUP), lambda p: (image, p))
    column = pl.BlockSpec((span, GROUP), lambda p: (0, p))
    return launch(
        functools.partial(attend_back_kernel, span),
        tokens,
        grid=(width // GROUP,),
        in_specs=[block] * 5 + [pl.BlockSpec((1, GROUP // PAIR) + prior.shape[2:], lambda p: (image, p, 0, 0))],
        out_specs=[column] * 3,
        out_shape=[shaped((span, width), low), shaped((span, width), wide), shaped((span, width), wide)],
        cost_estimate=cost(32 * span * span * width, 24 * span * width),
        megabytes=20,
        name="attend_back",
    )(fq, fk, v, dn, w, prior)


def finish_kernel(images, span, *refs):
    locals_ = [refs[3 * image : 3 * image + 3] for image in range(images)]
    fk_ref, v_ref, later_ref, at_ref, dq_ref, dk_ref, dv_ref, mine_ref, other_ref = refs[3 * images :]
    half = mine_ref.shape[1]
    for image in range(images):
        rows = slice(image * span, (image + 1) * span)
        dqi_ref, dfk_ref, dvl_ref = locals_[image]
        dq_ref[rows, :] = dqi_ref[...]
        for pair in range(GROUP // PAIR):
            lanes = slice(pair * PAIR, (pair + 1) * PAIR)
            folded = later_ref[image, pair]
            high, rest = split_low(unfold_state(folded[:HEAD_DIM]))
            key, value = fk_ref[rows, lanes], v_ref[rows, lanes]
            dfk = dfk_ref[:, lanes] + folded[HEAD_DIM : HEAD_DIM + 1]
            dfk = dfk + mm(jnp.concatenate([value, value], axis=1), jnp.concatenate([high, rest], axis=0))
            dv = dvl_ref[:, lanes] + mt(
                jnp.concatenate([key, key], axis=1), jnp.concatenate([high, rest], axis=1)
            )
            dk_ref[rows, lanes] = (dfk * jnp.minimum(key.astype(wide), 1.0)).astype(low)
            dv_ref[rows, lanes] = dv.astype(low)
    for k, ref in enumerate((dq_ref, dk_ref, dv_ref)):
        mine_ref[k] = mm(at_ref[:half, :], ref[...]).astype(low)
        other_ref[k] = mm(at_ref[half:, :], ref[...]).astype(low)


def finish(side, parts, fk, v, later, at, images, span, tokens=()):
    rows, width = fk.shape
    half = width // 2
    groups = half // GROUP
    column = pl.BlockSpec((rows, GROUP), lambda g: (0, side * groups + g))
    part = pl.BlockSpec((span, GROUP), lambda g: (0, side * groups + g))
    result = pl.BlockSpec((rows, GROUP), lambda g: (0, g))
    grads = pl.BlockSpec((3, half, GROUP), lambda g: (0, 0, g))
    state = pl.BlockSpec((images, GROUP // PAIR) + later.shape[2:], lambda g: (0, side * groups + g, 0, 0))
    return launch(
        functools.partial(finish_kernel, images, span),
        tokens,
        grid=(groups,),
        in_specs=[part] * (3 * images) + [column] * 2 + [state, whole(at.shape)],
        out_specs=[result] * 3 + [grads, grads],
        out_shape=[shaped((rows, half), low)] * 3 + [shaped((3, half, half), low)] * 2,
        cost_estimate=cost(2 * rows * width * width, 15 * rows * width),
        megabytes=28,
        name="finish",
    )(*[array for image in parts for array in image], fk, v, later, at)


def enter_kernel(spots, core_ref, *refs):
    lefts, rights, weights = refs[:3], refs[3:6], refs[6:12]
    x_ref, dres_ref, vec_ref, grad_ref, sums_ref = refs[12:]
    half = x_ref.shape[1] // 2
    parts = []
    for side in range(2):
        total = None
        for k in range(3):
            weight = flat(weights[2 * k + side])
            part = mt(lefts[k][...], weight[:, :half]) + mt(rights[k][...], weight[:, half:])
            total = part if total is None else total + part
        parts.append(total)
    da = jnp.concatenate(parts, axis=1)
    unit, scale = normalised(x_ref[...].astype(wide))
    sums_ref[0:1, :] = jnp.sum(da * unit, axis=0, keepdims=True)
    sums_ref[1:2, :] = jnp.sum(da, axis=0, keepdims=True)
    sums_ref[2:, :] = jnp.zeros_like(sums_ref[2:, :])
    p = da * vec_ref[0:1, :]
    back = p - jnp.mean(p, axis=-1, keepdims=True) - unit * jnp.mean(p * unit, axis=-1, keepdims=True)
    put_natural(grad_ref, (dres_ref[...] + scale * back).astype(low), core_ref, spots)


def enter(image, core, spots, left, right, weights, x, dres, vec, span, tokens=()):
    width = x.shape[1]
    half = width // 2
    rows = pl.BlockSpec((span, width), lambda g, core: (image, 0))
    part = pl.BlockSpec((span, half), lambda g, core: (image, 0))
    blocks = [owned_block(array, which, flipped, width, lambda g: 0) for array, which in weights for flipped in range(2)]
    return launch_at(
        functools.partial(enter_kernel, spots),
        core,
        tokens,
        grid=(1,),
        in_specs=[part] * 6 + blocks + [rows, rows, whole(vec.shape)],
        out_specs=[whole((span, width)), whole((8, width))],
        out_shape=[shaped((span, width), low), shaped((8, width), wide)],
        cost_estimate=cost(3 * span * width * width, 14 * span * width + 6 * width * width),
        megabytes=40,
        name="enter",
    )(*left, *right, *[array for array, _ in weights for _ in range(2)], x, dres, vec)


def adam_update(master, moment, second, average, gradient, factor, rate):
    clipped = gradient * factor
    moment = beta_first * moment + (1.0 - beta_first) * clipped
    second = beta_second * second + (1.0 - beta_second) * clipped * clipped
    first_hat = moment / (1.0 - beta_first**STEP)
    second_hat = second / (1.0 - beta_second**STEP)
    master = master - rate * (first_hat / (jnp.sqrt(second_hat) + eps_adam) + weight_decay * master)
    average = average_decay * average + (1.0 - average_decay) * master
    return (master, moment, second, average)


def flip_pairs(count, bit):
    return [(i, i ^ bit) for i in range(count)]


def powers(count):
    return [1 << k for k in range(count.bit_length() - 1)]


def flip(array, axis, bit=1):
    return lax.ppermute(array, axis, flip_pairs(lax.axis_size(axis), bit))


def fold_kernel(counts, spot_ref, *refs):
    total = sum(counts)
    ins, outs = refs[: 2 * total], refs[2 * total :]
    for k in range(total):
        value = ins[2 * k][...].astype(wide) + ins[2 * k + 1][...].astype(wide)
        outs[k][...] = value.astype(outs[k].dtype)


def fold(chains, tokens=()):
    steps = 4
    in_specs, out_specs, out_shape, arrays, counts, spots, moved = [], [], [], [], [], [], 0
    for k, (kept, came, pre, ways, own) in enumerate(chains):
        columns = kept.shape[-1]
        first = kept.dtype == low
        rows = kept.size // (columns * pre * ways)
        kept, came = (array.reshape(pre, ways, rows, columns) for array in (kept, came))
        counts.append(ways)
        spots.append(own)
        moved += 8 * kept.size
        for j in range(ways):
            block = (pre, 1, rows, columns // steps)
            spec = pl.BlockSpec(block, lambda c, spot, k=k, j=j: (0, spot[k] ^ j, 0, c))
            in_specs += [spec, spec]
            arrays += [kept, came]
            out_specs.append(pl.BlockSpec(block, lambda c, spot: (0, 0, 0, c)))
            out_shape.append(shaped((pre, 1, rows, columns), low if j or first else wide))
    total, extra = len(in_specs), len(tokens)

    def run(spot_ref, *refs):
        fold_kernel(counts, spot_ref, *refs[:total], *refs[total + extra :])

    results = pl.pallas_call(
        run,
        grid_spec=pltpu.PrefetchScalarGridSpec(
            num_scalar_prefetch=1,
            grid=(steps,),
            in_specs=in_specs + [pl.BlockSpec(memory_space=pl.ANY)] * extra,
            out_specs=out_specs,
        ),
        out_shape=out_shape,
        compiler_params=params(20),
        cost_estimate=cost(1, moved),
        name="fold",
    )(jnp.stack(spots).astype(jnp.int32), *arrays, *tokens)
    groups = []
    for ways in counts:
        groups.append([part.reshape(part.shape[0], part.shape[2], part.shape[3]) for part in results[:ways]])
        results = results[ways:]
    return groups


class Chain:
    def __init__(self, kept, sent, order):
        self.lead = kept.shape[0] if kept.ndim == 3 else 1
        self.kept = kept
        self.sends = [sent]
        self.hops = [("core", 1)]
        self.axis = "pos"
        self.bits = powers(lax.axis_size("pos"))[::order]
        self.left = powers(lax.axis_size("pos"))[::-1]

    def start(self):
        self.came = [flip(array, axis, bit) for array, (axis, bit) in zip(self.sends, self.hops)]

    def cut(self):
        bit = next(bit for bit in self.bits if bit in self.left)
        pre = self.lead << self.left.index(bit)
        self.left.remove(bit)
        self.hops = [(self.axis, bit)]
        return (self.kept, self.came[0], pre, 2, (lax.axis_index(self.axis) // bit) % 2)

    def take(self, parts):
        self.kept, self.sends = parts[0], list(parts[1:])


def advance(chains, tokens=()):
    groups = fold([chain.cut() for chain in chains], tokens)
    for chain, parts in zip(chains, groups):
        chain.take(parts)
        chain.start()
    return [array for chain in chains for array in chain.sends]


def last_kernel(ways, lead, pieces, spot_ref, *refs):
    ins, outs = refs[: 2 * pieces], refs[2 * pieces :]
    at = 0
    for k in range(pieces):
        columns = ins[2 * k].shape[-1]
        for j in range(ways):
            place = spot_ref[0] ^ j
            for n in range(lead):
                value = ins[2 * k][n, place].astype(wide) + ins[2 * k + 1][n, place].astype(wide)
                outs[j][n, :, at : at + columns] = value.astype(outs[j].dtype)
        at += columns


class Last:
    def __init__(self, chains, tokens=(), slowly=False):
        ways = 2 if slowly else lax.axis_size("img")
        lead = chains[0].lead
        pre = lead * lax.axis_size("img") // ways
        arrays = []
        for chain in chains:
            for array in (chain.kept, chain.came[0]):
                arrays.append(array.reshape(pre, ways, -1, array.shape[-1]))
        self.widths = [array.shape[-1] for array in arrays[::2]]
        rows = chains[0].kept.size // (chains[0].kept.shape[-1] * pre * ways)
        inside = pl.BlockSpec(memory_space=pltpu.VMEM)
        parts = launch(
            functools.partial(last_kernel, ways, pre, len(chains)),
            tokens,
            in_specs=[pl.BlockSpec(memory_space=pltpu.SMEM)] + [inside] * len(arrays),
            out_specs=[inside] * ways,
            out_shape=[shaped((pre, rows, sum(self.widths)), low if j else wide) for j in range(ways)],
            cost_estimate=cost(1, 4 * sum(array.size for array in arrays)),
            megabytes=16,
        name="last",
        )((lax.axis_index("img") % ways).reshape(1), *arrays)
        self.lead = lead
        self.kept, self.sends = parts[0], list(parts[1:])
        self.axis = "img"
        self.hops = [("img", j + 1) for j in range(ways - 1)]
        self.bits = powers(lax.axis_size("img"))[1:] if slowly else []
        self.left = self.bits[::-1]
        self.start()

    start, cut, take = Chain.start, Chain.cut, Chain.take

    def result(self):
        while self.left:
            advance([self])
        total = self.kept
        for came in self.came:
            total = total + came.astype(wide)
        self.total = total
        return total

    def pieces(self):
        at, found = 0, []
        for columns in self.widths:
            found.append(self.total[..., at : at + columns])
            at += columns
        return found


def sum_slowly(array):
    for axis in ("core", "pos", "img"):
        for bit in powers(lax.axis_size(axis)):
            array = array + flip(array, axis, bit)
    return array


def sum_all(array):
    for axis in ("img", "pos", "core"):
        came = [flip(array, axis, j) for j in range(1, lax.axis_size(axis))]
        for other in came:
            array = array + other
    return array


def assemble_kernel(plan, spot_ref, *refs):
    outs = sorted({out for _, _, out, _ in plan})
    count = len(refs) - 1 - len(outs)
    sems = refs[-1]
    copies = []
    for k, (piece, cut, out, where) in enumerate(plan):
        source = refs[piece].at[cut] if cut is not None else refs[piece]
        target = refs[count + out].at[where(spot_ref)]
        copies.append(pltpu.make_async_copy(source, target, sems.at[k]))
    for copy in copies:
        copy.start()
    for copy in copies:
        copy.wait()


def assemble(plan, spots, pieces, shapes, tokens=()):
    anywhere = pl.BlockSpec(memory_space=pl.ANY)
    return launch(
        functools.partial(assemble_kernel, plan),
        tokens,
        in_specs=[pl.BlockSpec(memory_space=pltpu.SMEM)] + [anywhere] * len(pieces),
        out_specs=[pl.BlockSpec(memory_space=pltpu.VMEM)] * len(shapes),
        out_shape=[shaped(shape, low) for shape in shapes],
        scratch_shapes=[pltpu.SemaphoreType.DMA((len(plan),))],
        cost_estimate=cost(1, 2 * sum(2 * piece.size for piece in pieces)),
        megabytes=12,
        name="assemble",
    )(jnp.stack(spots).astype(jnp.int32), *pieces)


class Gather:
    def __init__(self, packed, cuts, shapes, order):
        self.packed, self.cuts, self.shapes = packed, cuts, shapes
        self.orders = [order, -order]

    def start_slices(self):
        self.pieces = [self.packed] + [flip(self.packed, "img", j) for j in range(1, lax.axis_size("img"))]

    def finish_slices(self, tokens=()):
        slices = len(self.pieces)
        plan = [
            (j, cut, out, lambda spot, j=j: (slice(None), spot[0] ^ j))
            for j in range(slices)
            for out, cut in enumerate(self.cuts)
        ]
        shapes = [(k, slices, r, c) for k, r, c in self.shapes]
        parts = assemble(plan, [lax.axis_index("img")], self.pieces, shapes, tokens)
        self.parts = [part.reshape(k, slices * r, c) for part, (k, r, c) in zip(parts, self.shapes)]
        self.dims = [[], []]
        return self.parts

    def start_pos(self):
        self.bits = [powers(lax.axis_size("pos"))[::order][len(dims)] for order, dims in zip(self.orders, self.dims)]
        self.came = [flip(part, "pos", bit) for part, bit in zip(self.parts, self.bits)]

    def finish_pos(self, tokens=()):
        plan, shapes, places = [], [], []
        for out, (part, bit, dims) in enumerate(zip(self.parts, self.bits, self.dims)):
            place = 1 + sum(other > bit for other in dims)
            places.append(place)
            shapes.append(part.shape[:place] + (2,) + part.shape[place:])
            ahead = (slice(None),) * place
            plan.append((2 * out, None, out, lambda spot, ahead=ahead, out=out: ahead + (spot[out],)))
            plan.append((2 * out + 1, None, out, lambda spot, ahead=ahead, out=out: ahead + (1 - spot[out],)))
            dims.append(bit)
        spots = [(lax.axis_index("pos") // bit) % 2 for bit in self.bits]
        pieces = [array for pair in zip(self.parts, self.came) for array in pair]
        self.parts = assemble(plan, spots, pieces, shapes, tokens)
        return self.parts

    def start_core(self):
        self.mine = [part.reshape(part.shape[0], -1, part.shape[-1]) for part in self.parts]
        self.other = [flip(part, "core") for part in self.mine]
        return list(zip(self.mine, self.other))


def narrow_kernel(plan, *refs):
    out_ref = refs[-1]
    for k, (ref, member, columns) in enumerate(plan):
        out_ref[k] = refs[ref][member, :, columns].astype(low)


def narrow(plan, weights, tokens=()):
    owned = weights[0].shape[1]
    inside = pl.BlockSpec(memory_space=pltpu.VMEM)
    return launch(
        functools.partial(narrow_kernel, plan),
        tokens,
        in_specs=[inside] * len(weights),
        out_specs=inside,
        out_shape=shaped((len(plan), owned, SLAB), low),
        cost_estimate=cost(1, 6 * len(plan) * owned * SLAB),
        megabytes=12,
        name="narrow",
    )(*weights)


def passing(own, backward):
    total = own
    outside = jnp.zeros_like(own)
    for axis in ("core", "pos"):
        for bit in powers(lax.axis_size(axis)):
            came = flip(total.astype(low), axis, bit).astype(wide)
            upper = (lax.axis_index(axis) // bit) % 2
            counts = upper == (0 if backward else 1)
            outside = outside + jnp.where(counts, came, 0.0)
            total = total + came
    return outside


def body(
    images,
    cotangent,
    attention_weight,
    feedforward_weight,
    norm_vectors,
    attention_moment,
    feedforward_moment,
    norm_moment,
    attention_second,
    feedforward_second,
    norm_second,
    attention_average,
    feedforward_average,
    norm_average,
):
    count, span, width = images.shape
    tokens = count * span
    spots = lax.axis_size("pos")
    slices = lax.axis_size("img")
    core = lax.axis_index("core")
    owned = attention_weight.shape[1]
    hidden_width = feedforward_weight.shape[2]
    slabs = hidden_width // SLAB

    weights = (attention_weight, feedforward_weight)
    steps = len(powers(spots))
    half = slabs // 2
    every = slice(None)

    def stretch(k):
        return slice(k * SLAB, (k + 1) * SLAB)

    def feed_group(first, order, tokens=()):
        plan = [(1, k, stretch(first + n)) for k in range(2) for n in range(half)]
        packed = narrow(plan, weights, tokens)
        return Gather(packed, [slice(0, half), slice(half, 2 * half)], [(half, owned, SLAB)] * 2, order)

    def gather_all(array):
        return lax.all_gather(array, ("pos", "core", "img"), axis=1, tiled=True)

    vectors = jnp.pad(norm_vectors.astype(low).T[None], ((1, 0), (0, 0), (0, 124)))
    inner_all = gather_all(jnp.concatenate([attention_weight[1:3].astype(low), vectors], axis=2))
    inner_weights = inner_all.reshape(2, spots, 2, -1, width + 128)
    outer_all = gather_all(jnp.stack([attention_weight[0], attention_weight[3]]).astype(low))
    outer_weights = outer_all.reshape(2, spots, 2, -1, width)

    one = feed_group(0, 1)
    one.start_slices()
    x, e, et = prepare(images.reshape(tokens, width), cotangent.reshape(tokens, width), core, spots, count, span)
    marks = one.finish_slices([et])
    et = turned_whole(et)
    one.start_pos()
    two = feed_group(half, -1, marks)
    two.start_slices()
    for step in range(steps - 1):
        marks = one.finish_pos([two.packed])
        one.start_pos()
    vec = swap_blocks(inner_all[1, :, width : width + 4].astype(wide).T, core, spots, False)
    fk, v, a1, a1t, state = project(core, x, vec, inner_weights, count, span, marks)
    prior = passing(state, False)
    marks = two.finish_slices([state])
    two.start_pos()
    marks = one.finish_pos(marks)
    up_first, down_first = one.start_core()
    for step in range(steps - 1):
        marks = two.finish_pos(marks)
        two.start_pos()
    fq = query(core, a1, outer_weights, marks)
    num, den = attend(fq, fk, v, count, span)
    wo = arrange(outer_all, core, spots, [num])
    mixed, rden, resid, a2, a2t = mix(x, vec, wo, fq, num, den, prior, count, span)
    a2t = turned_whole(a2t)
    marks = two.finish_pos([resid])
    up_second, down_second = two.start_core()

    early = feed(up_first, down_first, a2, a2t, e, et, None, marks)
    firsts = [Chain(early[2], early[3], 1), Chain(early[4], early[5], -1)]
    for chain in firsts:
        chain.start()
    late = feed(up_second, down_second, a2, a2t, e, et, early[:2])
    seconds = [Chain(late[2], late[3], 1), Chain(late[4], late[5], -1)]
    for chain in seconds:
        chain.start()
    marks = advance(firsts)
    output, dres, branch, dn, w, dstate, sums_second = turn_back(
        core, spots, late[0], late[1], resid, e, vec, wo, mixed, rden, fq, count, span, marks
    )
    later = passing(dstate, True)
    outs = [Chain(*outer(core, spots, mixed, branch), 1)]
    marks = advance(seconds) + advance(firsts)
    parts = []
    for image in range(count):
        parts.append(attend_back(image, fq, fk, v, dn, w, prior, span, marks))
        if image == 0:
            outs[0].start()
            marks = advance(outs, [parts[0][0]])
            for step in range(steps - 2):
                advance(firsts)
            firsts_last = Last(firsts, [parts[0][0]], True)
            marks = marks + firsts_last.sends
    for step in range(steps - 2):
        advance(seconds)
        advance(outs)
    marks = advance(seconds + outs, [parts[-1][0]])
    if firsts_last.left:
        marks = marks + advance([firsts_last], [parts[-1][0]])
    left = finish(0, parts, fk, v, later, a1t, count, span, marks)
    inner = [Chain(left[3], left[4], 1)]
    inner[0].start()
    firsts_last.result()
    seconds_last = Last(seconds + outs, [left[0]], True)
    marks = seconds_last.sends + [firsts_last.total]
    right = finish(1, parts, fk, v, later, a1t, count, span, marks)
    inner.append(Chain(right[3], right[4], -1))
    inner[1].start()
    marks = advance(inner[:1], [right[0]])
    if seconds_last.left:
        marks = marks + advance([seconds_last], [right[0]])
    projections = ((outer_weights, 0), (inner_weights, 0), (inner_weights, 1))
    grads_in = []
    for image in range(count):
        grads_in.append(
            enter(image, core, spots, left[:3], right[:3], projections, x, dres, vec, span, marks)
        )
        if image == 0:
            seconds_last.result()
            marks = advance(inner[1:], [grads_in[0][1]]) + [seconds_last.total]
    input_grad = jnp.stack([part[0] for part in grads_in])
    sums_first = sum(part[1] for part in grads_in)
    vector_grad = jnp.concatenate([swap_blocks(part[:2], core, spots, True) for part in (sums_first, sums_second)], axis=0)
    vector_grad = sum_slowly(vector_grad)
    device = (lax.axis_index("pos") * 2 + core) * slices + lax.axis_index("img")
    vector_shard = lax.dynamic_slice_in_dim(vector_grad, device * norm_vectors.shape[1], norm_vectors.shape[1], 1)
    advance(inner)
    while inner[0].left:
        advance(inner)
    inner_last = Last(inner, [vector_shard])
    inner_shard = inner_last.result()
    up_late, down_late, out_shard = seconds_last.pieces()
    up_early, down_early = firsts_last.pieces()
    out_shard = swap_blocks(out_shard, core, spots, True)
    attn_shard = jnp.concatenate([inner_shard, out_shard], axis=0)
    feed_shard = jnp.concatenate(
        [jnp.concatenate([up_early, up_late], axis=2), jnp.concatenate([down_early, down_late], axis=2)], axis=0
    )
    if (width // (2 * spots)) % 128:
        output = swap_blocks(output, core, spots, True)
        input_grad = swap_blocks(input_grad, core, spots, True)

    local_squares = (
        jnp.sum(attn_shard * attn_shard) + jnp.sum(feed_shard * feed_shard) + jnp.sum(vector_shard * vector_shard)
    )
    grad_norm = jnp.sqrt(sum_all(jnp.full((8, 128), local_squares))[0, 0])
    factor = clip_bound / jnp.maximum(grad_norm, clip_bound)
    attn_new = adam_update(
        attention_weight, attention_moment, attention_second, attention_average, attn_shard, factor, learn_rate
    )
    feed_new = adam_update(
        feedforward_weight, feedforward_moment, feedforward_second, feedforward_average, feed_shard, factor, learn_rate
    )
    norm_new = adam_update(norm_vectors, norm_moment, norm_second, norm_average, vector_shard, factor, norm_rate)
    output = output.reshape(images.shape)
    input_grad = input_grad.reshape(images.shape)
    return (output, input_grad, grad_norm) + attn_new + feed_new + norm_new


def solution(mesh):
    seq, img = mesh.devices.shape
    inner = Mesh(mesh.devices.reshape(seq // 2, 2, img), ("pos", "core", "img"))
    tokens = P("img", ("pos", "core"), None)
    rows = P(None, ("pos", "core", "img"), None)
    vectors = P(None, ("pos", "core", "img"))
    group = (rows, rows, vectors)
    return jax.shard_map(
        body,
        mesh=inner,
        in_specs=(tokens, tokens) + group * 4,
        out_specs=(tokens, tokens, P()) + (rows,) * 8 + (vectors,) * 4,
        check_vma=False,
    )
```

```python
import functools

import jax
import jax.numpy as jnp
import numpy as np
from jax import lax
from jax.experimental import pallas as pl
from jax.experimental.pallas import tpu as pltpu
from jax.sharding import PartitionSpec as P

HEADS = 16
HEAD_DIM = 64
STEP = 10

beta_first = 0.9
beta_second = 0.95
learn_rate = 0.02
norm_rate = 0.2
weight_decay = 0.1
average_decay = 0.75
clip_bound = 1.0
eps_norm = 1e-05
eps_adam = 1e-08

PAIR = 2 * HEAD_DIM
STATE_ROWS = HEAD_DIM + 16
SLAB = 1024
TILE = 512
GROUP = 256

low = jnp.bfloat16
wide = jnp.float32


def params(megabytes=56):
    return pltpu.CompilerParams(vmem_limit_bytes=megabytes * 1024 * 1024)


def cost(products, elements):
    return pl.CostEstimate(flops=products // 4, bytes_accessed=elements // 8, transcendentals=0)


def launch(kernel, tokens, in_specs, megabytes=56, **keys):
    known, extra = len(in_specs), len(tokens)

    def run(*refs):
        kernel(*refs[:known], *refs[known + extra :])

    call = pl.pallas_call(
        run, in_specs=list(in_specs) + [pl.BlockSpec(memory_space=pl.ANY)] * extra, compiler_params=params(megabytes), **keys
    )
    return lambda *args: call(*args, *tokens)


def launch_at(kernel, spot, tokens, grid, in_specs, out_specs, megabytes=56, scratch_shapes=(), **keys):
    known, extra = len(in_specs), len(tokens)

    def run(spot_ref, *refs):
        kernel(spot_ref, *refs[:known], *refs[known + extra :])

    call = pl.pallas_call(
        run,
        grid_spec=pltpu.PrefetchScalarGridSpec(
            num_scalar_prefetch=1,
            grid=grid,
            in_specs=list(in_specs) + [pl.BlockSpec(memory_space=pl.ANY)] * extra,
            out_specs=out_specs,
            scratch_shapes=scratch_shapes,
        ),
        compiler_params=params(megabytes),
        **keys,
    )
    return lambda *args: call(spot.reshape(-1).astype(jnp.int32), *args, *tokens)


def reversed_bits(value, count):
    return sum(((value >> k) & 1) << (count - 1 - k) for k in range(count))


def join(target_ref, bits, spot_ref, own_ref, came_ref, own_other_ref, came_other_ref):
    core, high, lowest = spot_ref[0], spot_ref[1], spot_ref[2]
    runs = 1 << (bits - 1)
    rows = target_ref.shape[1] // (2 * runs)
    for run in range(runs):
        source = slice(run * rows, (run + 1) * rows)
        turned = reversed_bits(run, bits)
        for place in range(2):
            first = (high ^ place) * runs + run
            second = turned + (lowest ^ place)
            for ref, slot in (((own_ref, came_ref)[place], core), ((own_other_ref, came_other_ref)[place], 1 - core)):
                at = jnp.where(slot == 0, first, second)
                target_ref[slot, pl.ds(pl.multiple_of(at * rows, rows), rows), :] = ref[source, :]


class Pieces:
    def __init__(self, arrays):
        self.arrays = [array.reshape(array.shape[0], -1, array.shape[-1]) for array in arrays]
        place = pos_index()
        self.bits = pos_bits()
        self.spot = jnp.stack([core_index(), place >> (self.bits - 1), place & 1])

    def blocks(self, columns, place):
        rows = self.arrays[0].shape[1]
        return [pl.BlockSpec((None, rows, columns), place)] * 4

    def second(self, columns):
        mine, others = (
            [part[0, :, columns].reshape(1 << (self.bits - 1), 1, -1, columns.stop - columns.start) for part in pair]
            for pair in (self.arrays[:2], self.arrays[2:])
        )
        own, came = (jnp.where(core_index() == 1, left, right) for left, right in zip(mine, others))
        straight, turned = jnp.concatenate([own, came], axis=1), jnp.concatenate([came, own], axis=1)
        runs = jnp.where(self.spot[2] == 0, straight, turned)
        order = [reversed_bits(run, self.bits - 1) for run in range(1 << (self.bits - 1))]
        return jnp.stack([runs[run] for run in order]).reshape(-1, columns.stop - columns.start)


def shaped(shape, kind):
    return jax.ShapeDtypeStruct(shape, kind)


def whole(shape):
    return pl.BlockSpec(shape, lambda *_: (0,) * len(shape))


def mm(left, right):
    return lax.dot_general(left, right, (((1,), (0,)), ((), ())), preferred_element_type=wide)


def mt(left, right):
    return lax.dot_general(left, right, (((1,), (1,)), ((), ())), preferred_element_type=wide)


def tm(left, right):
    return lax.dot_general(left, right, (((0,), (0,)), ((), ())), preferred_element_type=wide)


def pair_mm(first, second):
    if first[0].shape[1] % 128:
        return mm(*first) + mm(*second)
    return mm(jnp.concatenate([first[0], second[0]], axis=1), jnp.concatenate([first[1], second[1]], axis=0))


def causal_mask(span, below):
    rows = lax.broadcasted_iota(jnp.int32, (span, span), 0)
    columns = lax.broadcasted_iota(jnp.int32, (span, span), 1)
    return (rows >= columns if below else rows <= columns).astype(wide).astype(low)


def first_head(rows):
    return lax.broadcasted_iota(jnp.int32, (rows, PAIR), 1) < HEAD_DIM


def fold_state(product):
    return jnp.where(first_head(HEAD_DIM), product[:HEAD_DIM], product[HEAD_DIM:])


def unfold_state(folded):
    own = first_head(HEAD_DIM)
    zero = jnp.zeros_like(folded)
    return jnp.concatenate([jnp.where(own, folded, zero), jnp.where(own, zero, folded)], axis=0)


def unfold_total(row):
    tall = jnp.broadcast_to(row, (PAIR, PAIR))
    lanes = lax.broadcasted_iota(jnp.int32, (PAIR, PAIR), 1) < HEAD_DIM
    rows = lax.broadcasted_iota(jnp.int32, (PAIR, PAIR), 0) < HEAD_DIM
    return jnp.where(lanes == rows, tall, jnp.zeros_like(tall))


def split_low(values):
    high = values.astype(low)
    return high, (values - high.astype(wide)).astype(low)


def normalised(values):
    centre = jnp.mean(values, axis=-1, keepdims=True)
    centred = values - centre
    spread = jnp.mean(centred * centred, axis=-1, keepdims=True)
    scale = lax.rsqrt(spread + eps_norm)
    return centred * scale, scale


def feature(raw):
    return jnp.where(raw > 0, raw + 1.0, jnp.exp(jnp.minimum(raw, 0.0))).astype(low)


def project_kernel(images, span, bits, spot_ref, x_ref, vec_ref, *refs):
    fk_ref, v_ref, a_ref, at_ref, state_ref, wk_ref, wv_ref, joined_ref = refs[4:]

    @pl.when(pl.program_id(0) == 0)
    def _():
        gain, shift = vec_ref[0:1, :], vec_ref[1:2, :]
        step = span // 3
        for start in range(0, images * span, step):
            rows = slice(start, start + step)
            unit, _ = normalised(x_ref[rows, :].astype(wide))
            a_ref[rows, :] = (unit * gain + shift).astype(low)
        at_ref[...] = a_ref[...].T

    join(joined_ref, bits, spot_ref, *refs[:4])
    keys, values = joined_ref[0], joined_ref[1]
    wk_ref[...] = keys
    wv_ref[...] = values
    fk_ref[...] = feature(mm(a_ref[...], keys))
    v_ref[...] = mm(a_ref[...], values).astype(low)
    ones = jnp.ones((16, span), low)
    for image in range(images):
        rows = slice(image * span, (image + 1) * span)
        for pair in range(GROUP // PAIR):
            lanes = slice(pair * PAIR, (pair + 1) * PAIR)
            key, value = fk_ref[rows, lanes], v_ref[rows, lanes]
            state_ref[image, pair, :HEAD_DIM, :] = fold_state(tm(value, key))
            state_ref[image, pair, HEAD_DIM:, :] = mm(ones, key)


def project(x, vec, pieces, images, span, tokens=()):
    count, width = x.shape
    pairs = GROUP // PAIR
    column = pl.BlockSpec((count, GROUP), lambda g, spot: (0, g))
    weight = pl.BlockSpec((width, GROUP), lambda g, spot: (0, g))
    return launch_at(
        functools.partial(project_kernel, images, span, pieces.bits),
        pieces.spot,
        tokens,
        grid=(width // GROUP,),
        in_specs=[whole((count, width)), whole(vec.shape)] + pieces.blocks(GROUP, lambda g, spot: (0, 0, g)),
        out_specs=[
            column,
            column,
            whole((count, width)),
            whole((width, count)),
            pl.BlockSpec((images, pairs, STATE_ROWS, PAIR), lambda g, spot: (0, g, 0, 0)),
            weight,
            weight,
        ],
        out_shape=[
            shaped((count, width), low),
            shaped((count, width), low),
            shaped((count, width), low),
            shaped((width, count), low),
            shaped((images, width // PAIR, STATE_ROWS, PAIR), wide),
            shaped((width, width), low),
            shaped((width, width), low),
        ],
        scratch_shapes=[pltpu.VMEM((2, width, GROUP), low)],
        cost_estimate=cost(2 * count * width * width, 8 * width * width + 12 * count * width),
        megabytes=40,
        name="project",
    )(x, vec, *pieces.arrays)


def query_kernel(bits, spot_ref, a_ref, *refs):
    fq_ref, wq_ref, wo_ref, joined_ref = refs[4:]
    join(joined_ref, bits, spot_ref, *refs[:4])
    wq_ref[...] = joined_ref[0]
    wo_ref[...] = joined_ref[1]
    fq_ref[...] = feature(mm(a_ref[...], joined_ref[0]))


def query(a, pieces, tokens=()):
    count, width = a.shape
    weight = pl.BlockSpec((width, GROUP), lambda g, spot: (0, g))
    return launch_at(
        functools.partial(query_kernel, pieces.bits),
        pieces.spot,
        tokens,
        grid=(width // GROUP,),
        in_specs=[whole((count, width))] + pieces.blocks(GROUP, lambda g, spot: (0, 0, g)),
        out_specs=[pl.BlockSpec((count, GROUP), lambda g, spot: (0, g)), weight, weight],
        out_shape=[shaped((count, width), low)] + [shaped((width, width), low)] * 2,
        scratch_shapes=[pltpu.VMEM((2, width, GROUP), low)],
        cost_estimate=cost(count * width * width, 6 * width * width + 4 * count * width),
        megabytes=24,
        name="query",
    )(a, *pieces.arrays)


def turn_kernel(x_ref, out_ref):
    out_ref[...] = x_ref[...].T


def turn(x, images, span, tokens=()):
    count, width = x.shape
    return turned_whole(
        launch(
            turn_kernel,
            tokens,
            grid=(images,),
            in_specs=[pl.BlockSpec((span, width), lambda b: (b, 0))],
            out_specs=turned_block(width, span),
            out_shape=turned_shape(images, width, span),
            cost_estimate=cost(1, 4 * count * width),
            megabytes=16,
            name="turn",
        )(x)
    )


def attend_kernel(span, fq_ref, fk_ref, v_ref, num_ref, den_ref):
    own = first_head(span)
    causal = causal_mask(span, True)
    one = jnp.ones((span, PAIR), low)
    zero = jnp.zeros((span, PAIR), low)
    for pair in range(GROUP // PAIR):
        lanes = slice(pair * PAIR, (pair + 1) * PAIR)
        query, key, value = fq_ref[:, lanes], fk_ref[:, lanes], v_ref[:, lanes]
        products = []
        for mask in (own, jnp.logical_not(own)):
            scores = mt(jnp.where(mask, query, zero), key).astype(low) * causal
            right = jnp.concatenate([jnp.where(mask, value, zero), jnp.where(mask, one, zero)], axis=1)
            products.append((scores, right))
        total = pair_mm(*products)
        num_ref[:, lanes] = total[:, :PAIR]
        den_ref[:, lanes] = total[:, PAIR:]


def attend(fq, fk, v, images, span, tokens=()):
    rows, width = fq.shape
    block = pl.BlockSpec((span, GROUP), lambda b, p: (b, p))
    return launch(
        functools.partial(attend_kernel, span),
        tokens,
        grid=(images, width // GROUP),
        in_specs=[block] * 3,
        out_specs=[block] * 2,
        out_shape=[shaped((rows, width), wide)] * 2,
        cost_estimate=cost(16 * rows * span * width, 14 * rows * width),
        megabytes=16,
        name="attend",
    )(fq, fk, v)


def turned_block(width, span):
    if span % 128:
        return pl.BlockSpec((None, width, span), lambda b: (b, 0, 0))
    return pl.BlockSpec((width, span), lambda b: (0, b))


def turned_shape(images, width, span):
    return shaped((images, width, span) if span % 128 else (width, images * span), low)


def turned_whole(array):
    if array.ndim == 2:
        return array
    return jnp.swapaxes(array, 0, 1).reshape(array.shape[1], -1)


def mix_kernel(x_ref, vec_ref, wo_ref, fq_ref, num_ref, den_ref, prior_ref, mixed_ref, rden_ref, resid_ref, a_ref, at_ref):
    width = x_ref.shape[1]
    for pair in range(width // PAIR):
        lanes = slice(pair * PAIR, (pair + 1) * PAIR)
        folded = prior_ref[0, pair]
        matrix = jnp.concatenate(
            [unfold_state(folded[:HEAD_DIM]), unfold_total(folded[HEAD_DIM : HEAD_DIM + 1])], axis=0
        )
        high, rest = split_low(matrix)
        query = fq_ref[:, lanes]
        both = mt(jnp.concatenate([query, query], axis=1), jnp.concatenate([high, rest], axis=1))
        scale = 1.0 / (den_ref[:, lanes] + both[:, PAIR:])
        rden_ref[:, lanes] = scale
        mixed_ref[:, lanes] = ((num_ref[:, lanes] + both[:, :PAIR]) * scale).astype(low)
    resid = x_ref[...].astype(wide) + mm(mixed_ref[...], wo_ref[...])
    resid_ref[...] = resid
    unit, _ = normalised(resid)
    normed = (unit * vec_ref[2:3, :] + vec_ref[3:4, :]).astype(low)
    a_ref[...] = normed
    at_ref[...] = normed.T


def mix(x, vec, wo, fq, num, den, prior, images, span, tokens=()):
    rows_, width = x.shape
    rows = pl.BlockSpec((span, width), lambda b: (b, 0))
    return launch(
        mix_kernel,
        tokens,
        grid=(images,),
        in_specs=[
            rows,
            whole(vec.shape),
            whole(wo.shape),
            rows,
            rows,
            rows,
            pl.BlockSpec((1,) + prior.shape[1:], lambda b: (b, 0, 0, 0)),
        ],
        out_specs=[rows, rows, rows, rows, turned_block(width, span)],
        out_shape=[
            shaped((rows_, width), low),
            shaped((rows_, width), wide),
            shaped((rows_, width), wide),
            shaped((rows_, width), low),
            turned_shape(images, width, span),
        ],
        cost_estimate=cost(4 * rows_ * width * width, 24 * rows_ * width + 2 * width * width),
        megabytes=36,
        name="mix",
    )(x, vec, wo, fq, num, den, prior)


gelu_scale = 0.7978845608028654
gelu_cubic = 0.044715


def feed_kernel(fresh, bits, spot_ref, *refs):
    a_ref, at_ref, e_ref, et_ref = refs[:4]
    out_ref, da_ref, kept_ref, sent_ref, joined_ref = refs[-5:]
    join(joined_ref, bits, spot_ref, *refs[4:8])

    @pl.when(pl.program_id(0) == 0)
    def _():
        if fresh:
            out_ref[...] = jnp.zeros_like(out_ref)
            da_ref[...] = jnp.zeros_like(da_ref)
        else:
            out_ref[...] = refs[8][...]
            da_ref[...] = refs[9][...]

    up, down = joined_ref[0], joined_ref[1]
    upper = mm(a_ref[...], up)
    grad = mm(e_ref[...], down)
    square = upper * upper
    bend = jnp.tanh(gelu_scale * upper * (1.0 + gelu_cubic * square))
    gate = 0.5 + 0.5 * bend
    hidden = (upper * gate).astype(low)
    slope = gate + 0.5 * upper * (1.0 - bend * bend) * (gelu_scale * (1.0 + 3.0 * gelu_cubic * square))
    dupper = (grad * slope).astype(low)
    out_ref[...] += mt(hidden, down)
    da_ref[...] += mt(dupper, up)
    to_up = mm(at_ref[...], dupper).astype(low)
    to_down = mm(et_ref[...], hidden).astype(low)
    first = spot_ref[0] == 0
    kept_ref[...] = jnp.where(first, to_up, to_down)
    sent_ref[...] = jnp.where(first, to_down, to_up)


def feed(pieces, a, at, e, et, carried, tokens=()):
    rows, width = a.shape
    slabs = pieces.arrays[0].shape[0]
    tiles = SLAB // TILE
    grads = pl.BlockSpec((width, TILE), lambda g, spot: (0, g))
    full = whole((rows, width))
    turned = whole((width, rows))
    fresh = carried is None
    return launch_at(
        functools.partial(feed_kernel, fresh, pieces.bits),
        pieces.spot,
        tokens,
        grid=(slabs * tiles,),
        in_specs=[full, turned, full, turned]
        + pieces.blocks(TILE, lambda g, spot: (g // tiles, 0, g % tiles))
        + ([] if fresh else [full, full]),
        out_specs=[full, full, grads, grads],
        out_shape=[shaped((rows, width), wide)] * 2 + [shaped((width, slabs * SLAB), low)] * 2,
        scratch_shapes=[pltpu.VMEM((2, width, TILE), low)],
        cost_estimate=cost(6 * rows * width * slabs * SLAB, 8 * width * slabs * SLAB + 20 * rows * width),
        megabytes=36,
        name="feed",
    )(a, at, e, et, *pieces.arrays, *(() if fresh else carried))


def outer_kernel(core_ref, mixed_ref, branch_ref, kept_ref, sent_ref):
    product = tm(mixed_ref[...], branch_ref[...]).astype(low)
    half = product.shape[1] // 2
    first = core_ref[0] == 0
    kept_ref[...] = jnp.where(first, product[:, :half], product[:, half:])
    sent_ref[...] = jnp.where(first, product[:, half:], product[:, :half])


def outer(mixed, branch, tokens=()):
    rows, width = mixed.shape
    result = pl.BlockSpec((GROUP, width // 2), lambda g, core: (g, 0))
    return launch_at(
        outer_kernel,
        core_index(),
        tokens,
        grid=(width // GROUP,),
        in_specs=[pl.BlockSpec((rows, GROUP), lambda g, core: (0, g)), whole((rows, width))],
        out_specs=[result, result],
        out_shape=[shaped((width, width // 2), low)] * 2,
        cost_estimate=cost(rows * width * width, 4 * rows * width + 2 * width * width),
        megabytes=20,
        name="outer",
    )(mixed, branch)


def turn_back_kernel(x_out_ref, da_ref, resid_ref, e_ref, vec_ref, wo_ref, mixed_ref, rden_ref, fq_ref,
                     out_ref, dres_ref, branch_ref, dn_ref, w_ref, state_ref, sums_ref):
    width = da_ref.shape[1]
    resid = resid_ref[...]
    out_ref[...] = (resid + x_out_ref[...]).astype(low)
    unit, scale = normalised(resid)
    da = da_ref[...]

    @pl.when(pl.program_id(0) == 0)
    def _():
        sums_ref[...] = jnp.zeros_like(sums_ref)

    sums_ref[0:1, :] += jnp.sum(da * unit, axis=0, keepdims=True)
    sums_ref[1:2, :] += jnp.sum(da, axis=0, keepdims=True)
    p = da * vec_ref[2:3, :]
    back = p - jnp.mean(p, axis=-1, keepdims=True) - unit * jnp.mean(p * unit, axis=-1, keepdims=True)
    dres = e_ref[...].astype(wide) + scale * back
    dres_ref[...] = dres
    branch = dres.astype(low)
    branch_ref[...] = branch
    dmixed = mt(branch, wo_ref[...]).astype(low).astype(wide)
    dnumer = dmixed * rden_ref[...]
    dn_ref[...] = dnumer.astype(low)
    w_ref[...] = (-dnumer * mixed_ref[...].astype(wide)).astype(low)
    for pair in range(width // PAIR):
        lanes = slice(pair * PAIR, (pair + 1) * PAIR)
        query = fq_ref[:, lanes]
        state_ref[0, pair, :HEAD_DIM, :] = fold_state(tm(dn_ref[:, lanes], query))
        total = jnp.sum(fold_state(tm(w_ref[:, lanes], query)), axis=0, keepdims=True)
        state_ref[0, pair, HEAD_DIM:, :] = jnp.broadcast_to(total, (STATE_ROWS - HEAD_DIM, PAIR))


def turn_back(x_out, da, resid, e, vec, wo, mixed, rden, fq, images, span, tokens=()):
    rows_, width = da.shape
    rows = pl.BlockSpec((span, width), lambda b: (b, 0))
    state = (images, width // PAIR, STATE_ROWS, PAIR)
    return launch(
        turn_back_kernel,
        tokens,
        grid=(images,),
        in_specs=[rows, rows, rows, rows, whole(vec.shape), whole(wo.shape), rows, rows, rows],
        out_specs=[rows] * 5 + [pl.BlockSpec((1,) + state[1:], lambda b: (b, 0, 0, 0)), whole((8, width))],
        out_shape=[
            shaped((rows_, width), low),
            shaped((rows_, width), wide),
            shaped((rows_, width), low),
            shaped((rows_, width), low),
            shaped((rows_, width), low),
            shaped(state, wide),
            shaped((8, width), wide),
        ],
        cost_estimate=cost(5 * rows_ * width * width, 30 * rows_ * width),
        megabytes=44,
        name="turn_back",
    )(x_out, da, resid, e, vec, wo, mixed, rden, fq)


def attend_back_kernel(span, fq_ref, fk_ref, v_ref, dn_ref, w_ref, prior_ref, dq_ref, dfk_ref, dv_ref):
    own = first_head(span)
    own_twice = jnp.concatenate([own, own], axis=1)
    below, above = causal_mask(span, True), causal_mask(span, False)
    one = jnp.ones((span, PAIR), low)
    zero = jnp.zeros((span, PAIR), low)
    zero_twice = jnp.zeros((span, 2 * PAIR), low)
    for pair in range(GROUP // PAIR):
        lanes = slice(pair * PAIR, (pair + 1) * PAIR)
        query, key, value = fq_ref[:, lanes], fk_ref[:, lanes], v_ref[:, lanes]
        grads = jnp.concatenate([dn_ref[:, lanes], w_ref[:, lanes]], axis=1)
        extended = jnp.concatenate([value, one], axis=1)
        folded = prior_ref[0, pair]
        matrix = jnp.concatenate(
            [unfold_state(folded[:HEAD_DIM]), unfold_total(folded[HEAD_DIM : HEAD_DIM + 1])], axis=0
        )
        high, rest = split_low(matrix)
        dfq = mm(jnp.concatenate([grads, grads], axis=1), jnp.concatenate([high, rest], axis=0))
        to_query, to_key, to_value = [], [], []
        for mask, both in ((own, own_twice), (jnp.logical_not(own), jnp.logical_not(own_twice))):
            head_grads = jnp.where(both, grads, zero_twice)
            head_query = jnp.where(mask, query, zero)
            head_key = jnp.where(mask, key, zero)
            to_query.append((mt(head_grads, extended).astype(low) * below, head_key))
            to_key.append((mt(extended, head_grads).astype(low) * above, head_query))
            to_value.append((mt(head_key, query).astype(low) * above, head_grads[:, :PAIR]))
        dfq = dfq + pair_mm(*to_query)
        dq_ref[:, lanes] = (dfq * jnp.minimum(query.astype(wide), 1.0)).astype(low)
        dfk_ref[:, lanes] = pair_mm(*to_key)
        dv_ref[:, lanes] = pair_mm(*to_value)


def attend_back(image, fq, fk, v, dn, w, prior, span, tokens=()):
    width = fq.shape[1]
    block = pl.BlockSpec((span, GROUP), lambda p: (image, p))
    column = pl.BlockSpec((span, GROUP), lambda p: (0, p))
    return launch(
        functools.partial(attend_back_kernel, span),
        tokens,
        grid=(width // GROUP,),
        in_specs=[block] * 5 + [pl.BlockSpec((1, GROUP // PAIR) + prior.shape[2:], lambda p: (image, p, 0, 0))],
        out_specs=[column] * 3,
        out_shape=[shaped((span, width), low), shaped((span, width), wide), shaped((span, width), wide)],
        cost_estimate=cost(32 * span * span * width, 24 * span * width),
        megabytes=20,
        name="attend_back",
    )(fq, fk, v, dn, w, prior)


def finish_kernel(images, span, core_ref, *refs):
    locals_ = [refs[3 * image : 3 * image + 3] for image in range(images)]
    fk_ref, v_ref, later_ref, at_ref, dq_ref, dk_ref, dv_ref, kept_ref, sent_ref = refs[3 * images :]
    keeps = pl.program_id(0) == core_ref[0]
    for image in range(images):
        rows = slice(image * span, (image + 1) * span)
        dqi_ref, dfk_ref, dvl_ref = locals_[image]
        dq_ref[rows, :] = dqi_ref[...]
        for pair in range(GROUP // PAIR):
            lanes = slice(pair * PAIR, (pair + 1) * PAIR)
            folded = later_ref[image, pair]
            high, rest = split_low(unfold_state(folded[:HEAD_DIM]))
            key, value = fk_ref[rows, lanes], v_ref[rows, lanes]
            dfk = dfk_ref[:, lanes] + folded[HEAD_DIM : HEAD_DIM + 1]
            dfk = dfk + mm(jnp.concatenate([value, value], axis=1), jnp.concatenate([high, rest], axis=0))
            dv = dvl_ref[:, lanes] + mt(
                jnp.concatenate([key, key], axis=1), jnp.concatenate([high, rest], axis=1)
            )
            dk_ref[rows, lanes] = (dfk * jnp.minimum(key.astype(wide), 1.0)).astype(low)
            dv_ref[rows, lanes] = dv.astype(low)
    for k, ref in enumerate((dq_ref, dk_ref, dv_ref)):
        product = mm(at_ref[...], ref[...]).astype(low)

        @pl.when(keeps)
        def _():
            kept_ref[k] = product

        @pl.when(jnp.logical_not(keeps))
        def _():
            sent_ref[k] = product


def finish(side, parts, fk, v, later, at, images, span, tokens=()):
    rows, width = fk.shape
    half = width // 2
    columns = half // 2
    column = pl.BlockSpec((rows, columns), lambda g, core: (0, side * 2 + g))
    part = pl.BlockSpec((span, columns), lambda g, core: (0, side * 2 + g))
    result = pl.BlockSpec((rows, columns), lambda g, core: (0, g))
    grads = whole((3, width, columns))
    state = pl.BlockSpec((images, columns // PAIR) + later.shape[2:], lambda g, core: (0, side * 2 + g, 0, 0))
    return launch_at(
        functools.partial(finish_kernel, images, span),
        core_index(),
        tokens,
        grid=(2,),
        in_specs=[part] * (3 * images) + [column] * 2 + [state, whole(at.shape)],
        out_specs=[result] * 3 + [grads, grads],
        out_shape=[shaped((rows, half), low)] * 3 + [shaped((3, width, columns), low)] * 2,
        cost_estimate=cost(2 * rows * width * width, 15 * rows * width),
        megabytes=28,
        name="finish",
    )(*[array for image in parts for array in image], fk, v, later, at)


def enter_kernel(*refs):
    lefts, rights, weights = refs[:3], refs[3:6], refs[6:9]
    x_ref, dres_ref, vec_ref, grad_ref, sums_ref = refs[9:]
    half = x_ref.shape[1] // 2
    da = None
    for left, right, weight in zip(lefts, rights, weights):
        part = mt(left[...], weight[:, :half]) + mt(right[...], weight[:, half:])
        da = part if da is None else da + part
    unit, scale = normalised(x_ref[...].astype(wide))
    sums_ref[0:1, :] = jnp.sum(da * unit, axis=0, keepdims=True)
    sums_ref[1:2, :] = jnp.sum(da, axis=0, keepdims=True)
    sums_ref[2:, :] = jnp.zeros_like(sums_ref[2:, :])
    p = da * vec_ref[0:1, :]
    back = p - jnp.mean(p, axis=-1, keepdims=True) - unit * jnp.mean(p * unit, axis=-1, keepdims=True)
    grad_ref[...] = (dres_ref[...] + scale * back).astype(low)


def enter(image, left, right, weights, x, dres, vec, span, tokens=()):
    width = x.shape[1]
    rows = pl.BlockSpec((span, width), lambda g: (image, 0))
    part = pl.BlockSpec((span, width // 2), lambda g: (image, 0))
    return launch(
        enter_kernel,
        tokens,
        grid=(1,),
        in_specs=[part] * 6 + [whole((width, width))] * 3 + [rows, rows, whole(vec.shape)],
        out_specs=[whole((span, width)), whole((8, width))],
        out_shape=[shaped((span, width), low), shaped((8, width), wide)],
        cost_estimate=cost(3 * span * width * width, 14 * span * width + 6 * width * width),
        megabytes=40,
        name="enter",
    )(*left, *right, *weights, x, dres, vec)


def adam_update(master, moment, second, average, gradient, factor, rate):
    clipped = gradient * factor
    moment = beta_first * moment + (1.0 - beta_first) * clipped
    second = beta_second * second + (1.0 - beta_second) * clipped * clipped
    first_hat = moment / (1.0 - beta_first**STEP)
    second_hat = second / (1.0 - beta_second**STEP)
    master = master - rate * (first_hat / (jnp.sqrt(second_hat) + eps_adam) + weight_decay * master)
    average = average_decay * average + (1.0 - average_decay) * master
    return (master, moment, second, average)


def powers(count):
    return [1 << k for k in range(count.bit_length() - 1)]


def core_index():
    return lax.axis_index("seq") % 2


def pos_index():
    return lax.axis_index("seq") // 2


def pos_bits():
    return (lax.axis_size("seq") // 2).bit_length() - 1


def flip(array, axis, bit):
    return lax.ppermute(array, axis, [(i, i ^ bit) for i in range(lax.axis_size(axis))])


def flip_core(array):
    return flip(array, "seq", 1)


def flip_pos(array, stage):
    bits = pos_bits()
    pairs = [(i, i ^ (2 << (stage if i % 2 == 0 else bits - 1 - stage))) for i in range(lax.axis_size("seq"))]
    return lax.ppermute(array, "seq", pairs)


def own_bit(stage):
    bits = pos_bits()
    return jnp.where(core_index() == 0, pos_index() >> stage, pos_index() >> (bits - 1 - stage)) & 1


def halves(shape, dim):
    index = np.arange(int(np.prod(shape))).reshape(shape)
    return np.stack([index.take(side, axis=dim).ravel() for side in range(2)])


def fold_kernel(chains, spot_ref, *refs):
    ins, outs = refs[: 4 * chains], refs[4 * chains :]
    for k in range(2 * chains):
        value = ins[2 * k][...].astype(wide) + ins[2 * k + 1][...].astype(wide)
        outs[k][...] = value.astype(outs[k].dtype)


def fold(cuts, tokens=()):
    count = cuts[0][2].shape[0]
    steps = 4 if all(kept.shape[-1] >= 512 for kept, *_ in cuts) else 2
    in_specs, out_specs, out_shape, arrays, moved = [], [], [], [], 0
    for k, (kept, came, keeps, sends) in enumerate(cuts):
        lead, _, rows, columns = kept.shape
        block = (lead, 1, rows, columns // steps)
        for side in range(2):
            at = 2 * k * count + side * count
            spec = pl.BlockSpec(block, lambda g, c, spot, at=at: (0, spot[at + g], 0, c))
            in_specs += [spec, spec]
            arrays += [kept, came]
            out_specs.append(pl.BlockSpec(block, lambda g, c, spot: (0, g, 0, c)))
            out_shape.append(shaped((lead, count, rows, columns), low if side or kept.dtype == low else wide))
        moved += 8 * kept.size
    results = launch_at(
        functools.partial(fold_kernel, len(cuts)),
        jnp.concatenate([part for _, _, keeps, sends in cuts for part in (keeps, sends)]),
        tokens,
        grid=(count, steps),
        in_specs=in_specs,
        out_specs=out_specs,
        out_shape=out_shape,
        cost_estimate=cost(1, moved),
        megabytes=20,
        name="fold",
    )(*arrays)
    return [results[2 * k : 2 * k + 2] for k in range(len(cuts))]


class Chain:
    def __init__(self, kept, sent):
        self.lead = kept.shape[0] if kept.ndim == 3 else 1
        self.stage = -1
        self.left = [list(range(pos_bits()))[::-1]] * 2
        shape = (self.lead, 2 ** pos_bits(), -1, kept.shape[-1])
        self.kept, self.sends = kept.reshape(shape), [sent.reshape(shape)]

    def start(self):
        if self.stage < 0:
            self.came = [flip_core(self.sends[0])]
        else:
            self.came = [flip_pos(self.sends[0], self.stage)]

    def cut(self):
        self.stage += 1
        tables = []
        for kind in range(2):
            bit = self.stage if kind == 0 else pos_bits() - 1 - self.stage
            left = self.left[kind]
            tables.append(halves((2,) * len(left), left.index(bit)))
            self.left[kind] = [other for other in left if other != bit]
        table = jnp.where(core_index() == 0, *[jnp.asarray(part, jnp.int32) for part in tables])
        own = own_bit(self.stage)
        return (self.kept, self.came[0], table[own], table[1 - own])

    def take(self, parts):
        self.kept, self.sends = parts[0], [parts[1]]


def advance(chains, tokens=()):
    parts = fold([chain.cut() for chain in chains], tokens)
    for chain, part in zip(chains, parts):
        chain.take(part)
        chain.start()
    return [array for chain in chains for array in chain.sends]


def last_kernel(ways, pre, pieces, spot_ref, *refs):
    ins, outs = refs[: 2 * pieces], refs[2 * pieces :]
    at = 0
    for k in range(pieces):
        columns = ins[2 * k].shape[-1]
        for j in range(ways):
            place = spot_ref[0] ^ j
            for n in range(pre):
                value = ins[2 * k][n, place].astype(wide) + ins[2 * k + 1][n, place].astype(wide)
                outs[j][n, :, at : at + columns] = value.astype(outs[j].dtype)
        at += columns


class Last:
    def __init__(self, chains, tokens=(), slowly=False):
        slices = lax.axis_size("img")
        ways = 2 if slowly else slices
        self.lead = chains[0].lead
        pre = self.lead * 2 * slices // ways
        arrays = []
        for chain in chains:
            for array in (chain.kept, chain.came[0]):
                arrays.append(array.reshape(pre, ways, -1, array.shape[-1]))
        self.widths = [array.shape[-1] for array in arrays[::2]]
        inside = pl.BlockSpec(memory_space=pltpu.VMEM)
        parts = launch(
            functools.partial(last_kernel, ways, pre, len(chains)),
            tokens,
            in_specs=[pl.BlockSpec(memory_space=pltpu.SMEM)] + [inside] * len(arrays),
            out_specs=[inside] * ways,
            out_shape=[shaped((pre, arrays[0].shape[2], sum(self.widths)), low if j else wide) for j in range(ways)],
            cost_estimate=cost(1, 4 * sum(array.size for array in arrays)),
            megabytes=16,
            name="last",
        )((lax.axis_index("img") % ways).reshape(1), *arrays)
        self.kept, self.sends = parts[0], list(parts[1:])
        self.hops = list(range(1, ways))
        self.left = powers(slices)[1:][::-1] if slowly else []
        self.start()

    def start(self):
        self.came = [flip(array, "img", hop) for array, hop in zip(self.sends, self.hops)]

    def cut(self):
        bit = self.left[-1]
        entries = self.kept.reshape((1, -1) + self.kept.shape[-2:])
        dims = (2 * self.lead,) + (2,) * len(self.left)
        table = jnp.asarray(halves(dims, len(dims) - 1), jnp.int32)
        own = (lax.axis_index("img") // bit) % 2
        self.left = self.left[:-1]
        self.hops = [bit]
        return (entries, self.came[0].reshape(entries.shape), table[own], table[1 - own])

    def take(self, parts):
        self.kept, self.sends = parts[0][0], [parts[1][0]]

    def total(self):
        while self.left:
            advance([self])
        total = self.kept
        for came in self.came:
            total = total + came.astype(wide)
        return total

    def finish(self):
        core = core_index()
        total = self.total()
        total = total.reshape((self.lead, 2) + total.shape[-2:])
        own = lax.dynamic_index_in_dim(total, core, 1, False)
        came = flip_core(lax.dynamic_index_in_dim(total, 1 - core, 1, False))
        first, second = jnp.where(core == 0, own, came), jnp.where(core == 0, came, own)
        at, found = 0, []
        for columns in self.widths:
            found.append((first[..., at : at + columns], second[..., at : at + columns]))
            at += columns
        return found


def sum_slowly(array):
    for axis in ("seq", "img"):
        for bit in powers(lax.axis_size(axis)):
            array = array + flip(array, axis, bit)
    return array


def sum_all(array):
    rounds = [("img", range(1, lax.axis_size("img"))), ("seq", range(2, lax.axis_size("seq"), 2)), ("seq", [1])]
    for axis, hops in rounds:
        came = [flip(array, axis, hop) for hop in hops]
        for other in came:
            array = array + other
    return array


def assemble_kernel(plan, spot_ref, *refs):
    outs = sorted({out for _, _, out, _ in plan})
    count = len(refs) - 1 - len(outs)
    sems = refs[-1]
    copies = []
    for k, (piece, cut, out, where) in enumerate(plan):
        source = refs[piece].at[cut] if cut is not None else refs[piece]
        target = refs[count + out].at[where(spot_ref)]
        copies.append(pltpu.make_async_copy(source, target, sems.at[k]))
    for copy in copies:
        copy.start()
    for copy in copies:
        copy.wait()


def assemble(plan, spots, pieces, shapes, tokens=()):
    anywhere = pl.BlockSpec(memory_space=pl.ANY)
    return launch(
        functools.partial(assemble_kernel, plan),
        tokens,
        in_specs=[pl.BlockSpec(memory_space=pltpu.SMEM)] + [anywhere] * len(pieces),
        out_specs=[pl.BlockSpec(memory_space=pltpu.VMEM)] * len(shapes),
        out_shape=[shaped(shape, low) for shape in shapes],
        scratch_shapes=[pltpu.SemaphoreType.DMA((len(plan),))],
        cost_estimate=cost(1, 2 * sum(2 * piece.size for piece in pieces)),
        megabytes=12,
        name="assemble",
    )(jnp.stack(spots).astype(jnp.int32), *pieces)


def gate_kernel(in_ref, out_ref):
    pass


def gate(array, tokens):
    anywhere = pl.BlockSpec(memory_space=pl.ANY)
    return launch(
        gate_kernel,
        tokens,
        in_specs=[anywhere],
        out_specs=anywhere,
        out_shape=shaped(array.shape, array.dtype),
        input_output_aliases={0: 0},
        cost_estimate=cost(1, 1),
        megabytes=4,
        name="gate",
    )(array)


class Gather:
    def __init__(self, own, other):
        self.own, self.other = own, other
        self.stage = 0

    def start_slices(self):
        came = flip_core(self.other)
        pairs = [jnp.stack([self.own, came], axis=1), jnp.stack([came, self.own], axis=1)]
        self.pieces = [jnp.where(core_index() == 0, *pairs)]
        for j in range(1, lax.axis_size("img")):
            bit = j & -j
            self.pieces.append(flip(self.pieces[j - bit], "img", bit))

    def finish_slices(self, tokens=()):
        slices = len(self.pieces)
        every = slice(None)
        plan = [(j, None, 0, lambda spot, j=j: (every, every, spot[0] ^ j)) for j in range(slices)]
        k, _, rows, columns = self.pieces[0].shape
        shape = (k, 2, slices, rows, columns)
        self.part = assemble(plan, [lax.axis_index("img")], self.pieces, [shape], tokens)[0]
        self.part = self.part.reshape(k, 1, 2 * slices * rows, columns)
        return [self.part]

    def start_pos(self):
        self.came = flip_pos(self.part, self.stage)
        self.stage += 1

    def finish_pos(self, tokens=()):
        every = slice(None)
        plan = [
            (0, None, 0, lambda spot: (every, spot[0])),
            (1, None, 0, lambda spot: (every, 1 - spot[0])),
        ]
        shape = self.part.shape[:1] + (2,) + self.part.shape[1:]
        self.part = assemble(plan, [own_bit(self.stage - 1)], [self.part, self.came], [shape], tokens)[0]
        self.part = self.part.reshape((shape[0], -1) + shape[3:])
        return [self.part]

    def start_last(self):
        self.start_pos()

    def finish_last(self, tokens=()):
        if tokens:
            self.came = gate(self.came, tokens)
        return Pieces([self.part, self.came, flip_core(self.part), flip_core(self.came)])


def narrow_kernel(plans, core_ref, *refs):
    own_ref, other_ref = refs[-2:]
    first = core_ref[0] == 0
    for k, ((ref, member, columns), (ref_b, member_b, columns_b)) in enumerate(zip(*plans)):
        left = refs[ref][member, :, columns].astype(low)
        right = refs[ref_b][member_b, :, columns_b].astype(low)
        own_ref[k] = jnp.where(first, left, right)
        other_ref[k] = jnp.where(first, right, left)


def narrow(plans, weights, tokens=()):
    owned = weights[0].shape[1]
    inside = pl.BlockSpec(memory_space=pltpu.VMEM)
    return Gather(
        *launch(
            functools.partial(narrow_kernel, plans),
            tokens,
            in_specs=[pl.BlockSpec(memory_space=pltpu.SMEM)] + [inside] * len(weights),
            out_specs=[inside, inside],
            out_shape=[shaped((len(plans[0]), owned, SLAB), low)] * 2,
            cost_estimate=cost(1, 12 * len(plans[0]) * owned * SLAB),
            megabytes=12,
            name="narrow",
        )(core_index().reshape(1), *weights)
    )


def passing(own, backward):
    total = own
    outside = jnp.zeros_like(own)
    for bit in powers(lax.axis_size("seq")):
        came = flip(total.astype(low), "seq", bit).astype(wide)
        upper = (lax.axis_index("seq") // bit) % 2
        outside = outside + jnp.where(upper == (0 if backward else 1), came, 0.0)
        total = total + came
    return outside


def body(
    images,
    cotangent,
    attention_weight,
    feedforward_weight,
    norm_vectors,
    attention_moment,
    feedforward_moment,
    norm_moment,
    attention_second,
    feedforward_second,
    norm_second,
    attention_average,
    feedforward_average,
    norm_average,
):
    count, span, width = images.shape
    tokens = count * span
    owned = attention_weight.shape[1]
    slabs = feedforward_weight.shape[2] // SLAB
    weights = (attention_weight, feedforward_weight)
    stages = pos_bits()
    half = slabs // 2
    every = slice(None)

    def feed_group(first, marks=()):
        plans = [[(1, kind, slice((first + n) * SLAB, (first + n + 1) * SLAB)) for n in range(half)] for kind in range(2)]
        return narrow(plans, weights, marks)

    def inner_stages(group, marks):
        for _ in range(stages - 1):
            group.start_pos()
            marks = group.finish_pos(marks)
        return marks

    x, e = images.reshape(tokens, width), cotangent.reshape(tokens, width)
    keys = jnp.pad(attention_weight[1].astype(low), ((0, 0), (0, 128)))
    vectors = jnp.pad(norm_vectors.astype(low).T, ((0, 0), (0, 124)))
    values = jnp.concatenate([attention_weight[2].astype(low), vectors], axis=1)
    first_core = core_index() == 0
    one = Gather(jnp.where(first_core, keys, values)[None], jnp.where(first_core, values, keys)[None])
    one.start_slices()
    two = narrow([[(0, 0, every)], [(0, 3, every)]], weights, [one.other])
    two.start_slices()
    et = turn(e, count, span)
    marks = inner_stages(one, one.finish_slices([et]))
    one.start_last()
    inner_pieces = one.finish_last()
    marks = two.finish_slices(marks)
    three = feed_group(0, marks)
    three.start_slices()
    marks = inner_stages(two, marks)
    two.start_last()
    outer_pieces = two.finish_last()
    vec = inner_pieces.second(slice(width, width + 4)).astype(wide).T
    fk, v, a1, a1t, state, wk, wv = project(x, vec, inner_pieces, count, span, marks)
    prior = passing(state, False)
    marks = three.finish_slices([state])
    four = feed_group(half, marks)
    four.start_slices()
    fq, wq, wo = query(a1, outer_pieces, marks)
    marks = inner_stages(three, [fq])
    three.start_last()
    first_pieces = three.finish_last()
    num, den = attend(fq, fk, v, count, span, marks)
    marks = four.finish_slices([num])
    mixed, rden, resid, a2, a2t = mix(x, vec, wo, fq, num, den, prior, count, span, marks)
    a2t = turned_whole(a2t)
    marks = inner_stages(four, [resid])
    four.start_last()

    early = feed(first_pieces, a2, a2t, e, et, None, marks)
    firsts = [Chain(*early[2:])]
    firsts[0].start()
    second_pieces = four.finish_last([early[0]])
    late = feed(second_pieces, a2, a2t, e, et, early[:2])
    seconds = [Chain(*late[2:])]
    seconds[0].start()
    marks = advance(firsts)
    output, dres, branch, dn, w, dstate, sums_second = turn_back(
        late[0], late[1], resid, e, vec, wo, mixed, rden, fq, count, span, marks
    )
    later = passing(dstate, True)
    outs = [Chain(*outer(mixed, branch))]
    outs[0].start()
    marks = advance(seconds)
    for _ in range(stages - 1):
        marks = marks + advance(firsts)
    parts = []
    for image in range(count):
        parts.append(attend_back(image, fq, fk, v, dn, w, prior, span, marks))
        if image == 0:
            marks = advance(outs, [parts[0][0]])
            firsts_last = Last(firsts, [parts[0][0]], True)
            marks = marks + firsts_last.sends
    for _ in range(stages - 1):
        marks = advance(seconds + outs, [parts[-1][0]])
    while firsts_last.left:
        marks = marks + advance([firsts_last], [parts[-1][0]])
    left = finish(0, parts, fk, v, later, a1t, count, span, marks)
    inner = [Chain(*left[3:])]
    inner[0].start()
    early_shard = firsts_last.finish()[0]
    seconds_last = Last(seconds + outs, [left[0]], True)
    right = finish(1, parts, fk, v, later, a1t, count, span, seconds_last.sends)
    inner.append(Chain(*right[3:]))
    inner[1].start()
    marks = advance(inner[:1], [right[0]]) + [early_shard[0]]
    while seconds_last.left:
        marks = marks + advance([seconds_last], [right[0]])
    grads_in = []
    for image in range(count):
        grads_in.append(enter(image, left[:3], right[:3], (wq, wk, wv), x, dres, vec, span, marks))
        if image == 0:
            late_shard, out_shard = seconds_last.finish()
            marks = advance(inner[1:], [grads_in[0][1]])
    input_grad = jnp.stack([part[0] for part in grads_in])
    sums_first = sum(part[1] for part in grads_in)
    vector_grad = sum_slowly(jnp.concatenate([sums_first[:2], sums_second[:2]], axis=0))
    device = lax.axis_index("seq") * lax.axis_size("img") + lax.axis_index("img")
    vector_shard = lax.dynamic_slice_in_dim(vector_grad, device * owned, owned, 1)
    for _ in range(stages - 1):
        advance(inner)
    inner_shard = Last(inner, [vector_shard, late_shard[0]]).finish()
    inner_shard = jnp.concatenate([part for pair in inner_shard for part in pair], axis=2)
    attn_shard = jnp.concatenate([inner_shard, jnp.concatenate(out_shard, axis=2)], axis=0)
    feed_shard = jnp.concatenate([jnp.concatenate(pair, axis=2) for pair in zip(early_shard, late_shard)], axis=0)

    local_squares = (
        jnp.sum(attn_shard * attn_shard) + jnp.sum(feed_shard * feed_shard) + jnp.sum(vector_shard * vector_shard)
    )
    grad_norm = jnp.sqrt(sum_all(jnp.full((8, 128), local_squares))[0, 0])
    factor = clip_bound / jnp.maximum(grad_norm, clip_bound)
    attn_new = adam_update(
        attention_weight, attention_moment, attention_second, attention_average, attn_shard, factor, learn_rate
    )
    feed_new = adam_update(
        feedforward_weight, feedforward_moment, feedforward_second, feedforward_average, feed_shard, factor, learn_rate
    )
    norm_new = adam_update(norm_vectors, norm_moment, norm_second, norm_average, vector_shard, factor, norm_rate)
    output = output.reshape(images.shape)
    input_grad = input_grad.reshape(images.shape)
    return (output, input_grad, grad_norm) + attn_new + feed_new + norm_new


def solution(mesh):
    tokens = P("img", "seq", None)
    rows = P(None, ("seq", "img"), None)
    vectors = P(None, ("seq", "img"))
    group = (rows, rows, vectors)
    return jax.shard_map(
        body,
        mesh=mesh,
        in_specs=(tokens, tokens) + group * 4,
        out_specs=(tokens, tokens, P()) + (rows,) * 8 + (vectors,) * 4,
        check_vma=False,
    )
```

```python
import functools

import jax
import jax.numpy as jnp
import numpy as np
from jax import lax
from jax.experimental import pallas as pl
from jax.experimental.pallas import tpu as pltpu
from jax.sharding import PartitionSpec as P

HEADS = 16
HEAD_DIM = 64
STEP = 10

beta_first = 0.9
beta_second = 0.95
learn_rate = 0.02
norm_rate = 0.2
weight_decay = 0.1
average_decay = 0.75
clip_bound = 1.0
eps_norm = 1e-05
eps_adam = 1e-08

PAIR = 2 * HEAD_DIM
STATE_ROWS = HEAD_DIM + 16
SLAB = 1024
TILE = 512
GROUP = 256

low = jnp.bfloat16
wide = jnp.float32


def params(megabytes=56):
    return pltpu.CompilerParams(vmem_limit_bytes=megabytes * 1024 * 1024)


def cost(products, elements):
    return pl.CostEstimate(flops=2 * products, bytes_accessed=elements, transcendentals=0)


def launch(kernel, tokens, in_specs, megabytes=56, **keys):
    known, extra = len(in_specs), len(tokens)

    def run(*refs):
        kernel(*refs[:known], *refs[known + extra :])

    call = pl.pallas_call(
        run, in_specs=list(in_specs) + [pl.BlockSpec(memory_space=pl.ANY)] * extra, compiler_params=params(megabytes), **keys
    )
    return lambda *args: call(*args, *tokens)


def launch_at(kernel, spot, tokens, grid, in_specs, out_specs, megabytes=56, scratch_shapes=(), **keys):
    known, extra = len(in_specs), len(tokens)

    def run(spot_ref, *refs):
        kernel(spot_ref, *refs[:known], *refs[known + extra :])

    call = pl.pallas_call(
        run,
        grid_spec=pltpu.PrefetchScalarGridSpec(
            num_scalar_prefetch=1,
            grid=grid,
            in_specs=list(in_specs) + [pl.BlockSpec(memory_space=pl.ANY)] * extra,
            out_specs=out_specs,
            scratch_shapes=scratch_shapes,
        ),
        compiler_params=params(megabytes),
        **keys,
    )
    return lambda *args: call(spot.reshape(-1).astype(jnp.int32), *args, *tokens)


def reversed_bits(value, count):
    return sum(((value >> k) & 1) << (count - 1 - k) for k in range(count))


def join(target_ref, bits, spot_ref, own_ref, came_ref, own_other_ref, came_other_ref):
    core, high, lowest = spot_ref[0], spot_ref[1], spot_ref[2]
    runs = 1 << (bits - 1)
    rows = target_ref.shape[1] // (2 * runs)
    for run in range(runs):
        source = slice(run * rows, (run + 1) * rows)
        turned = reversed_bits(run, bits)
        for place in range(2):
            first = (high ^ place) * runs + run
            second = turned + (lowest ^ place)
            for ref, slot in (((own_ref, came_ref)[place], core), ((own_other_ref, came_other_ref)[place], 1 - core)):
                at = jnp.where(slot == 0, first, second)
                target_ref[slot, pl.ds(pl.multiple_of(at * rows, rows), rows), :] = ref[source, :]


class Pieces:
    def __init__(self, arrays):
        self.arrays = [array.reshape(array.shape[0], -1, array.shape[-1]) for array in arrays]
        place = pos_index()
        self.bits = pos_bits()
        self.spot = jnp.stack([core_index(), place >> (self.bits - 1), place & 1])

    def blocks(self, columns, place):
        rows = self.arrays[0].shape[1]
        return [pl.BlockSpec((None, rows, columns), place)] * 4

    def second(self, columns):
        mine, others = (
            [part[0, :, columns].reshape(1 << (self.bits - 1), 1, -1, columns.stop - columns.start) for part in pair]
            for pair in (self.arrays[:2], self.arrays[2:])
        )
        own, came = (jnp.where(core_index() == 1, left, right) for left, right in zip(mine, others))
        straight, turned = jnp.concatenate([own, came], axis=1), jnp.concatenate([came, own], axis=1)
        runs = jnp.where(self.spot[2] == 0, straight, turned)
        order = [reversed_bits(run, self.bits - 1) for run in range(1 << (self.bits - 1))]
        return jnp.stack([runs[run] for run in order]).reshape(-1, columns.stop - columns.start)


def shaped(shape, kind):
    return jax.ShapeDtypeStruct(shape, kind)


def whole(shape):
    return pl.BlockSpec(shape, lambda *_: (0,) * len(shape))


def mm(left, right):
    return lax.dot_general(left, right, (((1,), (0,)), ((), ())), preferred_element_type=wide)


def mt(left, right):
    return lax.dot_general(left, right, (((1,), (1,)), ((), ())), preferred_element_type=wide)


def tm(left, right):
    return lax.dot_general(left, right, (((0,), (0,)), ((), ())), preferred_element_type=wide)


def pair_mm(first, second):
    if first[0].shape[1] % 128:
        return mm(*first) + mm(*second)
    return mm(jnp.concatenate([first[0], second[0]], axis=1), jnp.concatenate([first[1], second[1]], axis=0))


def causal_mask(span, below):
    rows = lax.broadcasted_iota(jnp.int32, (span, span), 0)
    columns = lax.broadcasted_iota(jnp.int32, (span, span), 1)
    return (rows >= columns if below else rows <= columns).astype(wide).astype(low)


def first_head(rows):
    return lax.broadcasted_iota(jnp.int32, (rows, PAIR), 1) < HEAD_DIM


def fold_state(product):
    return jnp.where(first_head(HEAD_DIM), product[:HEAD_DIM], product[HEAD_DIM:])


def unfold_state(folded):
    own = first_head(HEAD_DIM)
    zero = jnp.zeros_like(folded)
    return jnp.concatenate([jnp.where(own, folded, zero), jnp.where(own, zero, folded)], axis=0)


def unfold_total(row):
    tall = jnp.broadcast_to(row, (PAIR, PAIR))
    lanes = lax.broadcasted_iota(jnp.int32, (PAIR, PAIR), 1) < HEAD_DIM
    rows = lax.broadcasted_iota(jnp.int32, (PAIR, PAIR), 0) < HEAD_DIM
    return jnp.where(lanes == rows, tall, jnp.zeros_like(tall))


def split_low(values):
    high = values.astype(low)
    return high, (values - high.astype(wide)).astype(low)


def normalised(values):
    centre = jnp.mean(values, axis=-1, keepdims=True)
    centred = values - centre
    spread = jnp.mean(centred * centred, axis=-1, keepdims=True)
    scale = lax.rsqrt(spread + eps_norm)
    return centred * scale, scale


def feature(raw):
    return jnp.where(raw > 0, raw + 1.0, jnp.exp(jnp.minimum(raw, 0.0))).astype(low)


def project_kernel(images, span, bits, spot_ref, x_ref, vec_ref, *refs):
    fk_ref, v_ref, a_ref, at_ref, state_ref, wk_ref, wv_ref, joined_ref = refs[4:]

    @pl.when(pl.program_id(0) == 0)
    def _():
        gain, shift = vec_ref[0:1, :], vec_ref[1:2, :]
        step = span // 3
        for start in range(0, images * span, step):
            rows = slice(start, start + step)
            unit, _ = normalised(x_ref[rows, :].astype(wide))
            a_ref[rows, :] = (unit * gain + shift).astype(low)
        at_ref[...] = a_ref[...].T

    join(joined_ref, bits, spot_ref, *refs[:4])
    keys, values = joined_ref[0], joined_ref[1]
    wk_ref[...] = keys
    wv_ref[...] = values
    fk_ref[...] = feature(mm(a_ref[...], keys))
    v_ref[...] = mm(a_ref[...], values).astype(low)
    ones = jnp.ones((16, span), low)
    for image in range(images):
        rows = slice(image * span, (image + 1) * span)
        for pair in range(GROUP // PAIR):
            lanes = slice(pair * PAIR, (pair + 1) * PAIR)
            key, value = fk_ref[rows, lanes], v_ref[rows, lanes]
            state_ref[image, pair, :HEAD_DIM, :] = fold_state(tm(value, key))
            state_ref[image, pair, HEAD_DIM:, :] = mm(ones, key)


def project(x, vec, pieces, images, span, tokens=()):
    count, width = x.shape
    pairs = GROUP // PAIR
    column = pl.BlockSpec((count, GROUP), lambda g, spot: (0, g))
    weight = pl.BlockSpec((width, GROUP), lambda g, spot: (0, g))
    return launch_at(
        functools.partial(project_kernel, images, span, pieces.bits),
        pieces.spot,
        tokens,
        grid=(width // GROUP,),
        in_specs=[whole((count, width)), whole(vec.shape)] + pieces.blocks(GROUP, lambda g, spot: (0, 0, g)),
        out_specs=[
            column,
            column,
            whole((count, width)),
            whole((width, count)),
            pl.BlockSpec((images, pairs, STATE_ROWS, PAIR), lambda g, spot: (0, g, 0, 0)),
            weight,
            weight,
        ],
        out_shape=[
            shaped((count, width), low),
            shaped((count, width), low),
            shaped((count, width), low),
            shaped((width, count), low),
            shaped((images, width // PAIR, STATE_ROWS, PAIR), wide),
            shaped((width, width), low),
            shaped((width, width), low),
        ],
        scratch_shapes=[pltpu.VMEM((2, width, GROUP), low)],
        cost_estimate=cost(2 * count * width * width, 8 * width * width + 12 * count * width),
        name="project",
    )(x, vec, *pieces.arrays)


def query_kernel(bits, spot_ref, a_ref, *refs):
    fq_ref, wq_ref, wo_ref, joined_ref = refs[4:]
    join(joined_ref, bits, spot_ref, *refs[:4])
    wq_ref[...] = joined_ref[0]
    wo_ref[...] = joined_ref[1]
    fq_ref[...] = feature(mm(a_ref[...], joined_ref[0]))


def query(a, pieces, tokens=()):
    count, width = a.shape
    weight = pl.BlockSpec((width, GROUP), lambda g, spot: (0, g))
    return launch_at(
        functools.partial(query_kernel, pieces.bits),
        pieces.spot,
        tokens,
        grid=(width // GROUP,),
        in_specs=[whole((count, width))] + pieces.blocks(GROUP, lambda g, spot: (0, 0, g)),
        out_specs=[pl.BlockSpec((count, GROUP), lambda g, spot: (0, g)), weight, weight],
        out_shape=[shaped((count, width), low)] + [shaped((width, width), low)] * 2,
        scratch_shapes=[pltpu.VMEM((2, width, GROUP), low)],
        cost_estimate=cost(count * width * width, 6 * width * width + 4 * count * width),
        name="query",
    )(a, *pieces.arrays)


def turn_kernel(x_ref, out_ref):
    out_ref[...] = x_ref[...].T


def turn(x, images, span, tokens=()):
    count, width = x.shape
    return turned_whole(
        launch(
            turn_kernel,
            tokens,
            grid=(images,),
            in_specs=[pl.BlockSpec((span, width), lambda b: (b, 0))],
            out_specs=turned_block(width, span),
            out_shape=turned_shape(images, width, span),
            cost_estimate=cost(1, 4 * count * width),
                name="turn",
        )(x)
    )


def attend_kernel(span, fq_ref, fk_ref, v_ref, num_ref, den_ref):
    own = first_head(span)
    causal = causal_mask(span, True)
    one = jnp.ones((span, PAIR), low)
    zero = jnp.zeros((span, PAIR), low)
    for pair in range(GROUP // PAIR):
        lanes = slice(pair * PAIR, (pair + 1) * PAIR)
        query, key, value = fq_ref[:, lanes], fk_ref[:, lanes], v_ref[:, lanes]
        products = []
        for mask in (own, jnp.logical_not(own)):
            scores = mt(jnp.where(mask, query, zero), key).astype(low) * causal
            right = jnp.concatenate([jnp.where(mask, value, zero), jnp.where(mask, one, zero)], axis=1)
            products.append((scores, right))
        total = pair_mm(*products)
        num_ref[:, lanes] = total[:, :PAIR]
        den_ref[:, lanes] = total[:, PAIR:]


def attend(fq, fk, v, images, span, tokens=()):
    rows, width = fq.shape
    block = pl.BlockSpec((span, GROUP), lambda b, p: (b, p))
    return launch(
        functools.partial(attend_kernel, span),
        tokens,
        grid=(images, width // GROUP),
        in_specs=[block] * 3,
        out_specs=[block] * 2,
        out_shape=[shaped((rows, width), wide)] * 2,
        cost_estimate=cost(16 * rows * span * width, 14 * rows * width),
        name="attend",
    )(fq, fk, v)


def turned_block(width, span):
    if span % 128:
        return pl.BlockSpec((None, width, span), lambda b: (b, 0, 0))
    return pl.BlockSpec((width, span), lambda b: (0, b))


def turned_shape(images, width, span):
    return shaped((images, width, span) if span % 128 else (width, images * span), low)


def turned_whole(array):
    if array.ndim == 2:
        return array
    return jnp.swapaxes(array, 0, 1).reshape(array.shape[1], -1)


def mix_kernel(x_ref, vec_ref, wo_ref, fq_ref, num_ref, den_ref, prior_ref, mixed_ref, rden_ref, resid_ref, a_ref, at_ref):
    width = x_ref.shape[1]
    for pair in range(width // PAIR):
        lanes = slice(pair * PAIR, (pair + 1) * PAIR)
        folded = prior_ref[0, pair]
        matrix = jnp.concatenate(
            [unfold_state(folded[:HEAD_DIM]), unfold_total(folded[HEAD_DIM : HEAD_DIM + 1])], axis=0
        )
        high, rest = split_low(matrix)
        query = fq_ref[:, lanes]
        both = mt(jnp.concatenate([query, query], axis=1), jnp.concatenate([high, rest], axis=1))
        scale = 1.0 / (den_ref[:, lanes] + both[:, PAIR:])
        rden_ref[:, lanes] = scale
        mixed_ref[:, lanes] = ((num_ref[:, lanes] + both[:, :PAIR]) * scale).astype(low)
    resid = x_ref[...].astype(wide) + mm(mixed_ref[...], wo_ref[...])
    resid_ref[...] = resid
    unit, _ = normalised(resid)
    normed = (unit * vec_ref[2:3, :] + vec_ref[3:4, :]).astype(low)
    a_ref[...] = normed
    at_ref[...] = normed.T


def mix(x, vec, wo, fq, num, den, prior, images, span, tokens=()):
    rows_, width = x.shape
    rows = pl.BlockSpec((span, width), lambda b: (b, 0))
    return launch(
        mix_kernel,
        tokens,
        grid=(images,),
        in_specs=[
            rows,
            whole(vec.shape),
            whole(wo.shape),
            rows,
            rows,
            rows,
            pl.BlockSpec((1,) + prior.shape[1:], lambda b: (b, 0, 0, 0)),
        ],
        out_specs=[rows, rows, rows, rows, turned_block(width, span)],
        out_shape=[
            shaped((rows_, width), low),
            shaped((rows_, width), wide),
            shaped((rows_, width), wide),
            shaped((rows_, width), low),
            turned_shape(images, width, span),
        ],
        cost_estimate=cost(4 * rows_ * width * width, 24 * rows_ * width + 2 * width * width),
        name="mix",
    )(x, vec, wo, fq, num, den, prior)


gelu_scale = 0.7978845608028654
gelu_cubic = 0.044715


def feed_kernel(fresh, bits, spot_ref, *refs):
    a_ref, at_ref, e_ref, et_ref = refs[:4]
    out_ref, da_ref, kept_ref, sent_ref, joined_ref = refs[-5:]
    join(joined_ref, bits, spot_ref, *refs[4:8])

    @pl.when(pl.program_id(0) == 0)
    def _():
        if fresh:
            out_ref[...] = jnp.zeros_like(out_ref)
            da_ref[...] = jnp.zeros_like(da_ref)
        else:
            out_ref[...] = refs[8][...]
            da_ref[...] = refs[9][...]

    up, down = joined_ref[0], joined_ref[1]
    upper = mm(a_ref[...], up)
    grad = mm(e_ref[...], down)
    square = upper * upper
    bend = jnp.tanh(gelu_scale * upper * (1.0 + gelu_cubic * square))
    gate = 0.5 + 0.5 * bend
    hidden = (upper * gate).astype(low)
    slope = gate + 0.5 * upper * (1.0 - bend * bend) * (gelu_scale * (1.0 + 3.0 * gelu_cubic * square))
    dupper = (grad * slope).astype(low)
    out_ref[...] += mt(hidden, down)
    da_ref[...] += mt(dupper, up)
    to_up = mm(at_ref[...], dupper).astype(low)
    to_down = mm(et_ref[...], hidden).astype(low)
    first = spot_ref[0] == 0
    kept_ref[...] = jnp.where(first, to_up, to_down)
    sent_ref[...] = jnp.where(first, to_down, to_up)


def feed(pieces, a, at, e, et, carried, tokens=()):
    rows, width = a.shape
    slabs = pieces.arrays[0].shape[0]
    tiles = SLAB // TILE
    grads = pl.BlockSpec((width, TILE), lambda g, spot: (0, g))
    full = whole((rows, width))
    turned = whole((width, rows))
    fresh = carried is None
    return launch_at(
        functools.partial(feed_kernel, fresh, pieces.bits),
        pieces.spot,
        tokens,
        grid=(slabs * tiles,),
        in_specs=[full, turned, full, turned]
        + pieces.blocks(TILE, lambda g, spot: (g // tiles, 0, g % tiles))
        + ([] if fresh else [full, full]),
        out_specs=[full, full, grads, grads],
        out_shape=[shaped((rows, width), wide)] * 2 + [shaped((width, slabs * SLAB), low)] * 2,
        scratch_shapes=[pltpu.VMEM((2, width, TILE), low)],
        cost_estimate=cost(6 * rows * width * slabs * SLAB, 8 * width * slabs * SLAB + 20 * rows * width),
        name="feed",
    )(a, at, e, et, *pieces.arrays, *(() if fresh else carried))


def outer_kernel(core_ref, mixed_ref, branch_ref, kept_ref, sent_ref):
    product = tm(mixed_ref[...], branch_ref[...]).astype(low)
    half = product.shape[1] // 2
    first = core_ref[0] == 0
    kept_ref[...] = jnp.where(first, product[:, :half], product[:, half:])
    sent_ref[...] = jnp.where(first, product[:, half:], product[:, :half])


def outer(mixed, branch, tokens=()):
    rows, width = mixed.shape
    result = pl.BlockSpec((GROUP, width // 2), lambda g, core: (g, 0))
    return launch_at(
        outer_kernel,
        core_index(),
        tokens,
        grid=(width // GROUP,),
        in_specs=[pl.BlockSpec((rows, GROUP), lambda g, core: (0, g)), whole((rows, width))],
        out_specs=[result, result],
        out_shape=[shaped((width, width // 2), low)] * 2,
        cost_estimate=cost(rows * width * width, 4 * rows * width + 2 * width * width),
        name="outer",
    )(mixed, branch)


def turn_back_kernel(x_out_ref, da_ref, resid_ref, e_ref, vec_ref, wo_ref, mixed_ref, rden_ref, fq_ref,
                     out_ref, dres_ref, branch_ref, dn_ref, w_ref, state_ref, sums_ref):
    width = da_ref.shape[1]
    resid = resid_ref[...]
    out_ref[...] = (resid + x_out_ref[...]).astype(low)
    unit, scale = normalised(resid)
    da = da_ref[...]

    @pl.when(pl.program_id(0) == 0)
    def _():
        sums_ref[...] = jnp.zeros_like(sums_ref)

    sums_ref[0:1, :] += jnp.sum(da * unit, axis=0, keepdims=True)
    sums_ref[1:2, :] += jnp.sum(da, axis=0, keepdims=True)
    p = da * vec_ref[2:3, :]
    back = p - jnp.mean(p, axis=-1, keepdims=True) - unit * jnp.mean(p * unit, axis=-1, keepdims=True)
    dres = e_ref[...].astype(wide) + scale * back
    dres_ref[...] = dres
    branch = dres.astype(low)
    branch_ref[...] = branch
    dmixed = mt(branch, wo_ref[...]).astype(low).astype(wide)
    dnumer = dmixed * rden_ref[...]
    dn_ref[...] = dnumer.astype(low)
    w_ref[...] = (-dnumer * mixed_ref[...].astype(wide)).astype(low)
    for pair in range(width // PAIR):
        lanes = slice(pair * PAIR, (pair + 1) * PAIR)
        query = fq_ref[:, lanes]
        state_ref[0, pair, :HEAD_DIM, :] = fold_state(tm(dn_ref[:, lanes], query))
        total = jnp.sum(fold_state(tm(w_ref[:, lanes], query)), axis=0, keepdims=True)
        state_ref[0, pair, HEAD_DIM:, :] = jnp.broadcast_to(total, (STATE_ROWS - HEAD_DIM, PAIR))


def turn_back(x_out, da, resid, e, vec, wo, mixed, rden, fq, images, span, tokens=()):
    rows_, width = da.shape
    rows = pl.BlockSpec((span, width), lambda b: (b, 0))
    state = (images, width // PAIR, STATE_ROWS, PAIR)
    return launch(
        turn_back_kernel,
        tokens,
        grid=(images,),
        in_specs=[rows, rows, rows, rows, whole(vec.shape), whole(wo.shape), rows, rows, rows],
        out_specs=[rows] * 5 + [pl.BlockSpec((1,) + state[1:], lambda b: (b, 0, 0, 0)), whole((8, width))],
        out_shape=[
            shaped((rows_, width), low),
            shaped((rows_, width), wide),
            shaped((rows_, width), low),
            shaped((rows_, width), low),
            shaped((rows_, width), low),
            shaped(state, wide),
            shaped((8, width), wide),
        ],
        cost_estimate=cost(5 * rows_ * width * width, 30 * rows_ * width),
        name="turn_back",
    )(x_out, da, resid, e, vec, wo, mixed, rden, fq)


def attend_back_kernel(span, fq_ref, fk_ref, v_ref, dn_ref, w_ref, prior_ref, dq_ref, dfk_ref, dv_ref):
    own = first_head(span)
    own_twice = jnp.concatenate([own, own], axis=1)
    below, above = causal_mask(span, True), causal_mask(span, False)
    one = jnp.ones((span, PAIR), low)
    zero = jnp.zeros((span, PAIR), low)
    zero_twice = jnp.zeros((span, 2 * PAIR), low)
    for pair in range(GROUP // PAIR):
        lanes = slice(pair * PAIR, (pair + 1) * PAIR)
        query, key, value = fq_ref[:, lanes], fk_ref[:, lanes], v_ref[:, lanes]
        grads = jnp.concatenate([dn_ref[:, lanes], w_ref[:, lanes]], axis=1)
        extended = jnp.concatenate([value, one], axis=1)
        folded = prior_ref[0, pair]
        matrix = jnp.concatenate(
            [unfold_state(folded[:HEAD_DIM]), unfold_total(folded[HEAD_DIM : HEAD_DIM + 1])], axis=0
        )
        high, rest = split_low(matrix)
        dfq = mm(jnp.concatenate([grads, grads], axis=1), jnp.concatenate([high, rest], axis=0))
        to_query, to_key, to_value = [], [], []
        for mask, both in ((own, own_twice), (jnp.logical_not(own), jnp.logical_not(own_twice))):
            head_grads = jnp.where(both, grads, zero_twice)
            head_query = jnp.where(mask, query, zero)
            head_key = jnp.where(mask, key, zero)
            to_query.append((mt(head_grads, extended).astype(low) * below, head_key))
            to_key.append((mt(extended, head_grads).astype(low) * above, head_query))
            to_value.append((mt(head_key, query).astype(low) * above, head_grads[:, :PAIR]))
        dfq = dfq + pair_mm(*to_query)
        dq_ref[:, lanes] = (dfq * jnp.minimum(query.astype(wide), 1.0)).astype(low)
        dfk_ref[:, lanes] = pair_mm(*to_key)
        dv_ref[:, lanes] = pair_mm(*to_value)


def attend_back(image, fq, fk, v, dn, w, prior, span, tokens=()):
    width = fq.shape[1]
    block = pl.BlockSpec((span, GROUP), lambda p: (image, p))
    column = pl.BlockSpec((span, GROUP), lambda p: (0, p))
    return launch(
        functools.partial(attend_back_kernel, span),
        tokens,
        grid=(width // GROUP,),
        in_specs=[block] * 5 + [pl.BlockSpec((1, GROUP // PAIR) + prior.shape[2:], lambda p: (image, p, 0, 0))],
        out_specs=[column] * 3,
        out_shape=[shaped((span, width), low), shaped((span, width), wide), shaped((span, width), wide)],
        cost_estimate=cost(32 * span * span * width, 24 * span * width),
        name="attend_back",
    )(fq, fk, v, dn, w, prior)


def finish_kernel(images, span, core_ref, *refs):
    locals_ = [refs[3 * image : 3 * image + 3] for image in range(images)]
    fk_ref, v_ref, later_ref, at_ref, dq_ref, dk_ref, dv_ref, kept_ref, sent_ref = refs[3 * images :]
    keeps = pl.program_id(0) == core_ref[0]
    for image in range(images):
        rows = slice(image * span, (image + 1) * span)
        dqi_ref, dfk_ref, dvl_ref = locals_[image]
        dq_ref[rows, :] = dqi_ref[...]
        for pair in range(GROUP // PAIR):
            lanes = slice(pair * PAIR, (pair + 1) * PAIR)
            folded = later_ref[image, pair]
            high, rest = split_low(unfold_state(folded[:HEAD_DIM]))
            key, value = fk_ref[rows, lanes], v_ref[rows, lanes]
            dfk = dfk_ref[:, lanes] + folded[HEAD_DIM : HEAD_DIM + 1]
            dfk = dfk + mm(jnp.concatenate([value, value], axis=1), jnp.concatenate([high, rest], axis=0))
            dv = dvl_ref[:, lanes] + mt(
                jnp.concatenate([key, key], axis=1), jnp.concatenate([high, rest], axis=1)
            )
            dk_ref[rows, lanes] = (dfk * jnp.minimum(key.astype(wide), 1.0)).astype(low)
            dv_ref[rows, lanes] = dv.astype(low)
    for k, ref in enumerate((dq_ref, dk_ref, dv_ref)):
        product = mm(at_ref[...], ref[...]).astype(low)

        @pl.when(keeps)
        def _():
            kept_ref[k] = product

        @pl.when(jnp.logical_not(keeps))
        def _():
            sent_ref[k] = product


def finish(side, parts, fk, v, later, at, images, span, tokens=()):
    rows, width = fk.shape
    half = width // 2
    columns = half // 2
    column = pl.BlockSpec((rows, columns), lambda g, core: (0, side * 2 + g))
    part = pl.BlockSpec((span, columns), lambda g, core: (0, side * 2 + g))
    result = pl.BlockSpec((rows, columns), lambda g, core: (0, g))
    grads = whole((3, width, columns))
    state = pl.BlockSpec((images, columns // PAIR) + later.shape[2:], lambda g, core: (0, side * 2 + g, 0, 0))
    return launch_at(
        functools.partial(finish_kernel, images, span),
        core_index(),
        tokens,
        grid=(2,),
        in_specs=[part] * (3 * images) + [column] * 2 + [state, whole(at.shape)],
        out_specs=[result] * 3 + [grads, grads],
        out_shape=[shaped((rows, half), low)] * 3 + [shaped((3, width, columns), low)] * 2,
        cost_estimate=cost(2 * rows * width * width, 15 * rows * width),
        name="finish",
    )(*[array for image in parts for array in image], fk, v, later, at)


def enter_kernel(*refs):
    lefts, rights, weights = refs[:3], refs[3:6], refs[6:9]
    x_ref, dres_ref, vec_ref, grad_ref, sums_ref = refs[9:]
    half = x_ref.shape[1] // 2
    da = None
    for left, right, weight in zip(lefts, rights, weights):
        part = mt(left[...], weight[:, :half]) + mt(right[...], weight[:, half:])
        da = part if da is None else da + part
    unit, scale = normalised(x_ref[...].astype(wide))
    sums_ref[0:1, :] = jnp.sum(da * unit, axis=0, keepdims=True)
    sums_ref[1:2, :] = jnp.sum(da, axis=0, keepdims=True)
    sums_ref[2:, :] = jnp.zeros_like(sums_ref[2:, :])
    p = da * vec_ref[0:1, :]
    back = p - jnp.mean(p, axis=-1, keepdims=True) - unit * jnp.mean(p * unit, axis=-1, keepdims=True)
    grad_ref[...] = (dres_ref[...] + scale * back).astype(low)


def enter(image, left, right, weights, x, dres, vec, span, tokens=()):
    width = x.shape[1]
    rows = pl.BlockSpec((span, width), lambda g: (image, 0))
    part = pl.BlockSpec((span, width // 2), lambda g: (image, 0))
    return launch(
        enter_kernel,
        tokens,
        grid=(1,),
        in_specs=[part] * 6 + [whole((width, width))] * 3 + [rows, rows, whole(vec.shape)],
        out_specs=[whole((span, width)), whole((8, width))],
        out_shape=[shaped((span, width), low), shaped((8, width), wide)],
        cost_estimate=cost(3 * span * width * width, 14 * span * width + 6 * width * width),
        name="enter",
    )(*left, *right, *weights, x, dres, vec)


def adam_update(master, moment, second, average, gradient, factor, rate):
    clipped = gradient * factor
    moment = beta_first * moment + (1.0 - beta_first) * clipped
    second = beta_second * second + (1.0 - beta_second) * clipped * clipped
    first_hat = moment / (1.0 - beta_first**STEP)
    second_hat = second / (1.0 - beta_second**STEP)
    master = master - rate * (first_hat / (jnp.sqrt(second_hat) + eps_adam) + weight_decay * master)
    average = average_decay * average + (1.0 - average_decay) * master
    return (master, moment, second, average)


def powers(count):
    return [1 << k for k in range(count.bit_length() - 1)]


def core_index():
    return lax.axis_index("seq") % 2


def pos_index():
    return lax.axis_index("seq") // 2


def pos_bits():
    return (lax.axis_size("seq") // 2).bit_length() - 1


def flip(array, axis, bit):
    return lax.ppermute(array, axis, [(i, i ^ bit) for i in range(lax.axis_size(axis))])


def flip_core(array):
    return flip(array, "seq", 1)


def flip_pos(array, stage):
    bits = pos_bits()
    pairs = [(i, i ^ (2 << (stage if i % 2 == 0 else bits - 1 - stage))) for i in range(lax.axis_size("seq"))]
    return lax.ppermute(array, "seq", pairs)


def own_bit(stage):
    bits = pos_bits()
    return jnp.where(core_index() == 0, pos_index() >> stage, pos_index() >> (bits - 1 - stage)) & 1


def halves(shape, dim):
    index = np.arange(int(np.prod(shape))).reshape(shape)
    return np.stack([index.take(side, axis=dim).ravel() for side in range(2)])


def fold_kernel(chains, spot_ref, *refs):
    ins, outs = refs[: 4 * chains], refs[4 * chains :]
    for k in range(2 * chains):
        value = ins[2 * k][...].astype(wide) + ins[2 * k + 1][...].astype(wide)
        outs[k][...] = value.astype(outs[k].dtype)


def fold(cuts, tokens=()):
    count = cuts[0][2].shape[0]
    steps = max(1, min(2, min(kept.shape[-1] for kept, *_ in cuts) // 256))
    in_specs, out_specs, out_shape, arrays, moved = [], [], [], [], 0
    for k, (kept, came, keeps, sends) in enumerate(cuts):
        lead, _, rows, columns = kept.shape
        block = (lead, 1, rows, columns // steps)
        for side in range(2):
            at = 2 * k * count + side * count
            spec = pl.BlockSpec(block, lambda g, c, spot, at=at: (0, spot[at + g], 0, c))
            in_specs += [spec, spec]
            arrays += [kept, came]
            out_specs.append(pl.BlockSpec(block, lambda g, c, spot: (0, g, 0, c)))
            out_shape.append(shaped((lead, count, rows, columns), low if side or kept.dtype == low else wide))
        moved += 8 * kept.size
    results = launch_at(
        functools.partial(fold_kernel, len(cuts)),
        jnp.concatenate([part for _, _, keeps, sends in cuts for part in (keeps, sends)]),
        tokens,
        grid=(count, steps),
        in_specs=in_specs,
        out_specs=out_specs,
        out_shape=out_shape,
        cost_estimate=cost(1, moved),
        name="fold",
    )(*arrays)
    return [results[2 * k : 2 * k + 2] for k in range(len(cuts))]


class Chain:
    def __init__(self, kept, sent):
        self.lead = kept.shape[0] if kept.ndim == 3 else 1
        self.stage = -1
        self.left = [list(range(pos_bits()))[::-1]] * 2
        shape = (self.lead, 2 ** pos_bits(), -1, kept.shape[-1])
        self.kept, self.sends = kept.reshape(shape), [sent.reshape(shape)]

    def start(self):
        if self.stage < 0:
            self.came = [flip_core(self.sends[0])]
        else:
            self.came = [flip_pos(self.sends[0], self.stage)]

    def cut(self):
        self.stage += 1
        tables = []
        for kind in range(2):
            bit = self.stage if kind == 0 else pos_bits() - 1 - self.stage
            left = self.left[kind]
            tables.append(halves((2,) * len(left), left.index(bit)))
            self.left[kind] = [other for other in left if other != bit]
        table = jnp.where(core_index() == 0, *[jnp.asarray(part, jnp.int32) for part in tables])
        own = own_bit(self.stage)
        return (self.kept, self.came[0], table[own], table[1 - own])

    def take(self, parts):
        self.kept, self.sends = parts[0], [parts[1]]


def advance(chains, tokens=()):
    parts = fold([chain.cut() for chain in chains], tokens)
    for chain, part in zip(chains, parts):
        chain.take(part)
        chain.start()
    return [array for chain in chains for array in chain.sends]


def last_kernel(ways, pre, pieces, spot_ref, *refs):
    ins, outs = refs[: 2 * pieces], refs[2 * pieces :]
    at = 0
    for k in range(pieces):
        columns = ins[2 * k].shape[-1]
        for j in range(ways):
            place = spot_ref[0] ^ j
            for n in range(pre):
                value = ins[2 * k][n, place].astype(wide) + ins[2 * k + 1][n, place].astype(wide)
                outs[j][n, :, at : at + columns] = value.astype(outs[j].dtype)
        at += columns


class Last:
    def __init__(self, chains, tokens=(), slowly=False):
        slices = lax.axis_size("img")
        ways = 2 if slowly else slices
        self.lead = chains[0].lead
        pre = self.lead * 2 * slices // ways
        arrays = []
        for chain in chains:
            for array in (chain.kept, chain.came[0]):
                arrays.append(array.reshape(pre, ways, -1, array.shape[-1]))
        self.widths = [array.shape[-1] for array in arrays[::2]]
        inside = pl.BlockSpec(memory_space=pltpu.VMEM)
        parts = launch(
            functools.partial(last_kernel, ways, pre, len(chains)),
            tokens,
            in_specs=[pl.BlockSpec(memory_space=pltpu.SMEM)] + [inside] * len(arrays),
            out_specs=[inside] * ways,
            out_shape=[shaped((pre, arrays[0].shape[2], sum(self.widths)), low if j else wide) for j in range(ways)],
            cost_estimate=cost(1, 4 * sum(array.size for array in arrays)),
                name="last",
        )((lax.axis_index("img") % ways).reshape(1), *arrays)
        self.kept, self.sends = parts[0], list(parts[1:])
        self.hops = list(range(1, ways))
        self.left = powers(slices)[1:][::-1] if slowly else []
        self.start()

    def start(self):
        self.came = [flip(array, "img", hop) for array, hop in zip(self.sends, self.hops)]

    def cut(self):
        bit = self.left[-1]
        entries = self.kept.reshape((1, -1) + self.kept.shape[-2:])
        dims = (2 * self.lead,) + (2,) * len(self.left)
        table = jnp.asarray(halves(dims, len(dims) - 1), jnp.int32)
        own = (lax.axis_index("img") // bit) % 2
        self.left = self.left[:-1]
        self.hops = [bit]
        return (entries, self.came[0].reshape(entries.shape), table[own], table[1 - own])

    def take(self, parts):
        self.kept, self.sends = parts[0][0], [parts[1][0]]

    def total(self, tokens=()):
        while self.left:
            advance([self])
        total = self.kept
        for came in gate(self.came, tokens) if tokens else self.came:
            total = total + came.astype(wide)
        return total

    def squares(self, tokens=()):
        self.sums = self.total(tokens)
        return jnp.sum(self.sums * self.sums)

    def finish(self):
        core = core_index()
        total = self.sums.reshape((self.lead, 2) + self.sums.shape[-2:])
        own = lax.dynamic_index_in_dim(total, core, 1, False)
        came = flip_core(lax.dynamic_index_in_dim(total, 1 - core, 1, False))
        first, second = jnp.where(core == 0, own, came), jnp.where(core == 0, came, own)
        at, found = 0, []
        for columns in self.widths:
            found.append((first[..., at : at + columns], second[..., at : at + columns]))
            at += columns
        return found


def sum_slowly(array):
    for axis in ("seq", "img"):
        for bit in powers(lax.axis_size(axis)):
            array = array + flip(array, axis, bit)
    return array


def sum_all(array):
    rounds = [("img", range(1, lax.axis_size("img"))), ("seq", range(2, lax.axis_size("seq"), 2)), ("seq", [1])]
    for axis, hops in rounds:
        came = [flip(array, axis, hop) for hop in hops]
        for other in came:
            array = array + other
    return array


def assemble_kernel(plan, spot_ref, *refs):
    outs = sorted({out for _, _, out, _ in plan})
    count = len(refs) - 1 - len(outs)
    sems = refs[-1]
    copies = []
    for k, (piece, cut, out, where) in enumerate(plan):
        source = refs[piece].at[cut] if cut is not None else refs[piece]
        target = refs[count + out].at[where(spot_ref)]
        copies.append(pltpu.make_async_copy(source, target, sems.at[k]))
    for copy in copies:
        copy.start()
    for copy in copies:
        copy.wait()


def assemble(plan, spots, pieces, shapes, tokens=()):
    anywhere = pl.BlockSpec(memory_space=pl.ANY)
    return launch(
        functools.partial(assemble_kernel, plan),
        tokens,
        in_specs=[pl.BlockSpec(memory_space=pltpu.SMEM)] + [anywhere] * len(pieces),
        out_specs=[pl.BlockSpec(memory_space=pltpu.VMEM)] * len(shapes),
        out_shape=[shaped(shape, low) for shape in shapes],
        scratch_shapes=[pltpu.SemaphoreType.DMA((len(plan),))],
        cost_estimate=cost(1, 2 * sum(2 * piece.size for piece in pieces)),
        name="assemble",
    )(jnp.stack(spots).astype(jnp.int32), *pieces)


def gate_kernel(*refs):
    pass


def gate(arrays, tokens):
    anywhere = pl.BlockSpec(memory_space=pl.ANY)
    return launch(
        gate_kernel,
        tokens,
        in_specs=[anywhere] * len(arrays),
        out_specs=[anywhere] * len(arrays),
        out_shape=[shaped(array.shape, array.dtype) for array in arrays],
        input_output_aliases={k: k for k in range(len(arrays))},
        cost_estimate=cost(1, 1),
        name="gate",
    )(*arrays)


class Gather:
    def __init__(self, own, other):
        self.own, self.other = own, other
        self.stage = 0

    def start_slices(self, hops=False):
        came = flip_core(self.other)
        pairs = [jnp.stack([self.own, came], axis=1), jnp.stack([came, self.own], axis=1)]
        self.pieces = [jnp.where(core_index() == 0, *pairs)]
        for j in range(1, lax.axis_size("img")):
            bit = j & -j if hops else j
            self.pieces.append(flip(self.pieces[j - bit], "img", bit))

    def finish_slices(self, tokens=()):
        slices = len(self.pieces)
        every = slice(None)
        plan = [(j, None, 0, lambda spot, j=j: (every, every, spot[0] ^ j)) for j in range(slices)]
        k, _, rows, columns = self.pieces[0].shape
        shape = (k, 2, slices, rows, columns)
        self.part = assemble(plan, [lax.axis_index("img")], self.pieces, [shape], tokens)[0]
        self.part = self.part.reshape(k, 1, 2 * slices * rows, columns)
        return [self.part]

    def start_pos(self):
        self.came = flip_pos(self.part, self.stage)
        self.stage += 1

    def finish_pos(self, tokens=()):
        every = slice(None)
        plan = [
            (0, None, 0, lambda spot: (every, spot[0])),
            (1, None, 0, lambda spot: (every, 1 - spot[0])),
        ]
        shape = self.part.shape[:1] + (2,) + self.part.shape[1:]
        self.part = assemble(plan, [own_bit(self.stage - 1)], [self.part, self.came], [shape], tokens)[0]
        self.part = self.part.reshape((shape[0], -1) + shape[3:])
        return [self.part]

    def start_last(self):
        self.start_pos()

    def finish_last(self, tokens=()):
        if tokens:
            (self.came,) = gate([self.came], tokens)
        return Pieces([self.part, self.came, flip_core(self.part), flip_core(self.came)])


def narrow_kernel(plans, core_ref, *refs):
    own_ref, other_ref = refs[-2:]
    first = core_ref[0] == 0
    for k, ((ref, member, columns), (ref_b, member_b, columns_b)) in enumerate(zip(*plans)):
        left = refs[ref][member, :, columns].astype(low)
        right = refs[ref_b][member_b, :, columns_b].astype(low)
        own_ref[k] = jnp.where(first, left, right)
        other_ref[k] = jnp.where(first, right, left)


def narrow(plans, weights, tokens=()):
    owned = weights[0].shape[1]
    inside = pl.BlockSpec(memory_space=pltpu.VMEM)
    return Gather(
        *launch(
            functools.partial(narrow_kernel, plans),
            tokens,
            in_specs=[pl.BlockSpec(memory_space=pltpu.SMEM)] + [inside] * len(weights),
            out_specs=[inside, inside],
            out_shape=[shaped((len(plans[0]), owned, SLAB), low)] * 2,
            cost_estimate=cost(1, 12 * len(plans[0]) * owned * SLAB),
                name="narrow",
        )(core_index().reshape(1), *weights)
    )


class Passing:
    def __init__(self, own, backward):
        self.backward = backward
        came = flip_core(own.astype(low)).astype(wide)
        self.outside = jnp.where(core_index() == (0 if backward else 1), came, 0.0)
        both = (own + came).astype(low)
        self.came = [flip(both, "seq", 2 * j) for j in range(1, lax.axis_size("seq") // 2)]

    def finish(self, tokens):
        total = self.outside
        for j, came in enumerate(gate(self.came, tokens), 1):
            earlier = (pos_index() ^ j) < pos_index()
            total = total + jnp.where(earlier != self.backward, came.astype(wide), 0.0)
        return total


def body(
    images,
    cotangent,
    attention_weight,
    feedforward_weight,
    norm_vectors,
    attention_moment,
    feedforward_moment,
    norm_moment,
    attention_second,
    feedforward_second,
    norm_second,
    attention_average,
    feedforward_average,
    norm_average,
):
    count, span, width = images.shape
    tokens = count * span
    owned = attention_weight.shape[1]
    slabs = feedforward_weight.shape[2] // SLAB
    weights = (attention_weight, feedforward_weight)
    stages = pos_bits()
    half = slabs // 2
    every = slice(None)

    def feed_group(first, marks=()):
        plans = [[(1, kind, slice((first + n) * SLAB, (first + n + 1) * SLAB)) for n in range(half)] for kind in range(2)]
        return narrow(plans, weights, marks)

    def inner_stages(group, marks):
        for _ in range(stages - 1):
            group.start_pos()
            marks = group.finish_pos(marks)
        return marks

    x, e = images.reshape(tokens, width), cotangent.reshape(tokens, width)
    keys = jnp.pad(attention_weight[1].astype(low), ((0, 0), (0, 128)))
    vectors = jnp.pad(norm_vectors.astype(low).T, ((0, 0), (0, 124)))
    values = jnp.concatenate([attention_weight[2].astype(low), vectors], axis=1)
    first_core = core_index() == 0
    one = Gather(jnp.where(first_core, keys, values)[None], jnp.where(first_core, values, keys)[None])
    one.start_slices(True)
    two = narrow([[(0, 0, every)], [(0, 3, every)]], weights, [one.other])
    two.start_slices()
    et = turn(e, count, span)
    marks = one.finish_slices([et])
    for _ in range(stages - 1):
        one.start_pos()
        marks = one.finish_pos(marks)
    one.start_last()
    marks = two.finish_slices(marks)
    three = feed_group(0, marks)
    three.start_slices()
    marks = inner_stages(two, marks)
    two.start_last()
    inner_pieces = one.finish_last()
    vec = inner_pieces.second(slice(width, width + 4)).astype(wide).T
    marks = three.finish_slices(marks)
    four = feed_group(half, marks)
    four.start_slices()
    fk, v, a1, a1t, state, wk, wv = project(x, vec, inner_pieces, count, span, marks + [four.pieces[0]])
    prior = Passing(state, False)
    marks = [prior.outside]
    outer_pieces = two.finish_last()
    marks = inner_stages(three, marks)
    three.start_last()
    fq, wq, wo = query(a1, outer_pieces, marks)
    marks = four.finish_slices([fq])
    num, den = attend(fq, fk, v, count, span, marks)
    prior = prior.finish([num])
    mixed, rden, resid, a2, a2t = mix(x, vec, wo, fq, num, den, prior, count, span)
    a2t = turned_whole(a2t)
    first_pieces = three.finish_last()
    marks = inner_stages(four, [resid])
    four.start_last()

    early = feed(first_pieces, a2, a2t, e, et, None, marks)
    firsts = [Chain(*early[2:])]
    firsts[0].start()
    second_pieces = four.finish_last([early[0]])
    late = feed(second_pieces, a2, a2t, e, et, early[:2])
    seconds = [Chain(*late[2:])]
    seconds[0].start()
    marks = advance(firsts)
    output, dres, branch, dn, w, dstate, sums_second = turn_back(
        late[0], late[1], resid, e, vec, wo, mixed, rden, fq, count, span, marks
    )
    later = Passing(dstate, True)
    outs = [Chain(*outer(mixed, branch, [dstate]))]
    outs[0].start()
    marks = [later.outside] + advance(seconds)
    for _ in range(stages - 1):
        marks = marks + advance(firsts)
    parts = [attend_back(0, fq, fk, v, dn, w, prior, span, marks)]
    marks = advance(outs, [parts[0][0]])
    firsts_last = Last(firsts, [parts[0][0]])
    marks = marks + list(firsts_last.sends)
    for _ in range(stages - 1):
        marks = marks + advance(seconds, [parts[0][0]])
    for image in range(1, count):
        parts.append(attend_back(image, fq, fk, v, dn, w, prior, span, marks))
    later = later.finish([parts[0][0]])
    for _ in range(stages - 1):
        marks = advance(outs, [parts[-1][0]])
    marks = marks + seconds[0].came
    left = finish(0, parts, fk, v, later, a1t, count, span, marks)
    inner = [Chain(*left[3:])]
    inner[0].start()
    local_squares = firsts_last.squares([left[0]])
    seconds_last = Last(seconds + outs, [left[0]])
    marks = seconds_last.sends + [firsts_last.sums]
    right = finish(1, parts, fk, v, later, a1t, count, span, marks)
    inner.append(Chain(*right[3:]))
    inner[1].start()
    marks = advance(inner[:1], [right[0]])
    grads_in = []
    for image in range(count):
        grads_in.append(enter(image, left[:3], right[:3], (wq, wk, wv), x, dres, vec, span, marks))
        if image == 0:
            local_squares = local_squares + seconds_last.squares([grads_in[0][1]])
            marks = advance(inner[1:], [grads_in[0][1]]) + [seconds_last.sums] + inner[0].came
    input_grad = jnp.stack([part[0] for part in grads_in])
    for _ in range(stages - 1):
        marks = advance(inner)
    (sums,) = gate([sum(part[1] for part in grads_in)], marks)
    vector_grad = sum_slowly(jnp.concatenate([sums[:2], sums_second[:2]], axis=0))
    device = lax.axis_index("seq") * lax.axis_size("img") + lax.axis_index("img")
    vector_shard = lax.dynamic_slice_in_dim(vector_grad, device * owned, owned, 1)
    inner_last = Last(inner, [seconds_last.sums])
    local_squares = local_squares + jnp.sum(vector_shard * vector_shard)
    local_squares = local_squares + inner_last.squares()
    grad_norm = jnp.sqrt(sum_all(jnp.full((8, 128), local_squares))[0, 0])
    (early_shard,) = firsts_last.finish()
    late_shard, out_shard = seconds_last.finish()
    inner_shard = jnp.concatenate([part for pair in inner_last.finish() for part in pair], axis=2)
    attn_shard = jnp.concatenate([inner_shard, jnp.concatenate(out_shard, axis=2)], axis=0)
    feed_shard = jnp.concatenate([jnp.concatenate(pair, axis=2) for pair in zip(early_shard, late_shard)], axis=0)
    factor = clip_bound / jnp.maximum(grad_norm, clip_bound)
    attn_new = adam_update(
        attention_weight, attention_moment, attention_second, attention_average, attn_shard, factor, learn_rate
    )
    feed_new = adam_update(
        feedforward_weight, feedforward_moment, feedforward_second, feedforward_average, feed_shard, factor, learn_rate
    )
    norm_new = adam_update(norm_vectors, norm_moment, norm_second, norm_average, vector_shard, factor, norm_rate)
    output = output.reshape(images.shape)
    input_grad = input_grad.reshape(images.shape)
    return (output, input_grad, grad_norm) + attn_new + feed_new + norm_new


def solution(mesh):
    tokens = P("img", "seq", None)
    rows = P(None, ("seq", "img"), None)
    vectors = P(None, ("seq", "img"))
    group = (rows, rows, vectors)
    return jax.shard_map(
        body,
        mesh=mesh,
        in_specs=(tokens, tokens) + group * 4,
        out_specs=(tokens, tokens, P()) + (rows,) * 8 + (vectors,) * 4,
        check_vma=False,
    )
```

```python
import functools

import jax
import jax.numpy as jnp
import numpy as np
from jax import lax
from jax.experimental import pallas as pl
from jax.experimental.pallas import tpu as pltpu
from jax.sharding import PartitionSpec as P

HEADS = 16
HEAD_DIM = 64
STEP = 10

beta_first = 0.9
beta_second = 0.95
learn_rate = 0.02
norm_rate = 0.2
weight_decay = 0.1
average_decay = 0.75
clip_bound = 1.0
eps_norm = 1e-05
eps_adam = 1e-08

PAIR = 2 * HEAD_DIM
STATE_ROWS = HEAD_DIM + 16
SLAB = 1024
TILE = 512
GROUP = 256

low = jnp.bfloat16
wide = jnp.float32


def params(megabytes=56):
    return pltpu.CompilerParams(vmem_limit_bytes=megabytes * 1024 * 1024)


def cost(products, elements):
    return pl.CostEstimate(flops=2 * products, bytes_accessed=elements, transcendentals=0)


def launch(kernel, tokens, in_specs, megabytes=56, **keys):
    known, extra = len(in_specs), len(tokens)

    def run(*refs):
        kernel(*refs[:known], *refs[known + extra :])

    call = pl.pallas_call(
        run, in_specs=list(in_specs) + [pl.BlockSpec(memory_space=pl.ANY)] * extra, compiler_params=params(megabytes), **keys
    )
    return lambda *args: call(*args, *tokens)


def launch_at(kernel, spot, tokens, grid, in_specs, out_specs, megabytes=56, scratch_shapes=(), **keys):
    known, extra = len(in_specs), len(tokens)

    def run(spot_ref, *refs):
        kernel(spot_ref, *refs[:known], *refs[known + extra :])

    call = pl.pallas_call(
        run,
        grid_spec=pltpu.PrefetchScalarGridSpec(
            num_scalar_prefetch=1,
            grid=grid,
            in_specs=list(in_specs) + [pl.BlockSpec(memory_space=pl.ANY)] * extra,
            out_specs=out_specs,
            scratch_shapes=scratch_shapes,
        ),
        compiler_params=params(megabytes),
        **keys,
    )
    return lambda *args: call(spot.reshape(-1).astype(jnp.int32), *args, *tokens)


def reversed_bits(value, count):
    return sum(((value >> k) & 1) << (count - 1 - k) for k in range(count))


def join(target_ref, bits, spot_ref, own_ref, came_ref, own_other_ref, came_other_ref):
    core, high, lowest = spot_ref[0], spot_ref[1], spot_ref[2]
    runs = 1 << (bits - 1)
    rows = target_ref.shape[1] // (2 * runs)
    for run in range(runs):
        source = slice(run * rows, (run + 1) * rows)
        turned = reversed_bits(run, bits)
        for place in range(2):
            first = (high ^ place) * runs + run
            second = turned + (lowest ^ place)
            for ref, slot in (((own_ref, came_ref)[place], core), ((own_other_ref, came_other_ref)[place], 1 - core)):
                at = jnp.where(slot == 0, first, second)
                target_ref[slot, pl.ds(pl.multiple_of(at * rows, rows), rows), :] = ref[source, :]


class Pieces:
    def __init__(self, arrays):
        self.arrays = [array.reshape(array.shape[0], -1, array.shape[-1]) for array in arrays]
        place = pos_index()
        self.bits = pos_bits()
        self.spot = jnp.stack([core_index(), place >> (self.bits - 1), place & 1])

    def blocks(self, columns, place):
        rows = self.arrays[0].shape[1]
        return [pl.BlockSpec((None, rows, columns), place)] * 4

    def second(self, columns):
        mine, others = (
            [part[0, :, columns].reshape(1 << (self.bits - 1), 1, -1, columns.stop - columns.start) for part in pair]
            for pair in (self.arrays[:2], self.arrays[2:])
        )
        own, came = (jnp.where(core_index() == 1, left, right) for left, right in zip(mine, others))
        straight, turned = jnp.concatenate([own, came], axis=1), jnp.concatenate([came, own], axis=1)
        runs = jnp.where(self.spot[2] == 0, straight, turned)
        order = [reversed_bits(run, self.bits - 1) for run in range(1 << (self.bits - 1))]
        return jnp.stack([runs[run] for run in order]).reshape(-1, columns.stop - columns.start)


def shaped(shape, kind):
    return jax.ShapeDtypeStruct(shape, kind)


def whole(shape):
    return pl.BlockSpec(shape, lambda *_: (0,) * len(shape))


def mm(left, right):
    return lax.dot_general(left, right, (((1,), (0,)), ((), ())), preferred_element_type=wide)


def mt(left, right):
    return lax.dot_general(left, right, (((1,), (1,)), ((), ())), preferred_element_type=wide)


def tm(left, right):
    return lax.dot_general(left, right, (((0,), (0,)), ((), ())), preferred_element_type=wide)


def pair_mm(first, second):
    if first[0].shape[1] % 128:
        return mm(*first) + mm(*second)
    return mm(jnp.concatenate([first[0], second[0]], axis=1), jnp.concatenate([first[1], second[1]], axis=0))


def causal_mask(span, below):
    rows = lax.broadcasted_iota(jnp.int32, (span, span), 0)
    columns = lax.broadcasted_iota(jnp.int32, (span, span), 1)
    return (rows >= columns if below else rows <= columns).astype(wide).astype(low)


def first_head(rows):
    return lax.broadcasted_iota(jnp.int32, (rows, PAIR), 1) < HEAD_DIM


def fold_state(product):
    return jnp.where(first_head(HEAD_DIM), product[:HEAD_DIM], product[HEAD_DIM:])


def unfold_state(folded):
    own = first_head(HEAD_DIM)
    zero = jnp.zeros_like(folded)
    return jnp.concatenate([jnp.where(own, folded, zero), jnp.where(own, zero, folded)], axis=0)


def unfold_total(row):
    tall = jnp.broadcast_to(row, (PAIR, PAIR))
    lanes = lax.broadcasted_iota(jnp.int32, (PAIR, PAIR), 1) < HEAD_DIM
    rows = lax.broadcasted_iota(jnp.int32, (PAIR, PAIR), 0) < HEAD_DIM
    return jnp.where(lanes == rows, tall, jnp.zeros_like(tall))


def split_low(values):
    high = values.astype(low)
    return high, (values - high.astype(wide)).astype(low)


def normalised(values):
    centre = jnp.mean(values, axis=-1, keepdims=True)
    centred = values - centre
    spread = jnp.mean(centred * centred, axis=-1, keepdims=True)
    scale = lax.rsqrt(spread + eps_norm)
    return centred * scale, scale


def feature(raw):
    return jnp.where(raw > 0, raw + 1.0, jnp.exp(jnp.minimum(raw, 0.0))).astype(low)


def project_kernel(images, span, bits, spot_ref, x_ref, vec_ref, *refs):
    fk_ref, v_ref, a_ref, at_ref, state_ref, wk_ref, wv_ref, joined_ref = refs[4:]

    @pl.when(pl.program_id(0) == 0)
    def _():
        gain, shift = vec_ref[0:1, :], vec_ref[1:2, :]
        step = span // 3
        for start in range(0, images * span, step):
            rows = slice(start, start + step)
            unit, _ = normalised(x_ref[rows, :].astype(wide))
            a_ref[rows, :] = (unit * gain + shift).astype(low)
        at_ref[...] = a_ref[...].T

    join(joined_ref, bits, spot_ref, *refs[:4])
    keys, values = joined_ref[0], joined_ref[1]
    wk_ref[...] = keys
    wv_ref[...] = values
    fk_ref[...] = feature(mm(a_ref[...], keys))
    v_ref[...] = mm(a_ref[...], values).astype(low)
    ones = jnp.ones((16, span), low)
    for image in range(images):
        rows = slice(image * span, (image + 1) * span)
        for pair in range(GROUP // PAIR):
            lanes = slice(pair * PAIR, (pair + 1) * PAIR)
            key, value = fk_ref[rows, lanes], v_ref[rows, lanes]
            state_ref[image, pair, :HEAD_DIM, :] = fold_state(tm(value, key))
            state_ref[image, pair, HEAD_DIM:, :] = mm(ones, key)


def project(x, vec, pieces, images, span, tokens=()):
    count, width = x.shape
    pairs = GROUP // PAIR
    column = pl.BlockSpec((count, GROUP), lambda g, spot: (0, g))
    weight = pl.BlockSpec((width, GROUP), lambda g, spot: (0, g))
    return launch_at(
        functools.partial(project_kernel, images, span, pieces.bits),
        pieces.spot,
        tokens,
        grid=(width // GROUP,),
        in_specs=[whole((count, width)), whole(vec.shape)] + pieces.blocks(GROUP, lambda g, spot: (0, 0, g)),
        out_specs=[
            column,
            column,
            whole((count, width)),
            whole((width, count)),
            pl.BlockSpec((images, pairs, STATE_ROWS, PAIR), lambda g, spot: (0, g, 0, 0)),
            weight,
            weight,
        ],
        out_shape=[
            shaped((count, width), low),
            shaped((count, width), low),
            shaped((count, width), low),
            shaped((width, count), low),
            shaped((images, width // PAIR, STATE_ROWS, PAIR), wide),
            shaped((width, width), low),
            shaped((width, width), low),
        ],
        scratch_shapes=[pltpu.VMEM((2, width, GROUP), low)],
        cost_estimate=cost(2 * count * width * width, 8 * width * width + 12 * count * width),
        name="project",
    )(x, vec, *pieces.arrays)


def query_kernel(bits, spot_ref, a_ref, *refs):
    fq_ref, wq_ref, wo_ref, joined_ref = refs[4:]
    join(joined_ref, bits, spot_ref, *refs[:4])
    wq_ref[...] = joined_ref[0]
    wo_ref[...] = joined_ref[1]
    fq_ref[...] = feature(mm(a_ref[...], joined_ref[0]))


def query(a, pieces, tokens=()):
    count, width = a.shape
    weight = pl.BlockSpec((width, GROUP), lambda g, spot: (0, g))
    return launch_at(
        functools.partial(query_kernel, pieces.bits),
        pieces.spot,
        tokens,
        grid=(width // GROUP,),
        in_specs=[whole((count, width))] + pieces.blocks(GROUP, lambda g, spot: (1, 0, g)),
        out_specs=[pl.BlockSpec((count, GROUP), lambda g, spot: (0, g)), weight, weight],
        out_shape=[shaped((count, width), low)] + [shaped((width, width), low)] * 2,
        scratch_shapes=[pltpu.VMEM((2, width, GROUP), low)],
        cost_estimate=cost(count * width * width, 6 * width * width + 4 * count * width),
        name="query",
    )(a, *pieces.arrays)


def turn_kernel(x_ref, out_ref):
    out_ref[...] = x_ref[...].T


def turn(x, images, span, tokens=()):
    count, width = x.shape
    return turned_whole(
        launch(
            turn_kernel,
            tokens,
            grid=(images,),
            in_specs=[pl.BlockSpec((span, width), lambda b: (b, 0))],
            out_specs=turned_block(width, span),
            out_shape=turned_shape(images, width, span),
            cost_estimate=cost(1, 4 * count * width),
                name="turn",
        )(x)
    )


def attend_kernel(span, fq_ref, fk_ref, v_ref, num_ref, den_ref):
    own = first_head(span)
    causal = causal_mask(span, True)
    one = jnp.ones((span, PAIR), low)
    zero = jnp.zeros((span, PAIR), low)
    for pair in range(GROUP // PAIR):
        lanes = slice(pair * PAIR, (pair + 1) * PAIR)
        query, key, value = fq_ref[:, lanes], fk_ref[:, lanes], v_ref[:, lanes]
        products = []
        for mask in (own, jnp.logical_not(own)):
            scores = mt(jnp.where(mask, query, zero), key).astype(low) * causal
            right = jnp.concatenate([jnp.where(mask, value, zero), jnp.where(mask, one, zero)], axis=1)
            products.append((scores, right))
        total = pair_mm(*products)
        num_ref[:, lanes] = total[:, :PAIR]
        den_ref[:, lanes] = total[:, PAIR:]


def attend(fq, fk, v, images, span, tokens=()):
    rows, width = fq.shape
    block = pl.BlockSpec((span, GROUP), lambda b, p: (b, p))
    return launch(
        functools.partial(attend_kernel, span),
        tokens,
        grid=(images, width // GROUP),
        in_specs=[block] * 3,
        out_specs=[block] * 2,
        out_shape=[shaped((rows, width), wide)] * 2,
        cost_estimate=cost(16 * rows * span * width, 14 * rows * width),
        name="attend",
    )(fq, fk, v)


def turned_block(width, span):
    if span % 128:
        return pl.BlockSpec((None, width, span), lambda b: (b, 0, 0))
    return pl.BlockSpec((width, span), lambda b: (0, b))


def turned_shape(images, width, span):
    return shaped((images, width, span) if span % 128 else (width, images * span), low)


def turned_whole(array):
    if array.ndim == 2:
        return array
    return jnp.swapaxes(array, 0, 1).reshape(array.shape[1], -1)


def mix_kernel(x_ref, vec_ref, wo_ref, fq_ref, num_ref, den_ref, prior_ref, mixed_ref, rden_ref, resid_ref, a_ref, at_ref):
    width = x_ref.shape[1]
    for pair in range(width // PAIR):
        lanes = slice(pair * PAIR, (pair + 1) * PAIR)
        folded = prior_ref[0, pair]
        matrix = jnp.concatenate(
            [unfold_state(folded[:HEAD_DIM]), unfold_total(folded[HEAD_DIM : HEAD_DIM + 1])], axis=0
        )
        high, rest = split_low(matrix)
        query = fq_ref[:, lanes]
        both = mt(jnp.concatenate([query, query], axis=1), jnp.concatenate([high, rest], axis=1))
        scale = 1.0 / (den_ref[:, lanes] + both[:, PAIR:])
        rden_ref[:, lanes] = scale
        mixed_ref[:, lanes] = ((num_ref[:, lanes] + both[:, :PAIR]) * scale).astype(low)
    resid = x_ref[...].astype(wide) + mm(mixed_ref[...], wo_ref[...])
    resid_ref[...] = resid
    unit, _ = normalised(resid)
    normed = (unit * vec_ref[2:3, :] + vec_ref[3:4, :]).astype(low)
    a_ref[...] = normed
    at_ref[...] = normed.T


def mix(x, vec, wo, fq, num, den, prior, images, span, tokens=()):
    rows_, width = x.shape
    rows = pl.BlockSpec((span, width), lambda b: (b, 0))
    return launch(
        mix_kernel,
        tokens,
        grid=(images,),
        in_specs=[
            rows,
            whole(vec.shape),
            whole(wo.shape),
            rows,
            rows,
            rows,
            pl.BlockSpec((1,) + prior.shape[1:], lambda b: (b, 0, 0, 0)),
        ],
        out_specs=[rows, rows, rows, rows, turned_block(width, span)],
        out_shape=[
            shaped((rows_, width), low),
            shaped((rows_, width), wide),
            shaped((rows_, width), wide),
            shaped((rows_, width), low),
            turned_shape(images, width, span),
        ],
        cost_estimate=cost(4 * rows_ * width * width, 24 * rows_ * width + 2 * width * width),
        name="mix",
    )(x, vec, wo, fq, num, den, prior)


gelu_scale = 0.7978845608028654
gelu_cubic = 0.044715


def feed_kernel(fresh, bits, spot_ref, *refs):
    a_ref, at_ref, e_ref, et_ref = refs[:4]
    out_ref, da_ref, kept_ref, sent_ref, joined_ref = refs[-5:]
    join(joined_ref, bits, spot_ref, *refs[4:8])

    @pl.when(pl.program_id(0) == 0)
    def _():
        if fresh:
            out_ref[...] = jnp.zeros_like(out_ref)
            da_ref[...] = jnp.zeros_like(da_ref)
        else:
            out_ref[...] = refs[8][...]
            da_ref[...] = refs[9][...]

    up, down = joined_ref[0], joined_ref[1]
    upper = mm(a_ref[...], up)
    grad = mm(e_ref[...], down)
    square = upper * upper
    bend = jnp.tanh(gelu_scale * upper * (1.0 + gelu_cubic * square))
    gate = 0.5 + 0.5 * bend
    hidden = (upper * gate).astype(low)
    slope = gate + 0.5 * upper * (1.0 - bend * bend) * (gelu_scale * (1.0 + 3.0 * gelu_cubic * square))
    dupper = (grad * slope).astype(low)
    out_ref[...] += mt(hidden, down)
    da_ref[...] += mt(dupper, up)
    to_up = mm(at_ref[...], dupper).astype(low)
    to_down = mm(et_ref[...], hidden).astype(low)
    first = spot_ref[0] == 0
    kept_ref[...] = jnp.where(first, to_up, to_down)
    sent_ref[...] = jnp.where(first, to_down, to_up)


def feed(pieces, a, at, e, et, carried, tokens=()):
    rows, width = a.shape
    slabs = pieces.arrays[0].shape[0]
    tiles = SLAB // TILE
    grads = pl.BlockSpec((width, TILE), lambda g, spot: (0, g))
    full = whole((rows, width))
    turned = whole((width, rows))
    fresh = carried is None
    return launch_at(
        functools.partial(feed_kernel, fresh, pieces.bits),
        pieces.spot,
        tokens,
        grid=(slabs * tiles,),
        in_specs=[full, turned, full, turned]
        + pieces.blocks(TILE, lambda g, spot: (g // tiles, 0, g % tiles))
        + ([] if fresh else [full, full]),
        out_specs=[full, full, grads, grads],
        out_shape=[shaped((rows, width), wide)] * 2 + [shaped((width, slabs * SLAB), low)] * 2,
        scratch_shapes=[pltpu.VMEM((2, width, TILE), low)],
        cost_estimate=cost(6 * rows * width * slabs * SLAB, 8 * width * slabs * SLAB + 20 * rows * width),
        name="feed",
    )(a, at, e, et, *pieces.arrays, *(() if fresh else carried))


def outer_kernel(core_ref, mixed_ref, branch_ref, kept_ref, sent_ref):
    product = tm(mixed_ref[...], branch_ref[...]).astype(low)
    half = product.shape[1] // 2
    first = core_ref[0] == 0
    kept_ref[...] = jnp.where(first, product[:, :half], product[:, half:])
    sent_ref[...] = jnp.where(first, product[:, half:], product[:, :half])


def outer(mixed, branch, tokens=()):
    rows, width = mixed.shape
    result = pl.BlockSpec((GROUP, width // 2), lambda g, core: (g, 0))
    return launch_at(
        outer_kernel,
        core_index(),
        tokens,
        grid=(width // GROUP,),
        in_specs=[pl.BlockSpec((rows, GROUP), lambda g, core: (0, g)), whole((rows, width))],
        out_specs=[result, result],
        out_shape=[shaped((width, width // 2), low)] * 2,
        cost_estimate=cost(rows * width * width, 4 * rows * width + 2 * width * width),
        name="outer",
    )(mixed, branch)


def turn_back_kernel(x_out_ref, da_ref, resid_ref, e_ref, vec_ref, wo_ref, mixed_ref, rden_ref, fq_ref,
                     out_ref, dres_ref, branch_ref, dn_ref, w_ref, state_ref, sums_ref):
    width = da_ref.shape[1]
    resid = resid_ref[...]
    out_ref[...] = (resid + x_out_ref[...]).astype(low)
    unit, scale = normalised(resid)
    da = da_ref[...]

    @pl.when(pl.program_id(0) == 0)
    def _():
        sums_ref[...] = jnp.zeros_like(sums_ref)

    sums_ref[0:1, :] += jnp.sum(da * unit, axis=0, keepdims=True)
    sums_ref[1:2, :] += jnp.sum(da, axis=0, keepdims=True)
    p = da * vec_ref[2:3, :]
    back = p - jnp.mean(p, axis=-1, keepdims=True) - unit * jnp.mean(p * unit, axis=-1, keepdims=True)
    dres = e_ref[...].astype(wide) + scale * back
    dres_ref[...] = dres
    branch = dres.astype(low)
    branch_ref[...] = branch
    dmixed = mt(branch, wo_ref[...]).astype(low).astype(wide)
    dnumer = dmixed * rden_ref[...]
    dn_ref[...] = dnumer.astype(low)
    w_ref[...] = (-dnumer * mixed_ref[...].astype(wide)).astype(low)
    for pair in range(width // PAIR):
        lanes = slice(pair * PAIR, (pair + 1) * PAIR)
        query = fq_ref[:, lanes]
        state_ref[0, pair, :HEAD_DIM, :] = fold_state(tm(dn_ref[:, lanes], query))
        total = jnp.sum(fold_state(tm(w_ref[:, lanes], query)), axis=0, keepdims=True)
        state_ref[0, pair, HEAD_DIM:, :] = jnp.broadcast_to(total, (STATE_ROWS - HEAD_DIM, PAIR))


def turn_back(x_out, da, resid, e, vec, wo, mixed, rden, fq, images, span, tokens=()):
    rows_, width = da.shape
    rows = pl.BlockSpec((span, width), lambda b: (b, 0))
    state = (images, width // PAIR, STATE_ROWS, PAIR)
    return launch(
        turn_back_kernel,
        tokens,
        grid=(images,),
        in_specs=[rows, rows, rows, rows, whole(vec.shape), whole(wo.shape), rows, rows, rows],
        out_specs=[rows] * 5 + [pl.BlockSpec((1,) + state[1:], lambda b: (b, 0, 0, 0)), whole((8, width))],
        out_shape=[
            shaped((rows_, width), low),
            shaped((rows_, width), wide),
            shaped((rows_, width), low),
            shaped((rows_, width), low),
            shaped((rows_, width), low),
            shaped(state, wide),
            shaped((8, width), wide),
        ],
        cost_estimate=cost(5 * rows_ * width * width, 30 * rows_ * width),
        name="turn_back",
    )(x_out, da, resid, e, vec, wo, mixed, rden, fq)


def attend_back_kernel(span, fq_ref, fk_ref, v_ref, dn_ref, w_ref, prior_ref, dq_ref, dfk_ref, dv_ref):
    own = first_head(span)
    own_twice = jnp.concatenate([own, own], axis=1)
    below, above = causal_mask(span, True), causal_mask(span, False)
    one = jnp.ones((span, PAIR), low)
    zero = jnp.zeros((span, PAIR), low)
    zero_twice = jnp.zeros((span, 2 * PAIR), low)
    for pair in range(GROUP // PAIR):
        lanes = slice(pair * PAIR, (pair + 1) * PAIR)
        query, key, value = fq_ref[:, lanes], fk_ref[:, lanes], v_ref[:, lanes]
        grads = jnp.concatenate([dn_ref[:, lanes], w_ref[:, lanes]], axis=1)
        extended = jnp.concatenate([value, one], axis=1)
        folded = prior_ref[0, pair]
        matrix = jnp.concatenate(
            [unfold_state(folded[:HEAD_DIM]), unfold_total(folded[HEAD_DIM : HEAD_DIM + 1])], axis=0
        )
        high, rest = split_low(matrix)
        dfq = mm(jnp.concatenate([grads, grads], axis=1), jnp.concatenate([high, rest], axis=0))
        to_query, to_key, to_value = [], [], []
        for mask, both in ((own, own_twice), (jnp.logical_not(own), jnp.logical_not(own_twice))):
            head_grads = jnp.where(both, grads, zero_twice)
            head_query = jnp.where(mask, query, zero)
            head_key = jnp.where(mask, key, zero)
            to_query.append((mt(head_grads, extended).astype(low) * below, head_key))
            to_key.append((mt(extended, head_grads).astype(low) * above, head_query))
            to_value.append((mt(head_key, query).astype(low) * above, head_grads[:, :PAIR]))
        dfq = dfq + pair_mm(*to_query)
        dq_ref[:, lanes] = (dfq * jnp.minimum(query.astype(wide), 1.0)).astype(low)
        dfk_ref[:, lanes] = pair_mm(*to_key)
        dv_ref[:, lanes] = pair_mm(*to_value)


def attend_back(image, fq, fk, v, dn, w, prior, span, tokens=()):
    width = fq.shape[1]
    block = pl.BlockSpec((span, GROUP), lambda p: (image, p))
    column = pl.BlockSpec((span, GROUP), lambda p: (0, p))
    return launch(
        functools.partial(attend_back_kernel, span),
        tokens,
        grid=(width // GROUP,),
        in_specs=[block] * 5 + [pl.BlockSpec((1, GROUP // PAIR) + prior.shape[2:], lambda p: (image, p, 0, 0))],
        out_specs=[column] * 3,
        out_shape=[shaped((span, width), low), shaped((span, width), wide), shaped((span, width), wide)],
        cost_estimate=cost(32 * span * span * width, 24 * span * width),
        name="attend_back",
    )(fq, fk, v, dn, w, prior)


def finish_kernel(images, span, core_ref, *refs):
    locals_ = [refs[3 * image : 3 * image + 3] for image in range(images)]
    fk_ref, v_ref, later_ref, at_ref, dq_ref, dk_ref, dv_ref, kept_ref, sent_ref = refs[3 * images :]
    keeps = pl.program_id(0) == core_ref[0]
    for image in range(images):
        rows = slice(image * span, (image + 1) * span)
        dqi_ref, dfk_ref, dvl_ref = locals_[image]
        dq_ref[rows, :] = dqi_ref[...]
        for pair in range(GROUP // PAIR):
            lanes = slice(pair * PAIR, (pair + 1) * PAIR)
            folded = later_ref[image, pair]
            high, rest = split_low(unfold_state(folded[:HEAD_DIM]))
            key, value = fk_ref[rows, lanes], v_ref[rows, lanes]
            dfk = dfk_ref[:, lanes] + folded[HEAD_DIM : HEAD_DIM + 1]
            dfk = dfk + mm(jnp.concatenate([value, value], axis=1), jnp.concatenate([high, rest], axis=0))
            dv = dvl_ref[:, lanes] + mt(
                jnp.concatenate([key, key], axis=1), jnp.concatenate([high, rest], axis=1)
            )
            dk_ref[rows, lanes] = (dfk * jnp.minimum(key.astype(wide), 1.0)).astype(low)
            dv_ref[rows, lanes] = dv.astype(low)
    grads = (dq_ref, dk_ref, dv_ref)

    @pl.when(keeps)
    def _():
        for k, ref in enumerate(grads):
            kept_ref[k] = mm(at_ref[...], ref[...]).astype(low)

    @pl.when(jnp.logical_not(keeps))
    def _():
        for k, ref in enumerate(grads):
            sent_ref[k] = mm(at_ref[...], ref[...]).astype(low)


def finish(side, parts, fk, v, later, at, images, span, tokens=()):
    rows, width = fk.shape
    half = width // 2
    columns = half // 2
    column = pl.BlockSpec((rows, columns), lambda g, core: (0, side * 2 + g))
    part = pl.BlockSpec((span, columns), lambda g, core: (0, side * 2 + g))
    result = pl.BlockSpec((rows, columns), lambda g, core: (0, g))
    grads = whole((3, width, columns))
    state = pl.BlockSpec((images, columns // PAIR) + later.shape[2:], lambda g, core: (0, side * 2 + g, 0, 0))
    return launch_at(
        functools.partial(finish_kernel, images, span),
        core_index(),
        tokens,
        grid=(2,),
        in_specs=[part] * (3 * images) + [column] * 2 + [state, whole(at.shape)],
        out_specs=[result] * 3 + [grads, grads],
        out_shape=[shaped((rows, half), low)] * 3 + [shaped((3, width, columns), low)] * 2,
        cost_estimate=cost(2 * rows * width * width, 15 * rows * width),
        name="finish",
    )(*[array for image in parts for array in image], fk, v, later, at)


def enter_kernel(*refs):
    lefts, rights, weights = refs[:3], refs[3:6], refs[6:9]
    x_ref, dres_ref, vec_ref, grad_ref, sums_ref = refs[9:]
    half = x_ref.shape[1] // 2
    da = None
    for left, right, weight in zip(lefts, rights, weights):
        part = mt(left[...], weight[:, :half]) + mt(right[...], weight[:, half:])
        da = part if da is None else da + part
    unit, scale = normalised(x_ref[...].astype(wide))
    sums_ref[0:1, :] = jnp.sum(da * unit, axis=0, keepdims=True)
    sums_ref[1:2, :] = jnp.sum(da, axis=0, keepdims=True)
    sums_ref[2:, :] = jnp.zeros_like(sums_ref[2:, :])
    p = da * vec_ref[0:1, :]
    back = p - jnp.mean(p, axis=-1, keepdims=True) - unit * jnp.mean(p * unit, axis=-1, keepdims=True)
    grad_ref[...] = (dres_ref[...] + scale * back).astype(low)


def enter(image, left, right, weights, x, dres, vec, span, tokens=()):
    width = x.shape[1]
    rows = pl.BlockSpec((span, width), lambda g: (image, 0))
    part = pl.BlockSpec((span, width // 2), lambda g: (image, 0))
    return launch(
        enter_kernel,
        tokens,
        grid=(1,),
        in_specs=[part] * 6 + [whole((width, width))] * 3 + [rows, rows, whole(vec.shape)],
        out_specs=[whole((span, width)), whole((8, width))],
        out_shape=[shaped((span, width), low), shaped((8, width), wide)],
        cost_estimate=cost(3 * span * width * width, 14 * span * width + 6 * width * width),
        name="enter",
    )(*left, *right, *weights, x, dres, vec)


def adam_update(master, moment, second, average, gradient, factor, rate):
    clipped = gradient * factor
    moment = beta_first * moment + (1.0 - beta_first) * clipped
    second = beta_second * second + (1.0 - beta_second) * clipped * clipped
    first_hat = moment / (1.0 - beta_first**STEP)
    second_hat = second / (1.0 - beta_second**STEP)
    master = master - rate * (first_hat / (jnp.sqrt(second_hat) + eps_adam) + weight_decay * master)
    average = average_decay * average + (1.0 - average_decay) * master
    return (master, moment, second, average)


def powers(count):
    return [1 << k for k in range(count.bit_length() - 1)]


def core_index():
    return lax.axis_index("seq") % 2


def pos_index():
    return lax.axis_index("seq") // 2


def pos_bits():
    return (lax.axis_size("seq") // 2).bit_length() - 1


def flip(array, axis, bit):
    return lax.ppermute(array, axis, [(i, i ^ bit) for i in range(lax.axis_size(axis))])


def flip_core(array):
    return flip(array, "seq", 1)


def flip_pos(array, stage):
    bits = pos_bits()
    pairs = [(i, i ^ (2 << (stage if i % 2 == 0 else bits - 1 - stage))) for i in range(lax.axis_size("seq"))]
    return lax.ppermute(array, "seq", pairs)


def own_bit(stage):
    bits = pos_bits()
    return jnp.where(core_index() == 0, pos_index() >> stage, pos_index() >> (bits - 1 - stage)) & 1


def halves(shape, dim):
    index = np.arange(int(np.prod(shape))).reshape(shape)
    return np.stack([index.take(side, axis=dim).ravel() for side in range(2)])


def fold_kernel(chains, spot_ref, *refs):
    ins, outs = refs[: 4 * chains], refs[4 * chains :]
    for k in range(2 * chains):
        value = ins[2 * k][...].astype(wide) + ins[2 * k + 1][...].astype(wide)
        outs[k][...] = value.astype(outs[k].dtype)


def fold(cuts, tokens=()):
    count = cuts[0][2].shape[0]
    steps = max(1, min(2, min(kept.shape[-1] for kept, *_ in cuts) // 256))
    in_specs, out_specs, out_shape, arrays, moved = [], [], [], [], 0
    for k, (kept, came, keeps, sends) in enumerate(cuts):
        lead, _, rows, columns = kept.shape
        block = (lead, 1, rows, columns // steps)
        for side in range(2):
            at = 2 * k * count + side * count
            spec = pl.BlockSpec(block, lambda g, c, spot, at=at: (0, spot[at + g], 0, c))
            in_specs += [spec, spec]
            arrays += [kept, came]
            out_specs.append(pl.BlockSpec(block, lambda g, c, spot: (0, g, 0, c)))
            out_shape.append(shaped((lead, count, rows, columns), low if side or kept.dtype == low else wide))
        moved += 8 * kept.size
    results = launch_at(
        functools.partial(fold_kernel, len(cuts)),
        jnp.concatenate([part for _, _, keeps, sends in cuts for part in (keeps, sends)]),
        tokens,
        grid=(count, steps),
        in_specs=in_specs,
        out_specs=out_specs,
        out_shape=out_shape,
        cost_estimate=cost(1, moved),
        name="fold",
    )(*arrays)
    return [results[2 * k : 2 * k + 2] for k in range(len(cuts))]


class Chain:
    def __init__(self, kept, sent):
        self.lead = kept.shape[0] if kept.ndim == 3 else 1
        self.stage = -1
        self.left = [list(range(pos_bits()))[::-1]] * 2
        shape = (self.lead, 2 ** pos_bits(), -1, kept.shape[-1])
        self.kept, self.sends = kept.reshape(shape), [sent.reshape(shape)]

    def start(self):
        if self.stage < 0:
            self.came = [flip_core(self.sends[0])]
        else:
            self.came = [flip_pos(self.sends[0], self.stage)]

    def cut(self):
        self.stage += 1
        tables = []
        for kind in range(2):
            bit = self.stage if kind == 0 else pos_bits() - 1 - self.stage
            left = self.left[kind]
            tables.append(halves((2,) * len(left), left.index(bit)))
            self.left[kind] = [other for other in left if other != bit]
        table = jnp.where(core_index() == 0, *[jnp.asarray(part, jnp.int32) for part in tables])
        own = own_bit(self.stage)
        return (self.kept, self.came[0], table[own], table[1 - own])

    def take(self, parts):
        self.kept, self.sends = parts[0], [parts[1]]


def advance(chains, tokens=()):
    parts = fold([chain.cut() for chain in chains], tokens)
    for chain, part in zip(chains, parts):
        chain.take(part)
        chain.start()
    return [array for chain in chains for array in chain.sends]


def last_kernel(ways, pre, pieces, spot_ref, *refs):
    ins, outs = refs[: 2 * pieces], refs[2 * pieces :]
    at = 0
    for k in range(pieces):
        columns = ins[2 * k].shape[-1]
        for j in range(ways):
            place = spot_ref[0] ^ j
            for n in range(pre):
                value = ins[2 * k][n, place].astype(wide) + ins[2 * k + 1][n, place].astype(wide)
                outs[j][n, :, at : at + columns] = value.astype(outs[j].dtype)
        at += columns


class Last:
    def __init__(self, chains, tokens=(), slowly=False):
        slices = lax.axis_size("img")
        ways = 2 if slowly else slices
        self.lead = chains[0].lead
        pre = self.lead * 2 * slices // ways
        arrays = []
        for chain in chains:
            for array in (chain.kept, chain.came[0]):
                arrays.append(array.reshape(pre, ways, -1, array.shape[-1]))
        self.widths = [array.shape[-1] for array in arrays[::2]]
        inside = pl.BlockSpec(memory_space=pltpu.VMEM)
        parts = launch(
            functools.partial(last_kernel, ways, pre, len(chains)),
            tokens,
            in_specs=[pl.BlockSpec(memory_space=pltpu.SMEM)] + [inside] * len(arrays),
            out_specs=[inside] * ways,
            out_shape=[shaped((pre, arrays[0].shape[2], sum(self.widths)), low if j else wide) for j in range(ways)],
            cost_estimate=cost(1, 4 * sum(array.size for array in arrays)),
                name="last",
        )((lax.axis_index("img") % ways).reshape(1), *arrays)
        self.kept, self.sends = parts[0], list(parts[1:])
        self.hops = list(range(1, ways))
        self.left = powers(slices)[1:][::-1] if slowly else []
        self.start()

    def start(self):
        self.came = [flip(array, "img", hop) for array, hop in zip(self.sends, self.hops)]

    def cut(self):
        bit = self.left[-1]
        entries = self.kept.reshape((1, -1) + self.kept.shape[-2:])
        dims = (2 * self.lead,) + (2,) * len(self.left)
        table = jnp.asarray(halves(dims, len(dims) - 1), jnp.int32)
        own = (lax.axis_index("img") // bit) % 2
        self.left = self.left[:-1]
        self.hops = [bit]
        return (entries, self.came[0].reshape(entries.shape), table[own], table[1 - own])

    def take(self, parts):
        self.kept, self.sends = parts[0][0], [parts[1][0]]

    def total(self, tokens=()):
        while self.left:
            advance([self])
        total = self.kept
        for came in gate(self.came, tokens) if tokens else self.came:
            total = total + came.astype(wide)
        return total

    def squares(self, tokens=()):
        self.sums = self.total(tokens)
        return jnp.sum(self.sums * self.sums)

    def finish(self):
        core = core_index()
        total = self.sums.reshape((self.lead, 2) + self.sums.shape[-2:])
        own = lax.dynamic_index_in_dim(total, core, 1, False)
        came = flip_core(lax.dynamic_index_in_dim(total, 1 - core, 1, False))
        first, second = jnp.where(core == 0, own, came), jnp.where(core == 0, came, own)
        at, found = 0, []
        for columns in self.widths:
            found.append((first[..., at : at + columns], second[..., at : at + columns]))
            at += columns
        return found


def sum_slowly(array):
    for axis in ("seq", "img"):
        for bit in powers(lax.axis_size(axis)):
            array = array + flip(array, axis, bit)
    return array


def sum_all(array):
    rounds = [("img", range(1, lax.axis_size("img"))), ("seq", range(2, lax.axis_size("seq"), 2)), ("seq", [1])]
    for axis, hops in rounds:
        came = [flip(array, axis, hop) for hop in hops]
        for other in came:
            array = array + other
    return array


def assemble_kernel(plan, spot_ref, *refs):
    outs = sorted({out for _, _, out, _ in plan})
    count = len(refs) - 1 - len(outs)
    sems = refs[-1]
    copies = []
    for k, (piece, cut, out, where) in enumerate(plan):
        source = refs[piece].at[cut] if cut is not None else refs[piece]
        target = refs[count + out].at[where(spot_ref)]
        copies.append(pltpu.make_async_copy(source, target, sems.at[k]))
    for copy in copies:
        copy.start()
    for copy in copies:
        copy.wait()


def assemble(plan, spots, pieces, shapes, tokens=()):
    anywhere = pl.BlockSpec(memory_space=pl.ANY)
    return launch(
        functools.partial(assemble_kernel, plan),
        tokens,
        in_specs=[pl.BlockSpec(memory_space=pltpu.SMEM)] + [anywhere] * len(pieces),
        out_specs=[pl.BlockSpec(memory_space=pltpu.VMEM)] * len(shapes),
        out_shape=[shaped(shape, low) for shape in shapes],
        scratch_shapes=[pltpu.SemaphoreType.DMA((len(plan),))],
        cost_estimate=cost(1, 2 * sum(2 * piece.size for piece in pieces)),
        name="assemble",
    )(jnp.stack(spots).astype(jnp.int32), *pieces)


def gate_kernel(*refs):
    pass


def gate(arrays, tokens):
    anywhere = pl.BlockSpec(memory_space=pl.ANY)
    return launch(
        gate_kernel,
        tokens,
        in_specs=[anywhere] * len(arrays),
        out_specs=[anywhere] * len(arrays),
        out_shape=[shaped(array.shape, array.dtype) for array in arrays],
        input_output_aliases={k: k for k in range(len(arrays))},
        cost_estimate=cost(1, 1),
        name="gate",
    )(*arrays)


class Gather:
    def __init__(self, own, other):
        self.own, self.other = own, other
        self.stage = 0

    def pair(self):
        came = flip_core(self.other)
        pairs = [jnp.stack([self.own, came], axis=1), jnp.stack([came, self.own], axis=1)]
        return jnp.where(core_index() == 0, *pairs)

    @staticmethod
    def exchange(both, tokens=()):
        if tokens:
            (both,) = gate([both], tokens)
        own, other = jnp.split(both, 2)
        every = slice(None)
        plan = [(0, None, 0, lambda spot: (every, spot[0])), (1, None, 0, lambda spot: (every, 1 - spot[0]))]
        k, rows, columns = own.shape
        found = Gather(None, None)
        found.part = assemble(plan, [core_index()], [own, flip_core(other)], [(k, 2, rows, columns)])[0]
        found.part = found.part.reshape(k, 1, 2 * rows, columns)
        return found

    def start_slices(self, hops=False):
        self.pieces = [self.pair()]
        for j in range(1, lax.axis_size("img")):
            bit = j & -j if hops else j
            self.pieces.append(flip(self.pieces[j - bit], "img", bit))

    def finish_slices(self, tokens=(), groups=1):
        slices = len(self.pieces)
        if tokens:
            self.pieces = self.pieces[:1] + list(gate(self.pieces[1:], tokens))
        every = slice(None)
        k, _, rows, columns = self.pieces[0].shape
        k = k // groups
        plan = [
            (j, slice(n * k, (n + 1) * k), n, lambda spot, j=j: (every, every, spot[0] ^ j))
            for n in range(groups)
            for j in range(slices)
        ]
        shape = (k, 2, slices, rows, columns)
        parts = assemble(plan, [lax.axis_index("img")], self.pieces, [shape] * groups)
        found = []
        for part in parts:
            found.append(Gather(None, None))
            found[-1].part = part.reshape(k, 1, 2 * slices * rows, columns)
        return found

    def start_pos(self, tokens=()):
        if tokens:
            (self.part,) = gate([self.part], tokens)
        self.came = flip_pos(self.part, self.stage)
        self.stage += 1

    def finish_pos(self, tokens=()):
        every = slice(None)
        if tokens:
            (self.came,) = gate([self.came], tokens)
        plan = [
            (0, None, 0, lambda spot: (every, spot[0])),
            (1, None, 0, lambda spot: (every, 1 - spot[0])),
        ]
        shape = self.part.shape[:1] + (2,) + self.part.shape[1:]
        self.part = assemble(plan, [own_bit(self.stage - 1)], [self.part, self.came], [shape])[0]
        self.part = self.part.reshape((shape[0], -1) + shape[3:])
        return [self.part]

    def start_last(self):
        self.start_pos()
        self.turned = flip_core(self.part)

    def finish_last(self, tokens, turned_tokens):
        (self.turned,) = gate([self.turned], turned_tokens)
        (self.came,) = gate([self.came], tokens)
        return Pieces([self.part, self.came, self.turned, flip_core(self.came)])


def narrow_kernel(core_ref, weight_ref, *out_refs):
    first = core_ref[0] == 0
    slabs = out_refs[0].shape[0] // 2
    for k, out_ref in enumerate(out_refs):
        for n in range(slabs):
            columns = slice((k * slabs + n) * SLAB, (k * slabs + n + 1) * SLAB)
            left, right = weight_ref[0, :, columns].astype(low), weight_ref[1, :, columns].astype(low)
            out_ref[n] = jnp.where(first, left, right)
            out_ref[slabs + n] = jnp.where(first, right, left)


def narrow(weight, groups, tokens):
    _, owned, hidden = weight.shape
    slabs = hidden // SLAB // groups
    inside = pl.BlockSpec(memory_space=pltpu.VMEM)
    return launch(
        narrow_kernel,
        tokens,
        in_specs=[pl.BlockSpec(memory_space=pltpu.SMEM), inside],
        out_specs=[inside] * groups,
        out_shape=[shaped((2 * slabs, owned, SLAB), low)] * groups,
        cost_estimate=cost(1, 12 * slabs * groups * owned * SLAB),
        name="narrow",
    )(core_index().reshape(1), weight)


class Passing:
    def __init__(self, own, backward):
        self.backward = backward
        came = flip_core(own.astype(low)).astype(wide)
        self.outside = jnp.where(core_index() == (0 if backward else 1), came, 0.0)
        both = (own + came).astype(low)
        self.came = [flip(both, "seq", 2 * j) for j in range(1, lax.axis_size("seq") // 2)]

    def finish(self, tokens):
        total = self.outside
        for j, came in enumerate(gate(self.came, tokens), 1):
            earlier = (pos_index() ^ j) < pos_index()
            total = total + jnp.where(earlier != self.backward, came.astype(wide), 0.0)
        return total


def body(
    images,
    cotangent,
    attention_weight,
    feedforward_weight,
    norm_vectors,
    attention_moment,
    feedforward_moment,
    norm_moment,
    attention_second,
    feedforward_second,
    norm_second,
    attention_average,
    feedforward_average,
    norm_average,
):
    count, span, width = images.shape
    tokens = count * span
    owned = attention_weight.shape[1]
    slabs = feedforward_weight.shape[2] // SLAB
    stages = pos_bits()
    half = slabs // 2
    every = slice(None)

    x, e = images.reshape(tokens, width), cotangent.reshape(tokens, width)
    low_weights = jnp.pad(attention_weight.astype(low), ((0, 0), (0, 0), (0, 128)))
    vectors = jnp.pad(norm_vectors.astype(low).T, ((0, 0), (width, 124)))
    query_weight, key_weight, value_weight, out_weight = low_weights
    kinds = jnp.stack([key_weight, query_weight]), jnp.stack([value_weight + vectors, out_weight])
    first_core = core_index() == 0
    one = Gather(jnp.where(first_core, *kinds), jnp.where(first_core, *kinds[::-1]))
    one.start_slices(True)
    et = turn(e, count, span)
    (one,) = one.finish_slices([et])
    one.start_pos()
    feeds = narrow(feedforward_weight, 2, [one.part])
    marks = [feeds[0]]
    feeds = [lax.all_gather(part, "img", axis=1, tiled=True) for part in feeds]
    for _ in range(stages - 2):
        one.finish_pos(marks)
        one.start_pos()
    one.finish_pos(marks)
    one.start_last()
    pieces = one.finish_last([one.part], [one.part])
    two = Gather.exchange(feeds[0])
    two.start_pos([one.came])
    vec = pieces.second(slice(width, width + 4)).astype(wide).T
    fk, v, a1, a1t, state, wk, wv = project(x, vec, pieces, count, span, [two.part])
    prior = Passing(state, False)
    for _ in range(stages - 2):
        two.finish_pos([state])
        two.start_pos()
    two.finish_pos([state])
    two.start_last()
    fq, wq, wo = query(a1, pieces, [prior.outside, two.part])
    num, den = attend(fq, fk, v, count, span, [two.turned])
    prior = prior.finish([num])
    first_pieces = two.finish_last([num], [fq])
    three = Gather.exchange(feeds[1], [num])
    three.start_pos()
    mixed, rden, resid, a2, a2t = mix(x, vec, wo, fq, num, den, prior, count, span)
    a2t = turned_whole(a2t)
    marks = [resid]
    for _ in range(stages - 2):
        three.finish_pos(marks)
        three.start_pos()
    three.finish_pos(marks)
    three.start_last()
    marks = [three.part]

    early = feed(first_pieces, a2, a2t, e, et, None, marks)
    firsts = [Chain(*early[2:])]
    firsts[0].start()
    second_pieces = three.finish_last([early[0]], [early[0]])
    late = feed(second_pieces, a2, a2t, e, et, early[:2])
    seconds = [Chain(*late[2:])]
    seconds[0].start()
    marks = advance(firsts)
    output, dres, branch, dn, w, dstate, sums_second = turn_back(
        late[0], late[1], resid, e, vec, wo, mixed, rden, fq, count, span, marks
    )
    later = Passing(dstate, True)
    outs = [Chain(*outer(mixed, branch, [dstate]))]
    outs[0].start()
    marks = [later.outside] + advance(seconds)
    for _ in range(stages - 1):
        marks = marks + advance(firsts)
    parts = [attend_back(0, fq, fk, v, dn, w, prior, span, marks)]
    marks = advance(outs, [parts[0][0]])
    firsts_last = Last(firsts, [parts[0][0]])
    marks = marks + list(firsts_last.sends)
    for _ in range(stages - 1):
        marks = marks + advance(seconds, [parts[0][0]])
    for image in range(1, count):
        parts.append(attend_back(image, fq, fk, v, dn, w, prior, span, marks))
    later = later.finish([parts[0][0]])
    for _ in range(stages - 1):
        marks = advance(outs, [parts[-1][0]])
    marks = marks + seconds[0].came
    left = finish(0, parts, fk, v, later, a1t, count, span, marks)
    inner = [Chain(*left[3:])]
    inner[0].start()
    local_squares = firsts_last.squares([left[0]])
    seconds_last = Last(seconds + outs, [left[0]])
    marks = seconds_last.sends + [firsts_last.sums]
    right = finish(1, parts, fk, v, later, a1t, count, span, marks)
    inner.append(Chain(*right[3:]))
    inner[1].start()
    marks = advance(inner[:1], [right[0]])
    grads_in = []
    for image in range(count):
        grads_in.append(enter(image, left[:3], right[:3], (wq, wk, wv), x, dres, vec, span, marks))
        if image == 0:
            local_squares = local_squares + seconds_last.squares([grads_in[0][1]])
            marks = advance(inner[1:], [grads_in[0][1]]) + [seconds_last.sums] + inner[0].came
    input_grad = jnp.stack([part[0] for part in grads_in])
    for _ in range(stages - 1):
        marks = advance(inner)
    (sums,) = gate([sum(part[1] for part in grads_in)], marks)
    vector_grad = sum_slowly(jnp.concatenate([sums[:2], sums_second[:2]], axis=0))
    device = lax.axis_index("seq") * lax.axis_size("img") + lax.axis_index("img")
    vector_shard = lax.dynamic_slice_in_dim(vector_grad, device * owned, owned, 1)
    inner_last = Last(inner, [seconds_last.sums])
    local_squares = local_squares + jnp.sum(vector_shard * vector_shard)
    local_squares = local_squares + inner_last.squares()
    grad_norm = jnp.sqrt(sum_all(jnp.full((8, 128), local_squares))[0, 0])
    (early_shard,) = firsts_last.finish()
    late_shard, out_shard = seconds_last.finish()
    inner_shard = jnp.concatenate([part for pair in inner_last.finish() for part in pair], axis=2)
    attn_shard = jnp.concatenate([inner_shard, jnp.concatenate(out_shard, axis=2)], axis=0)
    feed_shard = jnp.concatenate([jnp.concatenate(pair, axis=2) for pair in zip(early_shard, late_shard)], axis=0)
    factor = clip_bound / jnp.maximum(grad_norm, clip_bound)
    attn_new = adam_update(
        attention_weight, attention_moment, attention_second, attention_average, attn_shard, factor, learn_rate
    )
    feed_new = adam_update(
        feedforward_weight, feedforward_moment, feedforward_second, feedforward_average, feed_shard, factor, learn_rate
    )
    norm_new = adam_update(norm_vectors, norm_moment, norm_second, norm_average, vector_shard, factor, norm_rate)
    output = output.reshape(images.shape)
    input_grad = input_grad.reshape(images.shape)
    return (output, input_grad, grad_norm) + attn_new + feed_new + norm_new


def solution(mesh):
    tokens = P("img", "seq", None)
    rows = P(None, ("seq", "img"), None)
    vectors = P(None, ("seq", "img"))
    group = (rows, rows, vectors)
    return jax.shard_map(
        body,
        mesh=mesh,
        in_specs=(tokens, tokens) + group * 4,
        out_specs=(tokens, tokens, P()) + (rows,) * 8 + (vectors,) * 4,
        check_vma=False,
    )
```

```python
import functools

import jax
import jax.numpy as jnp
import numpy as np
from jax import lax
from jax.experimental import pallas as pl
from jax.experimental.pallas import tpu as pltpu
from jax.sharding import PartitionSpec as P

HEADS = 16
HEAD_DIM = 64
STEP = 10

beta_first = 0.9
beta_second = 0.95
learn_rate = 0.02
norm_rate = 0.2
weight_decay = 0.1
average_decay = 0.75
clip_bound = 1.0
eps_norm = 1e-05
eps_adam = 1e-08

PAIR = 2 * HEAD_DIM
STATE_ROWS = HEAD_DIM + 16
SLAB = 1024
TILE = 512
GROUP = 256

low = jnp.bfloat16
wide = jnp.float32


def params(megabytes=56):
    return pltpu.CompilerParams(vmem_limit_bytes=megabytes * 1024 * 1024)


def cost(products, elements):
    return pl.CostEstimate(flops=2 * products, bytes_accessed=elements, transcendentals=0)


def launch(kernel, tokens, in_specs, megabytes=56, **keys):
    known, extra = len(in_specs), len(tokens)

    def run(*refs):
        kernel(*refs[:known], *refs[known + extra :])

    call = pl.pallas_call(
        run, in_specs=list(in_specs) + [pl.BlockSpec(memory_space=pl.ANY)] * extra, compiler_params=params(megabytes), **keys
    )
    return lambda *args: call(*args, *tokens)


def launch_at(kernel, spot, tokens, grid, in_specs, out_specs, megabytes=56, scratch_shapes=(), **keys):
    known, extra = len(in_specs), len(tokens)

    def run(spot_ref, *refs):
        kernel(spot_ref, *refs[:known], *refs[known + extra :])

    call = pl.pallas_call(
        run,
        grid_spec=pltpu.PrefetchScalarGridSpec(
            num_scalar_prefetch=1,
            grid=grid,
            in_specs=list(in_specs) + [pl.BlockSpec(memory_space=pl.ANY)] * extra,
            out_specs=out_specs,
            scratch_shapes=scratch_shapes,
        ),
        compiler_params=params(megabytes),
        **keys,
    )
    return lambda *args: call(spot.reshape(-1).astype(jnp.int32), *args, *tokens)


def reversed_bits(value, count):
    return sum(((value >> k) & 1) << (count - 1 - k) for k in range(count))


def join(target_ref, bits, spot_ref, own_ref, came_ref, own_other_ref, came_other_ref):
    core, high, lowest = spot_ref[0], spot_ref[1], spot_ref[2]
    runs = 1 << (bits - 1)
    rows = target_ref.shape[1] // (2 * runs)
    for run in range(runs):
        source = slice(run * rows, (run + 1) * rows)
        turned = reversed_bits(run, bits)
        for place in range(2):
            first = (high ^ place) * runs + run
            second = turned + (lowest ^ place)
            for ref, slot in (((own_ref, came_ref)[place], core), ((own_other_ref, came_other_ref)[place], 1 - core)):
                at = jnp.where(slot == 0, first, second)
                target_ref[slot, pl.ds(pl.multiple_of(at * rows, rows), rows), :] = ref[source, :]


class Pieces:
    def __init__(self, arrays):
        self.arrays = [array.reshape(array.shape[0], -1, array.shape[-1]) for array in arrays]
        place = pos_index()
        self.bits = pos_bits()
        self.spot = jnp.stack([core_index(), place >> (self.bits - 1), place & 1])

    def blocks(self, columns, place):
        rows = self.arrays[0].shape[1]
        return [pl.BlockSpec((None, rows, columns), place)] * 4

    def second(self, columns):
        mine, others = (
            [part[0, :, columns].reshape(1 << (self.bits - 1), 1, -1, columns.stop - columns.start) for part in pair]
            for pair in (self.arrays[:2], self.arrays[2:])
        )
        own, came = (jnp.where(core_index() == 1, left, right) for left, right in zip(mine, others))
        straight, turned = jnp.concatenate([own, came], axis=1), jnp.concatenate([came, own], axis=1)
        runs = jnp.where(self.spot[2] == 0, straight, turned)
        order = [reversed_bits(run, self.bits - 1) for run in range(1 << (self.bits - 1))]
        return jnp.stack([runs[run] for run in order]).reshape(-1, columns.stop - columns.start)


def shaped(shape, kind):
    return jax.ShapeDtypeStruct(shape, kind)


def whole(shape):
    return pl.BlockSpec(shape, lambda *_: (0,) * len(shape))


def mm(left, right):
    return lax.dot_general(left, right, (((1,), (0,)), ((), ())), preferred_element_type=wide)


def mt(left, right):
    return lax.dot_general(left, right, (((1,), (1,)), ((), ())), preferred_element_type=wide)


def tm(left, right):
    return lax.dot_general(left, right, (((0,), (0,)), ((), ())), preferred_element_type=wide)


def pair_mm(first, second):
    if first[0].shape[1] % 128:
        return mm(*first) + mm(*second)
    return mm(jnp.concatenate([first[0], second[0]], axis=1), jnp.concatenate([first[1], second[1]], axis=0))


def causal_mask(span, below):
    rows = lax.broadcasted_iota(jnp.int32, (span, span), 0)
    columns = lax.broadcasted_iota(jnp.int32, (span, span), 1)
    return (rows >= columns if below else rows <= columns).astype(wide).astype(low)


def first_head(rows):
    return lax.broadcasted_iota(jnp.int32, (rows, PAIR), 1) < HEAD_DIM


def fold_state(product):
    return jnp.where(first_head(HEAD_DIM), product[:HEAD_DIM], product[HEAD_DIM:])


def unfold_state(folded):
    own = first_head(HEAD_DIM)
    zero = jnp.zeros_like(folded)
    return jnp.concatenate([jnp.where(own, folded, zero), jnp.where(own, zero, folded)], axis=0)


def unfold_total(row):
    tall = jnp.broadcast_to(row, (PAIR, PAIR))
    lanes = lax.broadcasted_iota(jnp.int32, (PAIR, PAIR), 1) < HEAD_DIM
    rows = lax.broadcasted_iota(jnp.int32, (PAIR, PAIR), 0) < HEAD_DIM
    return jnp.where(lanes == rows, tall, jnp.zeros_like(tall))


def split_low(values):
    high = values.astype(low)
    return high, (values - high.astype(wide)).astype(low)


def normalised(values):
    centre = jnp.mean(values, axis=-1, keepdims=True)
    centred = values - centre
    spread = jnp.mean(centred * centred, axis=-1, keepdims=True)
    scale = lax.rsqrt(spread + eps_norm)
    return centred * scale, scale


def feature(raw):
    return jnp.where(raw > 0, raw + 1.0, jnp.exp(jnp.minimum(raw, 0.0))).astype(low)


def project_kernel(images, span, bits, spot_ref, x_ref, vec_ref, *refs):
    fk_ref, v_ref, a_ref, at_ref, state_ref, wk_ref, wv_ref, joined_ref = refs[4:]

    @pl.when(pl.program_id(0) == 0)
    def _():
        gain, shift = vec_ref[0:1, :], vec_ref[1:2, :]
        step = span // 3
        for start in range(0, images * span, step):
            rows = slice(start, start + step)
            unit, _ = normalised(x_ref[rows, :].astype(wide))
            a_ref[rows, :] = (unit * gain + shift).astype(low)
        at_ref[...] = a_ref[...].T

    join(joined_ref, bits, spot_ref, *refs[:4])
    keys, values = joined_ref[0], joined_ref[1]
    wk_ref[...] = keys
    wv_ref[...] = values
    fk_ref[...] = feature(mm(a_ref[...], keys))
    v_ref[...] = mm(a_ref[...], values).astype(low)
    ones = jnp.ones((16, span), low)
    for image in range(images):
        rows = slice(image * span, (image + 1) * span)
        for pair in range(GROUP // PAIR):
            lanes = slice(pair * PAIR, (pair + 1) * PAIR)
            key, value = fk_ref[rows, lanes], v_ref[rows, lanes]
            state_ref[image, pair, :HEAD_DIM, :] = fold_state(tm(value, key))
            state_ref[image, pair, HEAD_DIM:, :] = mm(ones, key)


def project(x, vec, pieces, images, span, tokens=()):
    count, width = x.shape
    pairs = GROUP // PAIR
    column = pl.BlockSpec((count, GROUP), lambda g, spot: (0, g))
    weight = pl.BlockSpec((width, GROUP), lambda g, spot: (0, g))
    return launch_at(
        functools.partial(project_kernel, images, span, pieces.bits),
        pieces.spot,
        tokens,
        grid=(width // GROUP,),
        in_specs=[whole((count, width)), whole(vec.shape)] + pieces.blocks(GROUP, lambda g, spot: (0, 0, g)),
        out_specs=[
            column,
            column,
            whole((count, width)),
            whole((width, count)),
            pl.BlockSpec((images, pairs, STATE_ROWS, PAIR), lambda g, spot: (0, g, 0, 0)),
            weight,
            weight,
        ],
        out_shape=[
            shaped((count, width), low),
            shaped((count, width), low),
            shaped((count, width), low),
            shaped((width, count), low),
            shaped((images, width // PAIR, STATE_ROWS, PAIR), wide),
            shaped((width, width), low),
            shaped((width, width), low),
        ],
        scratch_shapes=[pltpu.VMEM((2, width, GROUP), low)],
        cost_estimate=cost(2 * count * width * width, 8 * width * width + 12 * count * width),
        name="project",
    )(x, vec, *pieces.arrays)


def query_kernel(bits, spot_ref, a_ref, *refs):
    fq_ref, wq_ref, wo_ref, joined_ref = refs[4:]
    join(joined_ref, bits, spot_ref, *refs[:4])
    wq_ref[...] = joined_ref[0]
    wo_ref[...] = joined_ref[1]
    fq_ref[...] = feature(mm(a_ref[...], joined_ref[0]))


def query(a, pieces, tokens=()):
    count, width = a.shape
    weight = pl.BlockSpec((width, GROUP), lambda g, spot: (0, g))
    return launch_at(
        functools.partial(query_kernel, pieces.bits),
        pieces.spot,
        tokens,
        grid=(width // GROUP,),
        in_specs=[whole((count, width))] + pieces.blocks(GROUP, lambda g, spot: (1, 0, g)),
        out_specs=[pl.BlockSpec((count, GROUP), lambda g, spot: (0, g)), weight, weight],
        out_shape=[shaped((count, width), low)] + [shaped((width, width), low)] * 2,
        scratch_shapes=[pltpu.VMEM((2, width, GROUP), low)],
        cost_estimate=cost(count * width * width, 6 * width * width + 4 * count * width),
        name="query",
    )(a, *pieces.arrays)


def turn_kernel(x_ref, out_ref):
    out_ref[...] = x_ref[...].T


def turn(x, images, span, tokens=()):
    count, width = x.shape
    return turned_whole(
        launch(
            turn_kernel,
            tokens,
            grid=(images,),
            in_specs=[pl.BlockSpec((span, width), lambda b: (b, 0))],
            out_specs=turned_block(width, span),
            out_shape=turned_shape(images, width, span),
            cost_estimate=cost(1, 4 * count * width),
                name="turn",
        )(x)
    )


def attend_kernel(span, fq_ref, fk_ref, v_ref, num_ref, den_ref):
    own = first_head(span)
    causal = causal_mask(span, True)
    one = jnp.ones((span, PAIR), low)
    zero = jnp.zeros((span, PAIR), low)
    for pair in range(GROUP // PAIR):
        lanes = slice(pair * PAIR, (pair + 1) * PAIR)
        query, key, value = fq_ref[:, lanes], fk_ref[:, lanes], v_ref[:, lanes]
        products = []
        for mask in (own, jnp.logical_not(own)):
            scores = mt(jnp.where(mask, query, zero), key).astype(low) * causal
            right = jnp.concatenate([jnp.where(mask, value, zero), jnp.where(mask, one, zero)], axis=1)
            products.append((scores, right))
        total = pair_mm(*products)
        num_ref[:, lanes] = total[:, :PAIR]
        den_ref[:, lanes] = total[:, PAIR:]


def attend(fq, fk, v, images, span, tokens=()):
    rows, width = fq.shape
    block = pl.BlockSpec((span, GROUP), lambda b, p: (b, p))
    return launch(
        functools.partial(attend_kernel, span),
        tokens,
        grid=(images, width // GROUP),
        in_specs=[block] * 3,
        out_specs=[block] * 2,
        out_shape=[shaped((rows, width), wide)] * 2,
        cost_estimate=cost(16 * rows * span * width, 14 * rows * width),
        name="attend",
    )(fq, fk, v)


def turned_block(width, span):
    if span % 128:
        return pl.BlockSpec((None, width, span), lambda b: (b, 0, 0))
    return pl.BlockSpec((width, span), lambda b: (0, b))


def turned_shape(images, width, span):
    return shaped((images, width, span) if span % 128 else (width, images * span), low)


def turned_whole(array):
    if array.ndim == 2:
        return array
    return jnp.swapaxes(array, 0, 1).reshape(array.shape[1], -1)


def mix_kernel(x_ref, vec_ref, wo_ref, fq_ref, num_ref, den_ref, prior_ref, mixed_ref, rden_ref, resid_ref, a_ref, at_ref, mt_ref):
    width = x_ref.shape[1]
    for pair in range(width // PAIR):
        lanes = slice(pair * PAIR, (pair + 1) * PAIR)
        folded = prior_ref[0, pair]
        matrix = jnp.concatenate(
            [unfold_state(folded[:HEAD_DIM]), unfold_total(folded[HEAD_DIM : HEAD_DIM + 1])], axis=0
        )
        high, rest = split_low(matrix)
        query = fq_ref[:, lanes]
        both = mt(jnp.concatenate([query, query], axis=1), jnp.concatenate([high, rest], axis=1))
        scale = 1.0 / (den_ref[:, lanes] + both[:, PAIR:])
        rden_ref[:, lanes] = scale
        mixed_ref[:, lanes] = ((num_ref[:, lanes] + both[:, :PAIR]) * scale).astype(low)
    resid = x_ref[...].astype(wide) + mm(mixed_ref[...], wo_ref[...])
    resid_ref[...] = resid
    unit, _ = normalised(resid)
    normed = (unit * vec_ref[2:3, :] + vec_ref[3:4, :]).astype(low)
    a_ref[...] = normed
    at_ref[...] = normed.T
    mt_ref[...] = mixed_ref[...].T


def mix(x, vec, wo, fq, num, den, prior, images, span, tokens=()):
    rows_, width = x.shape
    rows = pl.BlockSpec((span, width), lambda b: (b, 0))
    return launch(
        mix_kernel,
        tokens,
        grid=(images,),
        in_specs=[
            rows,
            whole(vec.shape),
            whole(wo.shape),
            rows,
            rows,
            rows,
            pl.BlockSpec((1,) + prior.shape[1:], lambda b: (b, 0, 0, 0)),
        ],
        out_specs=[rows, rows, rows, rows, turned_block(width, span), turned_block(width, span)],
        out_shape=[
            shaped((rows_, width), low),
            shaped((rows_, width), wide),
            shaped((rows_, width), wide),
            shaped((rows_, width), low),
            turned_shape(images, width, span),
            turned_shape(images, width, span),
        ],
        cost_estimate=cost(4 * rows_ * width * width, 24 * rows_ * width + 2 * width * width),
        name="mix",
    )(x, vec, wo, fq, num, den, prior)


gelu_scale = 0.7978845608028654
gelu_cubic = 0.044715


def feed_kernel(fresh, bits, spot_ref, *refs):
    a_ref, e_ref = refs[:2]
    out_ref, da_ref, kept_ref, sent_ref, joined_ref = refs[-5:]
    join(joined_ref, bits, spot_ref, *refs[2:6])

    @pl.when(pl.program_id(0) == 0)
    def _():
        if fresh:
            out_ref[...] = jnp.zeros_like(out_ref)
            da_ref[...] = jnp.zeros_like(da_ref)
        else:
            out_ref[...] = refs[6][...]
            da_ref[...] = refs[7][...]

    up, down = joined_ref[0], joined_ref[1]
    upper = mm(a_ref[...], up)
    grad = mm(e_ref[...], down)
    square = upper * upper
    bend = jnp.tanh(gelu_scale * upper * (1.0 + gelu_cubic * square))
    gate = 0.5 + 0.5 * bend
    hidden = (upper * gate).astype(low)
    slope = gate + 0.5 * upper * (1.0 - bend * bend) * (gelu_scale * (1.0 + 3.0 * gelu_cubic * square))
    dupper = (grad * slope).astype(low)
    out_ref[...] += mt(hidden, down)
    da_ref[...] += mt(dupper, up)
    first = spot_ref[0] == 0
    kept_ref[...] = jnp.where(first, dupper, hidden)
    sent_ref[...] = jnp.where(first, hidden, dupper)


def feed(pieces, a, e, carried, tokens=()):
    rows, width = a.shape
    slabs = pieces.arrays[0].shape[0]
    tiles = SLAB // TILE
    grads = pl.BlockSpec((rows, TILE), lambda g, spot: (0, g))
    full = whole((rows, width))
    fresh = carried is None
    return launch_at(
        functools.partial(feed_kernel, fresh, pieces.bits),
        pieces.spot,
        tokens,
        grid=(slabs * tiles,),
        in_specs=[full, full]
        + pieces.blocks(TILE, lambda g, spot: (g // tiles, 0, g % tiles))
        + ([] if fresh else [full, full]),
        out_specs=[full, full, grads, grads],
        out_shape=[shaped((rows, width), wide)] * 2 + [shaped((rows, slabs * SLAB), low)] * 2,
        scratch_shapes=[pltpu.VMEM((2, width, TILE), low)],
        cost_estimate=cost(4 * rows * width * slabs * SLAB, 4 * (width + rows) * slabs * SLAB + 20 * rows * width),
        name="feed",
    )(a, e, *pieces.arrays, *(() if fresh else carried))


def weigh_kernel(count, spot_ref, lt_ref, lt_other_ref, x_ref, x_other_ref, kept_ref, sent_ref, product_ref):
    rows = product_ref.shape[0] // (2 * count)
    product_ref[...] = mm(lt_ref[...], x_ref[...]) + mm(lt_other_ref[...], x_other_ref[...])
    for k in range(count):
        for ref, at in ((kept_ref, spot_ref[k]), (sent_ref, spot_ref[count + k])):
            ref[k] = product_ref[pl.ds(pl.multiple_of(at * rows, rows), rows), :].astype(low)


def weigh(chain, lt, lt_other, x, x_other, tokens=()):
    lead, rows, columns = x.shape
    width = lt.shape[0]
    keeps, sends = chain.table()
    count = keeps.shape[0]
    tile = min(TILE, columns)
    full = whole((width, rows))
    column = pl.BlockSpec((None, rows, tile), lambda n, g, spot: (n, 0, g))
    result = pl.BlockSpec((None, count, width // (2 * count), tile), lambda n, g, spot: (n, 0, 0, g))
    chain.take(
        launch_at(
            functools.partial(weigh_kernel, count),
            jnp.concatenate([keeps, sends]),
            tokens,
            grid=(lead, columns // tile),
            in_specs=[full, full, column, column],
            out_specs=[result, result],
            out_shape=[shaped((lead, count, width // (2 * count), columns), low)] * 2,
            scratch_shapes=[pltpu.VMEM((width, tile), wide)],
            cost_estimate=cost(2 * lead * rows * width * columns, 4 * lead * (rows + width) * columns + 4 * rows * width),
            name="weigh",
        )(lt, lt_other, x, x_other)
    )
    chain.start()
    return chain.sends


def turn_back_kernel(core_ref, x_out_ref, da_ref, resid_ref, e_ref, vec_ref, wo_ref, mixed_ref, rden_ref, fq_ref,
                     out_ref, dres_ref, kept_ref, sent_ref, dn_ref, w_ref, state_ref, sums_ref):
    width = da_ref.shape[1]
    resid = resid_ref[...]
    out_ref[...] = (resid + x_out_ref[...]).astype(low)
    unit, scale = normalised(resid)
    da = da_ref[...]

    @pl.when(pl.program_id(0) == 0)
    def _():
        sums_ref[...] = jnp.zeros_like(sums_ref)

    sums_ref[0:1, :] += jnp.sum(da * unit, axis=0, keepdims=True)
    sums_ref[1:2, :] += jnp.sum(da, axis=0, keepdims=True)
    p = da * vec_ref[2:3, :]
    back = p - jnp.mean(p, axis=-1, keepdims=True) - unit * jnp.mean(p * unit, axis=-1, keepdims=True)
    dres = e_ref[...].astype(wide) + scale * back
    dres_ref[...] = dres
    branch = dres.astype(low)
    left, right = branch[:, : width // 2], branch[:, width // 2 :]
    first = core_ref[0] == 0
    kept_ref[...] = jnp.where(first, left, right)
    sent_ref[...] = jnp.where(first, right, left)
    dmixed = mt(branch, wo_ref[...]).astype(low).astype(wide)
    dnumer = dmixed * rden_ref[...]
    dn_ref[...] = dnumer.astype(low)
    w_ref[...] = (-dnumer * mixed_ref[...].astype(wide)).astype(low)
    for pair in range(width // PAIR):
        lanes = slice(pair * PAIR, (pair + 1) * PAIR)
        query = fq_ref[:, lanes]
        state_ref[0, pair, :HEAD_DIM, :] = fold_state(tm(dn_ref[:, lanes], query))
        total = jnp.sum(fold_state(tm(w_ref[:, lanes], query)), axis=0, keepdims=True)
        state_ref[0, pair, HEAD_DIM:, :] = jnp.broadcast_to(total, (STATE_ROWS - HEAD_DIM, PAIR))


def turn_back(x_out, da, resid, e, vec, wo, mixed, rden, fq, images, span, tokens=()):
    rows_, width = da.shape
    rows = pl.BlockSpec((span, width), lambda b, core: (b, 0))
    state = (images, width // PAIR, STATE_ROWS, PAIR)
    half = pl.BlockSpec((span, width // 2), lambda b, core: (b, 0))
    return launch_at(
        turn_back_kernel,
        core_index(),
        tokens,
        grid=(images,),
        in_specs=[rows, rows, rows, rows, whole(vec.shape), whole(wo.shape), rows, rows, rows],
        out_specs=[rows, rows, half, half, rows, rows] + [pl.BlockSpec((1,) + state[1:], lambda b, core: (b, 0, 0, 0)), whole((8, width))],
        out_shape=[
            shaped((rows_, width), low),
            shaped((rows_, width), wide),
            shaped((rows_, width // 2), low),
            shaped((rows_, width // 2), low),
            shaped((rows_, width), low),
            shaped((rows_, width), low),
            shaped(state, wide),
            shaped((8, width), wide),
        ],
        cost_estimate=cost(5 * rows_ * width * width, 30 * rows_ * width),
        name="turn_back",
    )(x_out, da, resid, e, vec, wo, mixed, rden, fq)


def attend_back_kernel(span, fq_ref, fk_ref, v_ref, dn_ref, w_ref, prior_ref, dq_ref, dfk_ref, dv_ref):
    own = first_head(span)
    own_twice = jnp.concatenate([own, own], axis=1)
    below, above = causal_mask(span, True), causal_mask(span, False)
    one = jnp.ones((span, PAIR), low)
    zero = jnp.zeros((span, PAIR), low)
    zero_twice = jnp.zeros((span, 2 * PAIR), low)
    for pair in range(GROUP // PAIR):
        lanes = slice(pair * PAIR, (pair + 1) * PAIR)
        query, key, value = fq_ref[:, lanes], fk_ref[:, lanes], v_ref[:, lanes]
        grads = jnp.concatenate([dn_ref[:, lanes], w_ref[:, lanes]], axis=1)
        extended = jnp.concatenate([value, one], axis=1)
        folded = prior_ref[0, pair]
        matrix = jnp.concatenate(
            [unfold_state(folded[:HEAD_DIM]), unfold_total(folded[HEAD_DIM : HEAD_DIM + 1])], axis=0
        )
        high, rest = split_low(matrix)
        dfq = mm(jnp.concatenate([grads, grads], axis=1), jnp.concatenate([high, rest], axis=0))
        to_query, to_key, to_value = [], [], []
        for mask, both in ((own, own_twice), (jnp.logical_not(own), jnp.logical_not(own_twice))):
            head_grads = jnp.where(both, grads, zero_twice)
            head_query = jnp.where(mask, query, zero)
            head_key = jnp.where(mask, key, zero)
            to_query.append((mt(head_grads, extended).astype(low) * below, head_key))
            to_key.append((mt(extended, head_grads).astype(low) * above, head_query))
            to_value.append((mt(head_key, query).astype(low) * above, head_grads[:, :PAIR]))
        dfq = dfq + pair_mm(*to_query)
        dq_ref[:, lanes] = (dfq * jnp.minimum(query.astype(wide), 1.0)).astype(low)
        dfk_ref[:, lanes] = pair_mm(*to_key)
        dv_ref[:, lanes] = pair_mm(*to_value)


def attend_back(image, fq, fk, v, dn, w, prior, span, tokens=()):
    width = fq.shape[1]
    block = pl.BlockSpec((span, GROUP), lambda p: (image, p))
    column = pl.BlockSpec((span, GROUP), lambda p: (0, p))
    return launch(
        functools.partial(attend_back_kernel, span),
        tokens,
        grid=(width // GROUP,),
        in_specs=[block] * 5 + [pl.BlockSpec((1, GROUP // PAIR) + prior.shape[2:], lambda p: (image, p, 0, 0))],
        out_specs=[column] * 3,
        out_shape=[shaped((span, width), low), shaped((span, width), wide), shaped((span, width), wide)],
        cost_estimate=cost(32 * span * span * width, 24 * span * width),
        name="attend_back",
    )(fq, fk, v, dn, w, prior)


def finish_kernel(images, span, core_ref, *refs):
    fk_ref, v_ref, later_ref, kept_ref, sent_ref = refs[3 * images :]

    def run(out_ref):
        for image in range(images):
            rows = slice(image * span, (image + 1) * span)
            dq_ref, dfk_ref, dvl_ref = refs[3 * image : 3 * image + 3]
            out_ref[0, rows, :] = dq_ref[...]
            for pair in range(GROUP // PAIR):
                lanes = slice(pair * PAIR, (pair + 1) * PAIR)
                folded = later_ref[image, pair]
                high, rest = split_low(unfold_state(folded[:HEAD_DIM]))
                key, value = fk_ref[rows, lanes], v_ref[rows, lanes]
                dfk = dfk_ref[:, lanes] + folded[HEAD_DIM : HEAD_DIM + 1]
                dfk = dfk + mm(jnp.concatenate([value, value], axis=1), jnp.concatenate([high, rest], axis=0))
                dv = dvl_ref[:, lanes] + mt(
                    jnp.concatenate([key, key], axis=1), jnp.concatenate([high, rest], axis=1)
                )
                out_ref[1, rows, lanes] = (dfk * jnp.minimum(key.astype(wide), 1.0)).astype(low)
                out_ref[2, rows, lanes] = dv.astype(low)

    @pl.when(pl.program_id(0) < pl.num_programs(0) // 2)
    def _():
        run(kept_ref)

    @pl.when(pl.program_id(0) >= pl.num_programs(0) // 2)
    def _():
        run(sent_ref)


def finish(parts, fk, v, later, images, span, tokens=()):
    rows, width = fk.shape
    groups = width // GROUP // 2

    def column(g, core):
        return ((g // groups) ^ core[0]) * groups + g % groups

    block = pl.BlockSpec((rows, GROUP), lambda g, core: (0, column(g, core)))
    part = pl.BlockSpec((span, GROUP), lambda g, core: (0, column(g, core)))
    state = pl.BlockSpec((images, GROUP // PAIR) + later.shape[2:], lambda g, core: (0, column(g, core), 0, 0))
    return launch_at(
        functools.partial(finish_kernel, images, span),
        core_index(),
        tokens,
        grid=(2 * groups,),
        in_specs=[part] * (3 * images) + [block] * 2 + [state],
        out_specs=[
            pl.BlockSpec((3, rows, GROUP), lambda g, core: (0, 0, jnp.minimum(g, groups - 1))),
            pl.BlockSpec((3, rows, GROUP), lambda g, core: (0, 0, jnp.maximum(g - groups, 0))),
        ],
        out_shape=[shaped((3, rows, width // 2), low)] * 2,
        cost_estimate=cost(rows * width * 512, 24 * rows * width),
        name="finish",
    )(*[array for image in parts for array in image], fk, v, later)


def enter_kernel(core_ref, kept_ref, sent_ref, *refs):
    weights = refs[:3]
    x_ref, dres_ref, vec_ref, grad_ref, sums_ref = refs[3:]
    half = x_ref.shape[1] // 2
    da = None
    for k, weight in enumerate(weights):
        for ref, side in ((kept_ref, core_ref[0]), (sent_ref, 1 - core_ref[0])):
            part = mt(ref[k], weight[:, pl.ds(pl.multiple_of(side * half, half), half)])
            da = part if da is None else da + part
    unit, scale = normalised(x_ref[...].astype(wide))
    sums_ref[0:1, :] = jnp.sum(da * unit, axis=0, keepdims=True)
    sums_ref[1:2, :] = jnp.sum(da, axis=0, keepdims=True)
    sums_ref[2:, :] = jnp.zeros_like(sums_ref[2:, :])
    p = da * vec_ref[0:1, :]
    back = p - jnp.mean(p, axis=-1, keepdims=True) - unit * jnp.mean(p * unit, axis=-1, keepdims=True)
    grad_ref[...] = (dres_ref[...] + scale * back).astype(low)


def enter(image, kept, sent, weights, x, dres, vec, span, tokens=()):
    width = x.shape[1]
    rows = pl.BlockSpec((span, width), lambda g, core: (image, 0))
    part = pl.BlockSpec((3, span, width // 2), lambda g, core: (0, image, 0))
    return launch_at(
        enter_kernel,
        core_index(),
        tokens,
        grid=(1,),
        in_specs=[part] * 2 + [whole((width, width))] * 3 + [rows, rows, whole(vec.shape)],
        out_specs=[whole((span, width)), whole((8, width))],
        out_shape=[shaped((span, width), low), shaped((8, width), wide)],
        cost_estimate=cost(3 * span * width * width, 14 * span * width + 6 * width * width),
        name="enter",
    )(kept, sent, *weights, x, dres, vec)


def adam_update(master, moment, second, average, gradient, factor, rate):
    clipped = gradient * factor
    moment = beta_first * moment + (1.0 - beta_first) * clipped
    second = beta_second * second + (1.0 - beta_second) * clipped * clipped
    first_hat = moment / (1.0 - beta_first**STEP)
    second_hat = second / (1.0 - beta_second**STEP)
    master = master - rate * (first_hat / (jnp.sqrt(second_hat) + eps_adam) + weight_decay * master)
    average = average_decay * average + (1.0 - average_decay) * master
    return (master, moment, second, average)


def powers(count):
    return [1 << k for k in range(count.bit_length() - 1)]


def core_index():
    return lax.axis_index("seq") % 2


def pos_index():
    return lax.axis_index("seq") // 2


def pos_bits():
    return (lax.axis_size("seq") // 2).bit_length() - 1


def flip(array, axis, bit):
    return lax.ppermute(array, axis, [(i, i ^ bit) for i in range(lax.axis_size(axis))])


def flip_core(array):
    return flip(array, "seq", 1)


def flip_pos(array, stage):
    bits = pos_bits()
    pairs = [(i, i ^ (2 << (stage if i % 2 == 0 else bits - 1 - stage))) for i in range(lax.axis_size("seq"))]
    return lax.ppermute(array, "seq", pairs)


def own_bit(stage):
    bits = pos_bits()
    return jnp.where(core_index() == 0, pos_index() >> stage, pos_index() >> (bits - 1 - stage)) & 1


def halves(shape, dim):
    index = np.arange(int(np.prod(shape))).reshape(shape)
    return np.stack([index.take(side, axis=dim).ravel() for side in range(2)])


def fold_kernel(chains, spot_ref, *refs):
    ins, outs = refs[: 4 * chains], refs[4 * chains :]
    for k in range(2 * chains):
        value = ins[2 * k][...].astype(wide) + ins[2 * k + 1][...].astype(wide)
        outs[k][...] = value.astype(outs[k].dtype)


def fold(cuts, tokens=()):
    count = cuts[0][2].shape[0]
    steps = max(1, min(2, min(kept.shape[-1] for kept, *_ in cuts) // 256))
    in_specs, out_specs, out_shape, arrays, moved = [], [], [], [], 0
    for k, (kept, came, keeps, sends) in enumerate(cuts):
        lead, _, rows, columns = kept.shape
        block = (lead, 1, rows, columns // steps)
        for side in range(2):
            at = 2 * k * count + side * count
            spec = pl.BlockSpec(block, lambda g, c, spot, at=at: (0, spot[at + g], 0, c))
            in_specs += [spec, spec]
            arrays += [kept, came]
            out_specs.append(pl.BlockSpec(block, lambda g, c, spot: (0, g, 0, c)))
            out_shape.append(shaped((lead, count, rows, columns), low if side else wide))
        moved += 8 * kept.size
    results = launch_at(
        functools.partial(fold_kernel, len(cuts)),
        jnp.concatenate([part for _, _, keeps, sends in cuts for part in (keeps, sends)]),
        tokens,
        grid=(count, steps),
        in_specs=in_specs,
        out_specs=out_specs,
        out_shape=out_shape,
        cost_estimate=cost(1, moved),
        name="fold",
    )(*arrays)
    return [results[2 * k : 2 * k + 2] for k in range(len(cuts))]


class Chain:
    def __init__(self, lead=1):
        self.lead = lead
        self.stage = -1
        self.left = [list(range(pos_bits()))[::-1]] * 2

    def start(self):
        self.came = [flip_pos(self.sends[0], self.stage)]

    def table(self):
        self.stage += 1
        tables = []
        for kind in range(2):
            bit = self.stage if kind == 0 else pos_bits() - 1 - self.stage
            left = self.left[kind]
            tables.append(halves((2,) * len(left), left.index(bit)))
            self.left[kind] = [other for other in left if other != bit]
        table = jnp.where(core_index() == 0, *[jnp.asarray(part, jnp.int32) for part in tables])
        own = own_bit(self.stage)
        return table[own], table[1 - own]

    def cut(self):
        return (self.kept, self.came[0], *self.table())

    def take(self, parts):
        self.kept, self.sends = parts[0], [parts[1]]


def advance(chains, tokens=()):
    parts = fold([chain.cut() for chain in chains], tokens)
    for chain, part in zip(chains, parts):
        chain.take(part)
        chain.start()
    return [array for chain in chains for array in chain.sends]


def last_kernel(ways, pre, pieces, spot_ref, *refs):
    ins, outs = refs[: 2 * pieces], refs[2 * pieces :]
    at = 0
    for k in range(pieces):
        columns = ins[2 * k].shape[-1]
        for j in range(ways):
            place = spot_ref[0] ^ j
            for n in range(pre):
                value = ins[2 * k][n, place].astype(wide) + ins[2 * k + 1][n, place].astype(wide)
                outs[j][n, :, at : at + columns] = value.astype(outs[j].dtype)
        at += columns


class Last:
    def __init__(self, chains, tokens=(), slowly=False):
        slices = lax.axis_size("img")
        ways = 2 if slowly else slices
        self.lead = chains[0].lead
        pre = self.lead * 2 * slices // ways
        arrays = []
        for chain in chains:
            for array in (chain.kept, chain.came[0]):
                arrays.append(array.reshape(pre, ways, -1, array.shape[-1]))
        self.widths = [array.shape[-1] for array in arrays[::2]]
        inside = pl.BlockSpec(memory_space=pltpu.VMEM)
        parts = launch(
            functools.partial(last_kernel, ways, pre, len(chains)),
            tokens,
            in_specs=[pl.BlockSpec(memory_space=pltpu.SMEM)] + [inside] * len(arrays),
            out_specs=[inside] * ways,
            out_shape=[shaped((pre, arrays[0].shape[2], sum(self.widths)), low if j else wide) for j in range(ways)],
            cost_estimate=cost(1, 4 * sum(array.size for array in arrays)),
                name="last",
        )((lax.axis_index("img") % ways).reshape(1), *arrays)
        self.kept, self.sends = parts[0], list(parts[1:])
        self.hops = list(range(1, ways))
        self.left = powers(slices)[1:][::-1] if slowly else []
        self.start()

    def start(self):
        self.came = [flip(array, "img", hop) for array, hop in zip(self.sends, self.hops)]

    def cut(self):
        bit = self.left[-1]
        entries = self.kept.reshape((1, -1) + self.kept.shape[-2:])
        dims = (2 * self.lead,) + (2,) * len(self.left)
        table = jnp.asarray(halves(dims, len(dims) - 1), jnp.int32)
        own = (lax.axis_index("img") // bit) % 2
        self.left = self.left[:-1]
        self.hops = [bit]
        return (entries, self.came[0].reshape(entries.shape), table[own], table[1 - own])

    def take(self, parts):
        self.kept, self.sends = parts[0][0], [parts[1][0]]

    def total(self):
        while self.left:
            advance([self])
        total = self.kept
        for came in self.came:
            total = total + came.astype(wide)
        return total

    def settle(self, stretch, tokens):
        self.came[stretch] = gate(self.came[stretch], tokens)
        return self.came[stretch]

    def squares(self):
        self.sums = self.total()
        return jnp.sum(self.sums * self.sums)

    def finish(self):
        core = core_index()
        total = self.sums.reshape((self.lead, 2) + self.sums.shape[-2:])
        own = lax.dynamic_index_in_dim(total, core, 1, False)
        came = flip_core(lax.dynamic_index_in_dim(total, 1 - core, 1, False))
        first, second = jnp.where(core == 0, own, came), jnp.where(core == 0, came, own)
        at, found = 0, []
        for columns in self.widths:
            found.append((first[..., at : at + columns], second[..., at : at + columns]))
            at += columns
        return found


def sum_slowly(array):
    for axis in ("seq", "img"):
        for bit in powers(lax.axis_size(axis)):
            array = array + flip(array, axis, bit)
    return array


def sum_all(array):
    rounds = [("img", range(1, lax.axis_size("img"))), ("seq", range(2, lax.axis_size("seq"), 2)), ("seq", [1])]
    for axis, hops in rounds:
        came = [flip(array, axis, hop) for hop in hops]
        for other in came:
            array = array + other
    return array


def assemble_kernel(plan, spot_ref, *refs):
    outs = sorted({out for _, _, out, _ in plan})
    count = len(refs) - 1 - len(outs)
    sems = refs[-1]
    copies = []
    for k, (piece, cut, out, where) in enumerate(plan):
        source = refs[piece].at[cut] if cut is not None else refs[piece]
        target = refs[count + out].at[where(spot_ref)]
        copies.append(pltpu.make_async_copy(source, target, sems.at[k]))
    for copy in copies:
        copy.start()
    for copy in copies:
        copy.wait()


def assemble(plan, spots, pieces, shapes, tokens=()):
    anywhere = pl.BlockSpec(memory_space=pl.ANY)
    return launch(
        functools.partial(assemble_kernel, plan),
        tokens,
        in_specs=[pl.BlockSpec(memory_space=pltpu.SMEM)] + [anywhere] * len(pieces),
        out_specs=[pl.BlockSpec(memory_space=pltpu.VMEM)] * len(shapes),
        out_shape=[shaped(shape, low) for shape in shapes],
        scratch_shapes=[pltpu.SemaphoreType.DMA((len(plan),))],
        cost_estimate=cost(1, 2 * sum(2 * piece.size for piece in pieces)),
        name="assemble",
    )(jnp.stack(spots).astype(jnp.int32), *pieces)


def gate_kernel(*refs):
    pass


def gate(arrays, tokens):
    anywhere = pl.BlockSpec(memory_space=pl.ANY)
    return launch(
        gate_kernel,
        tokens,
        in_specs=[anywhere] * len(arrays),
        out_specs=[anywhere] * len(arrays),
        out_shape=[shaped(array.shape, array.dtype) for array in arrays],
        input_output_aliases={k: k for k in range(len(arrays))},
        cost_estimate=cost(1, 1),
        name="gate",
    )(*arrays)


class Gather:
    def __init__(self, own, other):
        self.own, self.other = own, other
        self.stage = 0

    def pair(self):
        came = flip_core(self.other)
        pairs = [jnp.stack([self.own, came], axis=1), jnp.stack([came, self.own], axis=1)]
        return jnp.where(core_index() == 0, *pairs)

    @staticmethod
    def exchange(both, tokens=()):
        if tokens:
            (both,) = gate([both], tokens)
        own, other = jnp.split(both, 2)
        every = slice(None)
        plan = [(0, None, 0, lambda spot: (every, spot[0])), (1, None, 0, lambda spot: (every, 1 - spot[0]))]
        k, rows, columns = own.shape
        found = Gather(None, None)
        found.part = assemble(plan, [core_index()], [own, flip_core(other)], [(k, 2, rows, columns)])[0]
        found.part = found.part.reshape(k, 1, 2 * rows, columns)
        return found

    def start_slices(self, hops=False):
        self.pieces = [self.pair()]
        for j in range(1, lax.axis_size("img")):
            bit = j & -j if hops else j
            self.pieces.append(flip(self.pieces[j - bit], "img", bit))

    def finish_slices(self, tokens=(), groups=1):
        slices = len(self.pieces)
        if tokens:
            self.pieces = self.pieces[:1] + list(gate(self.pieces[1:], tokens))
        every = slice(None)
        k, _, rows, columns = self.pieces[0].shape
        k = k // groups
        plan = [
            (j, slice(n * k, (n + 1) * k), n, lambda spot, j=j: (every, every, spot[0] ^ j))
            for n in range(groups)
            for j in range(slices)
        ]
        shape = (k, 2, slices, rows, columns)
        parts = assemble(plan, [lax.axis_index("img")], self.pieces, [shape] * groups)
        found = []
        for part in parts:
            found.append(Gather(None, None))
            found[-1].part = part.reshape(k, 1, 2 * slices * rows, columns)
        return found

    def start_pos(self, tokens=()):
        if tokens:
            (self.part,) = gate([self.part], tokens)
        self.came = flip_pos(self.part, self.stage)
        self.stage += 1

    def finish_pos(self, tokens=()):
        every = slice(None)
        if tokens:
            (self.came,) = gate([self.came], tokens)
        plan = [
            (0, None, 0, lambda spot: (every, spot[0])),
            (1, None, 0, lambda spot: (every, 1 - spot[0])),
        ]
        shape = self.part.shape[:1] + (2,) + self.part.shape[1:]
        self.part = assemble(plan, [own_bit(self.stage - 1)], [self.part, self.came], [shape])[0]
        self.part = self.part.reshape((shape[0], -1) + shape[3:])
        return [self.part]

    def start_last(self):
        self.start_pos()
        self.turned = flip_core(self.part)

    def finish_last(self, tokens, turned_tokens):
        (self.turned,) = gate([self.turned], turned_tokens)
        (self.came,) = gate([self.came], tokens)
        return Pieces([self.part, self.came, self.turned, flip_core(self.came)])


def narrow_kernel(core_ref, weight_ref, *out_refs):
    first = core_ref[0] == 0
    slabs = out_refs[0].shape[0] // 2
    for k, out_ref in enumerate(out_refs):
        for n in range(slabs):
            columns = slice((k * slabs + n) * SLAB, (k * slabs + n + 1) * SLAB)
            left, right = weight_ref[0, :, columns].astype(low), weight_ref[1, :, columns].astype(low)
            out_ref[n] = jnp.where(first, left, right)
            out_ref[slabs + n] = jnp.where(first, right, left)


def narrow(weight, groups, tokens):
    _, owned, hidden = weight.shape
    slabs = hidden // SLAB // groups
    inside = pl.BlockSpec(memory_space=pltpu.VMEM)
    return launch(
        narrow_kernel,
        tokens,
        in_specs=[pl.BlockSpec(memory_space=pltpu.SMEM), inside],
        out_specs=[inside] * groups,
        out_shape=[shaped((2 * slabs, owned, SLAB), low)] * groups,
        cost_estimate=cost(1, 12 * slabs * groups * owned * SLAB),
        name="narrow",
    )(core_index().reshape(1), weight)


class Passing:
    def __init__(self, own, backward, direct):
        self.backward = backward
        came = flip_core(own.astype(low)).astype(wide)
        self.outside = jnp.where(core_index() == (0 if backward else 1), came, 0.0)
        self.total = own + came
        self.bits = powers(lax.axis_size("seq") // 2)
        if direct:
            both = self.total.astype(low)
            self.came = [flip(both, "seq", 2 * j) for j in range(1, lax.axis_size("seq") // 2)]

    def finish(self, tokens):
        total = self.outside
        for j, came in enumerate(gate(self.came, tokens), 1):
            earlier = (pos_index() ^ j) < pos_index()
            total = total + jnp.where(earlier != self.backward, came.astype(wide), 0.0)
        return total

    def hop(self, tokens):
        bit, *self.bits = self.bits
        (came,) = gate([flip(self.total.astype(low), "seq", 2 * bit)], tokens)
        came = came.astype(wide)
        earlier = (pos_index() ^ bit) < pos_index()
        self.outside = self.outside + jnp.where(earlier != self.backward, came, 0.0)
        self.total = self.total + came
        return self.outside


def body(
    images,
    cotangent,
    attention_weight,
    feedforward_weight,
    norm_vectors,
    attention_moment,
    feedforward_moment,
    norm_moment,
    attention_second,
    feedforward_second,
    norm_second,
    attention_average,
    feedforward_average,
    norm_average,
):
    count, span, width = images.shape
    tokens = count * span
    owned = attention_weight.shape[1]
    slabs = feedforward_weight.shape[2] // SLAB
    stages = pos_bits()
    half = slabs // 2
    every = slice(None)

    x, e = images.reshape(tokens, width), cotangent.reshape(tokens, width)
    low_weights = jnp.pad(attention_weight.astype(low), ((0, 0), (0, 0), (0, 128)))
    vectors = jnp.pad(norm_vectors.astype(low).T, ((0, 0), (width, 124)))
    query_weight, key_weight, value_weight, out_weight = low_weights
    kinds = jnp.stack([key_weight, query_weight]), jnp.stack([value_weight + vectors, out_weight])
    first_core = core_index() == 0
    one = Gather(jnp.where(first_core, *kinds), jnp.where(first_core, *kinds[::-1]))
    one.start_slices(True)
    et = turn(e, count, span)
    (one,) = one.finish_slices([et])
    one.start_pos()
    feeds = narrow(feedforward_weight, 2, [one.part])
    marks = [feeds[0]]
    feeds = [lax.all_gather(part, "img", axis=1, tiled=True) for part in feeds]
    for _ in range(stages - 2):
        one.finish_pos(marks)
        one.start_pos()
    one.finish_pos(marks)
    one.start_last()
    pieces = one.finish_last([one.part], [one.part])
    two = Gather.exchange(feeds[0])
    two.start_pos([one.came])
    vec = pieces.second(slice(width, width + 4)).astype(wide).T
    fk, v, a1, a1t, state, wk, wv = project(x, vec, pieces, count, span, [two.part])
    a1t_other = flip_core(a1t)
    prior = Passing(state, False, False)
    for _ in range(stages - 2):
        two.finish_pos([state])
        two.start_pos()
    two.finish_pos([state])
    two.start_last()
    fq, wq, wo = query(a1, pieces, [prior.outside, two.part])
    marks = [prior.hop([fq]), two.turned, a1t_other]
    num, den = attend(fq, fk, v, count, span, marks)
    while prior.bits:
        prior.hop([num])
    prior = prior.outside
    three = Gather.exchange(feeds[1], [num])
    three.start_pos()
    mixed, rden, resid, a2, a2t, mixed_t = mix(x, vec, wo, fq, num, den, prior, count, span, [three.part])
    a2t, mixed_t = turned_whole(a2t), turned_whole(mixed_t)
    lt = jnp.where(first_core, a2t, et)
    lt_other = flip_core(jnp.where(first_core, et, a2t))
    mixed_t_other = flip_core(mixed_t)
    first_pieces = two.finish_last([resid], [fq])
    marks = [resid]
    for _ in range(stages - 2):
        three.finish_pos(marks)
        three.start_pos()
    three.finish_pos(marks)
    three.start_last()
    marks = [three.part, three.turned]

    early = feed(first_pieces, a2, e, None, marks)
    early_other = flip_core(early[3])
    second_pieces = three.finish_last([early[0]], [early[0]])
    late = feed(second_pieces, a2, e, early[:2], [lt_other, mixed_t_other])
    late_other = flip_core(late[3])
    firsts, seconds, outs, inner = [Chain()], [Chain()], [Chain()], [Chain(3)]
    marks = weigh(firsts[0], lt, lt_other, early[2][None], early_other[None], [late[0]])
    output, dres, branch, branch_send, dn, w, dstate, sums_second = turn_back(
        late[0], late[1], resid, e, vec, wo, mixed, rden, fq, count, span, marks
    )
    later = Passing(dstate, True, True)
    branch_other = flip_core(branch_send)
    marks = [later.outside] + weigh(seconds[0], lt, lt_other, late[2][None], late_other[None], [dstate])
    marks = marks + weigh(outs[0], mixed_t, mixed_t_other, branch[None], branch_other[None], [dstate])
    for _ in range(stages - 1):
        marks = marks + advance(firsts)
    parts = [attend_back(0, fq, fk, v, dn, w, prior, span, marks)]
    firsts_last = Last(firsts, [parts[0][0]])
    marks = list(firsts_last.sends)
    for _ in range(stages - 1):
        marks = marks + advance(seconds + outs, [parts[0][0]])
    for image in range(1, count):
        parts.append(attend_back(image, fq, fk, v, dn, w, prior, span, marks))
    later = later.finish([parts[0][0]])
    marks = seconds[0].came + firsts_last.settle(slice(0, 2), [parts[-1][0]])
    kept, sent = finish(parts, fk, v, later, count, span, marks)
    marks = firsts_last.settle(slice(2, None), [kept])
    local_squares = firsts_last.squares()
    came = flip_core(sent)
    seconds_last = Last(seconds + outs, [kept])
    marks = marks + seconds_last.sends + [firsts_last.sums]
    grads_in = [enter(0, kept, sent, (wq, wk, wv), x, dres, vec, span, marks)]
    marks = seconds_last.settle(slice(0, 1), [grads_in[0][1]])
    marks = weigh(inner[0], a1t, a1t_other, kept, came, marks) + seconds_last.settle(slice(1, 2), [inner[0].kept])
    for image in range(1, count):
        grads_in.append(enter(image, kept, sent, (wq, wk, wv), x, dres, vec, span, marks))
    seconds_last.settle(slice(2, None), [grads_in[-1][1]])
    local_squares = local_squares + seconds_last.squares()
    input_grad = jnp.stack([part[0] for part in grads_in])
    marks = [seconds_last.sums]
    for _ in range(stages - 1):
        marks = advance(inner, marks)
    (sums,) = gate([sum(part[1] for part in grads_in)], marks)
    vector_grad = sum_slowly(jnp.concatenate([sums[:2], sums_second[:2]], axis=0))
    device = lax.axis_index("seq") * lax.axis_size("img") + lax.axis_index("img")
    vector_shard = lax.dynamic_slice_in_dim(vector_grad, device * owned, owned, 1)
    inner_last = Last(inner, [seconds_last.sums])
    local_squares = local_squares + jnp.sum(vector_shard * vector_shard)
    local_squares = local_squares + inner_last.squares()
    grad_norm = jnp.sqrt(sum_all(jnp.full((8, 128), local_squares))[0, 0])
    (early_shard,) = firsts_last.finish()
    late_shard, out_shard = seconds_last.finish()
    inner_shard = jnp.concatenate([part for pair in inner_last.finish() for part in pair], axis=2)
    attn_shard = jnp.concatenate([inner_shard, jnp.concatenate(out_shard, axis=2)], axis=0)
    feed_shard = jnp.concatenate([jnp.concatenate(pair, axis=2) for pair in zip(early_shard, late_shard)], axis=0)
    factor = clip_bound / jnp.maximum(grad_norm, clip_bound)
    attn_new = adam_update(
        attention_weight, attention_moment, attention_second, attention_average, attn_shard, factor, learn_rate
    )
    feed_new = adam_update(
        feedforward_weight, feedforward_moment, feedforward_second, feedforward_average, feed_shard, factor, learn_rate
    )
    norm_new = adam_update(norm_vectors, norm_moment, norm_second, norm_average, vector_shard, factor, norm_rate)
    output = output.reshape(images.shape)
    input_grad = input_grad.reshape(images.shape)
    return (output, input_grad, grad_norm) + attn_new + feed_new + norm_new


def solution(mesh):
    tokens = P("img", "seq", None)
    rows = P(None, ("seq", "img"), None)
    vectors = P(None, ("seq", "img"))
    group = (rows, rows, vectors)
    return jax.shard_map(
        body,
        mesh=mesh,
        in_specs=(tokens, tokens) + group * 4,
        out_specs=(tokens, tokens, P()) + (rows,) * 8 + (vectors,) * 4,
        check_vma=False,
    )
```

```python
import functools

import jax
import jax.numpy as jnp
import numpy as np
from jax import lax
from jax.experimental import pallas as pl
from jax.experimental.pallas import tpu as pltpu
from jax.sharding import PartitionSpec as P

HEADS = 16
HEAD_DIM = 64
STEP = 10

beta_first = 0.9
beta_second = 0.95
learn_rate = 0.02
norm_rate = 0.2
weight_decay = 0.1
average_decay = 0.75
clip_bound = 1.0
eps_norm = 1e-05
eps_adam = 1e-08

PAIR = 2 * HEAD_DIM
STATE_ROWS = HEAD_DIM + 16
SLAB = 1024
TILE = 512
GROUP = 256

low = jnp.bfloat16
wide = jnp.float32


def params(megabytes=56):
    return pltpu.CompilerParams(vmem_limit_bytes=megabytes * 1024 * 1024)


def cost(products, elements):
    return pl.CostEstimate(flops=2 * products, bytes_accessed=elements, transcendentals=0)


def launch(kernel, tokens, in_specs, megabytes=56, **keys):
    known, extra = len(in_specs), len(tokens)

    def run(*refs):
        kernel(*refs[:known], *refs[known + extra :])

    call = pl.pallas_call(
        run, in_specs=list(in_specs) + [pl.BlockSpec(memory_space=pl.ANY)] * extra, compiler_params=params(megabytes), **keys
    )
    return lambda *args: call(*args, *tokens)


def launch_at(kernel, spot, tokens, grid, in_specs, out_specs, megabytes=56, scratch_shapes=(), **keys):
    known, extra = len(in_specs), len(tokens)

    def run(spot_ref, *refs):
        kernel(spot_ref, *refs[:known], *refs[known + extra :])

    call = pl.pallas_call(
        run,
        grid_spec=pltpu.PrefetchScalarGridSpec(
            num_scalar_prefetch=1,
            grid=grid,
            in_specs=list(in_specs) + [pl.BlockSpec(memory_space=pl.ANY)] * extra,
            out_specs=out_specs,
            scratch_shapes=scratch_shapes,
        ),
        compiler_params=params(megabytes),
        **keys,
    )
    return lambda *args: call(spot.reshape(-1).astype(jnp.int32), *args, *tokens)


def reversed_bits(value, count):
    return sum(((value >> k) & 1) << (count - 1 - k) for k in range(count))


def join(target_ref, bits, spot_ref, own_ref, came_ref, own_other_ref, came_other_ref):
    core, high, lowest = spot_ref[0], spot_ref[1], spot_ref[2]
    runs = 1 << (bits - 1)
    rows = target_ref.shape[1] // (2 * runs)
    for run in range(runs):
        source = slice(run * rows, (run + 1) * rows)
        turned = reversed_bits(run, bits)
        for place in range(2):
            first = (high ^ place) * runs + run
            second = turned + (lowest ^ place)
            for ref, slot in (((own_ref, came_ref)[place], core), ((own_other_ref, came_other_ref)[place], 1 - core)):
                at = jnp.where(slot == 0, first, second)
                target_ref[slot, pl.ds(pl.multiple_of(at * rows, rows), rows), :] = ref[source, :]


class Pieces:
    def __init__(self, arrays):
        self.arrays = [array.reshape(array.shape[0], -1, array.shape[-1]) for array in arrays]
        place = pos_index()
        self.bits = pos_bits()
        self.spot = jnp.stack([core_index(), place >> (self.bits - 1), place & 1])

    def blocks(self, columns, place):
        rows = self.arrays[0].shape[1]
        return [pl.BlockSpec((None, rows, columns), place)] * 4

    def second(self, columns):
        mine, others = (
            [part[0, :, columns].reshape(1 << (self.bits - 1), 1, -1, columns.stop - columns.start) for part in pair]
            for pair in (self.arrays[:2], self.arrays[2:])
        )
        own, came = (jnp.where(core_index() == 1, left, right) for left, right in zip(mine, others))
        straight, turned = jnp.concatenate([own, came], axis=1), jnp.concatenate([came, own], axis=1)
        runs = jnp.where(self.spot[2] == 0, straight, turned)
        order = [reversed_bits(run, self.bits - 1) for run in range(1 << (self.bits - 1))]
        return jnp.stack([runs[run] for run in order]).reshape(-1, columns.stop - columns.start)


def shaped(shape, kind):
    return jax.ShapeDtypeStruct(shape, kind)


def whole(shape):
    return pl.BlockSpec(shape, lambda *_: (0,) * len(shape))


def mm(left, right):
    return lax.dot_general(left, right, (((1,), (0,)), ((), ())), preferred_element_type=wide)


def mt(left, right):
    return lax.dot_general(left, right, (((1,), (1,)), ((), ())), preferred_element_type=wide)


def tm(left, right):
    return lax.dot_general(left, right, (((0,), (0,)), ((), ())), preferred_element_type=wide)


def pair_mm(first, second):
    if first[0].shape[1] % 128:
        return mm(*first) + mm(*second)
    return mm(jnp.concatenate([first[0], second[0]], axis=1), jnp.concatenate([first[1], second[1]], axis=0))


def causal_mask(span, below):
    rows = lax.broadcasted_iota(jnp.int32, (span, span), 0)
    columns = lax.broadcasted_iota(jnp.int32, (span, span), 1)
    return (rows >= columns if below else rows <= columns).astype(wide).astype(low)


def first_head(rows):
    return lax.broadcasted_iota(jnp.int32, (rows, PAIR), 1) < HEAD_DIM


def fold_state(product):
    return jnp.where(first_head(HEAD_DIM), product[:HEAD_DIM], product[HEAD_DIM:])


def unfold_state(folded):
    own = first_head(HEAD_DIM)
    zero = jnp.zeros_like(folded)
    return jnp.concatenate([jnp.where(own, folded, zero), jnp.where(own, zero, folded)], axis=0)


def unfold_total(row):
    tall = jnp.broadcast_to(row, (PAIR, PAIR))
    lanes = lax.broadcasted_iota(jnp.int32, (PAIR, PAIR), 1) < HEAD_DIM
    rows = lax.broadcasted_iota(jnp.int32, (PAIR, PAIR), 0) < HEAD_DIM
    return jnp.where(lanes == rows, tall, jnp.zeros_like(tall))


def split_low(values):
    high = values.astype(low)
    return high, (values - high.astype(wide)).astype(low)


def normalised(values):
    centre = jnp.mean(values, axis=-1, keepdims=True)
    centred = values - centre
    spread = jnp.mean(centred * centred, axis=-1, keepdims=True)
    scale = lax.rsqrt(spread + eps_norm)
    return centred * scale, scale


def feature(raw):
    return jnp.where(raw > 0, raw + 1.0, jnp.exp(jnp.minimum(raw, 0.0))).astype(low)


def project_kernel(images, span, bits, spot_ref, x_ref, vec_ref, *refs):
    fk_ref, v_ref, a_ref, at_ref, state_ref, wk_ref, wv_ref, joined_ref = refs[4:]

    @pl.when(pl.program_id(0) == 0)
    def _():
        gain, shift = vec_ref[0:1, :], vec_ref[1:2, :]
        step = span // 3
        for start in range(0, images * span, step):
            rows = slice(start, start + step)
            unit, _ = normalised(x_ref[rows, :].astype(wide))
            a_ref[rows, :] = (unit * gain + shift).astype(low)
        at_ref[...] = a_ref[...].T

    join(joined_ref, bits, spot_ref, *refs[:4])
    keys, values = joined_ref[0], joined_ref[1]
    wk_ref[...] = keys
    wv_ref[...] = values
    fk_ref[...] = feature(mm(a_ref[...], keys))
    v_ref[...] = mm(a_ref[...], values).astype(low)
    ones = jnp.ones((16, span), low)
    for image in range(images):
        rows = slice(image * span, (image + 1) * span)
        for pair in range(GROUP // PAIR):
            lanes = slice(pair * PAIR, (pair + 1) * PAIR)
            key, value = fk_ref[rows, lanes], v_ref[rows, lanes]
            state_ref[image, pair, :HEAD_DIM, :] = fold_state(tm(value, key))
            state_ref[image, pair, HEAD_DIM:, :] = mm(ones, key)


def project(x, vec, pieces, images, span, tokens=()):
    count, width = x.shape
    pairs = GROUP // PAIR
    column = pl.BlockSpec((count, GROUP), lambda g, spot: (0, g))
    weight = pl.BlockSpec((width, GROUP), lambda g, spot: (0, g))
    return launch_at(
        functools.partial(project_kernel, images, span, pieces.bits),
        pieces.spot,
        tokens,
        grid=(width // GROUP,),
        in_specs=[whole((count, width)), whole(vec.shape)] + pieces.blocks(GROUP, lambda g, spot: (0, 0, g)),
        out_specs=[
            column,
            column,
            whole((count, width)),
            whole((width, count)),
            pl.BlockSpec((images, pairs, STATE_ROWS, PAIR), lambda g, spot: (0, g, 0, 0)),
            weight,
            weight,
        ],
        out_shape=[
            shaped((count, width), low),
            shaped((count, width), low),
            shaped((count, width), low),
            shaped((width, count), low),
            shaped((images, width // PAIR, STATE_ROWS, PAIR), wide),
            shaped((width, width), low),
            shaped((width, width), low),
        ],
        scratch_shapes=[pltpu.VMEM((2, width, GROUP), low)],
        cost_estimate=cost(2 * count * width * width, 8 * width * width + 12 * count * width),
        name="project",
    )(x, vec, *pieces.arrays)


def query_kernel(bits, spot_ref, a_ref, *refs):
    fq_ref, wq_ref, wo_ref, joined_ref = refs[4:]
    join(joined_ref, bits, spot_ref, *refs[:4])
    wq_ref[...] = joined_ref[0]
    wo_ref[...] = joined_ref[1]
    fq_ref[...] = feature(mm(a_ref[...], joined_ref[0]))


def query(a, pieces, tokens=()):
    count, width = a.shape
    weight = pl.BlockSpec((width, GROUP), lambda g, spot: (0, g))
    return launch_at(
        functools.partial(query_kernel, pieces.bits),
        pieces.spot,
        tokens,
        grid=(width // GROUP,),
        in_specs=[whole((count, width))] + pieces.blocks(GROUP, lambda g, spot: (1, 0, g)),
        out_specs=[pl.BlockSpec((count, GROUP), lambda g, spot: (0, g)), weight, weight],
        out_shape=[shaped((count, width), low)] + [shaped((width, width), low)] * 2,
        scratch_shapes=[pltpu.VMEM((2, width, GROUP), low)],
        cost_estimate=cost(count * width * width, 6 * width * width + 4 * count * width),
        name="query",
    )(a, *pieces.arrays)


def turn_kernel(x_ref, out_ref):
    out_ref[...] = x_ref[...].T


def turn(x, images, span, tokens=()):
    count, width = x.shape
    return turned_whole(
        launch(
            turn_kernel,
            tokens,
            grid=(images,),
            in_specs=[pl.BlockSpec((span, width), lambda b: (b, 0))],
            out_specs=turned_block(width, span),
            out_shape=turned_shape(images, width, span),
            cost_estimate=cost(1, 4 * count * width),
                name="turn",
        )(x)
    )


def attend_kernel(span, fq_ref, fk_ref, v_ref, num_ref, den_ref):
    own = first_head(span)
    causal = causal_mask(span, True)
    one = jnp.ones((span, PAIR), low)
    zero = jnp.zeros((span, PAIR), low)
    for pair in range(GROUP // PAIR):
        lanes = slice(pair * PAIR, (pair + 1) * PAIR)
        query, key, value = fq_ref[:, lanes], fk_ref[:, lanes], v_ref[:, lanes]
        products = []
        for mask in (own, jnp.logical_not(own)):
            scores = mt(jnp.where(mask, query, zero), key).astype(low) * causal
            right = jnp.concatenate([jnp.where(mask, value, zero), jnp.where(mask, one, zero)], axis=1)
            products.append((scores, right))
        total = pair_mm(*products)
        num_ref[:, lanes] = total[:, :PAIR]
        den_ref[:, lanes] = total[:, PAIR:]


def attend(fq, fk, v, images, span, tokens=()):
    rows, width = fq.shape
    block = pl.BlockSpec((span, GROUP), lambda b, p: (b, p))
    return launch(
        functools.partial(attend_kernel, span),
        tokens,
        grid=(images, width // GROUP),
        in_specs=[block] * 3,
        out_specs=[block] * 2,
        out_shape=[shaped((rows, width), wide)] * 2,
        cost_estimate=cost(16 * rows * span * width, 14 * rows * width),
        name="attend",
    )(fq, fk, v)


def turned_block(width, span):
    if span % 128:
        return pl.BlockSpec((None, width, span), lambda b: (b, 0, 0))
    return pl.BlockSpec((width, span), lambda b: (0, b))


def turned_shape(images, width, span):
    return shaped((images, width, span) if span % 128 else (width, images * span), low)


def turned_whole(array):
    if array.ndim == 2:
        return array
    return jnp.swapaxes(array, 0, 1).reshape(array.shape[1], -1)


def mix_kernel(x_ref, vec_ref, wo_ref, fq_ref, num_ref, den_ref, prior_ref, mixed_ref, rden_ref, resid_ref, a_ref, at_ref, mt_ref):
    width = x_ref.shape[1]
    for pair in range(width // PAIR):
        lanes = slice(pair * PAIR, (pair + 1) * PAIR)
        folded = prior_ref[0, pair]
        matrix = jnp.concatenate(
            [unfold_state(folded[:HEAD_DIM]), unfold_total(folded[HEAD_DIM : HEAD_DIM + 1])], axis=0
        )
        high, rest = split_low(matrix)
        query = fq_ref[:, lanes]
        both = mt(jnp.concatenate([query, query], axis=1), jnp.concatenate([high, rest], axis=1))
        scale = 1.0 / (den_ref[:, lanes] + both[:, PAIR:])
        rden_ref[:, lanes] = scale
        mixed_ref[:, lanes] = ((num_ref[:, lanes] + both[:, :PAIR]) * scale).astype(low)
    resid = x_ref[...].astype(wide) + mm(mixed_ref[...], wo_ref[...])
    resid_ref[...] = resid
    unit, _ = normalised(resid)
    normed = (unit * vec_ref[2:3, :] + vec_ref[3:4, :]).astype(low)
    a_ref[...] = normed
    at_ref[...] = normed.T
    mt_ref[...] = mixed_ref[...].T


def mix(x, vec, wo, fq, num, den, prior, images, span, tokens=()):
    rows_, width = x.shape
    rows = pl.BlockSpec((span, width), lambda b: (b, 0))
    return launch(
        mix_kernel,
        tokens,
        grid=(images,),
        in_specs=[
            rows,
            whole(vec.shape),
            whole(wo.shape),
            rows,
            rows,
            rows,
            pl.BlockSpec((1,) + prior.shape[1:], lambda b: (b, 0, 0, 0)),
        ],
        out_specs=[rows, rows, rows, rows, turned_block(width, span), turned_block(width, span)],
        out_shape=[
            shaped((rows_, width), low),
            shaped((rows_, width), wide),
            shaped((rows_, width), wide),
            shaped((rows_, width), low),
            turned_shape(images, width, span),
            turned_shape(images, width, span),
        ],
        cost_estimate=cost(4 * rows_ * width * width, 24 * rows_ * width + 2 * width * width),
        name="mix",
    )(x, vec, wo, fq, num, den, prior)


gelu_scale = 0.7978845608028654
gelu_cubic = 0.044715


def feed_kernel(fresh, bits, spot_ref, *refs):
    a_ref, e_ref = refs[:2]
    out_ref, da_ref, kept_ref, sent_ref, joined_ref = refs[-5:]
    join(joined_ref, bits, spot_ref, *refs[2:6])

    @pl.when(pl.program_id(0) == 0)
    def _():
        if fresh:
            out_ref[...] = jnp.zeros_like(out_ref)
            da_ref[...] = jnp.zeros_like(da_ref)
        else:
            out_ref[...] = refs[6][...]
            da_ref[...] = refs[7][...]

    up, down = joined_ref[0], joined_ref[1]
    upper = mm(a_ref[...], up)
    grad = mm(e_ref[...], down)
    square = upper * upper
    bend = jnp.tanh(gelu_scale * upper * (1.0 + gelu_cubic * square))
    gate = 0.5 + 0.5 * bend
    hidden = (upper * gate).astype(low)
    slope = gate + 0.5 * upper * (1.0 - bend * bend) * (gelu_scale * (1.0 + 3.0 * gelu_cubic * square))
    dupper = (grad * slope).astype(low)
    out_ref[...] += mt(hidden, down)
    da_ref[...] += mt(dupper, up)
    first = spot_ref[0] == 0
    kept_ref[...] = jnp.where(first, dupper, hidden)
    sent_ref[...] = jnp.where(first, hidden, dupper)


def feed(pieces, a, e, carried, tokens=()):
    rows, width = a.shape
    slabs = pieces.arrays[0].shape[0]
    tiles = SLAB // TILE
    grads = pl.BlockSpec((rows, TILE), lambda g, spot: (0, g))
    full = whole((rows, width))
    fresh = carried is None
    return launch_at(
        functools.partial(feed_kernel, fresh, pieces.bits),
        pieces.spot,
        tokens,
        grid=(slabs * tiles,),
        in_specs=[full, full]
        + pieces.blocks(TILE, lambda g, spot: (g // tiles, 0, g % tiles))
        + ([] if fresh else [full, full]),
        out_specs=[full, full, grads, grads],
        out_shape=[shaped((rows, width), wide)] * 2 + [shaped((rows, slabs * SLAB), low)] * 2,
        scratch_shapes=[pltpu.VMEM((2, width, TILE), low)],
        cost_estimate=cost(4 * rows * width * slabs * SLAB, 4 * (width + rows) * slabs * SLAB + 20 * rows * width),
        name="feed",
    )(a, e, *pieces.arrays, *(() if fresh else carried))


def weigh_kernel(count, spot_ref, lt_ref, lt_other_ref, x_ref, x_other_ref, kept_ref, sent_ref):
    rows = kept_ref.shape[1]
    for k in range(2):
        places = [pl.ds(pl.multiple_of(spot_ref[k * count + n] * rows, rows), rows) for n in range(count)]
        left, other = (jnp.concatenate([ref[place, :] for place in places], axis=0) for ref in (lt_ref, lt_other_ref))
        product = (mm(left, x_ref[...]) + mm(other, x_other_ref[...])).astype(low)
        (sent_ref if k else kept_ref)[...] = product.reshape(count, rows, -1)


def weigh(chain, lt, lt_other, x, x_other, tokens=()):
    lead, rows, columns = x.shape
    width = lt.shape[0]
    keeps, sends = chain.table()
    count = keeps.shape[0]
    tile = min(TILE, columns)
    full = whole((width, rows))
    column = pl.BlockSpec((None, rows, tile), lambda n, g, spot: (n, 0, g))
    result = pl.BlockSpec((None, count, width // (2 * count), tile), lambda n, g, spot: (n, 0, 0, g))
    chain.take(
        launch_at(
            functools.partial(weigh_kernel, count),
            jnp.concatenate([keeps, sends]),
            tokens,
            grid=(lead, columns // tile),
            in_specs=[full, full, column, column],
            out_specs=[result, result],
            out_shape=[shaped((lead, count, width // (2 * count), columns), low)] * 2,
            cost_estimate=cost(2 * lead * rows * width * columns, 4 * lead * (rows + width) * columns + 4 * rows * width),
            name="weigh",
        )(lt, lt_other, x, x_other)
    )
    chain.start()
    return chain.sends


def turn_back_kernel(core_ref, x_out_ref, da_ref, resid_ref, e_ref, vec_ref, wo_ref, mixed_ref, rden_ref, fq_ref,
                     out_ref, dres_ref, kept_ref, sent_ref, dn_ref, w_ref, state_ref, sums_ref):
    width = da_ref.shape[1]
    resid = resid_ref[...]
    out_ref[...] = (resid + x_out_ref[...]).astype(low)
    unit, scale = normalised(resid)
    da = da_ref[...]

    @pl.when(pl.program_id(0) == 0)
    def _():
        sums_ref[...] = jnp.zeros_like(sums_ref)

    sums_ref[0:1, :] += jnp.sum(da * unit, axis=0, keepdims=True)
    sums_ref[1:2, :] += jnp.sum(da, axis=0, keepdims=True)
    p = da * vec_ref[2:3, :]
    back = p - jnp.mean(p, axis=-1, keepdims=True) - unit * jnp.mean(p * unit, axis=-1, keepdims=True)
    dres = e_ref[...].astype(wide) + scale * back
    dres_ref[...] = dres
    branch = dres.astype(low)
    left, right = branch[:, : width // 2], branch[:, width // 2 :]
    first = core_ref[0] == 0
    kept_ref[...] = jnp.where(first, left, right)
    sent_ref[...] = jnp.where(first, right, left)
    dmixed = mt(branch, wo_ref[...]).astype(low).astype(wide)
    dnumer = dmixed * rden_ref[...]
    dn_ref[...] = dnumer.astype(low)
    w_ref[...] = (-dnumer * mixed_ref[...].astype(wide)).astype(low)
    for pair in range(width // PAIR):
        lanes = slice(pair * PAIR, (pair + 1) * PAIR)
        query = fq_ref[:, lanes]
        state_ref[0, pair, :HEAD_DIM, :] = fold_state(tm(dn_ref[:, lanes], query))
        total = jnp.sum(fold_state(tm(w_ref[:, lanes], query)), axis=0, keepdims=True)
        state_ref[0, pair, HEAD_DIM:, :] = jnp.broadcast_to(total, (STATE_ROWS - HEAD_DIM, PAIR))


def turn_back(x_out, da, resid, e, vec, wo, mixed, rden, fq, images, span, tokens=()):
    rows_, width = da.shape
    rows = pl.BlockSpec((span, width), lambda b, core: (b, 0))
    state = (images, width // PAIR, STATE_ROWS, PAIR)
    half = pl.BlockSpec((span, width // 2), lambda b, core: (b, 0))
    return launch_at(
        turn_back_kernel,
        core_index(),
        tokens,
        grid=(images,),
        in_specs=[rows, rows, rows, rows, whole(vec.shape), whole(wo.shape), rows, rows, rows],
        out_specs=[rows, rows, half, half, rows, rows] + [pl.BlockSpec((1,) + state[1:], lambda b, core: (b, 0, 0, 0)), whole((8, width))],
        out_shape=[
            shaped((rows_, width), low),
            shaped((rows_, width), wide),
            shaped((rows_, width // 2), low),
            shaped((rows_, width // 2), low),
            shaped((rows_, width), low),
            shaped((rows_, width), low),
            shaped(state, wide),
            shaped((8, width), wide),
        ],
        cost_estimate=cost(5 * rows_ * width * width, 30 * rows_ * width),
        name="turn_back",
    )(x_out, da, resid, e, vec, wo, mixed, rden, fq)


def attend_back_kernel(span, fq_ref, fk_ref, v_ref, dn_ref, w_ref, prior_ref, dq_ref, dfk_ref, dv_ref):
    own = first_head(span)
    own_twice = jnp.concatenate([own, own], axis=1)
    below, above = causal_mask(span, True), causal_mask(span, False)
    one = jnp.ones((span, PAIR), low)
    zero = jnp.zeros((span, PAIR), low)
    zero_twice = jnp.zeros((span, 2 * PAIR), low)
    for pair in range(GROUP // PAIR):
        lanes = slice(pair * PAIR, (pair + 1) * PAIR)
        query, key, value = fq_ref[:, lanes], fk_ref[:, lanes], v_ref[:, lanes]
        grads = jnp.concatenate([dn_ref[:, lanes], w_ref[:, lanes]], axis=1)
        extended = jnp.concatenate([value, one], axis=1)
        folded = prior_ref[0, pair]
        matrix = jnp.concatenate(
            [unfold_state(folded[:HEAD_DIM]), unfold_total(folded[HEAD_DIM : HEAD_DIM + 1])], axis=0
        )
        high, rest = split_low(matrix)
        dfq = mm(jnp.concatenate([grads, grads], axis=1), jnp.concatenate([high, rest], axis=0))
        to_query, to_key, to_value = [], [], []
        for mask, both in ((own, own_twice), (jnp.logical_not(own), jnp.logical_not(own_twice))):
            head_grads = jnp.where(both, grads, zero_twice)
            head_query = jnp.where(mask, query, zero)
            head_key = jnp.where(mask, key, zero)
            to_query.append((mt(head_grads, extended).astype(low) * below, head_key))
            to_key.append((mt(extended, head_grads).astype(low) * above, head_query))
            to_value.append((mt(head_key, query).astype(low) * above, head_grads[:, :PAIR]))
        dfq = dfq + pair_mm(*to_query)
        dq_ref[:, lanes] = (dfq * jnp.minimum(query.astype(wide), 1.0)).astype(low)
        dfk_ref[:, lanes] = pair_mm(*to_key)
        dv_ref[:, lanes] = pair_mm(*to_value)


def attend_back(image, fq, fk, v, dn, w, prior, span, tokens=()):
    width = fq.shape[1]
    block = pl.BlockSpec((span, GROUP), lambda p: (image, p))
    column = pl.BlockSpec((span, GROUP), lambda p: (0, p))
    return launch(
        functools.partial(attend_back_kernel, span),
        tokens,
        grid=(width // GROUP,),
        in_specs=[block] * 5 + [pl.BlockSpec((1, GROUP // PAIR) + prior.shape[2:], lambda p: (image, p, 0, 0))],
        out_specs=[column] * 3,
        out_shape=[shaped((span, width), low), shaped((span, width), wide), shaped((span, width), wide)],
        cost_estimate=cost(32 * span * span * width, 24 * span * width),
        name="attend_back",
    )(fq, fk, v, dn, w, prior)


def finish_kernel(images, span, core_ref, *refs):
    fk_ref, v_ref, later_ref, kept_ref, sent_ref = refs[3 * images :]

    def run(out_ref):
        for image in range(images):
            rows = slice(image * span, (image + 1) * span)
            dq_ref, dfk_ref, dvl_ref = refs[3 * image : 3 * image + 3]
            out_ref[0, rows, :] = dq_ref[...]
            for pair in range(GROUP // PAIR):
                lanes = slice(pair * PAIR, (pair + 1) * PAIR)
                folded = later_ref[image, pair]
                high, rest = split_low(unfold_state(folded[:HEAD_DIM]))
                key, value = fk_ref[rows, lanes], v_ref[rows, lanes]
                dfk = dfk_ref[:, lanes] + folded[HEAD_DIM : HEAD_DIM + 1]
                dfk = dfk + mm(jnp.concatenate([value, value], axis=1), jnp.concatenate([high, rest], axis=0))
                dv = dvl_ref[:, lanes] + mt(
                    jnp.concatenate([key, key], axis=1), jnp.concatenate([high, rest], axis=1)
                )
                out_ref[1, rows, lanes] = (dfk * jnp.minimum(key.astype(wide), 1.0)).astype(low)
                out_ref[2, rows, lanes] = dv.astype(low)

    @pl.when(pl.program_id(0) < pl.num_programs(0) // 2)
    def _():
        run(kept_ref)

    @pl.when(pl.program_id(0) >= pl.num_programs(0) // 2)
    def _():
        run(sent_ref)


def finish(parts, fk, v, later, images, span, tokens=()):
    rows, width = fk.shape
    groups = width // GROUP // 2

    def column(g, core):
        return ((g // groups) ^ core[0]) * groups + g % groups

    block = pl.BlockSpec((rows, GROUP), lambda g, core: (0, column(g, core)))
    part = pl.BlockSpec((span, GROUP), lambda g, core: (0, column(g, core)))
    state = pl.BlockSpec((images, GROUP // PAIR) + later.shape[2:], lambda g, core: (0, column(g, core), 0, 0))
    return launch_at(
        functools.partial(finish_kernel, images, span),
        core_index(),
        tokens,
        grid=(2 * groups,),
        in_specs=[part] * (3 * images) + [block] * 2 + [state],
        out_specs=[
            pl.BlockSpec((3, rows, GROUP), lambda g, core: (0, 0, jnp.minimum(g, groups - 1))),
            pl.BlockSpec((3, rows, GROUP), lambda g, core: (0, 0, jnp.maximum(g - groups, 0))),
        ],
        out_shape=[shaped((3, rows, width // 2), low)] * 2,
        cost_estimate=cost(rows * width * 512, 24 * rows * width),
        name="finish",
    )(*[array for image in parts for array in image], fk, v, later)


def enter_kernel(core_ref, kept_ref, sent_ref, *refs):
    weights = refs[:3]
    x_ref, dres_ref, vec_ref, grad_ref, sums_ref = refs[3:]
    half = x_ref.shape[1] // 2
    da = None
    for k, weight in enumerate(weights):
        for ref, side in ((kept_ref, core_ref[0]), (sent_ref, 1 - core_ref[0])):
            part = mt(ref[k], weight[:, pl.ds(pl.multiple_of(side * half, half), half)])
            da = part if da is None else da + part
    unit, scale = normalised(x_ref[...].astype(wide))
    sums_ref[0:1, :] = jnp.sum(da * unit, axis=0, keepdims=True)
    sums_ref[1:2, :] = jnp.sum(da, axis=0, keepdims=True)
    sums_ref[2:, :] = jnp.zeros_like(sums_ref[2:, :])
    p = da * vec_ref[0:1, :]
    back = p - jnp.mean(p, axis=-1, keepdims=True) - unit * jnp.mean(p * unit, axis=-1, keepdims=True)
    grad_ref[...] = (dres_ref[...] + scale * back).astype(low)


def enter(image, kept, sent, weights, x, dres, vec, span, tokens=()):
    width = x.shape[1]
    rows = pl.BlockSpec((span, width), lambda g, core: (image, 0))
    part = pl.BlockSpec((3, span, width // 2), lambda g, core: (0, image, 0))
    return launch_at(
        enter_kernel,
        core_index(),
        tokens,
        grid=(1,),
        in_specs=[part] * 2 + [whole((width, width))] * 3 + [rows, rows, whole(vec.shape)],
        out_specs=[whole((span, width)), whole((8, width))],
        out_shape=[shaped((span, width), low), shaped((8, width), wide)],
        cost_estimate=cost(3 * span * width * width, 14 * span * width + 6 * width * width),
        name="enter",
    )(kept, sent, *weights, x, dres, vec)


def adam_update(master, moment, second, average, gradient, factor, rate):
    clipped = gradient * factor
    moment = beta_first * moment + (1.0 - beta_first) * clipped
    second = beta_second * second + (1.0 - beta_second) * clipped * clipped
    first_hat = moment / (1.0 - beta_first**STEP)
    second_hat = second / (1.0 - beta_second**STEP)
    master = master - rate * (first_hat / (jnp.sqrt(second_hat) + eps_adam) + weight_decay * master)
    average = average_decay * average + (1.0 - average_decay) * master
    return (master, moment, second, average)


def powers(count):
    return [1 << k for k in range(count.bit_length() - 1)]


def core_index():
    return lax.axis_index("seq") % 2


def pos_index():
    return lax.axis_index("seq") // 2


def pos_bits():
    return (lax.axis_size("seq") // 2).bit_length() - 1


def flip(array, axis, bit):
    return lax.ppermute(array, axis, [(i, i ^ bit) for i in range(lax.axis_size(axis))])


def flip_core(array):
    return flip(array, "seq", 1)


def flip_pos(array, stage):
    bits = pos_bits()
    pairs = [(i, i ^ (2 << (stage if i % 2 == 0 else bits - 1 - stage))) for i in range(lax.axis_size("seq"))]
    return lax.ppermute(array, "seq", pairs)


def own_bit(stage):
    bits = pos_bits()
    return jnp.where(core_index() == 0, pos_index() >> stage, pos_index() >> (bits - 1 - stage)) & 1


def halves(shape, dim):
    index = np.arange(int(np.prod(shape))).reshape(shape)
    return np.stack([index.take(side, axis=dim).ravel() for side in range(2)])


def fold_kernel(chains, spot_ref, *refs):
    ins, outs = refs[: 4 * chains], refs[4 * chains :]
    for k in range(2 * chains):
        value = ins[2 * k][...].astype(wide) + ins[2 * k + 1][...].astype(wide)
        outs[k][...] = value.astype(outs[k].dtype)


def fold(cuts, tokens=()):
    count = cuts[0][2].shape[0]
    steps = max(1, min(2, min(kept.shape[-1] for kept, *_ in cuts) // 256))
    in_specs, out_specs, out_shape, arrays, moved = [], [], [], [], 0
    for k, (kept, came, keeps, sends) in enumerate(cuts):
        lead, _, rows, columns = kept.shape
        block = (lead, 1, rows, columns // steps)
        for side in range(2):
            at = 2 * k * count + side * count
            spec = pl.BlockSpec(block, lambda g, c, spot, at=at: (0, spot[at + g], 0, c))
            in_specs += [spec, spec]
            arrays += [kept, came]
            out_specs.append(pl.BlockSpec(block, lambda g, c, spot: (0, g, 0, c)))
            out_shape.append(shaped((lead, count, rows, columns), low if side else wide))
        moved += 8 * kept.size
    results = launch_at(
        functools.partial(fold_kernel, len(cuts)),
        jnp.concatenate([part for _, _, keeps, sends in cuts for part in (keeps, sends)]),
        tokens,
        grid=(count, steps),
        in_specs=in_specs,
        out_specs=out_specs,
        out_shape=out_shape,
        cost_estimate=cost(1, moved),
        name="fold",
    )(*arrays)
    return [results[2 * k : 2 * k + 2] for k in range(len(cuts))]


class Chain:
    def __init__(self, lead=1):
        self.lead = lead
        self.stage = -1
        self.left = [list(range(pos_bits()))[::-1]] * 2

    def start(self):
        self.came = [flip_pos(self.sends[0], self.stage)]

    def table(self):
        self.stage += 1
        tables = []
        for kind in range(2):
            bit = self.stage if kind == 0 else pos_bits() - 1 - self.stage
            left = self.left[kind]
            tables.append(halves((2,) * len(left), left.index(bit)))
            self.left[kind] = [other for other in left if other != bit]
        table = jnp.where(core_index() == 0, *[jnp.asarray(part, jnp.int32) for part in tables])
        own = own_bit(self.stage)
        return table[own], table[1 - own]

    def cut(self):
        return (self.kept, self.came[0], *self.table())

    def take(self, parts):
        self.kept, self.sends = parts[0], [parts[1]]


def advance(chains, tokens=()):
    parts = fold([chain.cut() for chain in chains], tokens)
    for chain, part in zip(chains, parts):
        chain.take(part)
        chain.start()
    return [array for chain in chains for array in chain.sends]


def last_kernel(ways, pre, pieces, spot_ref, *refs):
    ins, outs = refs[: 2 * pieces], refs[2 * pieces :]
    at = 0
    for k in range(pieces):
        columns = ins[2 * k].shape[-1]
        for j in range(ways):
            place = spot_ref[0] ^ j
            for n in range(pre):
                value = ins[2 * k][n, place].astype(wide) + ins[2 * k + 1][n, place].astype(wide)
                outs[j][n, :, at : at + columns] = value.astype(outs[j].dtype)
        at += columns


class Last:
    def __init__(self, chains, tokens=(), slowly=False):
        slices = lax.axis_size("img")
        ways = 2 if slowly else slices
        self.lead = chains[0].lead
        pre = self.lead * 2 * slices // ways
        arrays = []
        for chain in chains:
            for array in (chain.kept, chain.came[0]):
                arrays.append(array.reshape(pre, ways, -1, array.shape[-1]))
        self.widths = [array.shape[-1] for array in arrays[::2]]
        inside = pl.BlockSpec(memory_space=pltpu.VMEM)
        parts = launch(
            functools.partial(last_kernel, ways, pre, len(chains)),
            tokens,
            in_specs=[pl.BlockSpec(memory_space=pltpu.SMEM)] + [inside] * len(arrays),
            out_specs=[inside] * ways,
            out_shape=[shaped((pre, arrays[0].shape[2], sum(self.widths)), low if j else wide) for j in range(ways)],
            cost_estimate=cost(1, 4 * sum(array.size for array in arrays)),
                name="last",
        )((lax.axis_index("img") % ways).reshape(1), *arrays)
        self.kept, self.sends = parts[0], list(parts[1:])
        self.hops = list(range(1, ways))
        self.left = powers(slices)[1:][::-1] if slowly else []
        self.start()

    def start(self):
        self.came = [flip(array, "img", hop) for array, hop in zip(self.sends, self.hops)]

    def cut(self):
        bit = self.left[-1]
        entries = self.kept.reshape((1, -1) + self.kept.shape[-2:])
        dims = (2 * self.lead,) + (2,) * len(self.left)
        table = jnp.asarray(halves(dims, len(dims) - 1), jnp.int32)
        own = (lax.axis_index("img") // bit) % 2
        self.left = self.left[:-1]
        self.hops = [bit]
        return (entries, self.came[0].reshape(entries.shape), table[own], table[1 - own])

    def take(self, parts):
        self.kept, self.sends = parts[0][0], [parts[1][0]]

    def total(self):
        while self.left:
            advance([self])
        total = self.kept
        for came in self.came:
            total = total + came.astype(wide)
        return total

    def settle(self, stretch, tokens):
        self.came[stretch] = gate(self.came[stretch], tokens)
        return self.came[stretch]

    def squares(self):
        self.sums = self.total()
        return jnp.sum(self.sums * self.sums)

    def finish(self):
        core = core_index()
        total = self.sums.reshape((self.lead, 2) + self.sums.shape[-2:])
        own = lax.dynamic_index_in_dim(total, core, 1, False)
        came = flip_core(lax.dynamic_index_in_dim(total, 1 - core, 1, False))
        first, second = jnp.where(core == 0, own, came), jnp.where(core == 0, came, own)
        at, found = 0, []
        for columns in self.widths:
            found.append((first[..., at : at + columns], second[..., at : at + columns]))
            at += columns
        return found


def sum_slowly(array):
    for axis in ("seq", "img"):
        for bit in powers(lax.axis_size(axis)):
            array = array + flip(array, axis, bit)
    return array


def sum_all(array):
    rounds = [("img", range(1, lax.axis_size("img"))), ("seq", range(2, lax.axis_size("seq"), 2)), ("seq", [1])]
    for axis, hops in rounds:
        came = [flip(array, axis, hop) for hop in hops]
        for other in came:
            array = array + other
    return array


def assemble_kernel(plan, spot_ref, *refs):
    outs = sorted({out for _, _, out, _ in plan})
    count = len(refs) - 1 - len(outs)
    sems = refs[-1]
    copies = []
    for k, (piece, cut, out, where) in enumerate(plan):
        source = refs[piece].at[cut] if cut is not None else refs[piece]
        target = refs[count + out].at[where(spot_ref)]
        copies.append(pltpu.make_async_copy(source, target, sems.at[k]))
    for copy in copies:
        copy.start()
    for copy in copies:
        copy.wait()


def assemble(plan, spots, pieces, shapes, tokens=()):
    anywhere = pl.BlockSpec(memory_space=pl.ANY)
    return launch(
        functools.partial(assemble_kernel, plan),
        tokens,
        in_specs=[pl.BlockSpec(memory_space=pltpu.SMEM)] + [anywhere] * len(pieces),
        out_specs=[pl.BlockSpec(memory_space=pltpu.VMEM)] * len(shapes),
        out_shape=[shaped(shape, low) for shape in shapes],
        scratch_shapes=[pltpu.SemaphoreType.DMA((len(plan),))],
        cost_estimate=cost(1, 2 * sum(2 * piece.size for piece in pieces)),
        name="assemble",
    )(jnp.stack(spots).astype(jnp.int32), *pieces)


def gate_kernel(*refs):
    pass


def gate(arrays, tokens):
    anywhere = pl.BlockSpec(memory_space=pl.ANY)
    return launch(
        gate_kernel,
        tokens,
        in_specs=[anywhere] * len(arrays),
        out_specs=[anywhere] * len(arrays),
        out_shape=[shaped(array.shape, array.dtype) for array in arrays],
        input_output_aliases={k: k for k in range(len(arrays))},
        cost_estimate=cost(1, 1),
        name="gate",
    )(*arrays)


class Gather:
    def __init__(self, own, other):
        self.own, self.other = own, other
        self.stage = 0

    def pair(self):
        came = flip_core(self.other)
        pairs = [jnp.stack([self.own, came], axis=1), jnp.stack([came, self.own], axis=1)]
        return jnp.where(core_index() == 0, *pairs)

    @staticmethod
    def exchange(both, tokens=()):
        if tokens:
            (both,) = gate([both], tokens)
        own, other = jnp.split(both, 2)
        every = slice(None)
        plan = [(0, None, 0, lambda spot: (every, spot[0])), (1, None, 0, lambda spot: (every, 1 - spot[0]))]
        k, rows, columns = own.shape
        found = Gather(None, None)
        found.part = assemble(plan, [core_index()], [own, flip_core(other)], [(k, 2, rows, columns)])[0]
        found.part = found.part.reshape(k, 1, 2 * rows, columns)
        return found

    def start_slices(self, hops=False):
        self.pieces = [self.pair()]
        for j in range(1, lax.axis_size("img")):
            bit = j & -j if hops else j
            self.pieces.append(flip(self.pieces[j - bit], "img", bit))

    def finish_slices(self, tokens=(), groups=1):
        slices = len(self.pieces)
        if tokens:
            self.pieces = self.pieces[:1] + list(gate(self.pieces[1:], tokens))
        every = slice(None)
        k, _, rows, columns = self.pieces[0].shape
        k = k // groups
        plan = [
            (j, slice(n * k, (n + 1) * k), n, lambda spot, j=j: (every, every, spot[0] ^ j))
            for n in range(groups)
            for j in range(slices)
        ]
        shape = (k, 2, slices, rows, columns)
        parts = assemble(plan, [lax.axis_index("img")], self.pieces, [shape] * groups)
        found = []
        for part in parts:
            found.append(Gather(None, None))
            found[-1].part = part.reshape(k, 1, 2 * slices * rows, columns)
        return found

    def start_pos(self, tokens=()):
        if tokens:
            (self.part,) = gate([self.part], tokens)
        self.came = flip_pos(self.part, self.stage)
        self.stage += 1

    def finish_pos(self, tokens=()):
        every = slice(None)
        if tokens:
            (self.came,) = gate([self.came], tokens)
        plan = [
            (0, None, 0, lambda spot: (every, spot[0])),
            (1, None, 0, lambda spot: (every, 1 - spot[0])),
        ]
        shape = self.part.shape[:1] + (2,) + self.part.shape[1:]
        self.part = assemble(plan, [own_bit(self.stage - 1)], [self.part, self.came], [shape])[0]
        self.part = self.part.reshape((shape[0], -1) + shape[3:])
        return [self.part]

    def start_last(self):
        self.start_pos()
        self.turned = flip_core(self.part)

    def finish_last(self, tokens, turned_tokens):
        (self.turned,) = gate([self.turned], turned_tokens)
        (self.came,) = gate([self.came], tokens)
        return Pieces([self.part, self.came, self.turned, flip_core(self.came)])


def narrow_kernel(core_ref, weight_ref, *out_refs):
    first = core_ref[0] == 0
    slabs = out_refs[0].shape[0] // 2
    for k, out_ref in enumerate(out_refs):
        for n in range(slabs):
            columns = slice((k * slabs + n) * SLAB, (k * slabs + n + 1) * SLAB)
            left, right = weight_ref[0, :, columns].astype(low), weight_ref[1, :, columns].astype(low)
            out_ref[n] = jnp.where(first, left, right)
            out_ref[slabs + n] = jnp.where(first, right, left)


def narrow(weight, groups, tokens):
    _, owned, hidden = weight.shape
    slabs = hidden // SLAB // groups
    inside = pl.BlockSpec(memory_space=pltpu.VMEM)
    return launch(
        narrow_kernel,
        tokens,
        in_specs=[pl.BlockSpec(memory_space=pltpu.SMEM), inside],
        out_specs=[inside] * groups,
        out_shape=[shaped((2 * slabs, owned, SLAB), low)] * groups,
        cost_estimate=cost(1, 12 * slabs * groups * owned * SLAB),
        name="narrow",
    )(core_index().reshape(1), weight)


class Passing:
    def __init__(self, own, backward, direct):
        self.backward = backward
        came = flip_core(own.astype(low)).astype(wide)
        self.outside = jnp.where(core_index() == (0 if backward else 1), came, 0.0)
        self.total = own + came
        self.bits = powers(lax.axis_size("seq") // 2)
        if direct:
            both = self.total.astype(low)
            self.came = [flip(both, "seq", 2 * j) for j in range(1, lax.axis_size("seq") // 2)]

    def finish(self, tokens):
        total = self.outside
        for j, came in enumerate(gate(self.came, tokens), 1):
            earlier = (pos_index() ^ j) < pos_index()
            total = total + jnp.where(earlier != self.backward, came.astype(wide), 0.0)
        return total

    def hop(self, tokens):
        bit, *self.bits = self.bits
        (came,) = gate([flip(self.total.astype(low), "seq", 2 * bit)], tokens)
        came = came.astype(wide)
        earlier = (pos_index() ^ bit) < pos_index()
        self.outside = self.outside + jnp.where(earlier != self.backward, came, 0.0)
        self.total = self.total + came
        return self.outside


def body(
    images,
    cotangent,
    attention_weight,
    feedforward_weight,
    norm_vectors,
    attention_moment,
    feedforward_moment,
    norm_moment,
    attention_second,
    feedforward_second,
    norm_second,
    attention_average,
    feedforward_average,
    norm_average,
):
    count, span, width = images.shape
    tokens = count * span
    owned = attention_weight.shape[1]
    slabs = feedforward_weight.shape[2] // SLAB
    stages = pos_bits()
    half = slabs // 2
    every = slice(None)

    x, e = images.reshape(tokens, width), cotangent.reshape(tokens, width)
    low_weights = jnp.pad(attention_weight.astype(low), ((0, 0), (0, 0), (0, 128)))
    vectors = jnp.pad(norm_vectors.astype(low).T, ((0, 0), (width, 124)))
    query_weight, key_weight, value_weight, out_weight = low_weights
    kinds = jnp.stack([key_weight, query_weight]), jnp.stack([value_weight + vectors, out_weight])
    first_core = core_index() == 0
    one = Gather(jnp.where(first_core, *kinds), jnp.where(first_core, *kinds[::-1]))
    one.start_slices(True)
    et = turn(e, count, span)
    (one,) = one.finish_slices([et])
    one.start_pos()
    feeds = narrow(feedforward_weight, 2, [one.part])
    marks = [feeds[0]]
    feeds = [lax.all_gather(part, "img", axis=1, tiled=True) for part in feeds]
    for _ in range(stages - 2):
        one.finish_pos(marks)
        one.start_pos()
    one.finish_pos(marks)
    one.start_last()
    pieces = one.finish_last([one.part], [one.part])
    two = Gather.exchange(feeds[0])
    two.start_pos([one.came])
    vec = pieces.second(slice(width, width + 4)).astype(wide).T
    fk, v, a1, a1t, state, wk, wv = project(x, vec, pieces, count, span, [two.part])
    a1t_other = flip_core(a1t)
    prior = Passing(state, False, False)
    for _ in range(stages - 2):
        two.finish_pos([state])
        two.start_pos()
    two.finish_pos([state])
    two.start_last()
    fq, wq, wo = query(a1, pieces, [prior.outside, two.part])
    marks = [prior.hop([fq]), two.turned, a1t_other]
    num, den = attend(fq, fk, v, count, span, marks)
    while prior.bits:
        prior.hop([num])
    prior = prior.outside
    three = Gather.exchange(feeds[1], [num])
    three.start_pos()
    mixed, rden, resid, a2, a2t, mixed_t = mix(x, vec, wo, fq, num, den, prior, count, span, [three.part])
    a2t, mixed_t = turned_whole(a2t), turned_whole(mixed_t)
    lt = jnp.where(first_core, a2t, et)
    lt_other = flip_core(jnp.where(first_core, et, a2t))
    mixed_t_other = flip_core(mixed_t)
    first_pieces = two.finish_last([resid], [fq])
    marks = [resid]
    for _ in range(stages - 2):
        three.finish_pos(marks)
        three.start_pos()
    three.finish_pos(marks)
    three.start_last()
    marks = [three.part, three.turned]

    early = feed(first_pieces, a2, e, None, marks)
    early_other = flip_core(early[3])
    second_pieces = three.finish_last([early[0]], [early[0]])
    late = feed(second_pieces, a2, e, early[:2], [lt_other, mixed_t_other])
    late_other = flip_core(late[3])
    firsts, seconds, outs, inner = [Chain()], [Chain()], [Chain()], [Chain(3)]
    marks = weigh(firsts[0], lt, lt_other, early[2][None], early_other[None], [late[0]])
    output, dres, branch, branch_send, dn, w, dstate, sums_second = turn_back(
        late[0], late[1], resid, e, vec, wo, mixed, rden, fq, count, span, marks + [late_other]
    )
    later = Passing(dstate, True, False)
    marks = weigh(seconds[0], lt, lt_other, late[2][None], late_other[None], [dstate, later.outside])
    passed = later.hop([seconds[0].kept])
    for _ in range(stages - 1):
        marks = marks + advance(firsts, [passed])
    parts = [attend_back(0, fq, fk, v, dn, w, prior, span, marks)]
    branch_other = flip_core(gate([branch_send], [parts[0][0]])[0])
    firsts_last = Last(firsts, [parts[0][0]])
    marks = weigh(outs[0], mixed_t, mixed_t_other, branch[None], branch_other[None], firsts_last.sends)
    for _ in range(stages - 1):
        marks = marks + advance(seconds, [parts[0][0]])
    for image in range(1, count):
        parts.append(attend_back(image, fq, fk, v, dn, w, prior, span, marks))
    for _ in range(stages - 1):
        marks = advance(outs, [parts[-1][0]])
    marks = marks + seconds[0].came + firsts_last.settle(slice(0, None), [parts[-1][0]])
    while later.bits:
        later.hop([parts[-1][0]])
    later = later.outside
    kept, sent = finish(parts, fk, v, later, count, span, marks)
    local_squares = firsts_last.squares()
    came = flip_core(sent)
    seconds_last = Last(seconds + outs, [kept])
    marks = seconds_last.sends + [firsts_last.sums]
    grads_in = [enter(0, kept, sent, (wq, wk, wv), x, dres, vec, span, marks)]
    marks = seconds_last.settle(slice(0, 2), [grads_in[0][1]])
    marks = weigh(inner[0], a1t, a1t_other, kept, came, marks)
    for image in range(1, count):
        grads_in.append(enter(image, kept, sent, (wq, wk, wv), x, dres, vec, span, marks))
    seconds_last.settle(slice(2, None), [grads_in[-1][1]])
    local_squares = local_squares + seconds_last.squares()
    input_grad = jnp.stack([part[0] for part in grads_in])
    marks = [seconds_last.sums]
    for _ in range(stages - 1):
        marks = advance(inner, marks)
    (sums,) = gate([sum(part[1] for part in grads_in)], marks)
    vector_grad = sum_slowly(jnp.concatenate([sums[:2], sums_second[:2]], axis=0))
    device = lax.axis_index("seq") * lax.axis_size("img") + lax.axis_index("img")
    vector_shard = lax.dynamic_slice_in_dim(vector_grad, device * owned, owned, 1)
    inner_last = Last(inner, [seconds_last.sums])
    local_squares = local_squares + jnp.sum(vector_shard * vector_shard)
    local_squares = local_squares + inner_last.squares()
    grad_norm = jnp.sqrt(sum_all(jnp.full((8, 128), local_squares))[0, 0])
    (early_shard,) = firsts_last.finish()
    late_shard, out_shard = seconds_last.finish()
    inner_shard = jnp.concatenate([part for pair in inner_last.finish() for part in pair], axis=2)
    attn_shard = jnp.concatenate([inner_shard, jnp.concatenate(out_shard, axis=2)], axis=0)
    feed_shard = jnp.concatenate([jnp.concatenate(pair, axis=2) for pair in zip(early_shard, late_shard)], axis=0)
    factor = clip_bound / jnp.maximum(grad_norm, clip_bound)
    attn_new = adam_update(
        attention_weight, attention_moment, attention_second, attention_average, attn_shard, factor, learn_rate
    )
    feed_new = adam_update(
        feedforward_weight, feedforward_moment, feedforward_second, feedforward_average, feed_shard, factor, learn_rate
    )
    norm_new = adam_update(norm_vectors, norm_moment, norm_second, norm_average, vector_shard, factor, norm_rate)
    output = output.reshape(images.shape)
    input_grad = input_grad.reshape(images.shape)
    return (output, input_grad, grad_norm) + attn_new + feed_new + norm_new


def solution(mesh):
    tokens = P("img", "seq", None)
    rows = P(None, ("seq", "img"), None)
    vectors = P(None, ("seq", "img"))
    group = (rows, rows, vectors)
    return jax.shard_map(
        body,
        mesh=mesh,
        in_specs=(tokens, tokens) + group * 4,
        out_specs=(tokens, tokens, P()) + (rows,) * 8 + (vectors,) * 4,
        check_vma=False,
    )
```

```python
import functools

import jax
import jax.numpy as jnp
import numpy as np
from jax import lax
from jax.experimental import pallas as pl
from jax.experimental.pallas import tpu as pltpu
from jax.sharding import PartitionSpec as P

HEADS = 16
HEAD_DIM = 64
STEP = 10

beta_first = 0.9
beta_second = 0.95
learn_rate = 0.02
norm_rate = 0.2
weight_decay = 0.1
average_decay = 0.75
clip_bound = 1.0
eps_norm = 1e-05
eps_adam = 1e-08

PAIR = 2 * HEAD_DIM
STATE_ROWS = HEAD_DIM + 16
SLAB = 1024
TILE = 512
GROUP = 256

low = jnp.bfloat16
wide = jnp.float32


def params(megabytes=56):
    return pltpu.CompilerParams(vmem_limit_bytes=megabytes * 1024 * 1024)


def cost(products, elements):
    return pl.CostEstimate(flops=2 * products, bytes_accessed=elements, transcendentals=0)


def launch(kernel, tokens, in_specs, megabytes=56, **keys):
    known, extra = len(in_specs), len(tokens)

    def run(*refs):
        kernel(*refs[:known], *refs[known + extra :])

    call = pl.pallas_call(
        run, in_specs=list(in_specs) + [pl.BlockSpec(memory_space=pl.ANY)] * extra, compiler_params=params(megabytes), **keys
    )
    return lambda *args: call(*args, *tokens)


def launch_at(kernel, spot, tokens, grid, in_specs, out_specs, megabytes=56, scratch_shapes=(), **keys):
    known, extra = len(in_specs), len(tokens)

    def run(spot_ref, *refs):
        kernel(spot_ref, *refs[:known], *refs[known + extra :])

    call = pl.pallas_call(
        run,
        grid_spec=pltpu.PrefetchScalarGridSpec(
            num_scalar_prefetch=1,
            grid=grid,
            in_specs=list(in_specs) + [pl.BlockSpec(memory_space=pl.ANY)] * extra,
            out_specs=out_specs,
            scratch_shapes=scratch_shapes,
        ),
        compiler_params=params(megabytes),
        **keys,
    )
    return lambda *args: call(spot.reshape(-1).astype(jnp.int32), *args, *tokens)


def reversed_bits(value, count):
    return sum(((value >> k) & 1) << (count - 1 - k) for k in range(count))


def join(target_ref, bits, spot_ref, own_ref, came_ref, own_other_ref, came_other_ref):
    core, high, lowest = spot_ref[0], spot_ref[1], spot_ref[2]
    runs = 1 << (bits - 1)
    rows = target_ref.shape[1] // (2 * runs)
    for run in range(runs):
        source = slice(run * rows, (run + 1) * rows)
        turned = reversed_bits(run, bits)
        for place in range(2):
            first = (high ^ place) * runs + run
            second = turned + (lowest ^ place)
            for ref, slot in (((own_ref, came_ref)[place], core), ((own_other_ref, came_other_ref)[place], 1 - core)):
                at = jnp.where(slot == 0, first, second)
                target_ref[slot, pl.ds(pl.multiple_of(at * rows, rows), rows), :] = ref[source, :]


class Pieces:
    def __init__(self, arrays):
        self.arrays = [array.reshape(array.shape[0], -1, array.shape[-1]) for array in arrays]
        place = pos_index()
        self.bits = pos_bits()
        self.spot = jnp.stack([core_index(), place >> (self.bits - 1), place & 1])

    def blocks(self, columns, place):
        rows = self.arrays[0].shape[1]
        return [pl.BlockSpec((None, rows, columns), place)] * 4

def shaped(shape, kind):
    return jax.ShapeDtypeStruct(shape, kind)


def whole(shape):
    return pl.BlockSpec(shape, lambda *_: (0,) * len(shape))


def mm(left, right):
    return lax.dot_general(left, right, (((1,), (0,)), ((), ())), preferred_element_type=wide)


def mt(left, right):
    return lax.dot_general(left, right, (((1,), (1,)), ((), ())), preferred_element_type=wide)


def tm(left, right):
    return lax.dot_general(left, right, (((0,), (0,)), ((), ())), preferred_element_type=wide)


def pair_mm(first, second):
    if first[0].shape[1] % 128:
        return mm(*first) + mm(*second)
    return mm(jnp.concatenate([first[0], second[0]], axis=1), jnp.concatenate([first[1], second[1]], axis=0))


def causal_mask(span, below):
    rows = lax.broadcasted_iota(jnp.int32, (span, span), 0)
    columns = lax.broadcasted_iota(jnp.int32, (span, span), 1)
    return (rows >= columns if below else rows <= columns).astype(wide).astype(low)


def first_head(rows):
    return lax.broadcasted_iota(jnp.int32, (rows, PAIR), 1) < HEAD_DIM


def fold_state(product):
    return jnp.where(first_head(HEAD_DIM), product[:HEAD_DIM], product[HEAD_DIM:])


def unfold_state(folded):
    own = first_head(HEAD_DIM)
    zero = jnp.zeros_like(folded)
    return jnp.concatenate([jnp.where(own, folded, zero), jnp.where(own, zero, folded)], axis=0)


def unfold_total(row):
    tall = jnp.broadcast_to(row, (PAIR, PAIR))
    lanes = lax.broadcasted_iota(jnp.int32, (PAIR, PAIR), 1) < HEAD_DIM
    rows = lax.broadcasted_iota(jnp.int32, (PAIR, PAIR), 0) < HEAD_DIM
    return jnp.where(lanes == rows, tall, jnp.zeros_like(tall))


def split_low(values):
    high = values.astype(low)
    return high, (values - high.astype(wide)).astype(low)


def normalised(values):
    centre = jnp.mean(values, axis=-1, keepdims=True)
    centred = values - centre
    spread = jnp.mean(centred * centred, axis=-1, keepdims=True)
    scale = lax.rsqrt(spread + eps_norm)
    return centred * scale, scale


def feature(raw):
    return jnp.where(raw > 0, raw + 1.0, jnp.exp(jnp.minimum(raw, 0.0))).astype(low)


def project_kernel(images, span, bits, spot_ref, x_ref, vec_ref, *refs):
    fk_ref, v_ref, a_ref, at_ref, state_ref, wk_ref, wv_ref, joined_ref = refs[4:]

    @pl.when(pl.program_id(0) == 0)
    def _():
        gain, shift = vec_ref[0:1, :], vec_ref[1:2, :]
        step = span // 3
        for start in range(0, images * span, step):
            rows = slice(start, start + step)
            unit, _ = normalised(x_ref[rows, :].astype(wide))
            a_ref[rows, :] = (unit * gain + shift).astype(low)
        at_ref[...] = a_ref[...].T

    join(joined_ref, bits, spot_ref, *refs[:4])
    keys, values = joined_ref[0], joined_ref[1]
    wk_ref[...] = keys
    wv_ref[...] = values
    fk_ref[...] = feature(mm(a_ref[...], keys))
    v_ref[...] = mm(a_ref[...], values).astype(low)
    ones = jnp.ones((16, span), low)
    for image in range(images):
        rows = slice(image * span, (image + 1) * span)
        for pair in range(GROUP // PAIR):
            lanes = slice(pair * PAIR, (pair + 1) * PAIR)
            key, value = fk_ref[rows, lanes], v_ref[rows, lanes]
            state_ref[image, pair, :HEAD_DIM, :] = fold_state(tm(value, key))
            state_ref[image, pair, HEAD_DIM:, :] = mm(ones, key)


def project(x, vec, pieces, images, span, tokens=()):
    count, width = x.shape
    pairs = GROUP // PAIR
    column = pl.BlockSpec((count, GROUP), lambda g, spot: (0, g))
    weight = pl.BlockSpec((width, GROUP), lambda g, spot: (0, g))
    return launch_at(
        functools.partial(project_kernel, images, span, pieces.bits),
        pieces.spot,
        tokens,
        grid=(width // GROUP,),
        in_specs=[whole((count, width)), whole(vec.shape)] + pieces.blocks(GROUP, lambda g, spot: (0, 0, g)),
        out_specs=[
            column,
            column,
            whole((count, width)),
            whole((width, count)),
            pl.BlockSpec((images, pairs, STATE_ROWS, PAIR), lambda g, spot: (0, g, 0, 0)),
            weight,
            weight,
        ],
        out_shape=[
            shaped((count, width), low),
            shaped((count, width), low),
            shaped((count, width), low),
            shaped((width, count), low),
            shaped((images, width // PAIR, STATE_ROWS, PAIR), wide),
            shaped((width, width), low),
            shaped((width, width), low),
        ],
        scratch_shapes=[pltpu.VMEM((2, width, GROUP), low)],
        cost_estimate=cost(2 * count * width * width, 8 * width * width + 12 * count * width),
        name="project",
    )(x, vec, *pieces.arrays)


def query_kernel(bits, spot_ref, a_ref, *refs):
    fq_ref, wq_ref, wo_ref, joined_ref = refs[4:]
    join(joined_ref, bits, spot_ref, *refs[:4])
    wq_ref[...] = joined_ref[0]
    wo_ref[...] = joined_ref[1]
    fq_ref[...] = feature(mm(a_ref[...], joined_ref[0]))


def query(a, pieces, tokens=()):
    count, width = a.shape
    weight = pl.BlockSpec((width, GROUP), lambda g, spot: (0, g))
    return launch_at(
        functools.partial(query_kernel, pieces.bits),
        pieces.spot,
        tokens,
        grid=(width // GROUP,),
        in_specs=[whole((count, width))] + pieces.blocks(GROUP, lambda g, spot: (1, 0, g)),
        out_specs=[pl.BlockSpec((count, GROUP), lambda g, spot: (0, g)), weight, weight],
        out_shape=[shaped((count, width), low)] + [shaped((width, width), low)] * 2,
        scratch_shapes=[pltpu.VMEM((2, width, GROUP), low)],
        cost_estimate=cost(count * width * width, 6 * width * width + 4 * count * width),
        name="query",
    )(a, *pieces.arrays)


def turn_kernel(x_ref, out_ref):
    out_ref[...] = x_ref[...].T


def turn(x, images, span, tokens=()):
    count, width = x.shape
    return turned_whole(
        launch(
            turn_kernel,
            tokens,
            grid=(images,),
            in_specs=[pl.BlockSpec((span, width), lambda b: (b, 0))],
            out_specs=turned_block(width, span),
            out_shape=turned_shape(images, width, span),
            cost_estimate=cost(1, 4 * count * width),
                name="turn",
        )(x)
    )


def attend_kernel(span, fq_ref, fk_ref, v_ref, num_ref, den_ref):
    own = first_head(span)
    causal = causal_mask(span, True)
    one = jnp.ones((span, PAIR), low)
    zero = jnp.zeros((span, PAIR), low)
    for pair in range(GROUP // PAIR):
        lanes = slice(pair * PAIR, (pair + 1) * PAIR)
        query, key, value = fq_ref[:, lanes], fk_ref[:, lanes], v_ref[:, lanes]
        products = []
        for mask in (own, jnp.logical_not(own)):
            scores = mt(jnp.where(mask, query, zero), key).astype(low) * causal
            right = jnp.concatenate([jnp.where(mask, value, zero), jnp.where(mask, one, zero)], axis=1)
            products.append((scores, right))
        total = pair_mm(*products)
        num_ref[:, lanes] = total[:, :PAIR]
        den_ref[:, lanes] = total[:, PAIR:]


def attend(fq, fk, v, images, span, tokens=()):
    rows, width = fq.shape
    block = pl.BlockSpec((span, GROUP), lambda b, p: (b, p))
    return launch(
        functools.partial(attend_kernel, span),
        tokens,
        grid=(images, width // GROUP),
        in_specs=[block] * 3,
        out_specs=[block] * 2,
        out_shape=[shaped((rows, width), wide)] * 2,
        cost_estimate=cost(16 * rows * span * width, 14 * rows * width),
        name="attend",
    )(fq, fk, v)


def turned_block(width, span):
    if span % 128:
        return pl.BlockSpec((None, width, span), lambda b: (b, 0, 0))
    return pl.BlockSpec((width, span), lambda b: (0, b))


def turned_shape(images, width, span):
    return shaped((images, width, span) if span % 128 else (width, images * span), low)


def turned_whole(array):
    if array.ndim == 2:
        return array
    return jnp.swapaxes(array, 0, 1).reshape(array.shape[1], -1)


def mix_kernel(x_ref, vec_ref, wo_ref, fq_ref, num_ref, den_ref, prior_ref, mixed_ref, rden_ref, resid_ref, a_ref, at_ref, mt_ref):
    width = x_ref.shape[1]
    for pair in range(width // PAIR):
        lanes = slice(pair * PAIR, (pair + 1) * PAIR)
        folded = prior_ref[0, pair]
        matrix = jnp.concatenate(
            [unfold_state(folded[:HEAD_DIM]), unfold_total(folded[HEAD_DIM : HEAD_DIM + 1])], axis=0
        )
        high, rest = split_low(matrix)
        query = fq_ref[:, lanes]
        both = mt(jnp.concatenate([query, query], axis=1), jnp.concatenate([high, rest], axis=1))
        scale = 1.0 / (den_ref[:, lanes] + both[:, PAIR:])
        rden_ref[:, lanes] = scale
        mixed_ref[:, lanes] = ((num_ref[:, lanes] + both[:, :PAIR]) * scale).astype(low)
    resid = x_ref[...].astype(wide) + mm(mixed_ref[...], wo_ref[...])
    resid_ref[...] = resid
    unit, _ = normalised(resid)
    normed = (unit * vec_ref[2:3, :] + vec_ref[3:4, :]).astype(low)
    a_ref[...] = normed
    at_ref[...] = normed.T
    mt_ref[...] = mixed_ref[...].T


def mix(x, vec, wo, fq, num, den, prior, images, span, tokens=()):
    rows_, width = x.shape
    rows = pl.BlockSpec((span, width), lambda b: (b, 0))
    return launch(
        mix_kernel,
        tokens,
        grid=(images,),
        in_specs=[
            rows,
            whole(vec.shape),
            whole(wo.shape),
            rows,
            rows,
            rows,
            pl.BlockSpec((1,) + prior.shape[1:], lambda b: (b, 0, 0, 0)),
        ],
        out_specs=[rows, rows, rows, rows, turned_block(width, span), turned_block(width, span)],
        out_shape=[
            shaped((rows_, width), low),
            shaped((rows_, width), wide),
            shaped((rows_, width), wide),
            shaped((rows_, width), low),
            turned_shape(images, width, span),
            turned_shape(images, width, span),
        ],
        cost_estimate=cost(4 * rows_ * width * width, 24 * rows_ * width + 2 * width * width),
        name="mix",
    )(x, vec, wo, fq, num, den, prior)


gelu_scale = 0.7978845608028654
gelu_cubic = 0.044715


def feed_kernel(fresh, bits, spot_ref, *refs):
    a_ref, e_ref = refs[:2]
    out_ref, da_ref, kept_ref, sent_ref, joined_ref = refs[-5:]
    join(joined_ref, bits, spot_ref, *refs[2:6])

    @pl.when(pl.program_id(0) == 0)
    def _():
        if fresh:
            out_ref[...] = jnp.zeros_like(out_ref)
            da_ref[...] = jnp.zeros_like(da_ref)
        else:
            out_ref[...] = refs[6][...]
            da_ref[...] = refs[7][...]

    up, down = joined_ref[0], joined_ref[1]
    upper = mm(a_ref[...], up)
    grad = mm(e_ref[...], down)
    square = upper * upper
    bend = jnp.tanh(gelu_scale * upper * (1.0 + gelu_cubic * square))
    gate = 0.5 + 0.5 * bend
    hidden = (upper * gate).astype(low)
    slope = gate + 0.5 * upper * (1.0 - bend * bend) * (gelu_scale * (1.0 + 3.0 * gelu_cubic * square))
    dupper = (grad * slope).astype(low)
    out_ref[...] += mt(hidden, down)
    da_ref[...] += mt(dupper, up)
    first = spot_ref[0] == 0
    kept_ref[...] = jnp.where(first, dupper, hidden)
    sent_ref[...] = jnp.where(first, hidden, dupper)


def feed(pieces, a, e, carried, tokens=()):
    rows, width = a.shape
    slabs = pieces.arrays[0].shape[0]
    tiles = SLAB // TILE
    grads = pl.BlockSpec((rows, TILE), lambda g, spot: (0, g))
    full = whole((rows, width))
    fresh = carried is None
    return launch_at(
        functools.partial(feed_kernel, fresh, pieces.bits),
        pieces.spot,
        tokens,
        grid=(slabs * tiles,),
        in_specs=[full, full]
        + pieces.blocks(TILE, lambda g, spot: (g // tiles, 0, g % tiles))
        + ([] if fresh else [full, full]),
        out_specs=[full, full, grads, grads],
        out_shape=[shaped((rows, width), wide)] * 2 + [shaped((rows, slabs * SLAB), low)] * 2,
        scratch_shapes=[pltpu.VMEM((2, width, TILE), low)],
        cost_estimate=cost(4 * rows * width * slabs * SLAB, 4 * (width + rows) * slabs * SLAB + 20 * rows * width),
        name="feed",
    )(a, e, *pieces.arrays, *(() if fresh else carried))


def weigh_kernel(count, spot_ref, lt_ref, lt_other_ref, x_ref, x_other_ref, kept_ref, sent_ref):
    rows = kept_ref.shape[1]
    for k in range(2):
        places = [pl.ds(pl.multiple_of(spot_ref[k * count + n] * rows, rows), rows) for n in range(count)]
        left, other = (jnp.concatenate([ref[place, :] for place in places], axis=0) for ref in (lt_ref, lt_other_ref))
        product = (mm(left, x_ref[...]) + mm(other, x_other_ref[...])).astype(low)
        (sent_ref if k else kept_ref)[...] = product.reshape(count, rows, -1)


def weigh(chain, lt, lt_other, x, x_other, tokens=()):
    lead, rows, columns = x.shape
    width = lt.shape[0]
    keeps, sends = chain.table()
    count = keeps.shape[0]
    tile = min(TILE, columns)
    full = whole((width, rows))
    column = pl.BlockSpec((None, rows, tile), lambda n, g, spot: (n, 0, g))
    result = pl.BlockSpec((None, count, width // (2 * count), tile), lambda n, g, spot: (n, 0, 0, g))
    chain.take(
        launch_at(
            functools.partial(weigh_kernel, count),
            jnp.concatenate([keeps, sends]),
            tokens,
            grid=(lead, columns // tile),
            in_specs=[full, full, column, column],
            out_specs=[result, result],
            out_shape=[shaped((lead, count, width // (2 * count), columns), low)] * 2,
            cost_estimate=cost(2 * lead * rows * width * columns, 4 * lead * (rows + width) * columns + 4 * rows * width),
            name="weigh",
        )(lt, lt_other, x, x_other)
    )
    chain.start()
    return chain.sends


def turn_back_kernel(core_ref, x_out_ref, da_ref, resid_ref, e_ref, vec_ref, wo_ref, mixed_ref, rden_ref, fq_ref,
                     out_ref, dres_ref, kept_ref, sent_ref, dn_ref, w_ref, state_ref, sums_ref):
    width = da_ref.shape[1]
    resid = resid_ref[...]
    out_ref[...] = (resid + x_out_ref[...]).astype(low)
    unit, scale = normalised(resid)
    da = da_ref[...]

    @pl.when(pl.program_id(0) == 0)
    def _():
        sums_ref[...] = jnp.zeros_like(sums_ref)

    sums_ref[0:1, :] += jnp.sum(da * unit, axis=0, keepdims=True)
    sums_ref[1:2, :] += jnp.sum(da, axis=0, keepdims=True)
    p = da * vec_ref[2:3, :]
    back = p - jnp.mean(p, axis=-1, keepdims=True) - unit * jnp.mean(p * unit, axis=-1, keepdims=True)
    dres = e_ref[...].astype(wide) + scale * back
    dres_ref[...] = dres
    branch = dres.astype(low)
    left, right = branch[:, : width // 2], branch[:, width // 2 :]
    first = core_ref[0] == 0
    kept_ref[...] = jnp.where(first, left, right)
    sent_ref[...] = jnp.where(first, right, left)
    dmixed = mt(branch, wo_ref[...]).astype(low).astype(wide)
    dnumer = dmixed * rden_ref[...]
    dn_ref[...] = dnumer.astype(low)
    w_ref[...] = (-dnumer * mixed_ref[...].astype(wide)).astype(low)
    for pair in range(width // PAIR):
        lanes = slice(pair * PAIR, (pair + 1) * PAIR)
        query = fq_ref[:, lanes]
        state_ref[0, pair, :HEAD_DIM, :] = fold_state(tm(dn_ref[:, lanes], query))
        total = jnp.sum(fold_state(tm(w_ref[:, lanes], query)), axis=0, keepdims=True)
        state_ref[0, pair, HEAD_DIM:, :] = jnp.broadcast_to(total, (STATE_ROWS - HEAD_DIM, PAIR))


def turn_back(x_out, da, resid, e, vec, wo, mixed, rden, fq, images, span, tokens=()):
    rows_, width = da.shape
    rows = pl.BlockSpec((span, width), lambda b, core: (b, 0))
    state = (images, width // PAIR, STATE_ROWS, PAIR)
    half = pl.BlockSpec((span, width // 2), lambda b, core: (b, 0))
    return launch_at(
        turn_back_kernel,
        core_index(),
        tokens,
        grid=(images,),
        in_specs=[rows, rows, rows, rows, whole(vec.shape), whole(wo.shape), rows, rows, rows],
        out_specs=[rows, rows, half, half, rows, rows] + [pl.BlockSpec((1,) + state[1:], lambda b, core: (b, 0, 0, 0)), whole((8, width))],
        out_shape=[
            shaped((rows_, width), low),
            shaped((rows_, width), wide),
            shaped((rows_, width // 2), low),
            shaped((rows_, width // 2), low),
            shaped((rows_, width), low),
            shaped((rows_, width), low),
            shaped(state, wide),
            shaped((8, width), wide),
        ],
        cost_estimate=cost(5 * rows_ * width * width, 30 * rows_ * width),
        name="turn_back",
    )(x_out, da, resid, e, vec, wo, mixed, rden, fq)


def attend_back_kernel(span, fq_ref, fk_ref, v_ref, dn_ref, w_ref, prior_ref, dq_ref, dfk_ref, dv_ref):
    own = first_head(span)
    own_twice = jnp.concatenate([own, own], axis=1)
    below, above = causal_mask(span, True), causal_mask(span, False)
    one = jnp.ones((span, PAIR), low)
    zero = jnp.zeros((span, PAIR), low)
    zero_twice = jnp.zeros((span, 2 * PAIR), low)
    for pair in range(GROUP // PAIR):
        lanes = slice(pair * PAIR, (pair + 1) * PAIR)
        query, key, value = fq_ref[:, lanes], fk_ref[:, lanes], v_ref[:, lanes]
        grads = jnp.concatenate([dn_ref[:, lanes], w_ref[:, lanes]], axis=1)
        extended = jnp.concatenate([value, one], axis=1)
        folded = prior_ref[0, pair]
        matrix = jnp.concatenate(
            [unfold_state(folded[:HEAD_DIM]), unfold_total(folded[HEAD_DIM : HEAD_DIM + 1])], axis=0
        )
        high, rest = split_low(matrix)
        dfq = mm(jnp.concatenate([grads, grads], axis=1), jnp.concatenate([high, rest], axis=0))
        to_query, to_key, to_value = [], [], []
        for mask, both in ((own, own_twice), (jnp.logical_not(own), jnp.logical_not(own_twice))):
            head_grads = jnp.where(both, grads, zero_twice)
            head_query = jnp.where(mask, query, zero)
            head_key = jnp.where(mask, key, zero)
            to_query.append((mt(head_grads, extended).astype(low) * below, head_key))
            to_key.append((mt(extended, head_grads).astype(low) * above, head_query))
            to_value.append((mt(head_key, query).astype(low) * above, head_grads[:, :PAIR]))
        dfq = dfq + pair_mm(*to_query)
        dq_ref[:, lanes] = (dfq * jnp.minimum(query.astype(wide), 1.0)).astype(low)
        dfk_ref[:, lanes] = pair_mm(*to_key)
        dv_ref[:, lanes] = pair_mm(*to_value)


def attend_back(image, fq, fk, v, dn, w, prior, span, tokens=()):
    width = fq.shape[1]
    block = pl.BlockSpec((span, GROUP), lambda p: (image, p))
    column = pl.BlockSpec((span, GROUP), lambda p: (0, p))
    return launch(
        functools.partial(attend_back_kernel, span),
        tokens,
        grid=(width // GROUP,),
        in_specs=[block] * 5 + [pl.BlockSpec((1, GROUP // PAIR) + prior.shape[2:], lambda p: (image, p, 0, 0))],
        out_specs=[column] * 3,
        out_shape=[shaped((span, width), low), shaped((span, width), wide), shaped((span, width), wide)],
        cost_estimate=cost(32 * span * span * width, 24 * span * width),
        name="attend_back",
    )(fq, fk, v, dn, w, prior)


def finish_kernel(images, span, core_ref, *refs):
    fk_ref, v_ref, later_ref, kept_ref, sent_ref = refs[3 * images :]

    def run(out_ref):
        for image in range(images):
            rows = slice(image * span, (image + 1) * span)
            dq_ref, dfk_ref, dvl_ref = refs[3 * image : 3 * image + 3]
            out_ref[0, rows, :] = dq_ref[...]
            for pair in range(GROUP // PAIR):
                lanes = slice(pair * PAIR, (pair + 1) * PAIR)
                folded = later_ref[image, pair]
                high, rest = split_low(unfold_state(folded[:HEAD_DIM]))
                key, value = fk_ref[rows, lanes], v_ref[rows, lanes]
                dfk = dfk_ref[:, lanes] + folded[HEAD_DIM : HEAD_DIM + 1]
                dfk = dfk + mm(jnp.concatenate([value, value], axis=1), jnp.concatenate([high, rest], axis=0))
                dv = dvl_ref[:, lanes] + mt(
                    jnp.concatenate([key, key], axis=1), jnp.concatenate([high, rest], axis=1)
                )
                out_ref[1, rows, lanes] = (dfk * jnp.minimum(key.astype(wide), 1.0)).astype(low)
                out_ref[2, rows, lanes] = dv.astype(low)

    @pl.when(pl.program_id(0) < pl.num_programs(0) // 2)
    def _():
        run(kept_ref)

    @pl.when(pl.program_id(0) >= pl.num_programs(0) // 2)
    def _():
        run(sent_ref)


def finish(parts, fk, v, later, images, span, tokens=()):
    rows, width = fk.shape
    groups = width // GROUP // 2

    def column(g, core):
        return ((g // groups) ^ core[0]) * groups + g % groups

    block = pl.BlockSpec((rows, GROUP), lambda g, core: (0, column(g, core)))
    part = pl.BlockSpec((span, GROUP), lambda g, core: (0, column(g, core)))
    state = pl.BlockSpec((images, GROUP // PAIR) + later.shape[2:], lambda g, core: (0, column(g, core), 0, 0))
    return launch_at(
        functools.partial(finish_kernel, images, span),
        core_index(),
        tokens,
        grid=(2 * groups,),
        in_specs=[part] * (3 * images) + [block] * 2 + [state],
        out_specs=[
            pl.BlockSpec((3, rows, GROUP), lambda g, core: (0, 0, jnp.minimum(g, groups - 1))),
            pl.BlockSpec((3, rows, GROUP), lambda g, core: (0, 0, jnp.maximum(g - groups, 0))),
        ],
        out_shape=[shaped((3, rows, width // 2), low)] * 2,
        cost_estimate=cost(rows * width * 512, 24 * rows * width),
        name="finish",
    )(*[array for image in parts for array in image], fk, v, later)


def enter_kernel(core_ref, kept_ref, sent_ref, *refs):
    weights = refs[:3]
    x_ref, dres_ref, vec_ref, grad_ref, sums_ref = refs[3:]
    half = x_ref.shape[1] // 2
    da = None
    for k, weight in enumerate(weights):
        for ref, side in ((kept_ref, core_ref[0]), (sent_ref, 1 - core_ref[0])):
            part = mt(ref[k], weight[:, pl.ds(pl.multiple_of(side * half, half), half)])
            da = part if da is None else da + part
    unit, scale = normalised(x_ref[...].astype(wide))
    sums_ref[0:1, :] = jnp.sum(da * unit, axis=0, keepdims=True)
    sums_ref[1:2, :] = jnp.sum(da, axis=0, keepdims=True)
    sums_ref[2:, :] = jnp.zeros_like(sums_ref[2:, :])
    p = da * vec_ref[0:1, :]
    back = p - jnp.mean(p, axis=-1, keepdims=True) - unit * jnp.mean(p * unit, axis=-1, keepdims=True)
    grad_ref[...] = (dres_ref[...] + scale * back).astype(low)


def enter(image, kept, sent, weights, x, dres, vec, span, tokens=()):
    width = x.shape[1]
    rows = pl.BlockSpec((span, width), lambda g, core: (image, 0))
    part = pl.BlockSpec((3, span, width // 2), lambda g, core: (0, image, 0))
    return launch_at(
        enter_kernel,
        core_index(),
        tokens,
        grid=(1,),
        in_specs=[part] * 2 + [whole((width, width))] * 3 + [rows, rows, whole(vec.shape)],
        out_specs=[whole((span, width)), whole((8, width))],
        out_shape=[shaped((span, width), low), shaped((8, width), wide)],
        cost_estimate=cost(3 * span * width * width, 14 * span * width + 6 * width * width),
        name="enter",
    )(kept, sent, *weights, x, dres, vec)


def adam_update(master, moment, second, average, gradient, factor, rate):
    clipped = gradient * factor
    moment = beta_first * moment + (1.0 - beta_first) * clipped
    second = beta_second * second + (1.0 - beta_second) * clipped * clipped
    first_hat = moment / (1.0 - beta_first**STEP)
    second_hat = second / (1.0 - beta_second**STEP)
    master = master - rate * (first_hat / (jnp.sqrt(second_hat) + eps_adam) + weight_decay * master)
    average = average_decay * average + (1.0 - average_decay) * master
    return (master, moment, second, average)


def powers(count):
    return [1 << k for k in range(count.bit_length() - 1)]


def core_index():
    return lax.axis_index("seq") % 2


def pos_index():
    return lax.axis_index("seq") // 2


def pos_bits():
    return (lax.axis_size("seq") // 2).bit_length() - 1


def flip(array, axis, bit):
    return lax.ppermute(array, axis, [(i, i ^ bit) for i in range(lax.axis_size(axis))])


def flip_core(array):
    return flip(array, "seq", 1)


def flip_pos(array, stage):
    bits = pos_bits()
    pairs = [(i, i ^ (2 << (stage if i % 2 == 0 else bits - 1 - stage))) for i in range(lax.axis_size("seq"))]
    return lax.ppermute(array, "seq", pairs)


def own_bit(stage):
    bits = pos_bits()
    return jnp.where(core_index() == 0, pos_index() >> stage, pos_index() >> (bits - 1 - stage)) & 1


def halves(shape, dim):
    index = np.arange(int(np.prod(shape))).reshape(shape)
    return np.stack([index.take(side, axis=dim).ravel() for side in range(2)])


def fold_kernel(chains, spot_ref, *refs):
    ins, outs = refs[: 4 * chains], refs[4 * chains :]
    for k in range(2 * chains):
        value = ins[2 * k][...].astype(wide) + ins[2 * k + 1][...].astype(wide)
        outs[k][...] = value.astype(outs[k].dtype)


def fold(cuts, tokens=()):
    count = cuts[0][2].shape[0]
    steps = max(1, min(2, min(kept.shape[-1] for kept, *_ in cuts) // 256))
    in_specs, out_specs, out_shape, arrays, moved = [], [], [], [], 0
    for k, (kept, came, keeps, sends) in enumerate(cuts):
        lead, _, rows, columns = kept.shape
        block = (lead, 1, rows, columns // steps)
        for side in range(2):
            at = 2 * k * count + side * count
            spec = pl.BlockSpec(block, lambda g, c, spot, at=at: (0, spot[at + g], 0, c))
            in_specs += [spec, spec]
            arrays += [kept, came]
            out_specs.append(pl.BlockSpec(block, lambda g, c, spot: (0, g, 0, c)))
            out_shape.append(shaped((lead, count, rows, columns), low if side else wide))
        moved += 8 * kept.size
    results = launch_at(
        functools.partial(fold_kernel, len(cuts)),
        jnp.concatenate([part for _, _, keeps, sends in cuts for part in (keeps, sends)]),
        tokens,
        grid=(count, steps),
        in_specs=in_specs,
        out_specs=out_specs,
        out_shape=out_shape,
        cost_estimate=cost(1, moved),
        name="fold",
    )(*arrays)
    return [results[2 * k : 2 * k + 2] for k in range(len(cuts))]


class Chain:
    def __init__(self, lead=1):
        self.lead = lead
        self.stage = -1
        self.left = [list(range(pos_bits()))[::-1]] * 2

    def start(self):
        self.came = [flip_pos(self.sends[0], self.stage)]

    def table(self):
        self.stage += 1
        tables = []
        for kind in range(2):
            bit = self.stage if kind == 0 else pos_bits() - 1 - self.stage
            left = self.left[kind]
            tables.append(halves((2,) * len(left), left.index(bit)))
            self.left[kind] = [other for other in left if other != bit]
        table = jnp.where(core_index() == 0, *[jnp.asarray(part, jnp.int32) for part in tables])
        own = own_bit(self.stage)
        return table[own], table[1 - own]

    def cut(self):
        return (self.kept, self.came[0], *self.table())

    def take(self, parts):
        self.kept, self.sends = parts[0], [parts[1]]


def advance(chains, tokens=()):
    parts = fold([chain.cut() for chain in chains], tokens)
    for chain, part in zip(chains, parts):
        chain.take(part)
        chain.start()
    return [array for chain in chains for array in chain.sends]


def last_kernel(ways, pre, pieces, spot_ref, *refs):
    ins, outs = refs[: 2 * pieces], refs[2 * pieces :]
    at = 0
    for k in range(pieces):
        columns = ins[2 * k].shape[-1]
        for j in range(ways):
            place = spot_ref[0] ^ j
            for n in range(pre):
                value = ins[2 * k][n, place].astype(wide) + ins[2 * k + 1][n, place].astype(wide)
                outs[j][n, :, at : at + columns] = value.astype(outs[j].dtype)
        at += columns


class Last:
    def __init__(self, chains, tokens=(), slowly=False):
        slices = lax.axis_size("img")
        ways = 2 if slowly else slices
        self.lead = chains[0].lead
        pre = self.lead * 2 * slices // ways
        arrays = []
        for chain in chains:
            for array in (chain.kept, chain.came[0]):
                arrays.append(array.reshape(pre, ways, -1, array.shape[-1]))
        self.widths = [array.shape[-1] for array in arrays[::2]]
        inside = pl.BlockSpec(memory_space=pltpu.VMEM)
        parts = launch(
            functools.partial(last_kernel, ways, pre, len(chains)),
            tokens,
            in_specs=[pl.BlockSpec(memory_space=pltpu.SMEM)] + [inside] * len(arrays),
            out_specs=[inside] * ways,
            out_shape=[shaped((pre, arrays[0].shape[2], sum(self.widths)), low if j else wide) for j in range(ways)],
            cost_estimate=cost(1, 4 * sum(array.size for array in arrays)),
                name="last",
        )((lax.axis_index("img") % ways).reshape(1), *arrays)
        self.kept, self.sends = parts[0], list(parts[1:])
        self.hops = list(range(1, ways))
        self.left = powers(slices)[1:][::-1] if slowly else []
        self.start()

    def start(self):
        self.came = [flip(array, "img", hop) for array, hop in zip(self.sends, self.hops)]

    def cut(self):
        bit = self.left[-1]
        entries = self.kept.reshape((1, -1) + self.kept.shape[-2:])
        dims = (2 * self.lead,) + (2,) * len(self.left)
        table = jnp.asarray(halves(dims, len(dims) - 1), jnp.int32)
        own = (lax.axis_index("img") // bit) % 2
        self.left = self.left[:-1]
        self.hops = [bit]
        return (entries, self.came[0].reshape(entries.shape), table[own], table[1 - own])

    def take(self, parts):
        self.kept, self.sends = parts[0][0], [parts[1][0]]

    def total(self):
        while self.left:
            advance([self])
        total = self.kept
        for came in self.came:
            total = total + came.astype(wide)
        return total

    def settle(self, stretch, tokens):
        self.came[stretch] = gate(self.came[stretch], tokens)
        return self.came[stretch]

    def squares(self):
        self.sums = self.total()
        return jnp.sum(self.sums * self.sums)

    def finish(self):
        core = core_index()
        total = self.sums.reshape((self.lead, 2) + self.sums.shape[-2:])
        own = lax.dynamic_index_in_dim(total, core, 1, False)
        came = flip_core(lax.dynamic_index_in_dim(total, 1 - core, 1, False))
        first, second = jnp.where(core == 0, own, came), jnp.where(core == 0, came, own)
        at, found = 0, []
        for columns in self.widths:
            found.append((first[..., at : at + columns], second[..., at : at + columns]))
            at += columns
        return found


def sum_slowly(array):
    for axis in ("seq", "img"):
        for bit in powers(lax.axis_size(axis)):
            array = array + flip(array, axis, bit)
    return array


def sum_all(array):
    rounds = [("img", range(1, lax.axis_size("img"))), ("seq", range(2, lax.axis_size("seq"), 2)), ("seq", [1])]
    for axis, hops in rounds:
        came = [flip(array, axis, hop) for hop in hops]
        for other in came:
            array = array + other
    return array


def assemble_kernel(plan, spot_ref, *refs):
    outs = sorted({out for _, _, out, _ in plan})
    count = len(refs) - 1 - len(outs)
    sems = refs[-1]
    copies = []
    for k, (piece, cut, out, where) in enumerate(plan):
        source = refs[piece].at[cut] if cut is not None else refs[piece]
        target = refs[count + out].at[where(spot_ref)]
        copies.append(pltpu.make_async_copy(source, target, sems.at[k]))
    for copy in copies:
        copy.start()
    for copy in copies:
        copy.wait()


def assemble(plan, spots, pieces, shapes, tokens=()):
    anywhere = pl.BlockSpec(memory_space=pl.ANY)
    return launch(
        functools.partial(assemble_kernel, plan),
        tokens,
        in_specs=[pl.BlockSpec(memory_space=pltpu.SMEM)] + [anywhere] * len(pieces),
        out_specs=[pl.BlockSpec(memory_space=pltpu.VMEM)] * len(shapes),
        out_shape=[shaped(shape, low) for shape in shapes],
        scratch_shapes=[pltpu.SemaphoreType.DMA((len(plan),))],
        cost_estimate=cost(1, 2 * sum(2 * piece.size for piece in pieces)),
        name="assemble",
    )(jnp.stack(spots).astype(jnp.int32), *pieces)


def gate_kernel(*refs):
    pass


def gate(arrays, tokens):
    anywhere = pl.BlockSpec(memory_space=pl.ANY)
    return launch(
        gate_kernel,
        tokens,
        in_specs=[anywhere] * len(arrays),
        out_specs=[anywhere] * len(arrays),
        out_shape=[shaped(array.shape, array.dtype) for array in arrays],
        input_output_aliases={k: k for k in range(len(arrays))},
        cost_estimate=cost(1, 1),
        name="gate",
    )(*arrays)


class Gather:
    def __init__(self, own, other):
        self.own, self.other = own, other
        self.stage = 0

    def pair(self):
        came = flip_core(self.other)
        pairs = [jnp.stack([self.own, came], axis=1), jnp.stack([came, self.own], axis=1)]
        return jnp.where(core_index() == 0, *pairs)

    @staticmethod
    def exchange(both, tokens=()):
        if tokens:
            (both,) = gate([both], tokens)
        own, other = jnp.split(both, 2)
        every = slice(None)
        plan = [(0, None, 0, lambda spot: (every, spot[0])), (1, None, 0, lambda spot: (every, 1 - spot[0]))]
        k, rows, columns = own.shape
        found = Gather(None, None)
        found.part = assemble(plan, [core_index()], [own, flip_core(other)], [(k, 2, rows, columns)])[0]
        found.part = found.part.reshape(k, 1, 2 * rows, columns)
        return found

    def start_slices(self, hops=False):
        self.pieces = [self.pair()]
        for j in range(1, lax.axis_size("img")):
            bit = j & -j if hops else j
            self.pieces.append(flip(self.pieces[j - bit], "img", bit))

    def finish_slices(self, tokens=(), groups=1):
        slices = len(self.pieces)
        if tokens:
            self.pieces = self.pieces[:1] + list(gate(self.pieces[1:], tokens))
        every = slice(None)
        k, _, rows, columns = self.pieces[0].shape
        k = k // groups
        plan = [
            (j, slice(n * k, (n + 1) * k), n, lambda spot, j=j: (every, every, spot[0] ^ j))
            for n in range(groups)
            for j in range(slices)
        ]
        shape = (k, 2, slices, rows, columns)
        parts = assemble(plan, [lax.axis_index("img")], self.pieces, [shape] * groups)
        found = []
        for part in parts:
            found.append(Gather(None, None))
            found[-1].part = part.reshape(k, 1, 2 * slices * rows, columns)
        return found

    def start_pos(self, tokens=()):
        if tokens:
            (self.part,) = gate([self.part], tokens)
        self.came = flip_pos(self.part, self.stage)
        self.stage += 1

    def finish_pos(self, tokens=()):
        every = slice(None)
        if tokens:
            (self.came,) = gate([self.came], tokens)
        plan = [
            (0, None, 0, lambda spot: (every, spot[0])),
            (1, None, 0, lambda spot: (every, 1 - spot[0])),
        ]
        shape = self.part.shape[:1] + (2,) + self.part.shape[1:]
        self.part = assemble(plan, [own_bit(self.stage - 1)], [self.part, self.came], [shape])[0]
        self.part = self.part.reshape((shape[0], -1) + shape[3:])
        return [self.part]

    def start_last(self):
        self.start_pos()
        self.turned = flip_core(self.part)

    def finish_last(self, tokens, turned_tokens):
        (self.turned,) = gate([self.turned], turned_tokens)
        (self.came,) = gate([self.came], tokens)
        return Pieces([self.part, self.came, self.turned, flip_core(self.came)])


def narrow_kernel(core_ref, weight_ref, *out_refs):
    first = core_ref[0] == 0
    slabs = out_refs[0].shape[0] // 2
    for k, out_ref in enumerate(out_refs):
        for n in range(slabs):
            columns = slice((k * slabs + n) * SLAB, (k * slabs + n + 1) * SLAB)
            left, right = weight_ref[0, :, columns].astype(low), weight_ref[1, :, columns].astype(low)
            out_ref[n] = jnp.where(first, left, right)
            out_ref[slabs + n] = jnp.where(first, right, left)


def narrow(weight, groups, tokens):
    _, owned, hidden = weight.shape
    slabs = hidden // SLAB // groups
    inside = pl.BlockSpec(memory_space=pltpu.VMEM)
    return launch(
        narrow_kernel,
        tokens,
        in_specs=[pl.BlockSpec(memory_space=pltpu.SMEM), inside],
        out_specs=[inside] * groups,
        out_shape=[shaped((2 * slabs, owned, SLAB), low)] * groups,
        cost_estimate=cost(1, 12 * slabs * groups * owned * SLAB),
        name="narrow",
    )(core_index().reshape(1), weight)


class Passing:
    def __init__(self, own, backward, direct):
        self.backward = backward
        came = flip_core(own.astype(low)).astype(wide)
        self.outside = jnp.where(core_index() == (0 if backward else 1), came, 0.0)
        self.total = own + came
        self.bits = powers(lax.axis_size("seq") // 2)
        if direct:
            both = self.total.astype(low)
            self.came = [flip(both, "seq", 2 * j) for j in range(1, lax.axis_size("seq") // 2)]

    def finish(self, tokens):
        total = self.outside
        for j, came in enumerate(gate(self.came, tokens), 1):
            earlier = (pos_index() ^ j) < pos_index()
            total = total + jnp.where(earlier != self.backward, came.astype(wide), 0.0)
        return total

    def hop(self, tokens):
        bit, *self.bits = self.bits
        (came,) = gate([flip(self.total.astype(low), "seq", 2 * bit)], tokens)
        came = came.astype(wide)
        earlier = (pos_index() ^ bit) < pos_index()
        self.outside = self.outside + jnp.where(earlier != self.backward, came, 0.0)
        self.total = self.total + came
        return self.outside


def body(
    images,
    cotangent,
    attention_weight,
    feedforward_weight,
    norm_vectors,
    attention_moment,
    feedforward_moment,
    norm_moment,
    attention_second,
    feedforward_second,
    norm_second,
    attention_average,
    feedforward_average,
    norm_average,
):
    count, span, width = images.shape
    tokens = count * span
    owned = attention_weight.shape[1]
    slabs = feedforward_weight.shape[2] // SLAB
    stages = pos_bits()
    half = slabs // 2
    every = slice(None)

    x, e = images.reshape(tokens, width), cotangent.reshape(tokens, width)
    device = lax.axis_index("seq") * lax.axis_size("img") + lax.axis_index("img")
    placed = lax.dynamic_update_slice(
        jnp.zeros((4, width), wide), norm_vectors.astype(low).astype(wide), (0, device * owned)
    )
    query_weight, key_weight, value_weight, out_weight = attention_weight.astype(low)
    kinds = jnp.stack([key_weight, query_weight]), jnp.stack([value_weight, out_weight])
    first_core = core_index() == 0
    one = Gather(jnp.where(first_core, *kinds), jnp.where(first_core, *kinds[::-1]))
    one.start_slices(True)
    et = turn(e, count, span)
    vec = sum_slowly(placed)
    (one,) = one.finish_slices([et])
    one.start_pos()
    feeds = narrow(feedforward_weight, 2, [one.part])
    marks = [feeds[0], vec]
    feeds = [lax.all_gather(part, "img", axis=1, tiled=True) for part in feeds]
    for _ in range(stages - 2):
        one.finish_pos(marks)
        one.start_pos()
    one.finish_pos(marks)
    one.start_last()
    pieces = one.finish_last([one.part], [one.part])
    two = Gather.exchange(feeds[0])
    two.start_pos([one.came])
    fk, v, a1, a1t, state, wk, wv = project(x, vec, pieces, count, span, [two.part])
    a1t_other = flip_core(a1t)
    prior = Passing(state, False, False)
    for _ in range(stages - 2):
        two.finish_pos([state])
        two.start_pos()
    two.finish_pos([state])
    two.start_last()
    fq, wq, wo = query(a1, pieces, [prior.outside, two.part])
    marks = [prior.hop([fq]), two.turned, a1t_other]
    num, den = attend(fq, fk, v, count, span, marks)
    while prior.bits:
        prior.hop([num])
    prior = prior.outside
    three = Gather.exchange(feeds[1], [num])
    three.start_pos()
    mixed, rden, resid, a2, a2t, mixed_t = mix(x, vec, wo, fq, num, den, prior, count, span, [three.part])
    a2t, mixed_t = turned_whole(a2t), turned_whole(mixed_t)
    lt = jnp.where(first_core, a2t, et)
    lt_other = flip_core(jnp.where(first_core, et, a2t))
    first_pieces = two.finish_last([resid], [fq])
    marks = [resid]
    for _ in range(stages - 2):
        three.finish_pos(marks)
        three.start_pos()
    three.finish_pos(marks)
    three.start_last()
    marks = [three.part, three.turned, lt_other]

    early = feed(first_pieces, a2, e, None, marks)
    early_other = flip_core(early[3])
    second_pieces = three.finish_last([early[0]], [early[0]])
    late = feed(second_pieces, a2, e, early[:2])
    mixed_t_other = flip_core(gate([mixed_t], [late[0]])[0])
    late_other = flip_core(late[3])
    firsts, seconds, outs, inner = [Chain()], [Chain()], [Chain()], [Chain(3)]
    marks = weigh(firsts[0], lt, lt_other, early[2][None], early_other[None], [late[0]])
    output, dres, branch, branch_send, dn, w, dstate, sums_second = turn_back(
        late[0], late[1], resid, e, vec, wo, mixed, rden, fq, count, span, marks + [late_other, mixed_t_other]
    )
    later = Passing(dstate, True, False)
    marks = weigh(seconds[0], lt, lt_other, late[2][None], late_other[None], [dstate, later.outside])
    passed = later.hop([seconds[0].kept])
    for _ in range(stages - 1):
        marks = marks + advance(firsts, [passed])
    parts = [attend_back(0, fq, fk, v, dn, w, prior, span, marks)]
    branch_other = flip_core(gate([branch_send], [parts[0][0]])[0])
    firsts_last = Last(firsts, [parts[0][0]])
    marks = weigh(outs[0], mixed_t, mixed_t_other, branch[None], branch_other[None], firsts_last.sends)
    for _ in range(stages - 1):
        marks = marks + advance(seconds, [parts[0][0]])
    for image in range(1, count):
        parts.append(attend_back(image, fq, fk, v, dn, w, prior, span, marks))
    for _ in range(stages - 1):
        marks = advance(outs, [parts[-1][0]])
    marks = marks + seconds[0].came + firsts_last.settle(slice(0, None), [parts[-1][0]])
    while later.bits:
        later.hop([parts[-1][0]])
    later = later.outside
    kept, sent = finish(parts, fk, v, later, count, span, marks)
    local_squares = firsts_last.squares()
    came = flip_core(sent)
    seconds_last = Last(seconds + outs, [kept])
    marks = seconds_last.sends + [firsts_last.sums]
    grads_in = [enter(0, kept, sent, (wq, wk, wv), x, dres, vec, span, marks)]
    marks = seconds_last.settle(slice(0, 2), [grads_in[0][1]])
    marks = weigh(inner[0], a1t, a1t_other, kept, came, marks)
    for image in range(1, count):
        grads_in.append(enter(image, kept, sent, (wq, wk, wv), x, dres, vec, span, marks))
    seconds_last.settle(slice(2, None), [grads_in[-1][1]])
    local_squares = local_squares + seconds_last.squares()
    input_grad = jnp.stack([part[0] for part in grads_in])
    marks = [seconds_last.sums]
    for _ in range(stages - 1):
        marks = advance(inner, marks)
    inner_last = Last(inner, [seconds_last.sums])
    (sums,) = gate([sum(part[1] for part in grads_in)], inner_last.came[:1])
    vector_grad = sum_slowly(jnp.concatenate([sums[:2], sums_second[:2]], axis=0))
    vector_shard = lax.dynamic_slice_in_dim(vector_grad, device * owned, owned, 1)
    local_squares = local_squares + jnp.sum(vector_shard * vector_shard)
    local_squares = local_squares + inner_last.squares()
    grad_norm = jnp.sqrt(sum_all(jnp.full((8, 128), local_squares))[0, 0])
    (early_shard,) = firsts_last.finish()
    late_shard, out_shard = seconds_last.finish()
    inner_shard = jnp.concatenate([part for pair in inner_last.finish() for part in pair], axis=2)
    attn_shard = jnp.concatenate([inner_shard, jnp.concatenate(out_shard, axis=2)], axis=0)
    feed_shard = jnp.concatenate([jnp.concatenate(pair, axis=2) for pair in zip(early_shard, late_shard)], axis=0)
    factor = clip_bound / jnp.maximum(grad_norm, clip_bound)
    attn_new = adam_update(
        attention_weight, attention_moment, attention_second, attention_average, attn_shard, factor, learn_rate
    )
    feed_new = adam_update(
        feedforward_weight, feedforward_moment, feedforward_second, feedforward_average, feed_shard, factor, learn_rate
    )
    norm_new = adam_update(norm_vectors, norm_moment, norm_second, norm_average, vector_shard, factor, norm_rate)
    output = output.reshape(images.shape)
    input_grad = input_grad.reshape(images.shape)
    return (output, input_grad, grad_norm) + attn_new + feed_new + norm_new


def solution(mesh):
    tokens = P("img", "seq", None)
    rows = P(None, ("seq", "img"), None)
    vectors = P(None, ("seq", "img"))
    group = (rows, rows, vectors)
    return jax.shard_map(
        body,
        mesh=mesh,
        in_specs=(tokens, tokens) + group * 4,
        out_specs=(tokens, tokens, P()) + (rows,) * 8 + (vectors,) * 4,
        check_vma=False,
    )
```

```python
import functools

import jax
import jax.numpy as jnp
import numpy as np
from jax import lax
from jax.experimental import pallas as pl
from jax.experimental.pallas import tpu as pltpu
from jax.sharding import PartitionSpec as P

HEADS = 16
HEAD_DIM = 64
STEP = 10

beta_first = 0.9
beta_second = 0.95
learn_rate = 0.02
norm_rate = 0.2
weight_decay = 0.1
average_decay = 0.75
clip_bound = 1.0
eps_norm = 1e-05
eps_adam = 1e-08

PAIR = 2 * HEAD_DIM
STATE_ROWS = HEAD_DIM + 16
SLAB = 1024
FEED_TILE = 1024
GROUP = 256

low = jnp.bfloat16
wide = jnp.float32


def params(megabytes=56):
    return pltpu.CompilerParams(vmem_limit_bytes=megabytes * 1024 * 1024)


def cost(products, elements):
    return pl.CostEstimate(flops=2 * products, bytes_accessed=elements, transcendentals=0)


def launch(kernel, tokens, in_specs, megabytes=56, **keys):
    known, extra = len(in_specs), len(tokens)

    def run(*refs):
        kernel(*refs[:known], *refs[known + extra :])

    call = pl.pallas_call(
        run, in_specs=list(in_specs) + [pl.BlockSpec(memory_space=pl.ANY)] * extra, compiler_params=params(megabytes), **keys
    )
    return lambda *args: call(*args, *tokens)


def launch_at(kernel, spot, tokens, grid, in_specs, out_specs, megabytes=56, scratch_shapes=(), **keys):
    known, extra = len(in_specs), len(tokens)

    def run(spot_ref, *refs):
        kernel(spot_ref, *refs[:known], *refs[known + extra :])

    call = pl.pallas_call(
        run,
        grid_spec=pltpu.PrefetchScalarGridSpec(
            num_scalar_prefetch=1,
            grid=grid,
            in_specs=list(in_specs) + [pl.BlockSpec(memory_space=pl.ANY)] * extra,
            out_specs=out_specs,
            scratch_shapes=scratch_shapes,
        ),
        compiler_params=params(megabytes),
        **keys,
    )
    return lambda *args: call(spot.reshape(-1).astype(jnp.int32), *args, *tokens)


def reversed_bits(value, count):
    return sum(((value >> k) & 1) << (count - 1 - k) for k in range(count))


def join(target_ref, bits, spot_ref, own_ref, came_ref, own_other_ref, came_other_ref):
    core, high, lowest = spot_ref[0], spot_ref[1], spot_ref[2]
    runs = 1 << (bits - 1)
    rows = target_ref.shape[1] // (2 * runs)
    for run in range(runs):
        source = slice(run * rows, (run + 1) * rows)
        turned = reversed_bits(run, bits)
        for place in range(2):
            first = (high ^ place) * runs + run
            second = turned + (lowest ^ place)
            for ref, slot in (((own_ref, came_ref)[place], core), ((own_other_ref, came_other_ref)[place], 1 - core)):
                at = jnp.where(slot == 0, first, second)
                target_ref[slot, pl.ds(pl.multiple_of(at * rows, rows), rows), :] = ref[source, :]


class Pieces:
    def __init__(self, arrays):
        self.arrays = [array.reshape(array.shape[0], -1, array.shape[-1]) for array in arrays]
        place = pos_index()
        self.bits = pos_bits()
        self.spot = jnp.stack([core_index(), place >> (self.bits - 1), place & 1])

    def blocks(self, columns, place):
        rows = self.arrays[0].shape[1]
        return [pl.BlockSpec((None, rows, columns), place)] * 4

    def second(self, columns):
        mine, others = (
            [part[0, :, columns].reshape(1 << (self.bits - 1), 1, -1, columns.stop - columns.start) for part in pair]
            for pair in (self.arrays[:2], self.arrays[2:])
        )
        own, came = (jnp.where(core_index() == 1, left, right) for left, right in zip(mine, others))
        straight, turned = jnp.concatenate([own, came], axis=1), jnp.concatenate([came, own], axis=1)
        runs = jnp.where(self.spot[2] == 0, straight, turned)
        order = [reversed_bits(run, self.bits - 1) for run in range(1 << (self.bits - 1))]
        return jnp.stack([runs[run] for run in order]).reshape(-1, columns.stop - columns.start)


def shaped(shape, kind):
    return jax.ShapeDtypeStruct(shape, kind)


def whole(shape):
    return pl.BlockSpec(shape, lambda *_: (0,) * len(shape))


def mm(left, right):
    return lax.dot_general(left, right, (((1,), (0,)), ((), ())), preferred_element_type=wide)


def mt(left, right):
    return lax.dot_general(left, right, (((1,), (1,)), ((), ())), preferred_element_type=wide)


def tm(left, right):
    return lax.dot_general(left, right, (((0,), (0,)), ((), ())), preferred_element_type=wide)


def pair_mm(first, second):
    if first[0].shape[1] % 128:
        return mm(*first) + mm(*second)
    return mm(jnp.concatenate([first[0], second[0]], axis=1), jnp.concatenate([first[1], second[1]], axis=0))


def causal_mask(span, below):
    rows = lax.broadcasted_iota(jnp.int32, (span, span), 0)
    columns = lax.broadcasted_iota(jnp.int32, (span, span), 1)
    return (rows >= columns if below else rows <= columns).astype(wide).astype(low)


def first_head(rows):
    return lax.broadcasted_iota(jnp.int32, (rows, PAIR), 1) < HEAD_DIM


def fold_state(product):
    return jnp.where(first_head(HEAD_DIM), product[:HEAD_DIM], product[HEAD_DIM:])


def unfold_state(folded):
    own = first_head(HEAD_DIM)
    zero = jnp.zeros_like(folded)
    return jnp.concatenate([jnp.where(own, folded, zero), jnp.where(own, zero, folded)], axis=0)


def unfold_total(row):
    tall = jnp.broadcast_to(row, (PAIR, PAIR))
    lanes = lax.broadcasted_iota(jnp.int32, (PAIR, PAIR), 1) < HEAD_DIM
    rows = lax.broadcasted_iota(jnp.int32, (PAIR, PAIR), 0) < HEAD_DIM
    return jnp.where(lanes == rows, tall, jnp.zeros_like(tall))


def split_low(values):
    high = values.astype(low)
    return high, (values - high.astype(wide)).astype(low)


def normalised(values):
    centre = jnp.mean(values, axis=-1, keepdims=True)
    centred = values - centre
    spread = jnp.mean(centred * centred, axis=-1, keepdims=True)
    scale = lax.rsqrt(spread + eps_norm)
    return centred * scale, scale


def feature(raw):
    return jnp.where(raw > 0, raw + 1.0, jnp.exp(jnp.minimum(raw, 0.0))).astype(low)


def project_kernel(images, span, bits, spot_ref, x_ref, vec_ref, *refs):
    fk_ref, v_ref, a_ref, at_ref, state_ref, wk_ref, wv_ref, joined_ref = refs[4:]

    @pl.when(pl.program_id(0) == 0)
    def _():
        gain, shift = vec_ref[0:1, :], vec_ref[1:2, :]
        step = span // 3
        for start in range(0, images * span, step):
            rows = slice(start, start + step)
            unit, _ = normalised(x_ref[rows, :].astype(wide))
            a_ref[rows, :] = (unit * gain + shift).astype(low)
        at_ref[...] = a_ref[...].T

    join(joined_ref, bits, spot_ref, *refs[:4])
    keys, values = joined_ref[0], joined_ref[1]
    wk_ref[...] = keys
    wv_ref[...] = values
    fk_ref[...] = feature(mm(a_ref[...], keys))
    v_ref[...] = mm(a_ref[...], values).astype(low)
    ones = jnp.ones((16, span), low)
    for image in range(images):
        rows = slice(image * span, (image + 1) * span)
        for pair in range(GROUP // PAIR):
            lanes = slice(pair * PAIR, (pair + 1) * PAIR)
            key, value = fk_ref[rows, lanes], v_ref[rows, lanes]
            state_ref[image, pair, :HEAD_DIM, :] = fold_state(tm(value, key))
            state_ref[image, pair, HEAD_DIM:, :] = mm(ones, key)


def project(x, vec, pieces, images, span, tokens=()):
    count, width = x.shape
    pairs = GROUP // PAIR
    column = pl.BlockSpec((count, GROUP), lambda g, spot: (0, g))
    weight = pl.BlockSpec((width, GROUP), lambda g, spot: (0, g))
    return launch_at(
        functools.partial(project_kernel, images, span, pieces.bits),
        pieces.spot,
        tokens,
        grid=(width // GROUP,),
        in_specs=[whole((count, width)), whole(vec.shape)] + pieces.blocks(GROUP, lambda g, spot: (0, 0, g)),
        out_specs=[
            column,
            column,
            whole((count, width)),
            whole((width, count)),
            pl.BlockSpec((images, pairs, STATE_ROWS, PAIR), lambda g, spot: (0, g, 0, 0)),
            weight,
            weight,
        ],
        out_shape=[
            shaped((count, width), low),
            shaped((count, width), low),
            shaped((count, width), low),
            shaped((width, count), low),
            shaped((images, width // PAIR, STATE_ROWS, PAIR), wide),
            shaped((width, width), low),
            shaped((width, width), low),
        ],
        scratch_shapes=[pltpu.VMEM((2, width, GROUP), low)],
        cost_estimate=cost(2 * count * width * width, 8 * width * width + 12 * count * width),
        name="project",
    )(x, vec, *pieces.arrays)


def query_kernel(bits, spot_ref, a_ref, *refs):
    fq_ref, wq_ref, wo_ref, joined_ref = refs[4:]
    join(joined_ref, bits, spot_ref, *refs[:4])
    wq_ref[...] = joined_ref[0]
    wo_ref[...] = joined_ref[1]
    fq_ref[...] = feature(mm(a_ref[...], joined_ref[0]))


def query(a, pieces, tokens=()):
    count, width = a.shape
    weight = pl.BlockSpec((width, GROUP), lambda g, spot: (0, g))
    return launch_at(
        functools.partial(query_kernel, pieces.bits),
        pieces.spot,
        tokens,
        grid=(width // GROUP,),
        in_specs=[whole((count, width))] + pieces.blocks(GROUP, lambda g, spot: (1, 0, g)),
        out_specs=[pl.BlockSpec((count, GROUP), lambda g, spot: (0, g)), weight, weight],
        out_shape=[shaped((count, width), low)] + [shaped((width, width), low)] * 2,
        scratch_shapes=[pltpu.VMEM((2, width, GROUP), low)],
        cost_estimate=cost(count * width * width, 6 * width * width + 4 * count * width),
        name="query",
    )(a, *pieces.arrays)


def turn_kernel(x_ref, out_ref):
    out_ref[...] = x_ref[...].T


def turn(x, images, span, tokens=()):
    count, width = x.shape
    return turned_whole(
        launch(
            turn_kernel,
            tokens,
            grid=(images,),
            in_specs=[pl.BlockSpec((span, width), lambda b: (b, 0))],
            out_specs=turned_block(width, span),
            out_shape=turned_shape(images, width, span),
            cost_estimate=cost(1, 4 * count * width),
                name="turn",
        )(x)
    )


def attend_kernel(span, fq_ref, fk_ref, v_ref, num_ref, den_ref):
    own = first_head(span)
    causal = causal_mask(span, True)
    one = jnp.ones((span, PAIR), low)
    zero = jnp.zeros((span, PAIR), low)
    for pair in range(GROUP // PAIR):
        lanes = slice(pair * PAIR, (pair + 1) * PAIR)
        query, key, value = fq_ref[:, lanes], fk_ref[:, lanes], v_ref[:, lanes]
        products = []
        for mask in (own, jnp.logical_not(own)):
            scores = mt(jnp.where(mask, query, zero), key).astype(low) * causal
            right = jnp.concatenate([jnp.where(mask, value, zero), jnp.where(mask, one, zero)], axis=1)
            products.append((scores, right))
        total = pair_mm(*products)
        num_ref[:, lanes] = total[:, :PAIR]
        den_ref[:, lanes] = total[:, PAIR:]


def attend(fq, fk, v, images, span, tokens=()):
    rows, width = fq.shape
    block = pl.BlockSpec((span, GROUP), lambda b, p: (b, p))
    return launch(
        functools.partial(attend_kernel, span),
        tokens,
        grid=(images, width // GROUP),
        in_specs=[block] * 3,
        out_specs=[block] * 2,
        out_shape=[shaped((rows, width), wide)] * 2,
        cost_estimate=cost(16 * rows * span * width, 14 * rows * width),
        name="attend",
    )(fq, fk, v)


def turned_block(width, span):
    if span % 128:
        return pl.BlockSpec((None, width, span), lambda b: (b, 0, 0))
    return pl.BlockSpec((width, span), lambda b: (0, b))


def turned_shape(images, width, span):
    return shaped((images, width, span) if span % 128 else (width, images * span), low)


def turned_whole(array):
    if array.ndim == 2:
        return array
    return jnp.swapaxes(array, 0, 1).reshape(array.shape[1], -1)


def mix_kernel(x_ref, vec_ref, wo_ref, fq_ref, num_ref, den_ref, prior_ref, mixed_ref, rden_ref, resid_ref, a_ref, at_ref, mt_ref):
    width = x_ref.shape[1]
    for pair in range(width // PAIR):
        lanes = slice(pair * PAIR, (pair + 1) * PAIR)
        folded = prior_ref[0, pair]
        matrix = jnp.concatenate(
            [unfold_state(folded[:HEAD_DIM]), unfold_total(folded[HEAD_DIM : HEAD_DIM + 1])], axis=0
        )
        high, rest = split_low(matrix)
        query = fq_ref[:, lanes]
        both = mt(jnp.concatenate([query, query], axis=1), jnp.concatenate([high, rest], axis=1))
        scale = 1.0 / (den_ref[:, lanes] + both[:, PAIR:])
        rden_ref[:, lanes] = scale
        mixed_ref[:, lanes] = ((num_ref[:, lanes] + both[:, :PAIR]) * scale).astype(low)
    resid = x_ref[...].astype(wide) + mm(mixed_ref[...], wo_ref[...])
    resid_ref[...] = resid
    unit, _ = normalised(resid)
    normed = (unit * vec_ref[2:3, :] + vec_ref[3:4, :]).astype(low)
    a_ref[...] = normed
    at_ref[...] = normed.T
    mt_ref[...] = mixed_ref[...].T


def mix(x, vec, wo, fq, num, den, prior, images, span, tokens=()):
    rows_, width = x.shape
    rows = pl.BlockSpec((span, width), lambda b: (b, 0))
    return launch(
        mix_kernel,
        tokens,
        grid=(images,),
        in_specs=[
            rows,
            whole(vec.shape),
            whole(wo.shape),
            rows,
            rows,
            rows,
            pl.BlockSpec((1,) + prior.shape[1:], lambda b: (b, 0, 0, 0)),
        ],
        out_specs=[rows, rows, rows, rows, turned_block(width, span), turned_block(width, span)],
        out_shape=[
            shaped((rows_, width), low),
            shaped((rows_, width), wide),
            shaped((rows_, width), wide),
            shaped((rows_, width), low),
            turned_shape(images, width, span),
            turned_shape(images, width, span),
        ],
        cost_estimate=cost(4 * rows_ * width * width, 24 * rows_ * width + 2 * width * width),
        name="mix",
    )(x, vec, wo, fq, num, den, prior)


gelu_scale = 0.7978845608028654
gelu_cubic = 0.044715


def feed_kernel(fresh, bits, spot_ref, *refs):
    a_ref, e_ref = refs[:2]
    out_ref, da_ref, kept_ref, sent_ref, joined_ref = refs[-5:]
    join(joined_ref, bits, spot_ref, *refs[2:6])

    @pl.when(pl.program_id(0) == 0)
    def _():
        if fresh:
            out_ref[...] = jnp.zeros_like(out_ref)
            da_ref[...] = jnp.zeros_like(da_ref)
        else:
            out_ref[...] = refs[6][...]
            da_ref[...] = refs[7][...]

    up, down = joined_ref[0], joined_ref[1]
    upper = mm(a_ref[...], up)
    grad = mm(e_ref[...], down)
    square = upper * upper
    bend = jnp.tanh(gelu_scale * upper * (1.0 + gelu_cubic * square))
    gate = 0.5 + 0.5 * bend
    hidden = (upper * gate).astype(low)
    slope = gate + 0.5 * upper * (1.0 - bend * bend) * (gelu_scale * (1.0 + 3.0 * gelu_cubic * square))
    dupper = (grad * slope).astype(low)
    out_ref[...] += mt(hidden, down)
    da_ref[...] += mt(dupper, up)
    first = spot_ref[0] == 0
    kept_ref[...] = jnp.where(first, dupper, hidden)
    sent_ref[...] = jnp.where(first, hidden, dupper)


def feed(pieces, a, e, carried, tokens=()):
    rows, width = a.shape
    slabs = pieces.arrays[0].shape[0]
    tiles = SLAB // FEED_TILE
    grads = pl.BlockSpec((rows, FEED_TILE), lambda g, spot: (0, g))
    full = whole((rows, width))
    fresh = carried is None
    return launch_at(
        functools.partial(feed_kernel, fresh, pieces.bits),
        pieces.spot,
        tokens,
        grid=(slabs * tiles,),
        in_specs=[full, full]
        + pieces.blocks(FEED_TILE, lambda g, spot: (g // tiles, 0, g % tiles))
        + ([] if fresh else [full, full]),
        out_specs=[full, full, grads, grads],
        out_shape=[shaped((rows, width), wide)] * 2 + [shaped((rows, slabs * SLAB), low)] * 2,
        scratch_shapes=[pltpu.VMEM((2, width, FEED_TILE), low)],
        cost_estimate=cost(4 * rows * width * slabs * SLAB, 4 * (width + rows) * slabs * SLAB + 20 * rows * width),
        name="feed",
    )(a, e, *pieces.arrays, *(() if fresh else carried))


def weigh_kernel(count, spot_ref, lt_ref, lt_other_ref, x_ref, x_other_ref, kept_ref, sent_ref):
    rows = kept_ref.shape[1]
    for k in range(2):
        places = [pl.ds(pl.multiple_of(spot_ref[k * count + n] * rows, rows), rows) for n in range(count)]
        left, other = (jnp.concatenate([ref[place, :] for place in places], axis=0) for ref in (lt_ref, lt_other_ref))
        product = (mm(left, x_ref[...]) + mm(other, x_other_ref[...])).astype(low)
        (sent_ref if k else kept_ref)[...] = product.reshape(count, rows, -1)


def weigh(chain, lt, lt_other, x, x_other, tokens=()):
    lead, rows, columns = x.shape
    width = lt.shape[0]
    keeps, sends = chain.table()
    count = keeps.shape[0]
    tile = min(FEED_TILE, columns)
    full = whole((width, rows))
    column = pl.BlockSpec((None, rows, tile), lambda n, g, spot: (n, 0, g))
    result = pl.BlockSpec((None, count, width // (2 * count), tile), lambda n, g, spot: (n, 0, 0, g))
    chain.take(
        launch_at(
            functools.partial(weigh_kernel, count),
            jnp.concatenate([keeps, sends]),
            tokens,
            grid=(lead, columns // tile),
            in_specs=[full, full, column, column],
            out_specs=[result, result],
            out_shape=[shaped((lead, count, width // (2 * count), columns), low)] * 2,
            cost_estimate=cost(2 * lead * rows * width * columns, 4 * lead * (rows + width) * columns + 4 * rows * width),
            name="weigh",
        )(lt, lt_other, x, x_other)
    )
    chain.start()
    return chain.sends


def turn_back_kernel(core_ref, x_out_ref, da_ref, resid_ref, e_ref, vec_ref, wo_ref, mixed_ref, rden_ref, fq_ref,
                     out_ref, dres_ref, kept_ref, sent_ref, dn_ref, w_ref, state_ref, sums_ref):
    width = da_ref.shape[1]
    resid = resid_ref[...]
    out_ref[...] = (resid + x_out_ref[...]).astype(low)
    unit, scale = normalised(resid)
    da = da_ref[...]

    @pl.when(pl.program_id(0) == 0)
    def _():
        sums_ref[...] = jnp.zeros_like(sums_ref)

    sums_ref[0:1, :] += jnp.sum(da * unit, axis=0, keepdims=True)
    sums_ref[1:2, :] += jnp.sum(da, axis=0, keepdims=True)
    p = da * vec_ref[2:3, :]
    back = p - jnp.mean(p, axis=-1, keepdims=True) - unit * jnp.mean(p * unit, axis=-1, keepdims=True)
    dres = e_ref[...].astype(wide) + scale * back
    dres_ref[...] = dres
    branch = dres.astype(low)
    left, right = branch[:, : width // 2], branch[:, width // 2 :]
    first = core_ref[0] == 0
    kept_ref[...] = jnp.where(first, left, right)
    sent_ref[...] = jnp.where(first, right, left)
    dmixed = mt(branch, wo_ref[...]).astype(low).astype(wide)
    dnumer = dmixed * rden_ref[...]
    dn_ref[...] = dnumer.astype(low)
    w_ref[...] = (-dnumer * mixed_ref[...].astype(wide)).astype(low)
    for pair in range(width // PAIR):
        lanes = slice(pair * PAIR, (pair + 1) * PAIR)
        query = fq_ref[:, lanes]
        state_ref[0, pair, :HEAD_DIM, :] = fold_state(tm(dn_ref[:, lanes], query))
        total = jnp.sum(fold_state(tm(w_ref[:, lanes], query)), axis=0, keepdims=True)
        state_ref[0, pair, HEAD_DIM:, :] = jnp.broadcast_to(total, (STATE_ROWS - HEAD_DIM, PAIR))


def turn_back(x_out, da, resid, e, vec, wo, mixed, rden, fq, images, span, tokens=()):
    rows_, width = da.shape
    rows = pl.BlockSpec((span, width), lambda b, core: (b, 0))
    state = (images, width // PAIR, STATE_ROWS, PAIR)
    half = pl.BlockSpec((span, width // 2), lambda b, core: (b, 0))
    return launch_at(
        turn_back_kernel,
        core_index(),
        tokens,
        grid=(images,),
        in_specs=[rows, rows, rows, rows, whole(vec.shape), whole(wo.shape), rows, rows, rows],
        out_specs=[rows, rows, half, half, rows, rows] + [pl.BlockSpec((1,) + state[1:], lambda b, core: (b, 0, 0, 0)), whole((8, width))],
        out_shape=[
            shaped((rows_, width), low),
            shaped((rows_, width), wide),
            shaped((rows_, width // 2), low),
            shaped((rows_, width // 2), low),
            shaped((rows_, width), low),
            shaped((rows_, width), low),
            shaped(state, wide),
            shaped((8, width), wide),
        ],
        cost_estimate=cost(5 * rows_ * width * width, 30 * rows_ * width),
        name="turn_back",
    )(x_out, da, resid, e, vec, wo, mixed, rden, fq)


def attend_back_kernel(span, fq_ref, fk_ref, v_ref, dn_ref, w_ref, prior_ref, dq_ref, dfk_ref, dv_ref):
    own = first_head(span)
    own_twice = jnp.concatenate([own, own], axis=1)
    below, above = causal_mask(span, True), causal_mask(span, False)
    one = jnp.ones((span, PAIR), low)
    zero = jnp.zeros((span, PAIR), low)
    zero_twice = jnp.zeros((span, 2 * PAIR), low)
    for pair in range(GROUP // PAIR):
        lanes = slice(pair * PAIR, (pair + 1) * PAIR)
        query, key, value = fq_ref[:, lanes], fk_ref[:, lanes], v_ref[:, lanes]
        grads = jnp.concatenate([dn_ref[:, lanes], w_ref[:, lanes]], axis=1)
        extended = jnp.concatenate([value, one], axis=1)
        folded = prior_ref[0, pair]
        matrix = jnp.concatenate(
            [unfold_state(folded[:HEAD_DIM]), unfold_total(folded[HEAD_DIM : HEAD_DIM + 1])], axis=0
        )
        high, rest = split_low(matrix)
        dfq = mm(jnp.concatenate([grads, grads], axis=1), jnp.concatenate([high, rest], axis=0))
        to_query, to_key, to_value = [], [], []
        for mask, both in ((own, own_twice), (jnp.logical_not(own), jnp.logical_not(own_twice))):
            head_grads = jnp.where(both, grads, zero_twice)
            head_query = jnp.where(mask, query, zero)
            head_key = jnp.where(mask, key, zero)
            to_query.append((mt(head_grads, extended).astype(low) * below, head_key))
            to_key.append((mt(extended, head_grads).astype(low) * above, head_query))
            to_value.append((mt(head_key, query).astype(low) * above, head_grads[:, :PAIR]))
        dfq = dfq + pair_mm(*to_query)
        dq_ref[:, lanes] = (dfq * jnp.minimum(query.astype(wide), 1.0)).astype(low)
        dfk_ref[:, lanes] = pair_mm(*to_key)
        dv_ref[:, lanes] = pair_mm(*to_value)


def attend_back(image, fq, fk, v, dn, w, prior, span, tokens=()):
    width = fq.shape[1]
    block = pl.BlockSpec((span, GROUP), lambda p: (image, p))
    column = pl.BlockSpec((span, GROUP), lambda p: (0, p))
    return launch(
        functools.partial(attend_back_kernel, span),
        tokens,
        grid=(width // GROUP,),
        in_specs=[block] * 5 + [pl.BlockSpec((1, GROUP // PAIR) + prior.shape[2:], lambda p: (image, p, 0, 0))],
        out_specs=[column] * 3,
        out_shape=[shaped((span, width), low), shaped((span, width), wide), shaped((span, width), wide)],
        cost_estimate=cost(32 * span * span * width, 24 * span * width),
        name="attend_back",
    )(fq, fk, v, dn, w, prior)


def finish_kernel(images, span, core_ref, *refs):
    fk_ref, v_ref, later_ref, kept_ref, sent_ref = refs[3 * images :]

    def run(out_ref):
        for image in range(images):
            rows = slice(image * span, (image + 1) * span)
            dq_ref, dfk_ref, dvl_ref = refs[3 * image : 3 * image + 3]
            out_ref[0, rows, :] = dq_ref[...]
            for pair in range(GROUP // PAIR):
                lanes = slice(pair * PAIR, (pair + 1) * PAIR)
                folded = later_ref[image, pair]
                high, rest = split_low(unfold_state(folded[:HEAD_DIM]))
                key, value = fk_ref[rows, lanes], v_ref[rows, lanes]
                dfk = dfk_ref[:, lanes] + folded[HEAD_DIM : HEAD_DIM + 1]
                dfk = dfk + mm(jnp.concatenate([value, value], axis=1), jnp.concatenate([high, rest], axis=0))
                dv = dvl_ref[:, lanes] + mt(
                    jnp.concatenate([key, key], axis=1), jnp.concatenate([high, rest], axis=1)
                )
                out_ref[1, rows, lanes] = (dfk * jnp.minimum(key.astype(wide), 1.0)).astype(low)
                out_ref[2, rows, lanes] = dv.astype(low)

    @pl.when(pl.program_id(0) < pl.num_programs(0) // 2)
    def _():
        run(kept_ref)

    @pl.when(pl.program_id(0) >= pl.num_programs(0) // 2)
    def _():
        run(sent_ref)


def finish(parts, fk, v, later, images, span, tokens=()):
    rows, width = fk.shape
    groups = width // GROUP // 2

    def column(g, core):
        return ((g // groups) ^ core[0]) * groups + g % groups

    block = pl.BlockSpec((rows, GROUP), lambda g, core: (0, column(g, core)))
    part = pl.BlockSpec((span, GROUP), lambda g, core: (0, column(g, core)))
    state = pl.BlockSpec((images, GROUP // PAIR) + later.shape[2:], lambda g, core: (0, column(g, core), 0, 0))
    return launch_at(
        functools.partial(finish_kernel, images, span),
        core_index(),
        tokens,
        grid=(2 * groups,),
        in_specs=[part] * (3 * images) + [block] * 2 + [state],
        out_specs=[
            pl.BlockSpec((3, rows, GROUP), lambda g, core: (0, 0, jnp.minimum(g, groups - 1))),
            pl.BlockSpec((3, rows, GROUP), lambda g, core: (0, 0, jnp.maximum(g - groups, 0))),
        ],
        out_shape=[shaped((3, rows, width // 2), low)] * 2,
        cost_estimate=cost(rows * width * 512, 24 * rows * width),
        name="finish",
    )(*[array for image in parts for array in image], fk, v, later)


def enter_kernel(core_ref, kept_ref, sent_ref, *refs):
    weights = refs[:3]
    x_ref, dres_ref, vec_ref, grad_ref, sums_ref = refs[3:]
    half = x_ref.shape[1] // 2
    da = None
    for k, weight in enumerate(weights):
        for ref, side in ((kept_ref, core_ref[0]), (sent_ref, 1 - core_ref[0])):
            part = mt(ref[k], weight[:, pl.ds(pl.multiple_of(side * half, half), half)])
            da = part if da is None else da + part
    unit, scale = normalised(x_ref[...].astype(wide))
    sums_ref[0:1, :] = jnp.sum(da * unit, axis=0, keepdims=True)
    sums_ref[1:2, :] = jnp.sum(da, axis=0, keepdims=True)
    sums_ref[2:, :] = jnp.zeros_like(sums_ref[2:, :])
    p = da * vec_ref[0:1, :]
    back = p - jnp.mean(p, axis=-1, keepdims=True) - unit * jnp.mean(p * unit, axis=-1, keepdims=True)
    grad_ref[...] = (dres_ref[...] + scale * back).astype(low)


def enter(image, kept, sent, weights, x, dres, vec, span, tokens=()):
    width = x.shape[1]
    rows = pl.BlockSpec((span, width), lambda g, core: (image, 0))
    part = pl.BlockSpec((3, span, width // 2), lambda g, core: (0, image, 0))
    return launch_at(
        enter_kernel,
        core_index(),
        tokens,
        grid=(1,),
        in_specs=[part] * 2 + [whole((width, width))] * 3 + [rows, rows, whole(vec.shape)],
        out_specs=[whole((span, width)), whole((8, width))],
        out_shape=[shaped((span, width), low), shaped((8, width), wide)],
        cost_estimate=cost(3 * span * width * width, 14 * span * width + 6 * width * width),
        name="enter",
    )(kept, sent, *weights, x, dres, vec)


def adam_update(master, moment, second, average, gradient, factor, rate):
    clipped = gradient * factor
    moment = beta_first * moment + (1.0 - beta_first) * clipped
    second = beta_second * second + (1.0 - beta_second) * clipped * clipped
    first_hat = moment / (1.0 - beta_first**STEP)
    second_hat = second / (1.0 - beta_second**STEP)
    master = master - rate * (first_hat / (jnp.sqrt(second_hat) + eps_adam) + weight_decay * master)
    average = average_decay * average + (1.0 - average_decay) * master
    return (master, moment, second, average)


def powers(count):
    return [1 << k for k in range(count.bit_length() - 1)]


def core_index():
    return lax.axis_index("seq") % 2


def pos_index():
    return lax.axis_index("seq") // 2


def pos_bits():
    return (lax.axis_size("seq") // 2).bit_length() - 1


def flip(array, axis, bit):
    return lax.ppermute(array, axis, [(i, i ^ bit) for i in range(lax.axis_size(axis))])


def flip_core(array):
    return flip(array, "seq", 1)


def flip_pos(array, stage):
    bits = pos_bits()
    pairs = [(i, i ^ (2 << (stage if i % 2 == 0 else bits - 1 - stage))) for i in range(lax.axis_size("seq"))]
    return lax.ppermute(array, "seq", pairs)


def own_bit(stage):
    bits = pos_bits()
    return jnp.where(core_index() == 0, pos_index() >> stage, pos_index() >> (bits - 1 - stage)) & 1


def halves(shape, dim):
    index = np.arange(int(np.prod(shape))).reshape(shape)
    return np.stack([index.take(side, axis=dim).ravel() for side in range(2)])


def fold_kernel(chains, spot_ref, *refs):
    ins, outs = refs[: 4 * chains], refs[4 * chains :]
    for k in range(2 * chains):
        value = ins[2 * k][...].astype(wide) + ins[2 * k + 1][...].astype(wide)
        outs[k][...] = value.astype(outs[k].dtype)


def fold(cuts, tokens=()):
    count = cuts[0][2].shape[0]
    steps = max(1, min(2, min(kept.shape[-1] for kept, *_ in cuts) // 256))
    in_specs, out_specs, out_shape, arrays, moved = [], [], [], [], 0
    for k, (kept, came, keeps, sends) in enumerate(cuts):
        lead, _, rows, columns = kept.shape
        block = (lead, 1, rows, columns // steps)
        for side in range(2):
            at = 2 * k * count + side * count
            spec = pl.BlockSpec(block, lambda g, c, spot, at=at: (0, spot[at + g], 0, c))
            in_specs += [spec, spec]
            arrays += [kept, came]
            out_specs.append(pl.BlockSpec(block, lambda g, c, spot: (0, g, 0, c)))
            out_shape.append(shaped((lead, count, rows, columns), low if side else wide))
        moved += 8 * kept.size
    results = launch_at(
        functools.partial(fold_kernel, len(cuts)),
        jnp.concatenate([part for _, _, keeps, sends in cuts for part in (keeps, sends)]),
        tokens,
        grid=(count, steps),
        in_specs=in_specs,
        out_specs=out_specs,
        out_shape=out_shape,
        cost_estimate=cost(1, moved),
        name="fold",
    )(*arrays)
    return [results[2 * k : 2 * k + 2] for k in range(len(cuts))]


class Chain:
    def __init__(self, lead=1):
        self.lead = lead
        self.stage = -1
        self.left = [list(range(pos_bits()))[::-1]] * 2

    def start(self):
        self.came = [flip_pos(self.sends[0], self.stage)]

    def table(self):
        self.stage += 1
        tables = []
        for kind in range(2):
            bit = self.stage if kind == 0 else pos_bits() - 1 - self.stage
            left = self.left[kind]
            tables.append(halves((2,) * len(left), left.index(bit)))
            self.left[kind] = [other for other in left if other != bit]
        table = jnp.where(core_index() == 0, *[jnp.asarray(part, jnp.int32) for part in tables])
        own = own_bit(self.stage)
        return table[own], table[1 - own]

    def cut(self):
        return (self.kept, self.came[0], *self.table())

    def take(self, parts):
        self.kept, self.sends = parts[0], [parts[1]]


def advance(chains, tokens=()):
    parts = fold([chain.cut() for chain in chains], tokens)
    for chain, part in zip(chains, parts):
        chain.take(part)
        chain.start()
    return [array for chain in chains for array in chain.sends]


def last_kernel(ways, pre, pieces, spot_ref, *refs):
    ins, outs = refs[: 2 * pieces], refs[2 * pieces :]
    at = 0
    for k in range(pieces):
        columns = ins[2 * k].shape[-1]
        for j in range(ways):
            place = spot_ref[0] ^ j
            for n in range(pre):
                value = ins[2 * k][n, place].astype(wide) + ins[2 * k + 1][n, place].astype(wide)
                outs[j][n, :, at : at + columns] = value.astype(outs[j].dtype)
        at += columns


class Last:
    def __init__(self, chains, tokens=(), slowly=False):
        slices = lax.axis_size("img")
        ways = 2 if slowly else slices
        self.lead = chains[0].lead
        pre = self.lead * 2 * slices // ways
        arrays = []
        for chain in chains:
            for array in (chain.kept, chain.came[0]):
                arrays.append(array.reshape(pre, ways, -1, array.shape[-1]))
        self.widths = [array.shape[-1] for array in arrays[::2]]
        inside = pl.BlockSpec(memory_space=pltpu.VMEM)
        parts = launch(
            functools.partial(last_kernel, ways, pre, len(chains)),
            tokens,
            in_specs=[pl.BlockSpec(memory_space=pltpu.SMEM)] + [inside] * len(arrays),
            out_specs=[inside] * ways,
            out_shape=[shaped((pre, arrays[0].shape[2], sum(self.widths)), low if j else wide) for j in range(ways)],
            cost_estimate=cost(1, 4 * sum(array.size for array in arrays)),
                name="last",
        )((lax.axis_index("img") % ways).reshape(1), *arrays)
        self.kept, self.sends = parts[0], list(parts[1:])
        self.hops = list(range(1, ways))
        self.left = powers(slices)[1:][::-1] if slowly else []
        self.start()

    def start(self):
        self.came = [flip(array, "img", hop) for array, hop in zip(self.sends, self.hops)]

    def cut(self):
        bit = self.left[-1]
        entries = self.kept.reshape((1, -1) + self.kept.shape[-2:])
        dims = (2 * self.lead,) + (2,) * len(self.left)
        table = jnp.asarray(halves(dims, len(dims) - 1), jnp.int32)
        own = (lax.axis_index("img") // bit) % 2
        self.left = self.left[:-1]
        self.hops = [bit]
        return (entries, self.came[0].reshape(entries.shape), table[own], table[1 - own])

    def take(self, parts):
        self.kept, self.sends = parts[0][0], [parts[1][0]]

    def total(self):
        while self.left:
            advance([self])
        total = self.kept
        for came in self.came:
            total = total + came.astype(wide)
        return total

    def settle(self, stretch, tokens):
        self.came[stretch] = gate(self.came[stretch], tokens)
        return self.came[stretch]

    def squares(self):
        self.sums = self.total()
        return jnp.sum(self.sums * self.sums)

    def finish(self):
        core = core_index()
        total = self.sums.reshape((self.lead, 2) + self.sums.shape[-2:])
        own = lax.dynamic_index_in_dim(total, core, 1, False)
        came = flip_core(lax.dynamic_index_in_dim(total, 1 - core, 1, False))
        first, second = jnp.where(core == 0, own, came), jnp.where(core == 0, came, own)
        at, found = 0, []
        for columns in self.widths:
            found.append((first[..., at : at + columns], second[..., at : at + columns]))
            at += columns
        return found


def slow_hops():
    return [(axis, bit) for axis in ("seq", "img") for bit in powers(lax.axis_size(axis))]


def sum_all(array):
    rounds = [("img", range(1, lax.axis_size("img"))), ("seq", range(2, lax.axis_size("seq"), 2)), ("seq", [1])]
    for axis, hops in rounds:
        came = [flip(array, axis, hop) for hop in hops]
        for other in came:
            array = array + other
    return array


def assemble_kernel(plan, spot_ref, *refs):
    outs = sorted({out for _, _, out, _ in plan})
    count = len(refs) - 1 - len(outs)
    sems = refs[-1]
    copies = []
    for k, (piece, cut, out, where) in enumerate(plan):
        source = refs[piece].at[cut] if cut is not None else refs[piece]
        target = refs[count + out].at[where(spot_ref)]
        copies.append(pltpu.make_async_copy(source, target, sems.at[k]))
    for copy in copies:
        copy.start()
    for copy in copies:
        copy.wait()


def assemble(plan, spots, pieces, shapes, tokens=()):
    anywhere = pl.BlockSpec(memory_space=pl.ANY)
    return launch(
        functools.partial(assemble_kernel, plan),
        tokens,
        in_specs=[pl.BlockSpec(memory_space=pltpu.SMEM)] + [anywhere] * len(pieces),
        out_specs=[pl.BlockSpec(memory_space=pltpu.VMEM)] * len(shapes),
        out_shape=[shaped(shape, low) for shape in shapes],
        scratch_shapes=[pltpu.SemaphoreType.DMA((len(plan),))],
        cost_estimate=cost(1, 2 * sum(2 * piece.size for piece in pieces)),
        name="assemble",
    )(jnp.stack(spots).astype(jnp.int32), *pieces)


def gate_kernel(*refs):
    pass


def gate(arrays, tokens):
    anywhere = pl.BlockSpec(memory_space=pl.ANY)
    return launch(
        gate_kernel,
        tokens,
        in_specs=[anywhere] * len(arrays),
        out_specs=[anywhere] * len(arrays),
        out_shape=[shaped(array.shape, array.dtype) for array in arrays],
        input_output_aliases={k: k for k in range(len(arrays))},
        cost_estimate=cost(1, 1),
        name="gate",
    )(*arrays)


class Gather:
    def __init__(self, own, other):
        self.own, self.other = own, other
        self.stage = 0

    def pair(self):
        came = flip_core(self.other)
        pairs = [jnp.stack([self.own, came], axis=1), jnp.stack([came, self.own], axis=1)]
        return jnp.where(core_index() == 0, *pairs)

    @staticmethod
    def exchange(both, tokens=()):
        if tokens:
            (both,) = gate([both], tokens)
        own, other = jnp.split(both, 2)
        every = slice(None)
        plan = [(0, None, 0, lambda spot: (every, spot[0])), (1, None, 0, lambda spot: (every, 1 - spot[0]))]
        k, rows, columns = own.shape
        found = Gather(None, None)
        found.part = assemble(plan, [core_index()], [own, flip_core(other)], [(k, 2, rows, columns)])[0]
        found.part = found.part.reshape(k, 1, 2 * rows, columns)
        return found

    def start_slices(self, hops=False):
        self.pieces = [self.pair()]
        for j in range(1, lax.axis_size("img")):
            bit = j & -j if hops else j
            self.pieces.append(flip(self.pieces[j - bit], "img", bit))

    def finish_slices(self, tokens=(), groups=1):
        slices = len(self.pieces)
        if tokens:
            self.pieces = self.pieces[:1] + list(gate(self.pieces[1:], tokens))
        every = slice(None)
        k, _, rows, columns = self.pieces[0].shape
        k = k // groups
        plan = [
            (j, slice(n * k, (n + 1) * k), n, lambda spot, j=j: (every, every, spot[0] ^ j))
            for n in range(groups)
            for j in range(slices)
        ]
        shape = (k, 2, slices, rows, columns)
        parts = assemble(plan, [lax.axis_index("img")], self.pieces, [shape] * groups)
        found = []
        for part in parts:
            found.append(Gather(None, None))
            found[-1].part = part.reshape(k, 1, 2 * slices * rows, columns)
        return found

    def start_pos(self, tokens=()):
        if tokens:
            (self.part,) = gate([self.part], tokens)
        self.came = flip_pos(self.part, self.stage)
        self.stage += 1

    def finish_pos(self, tokens=()):
        every = slice(None)
        if tokens:
            (self.came,) = gate([self.came], tokens)
        plan = [
            (0, None, 0, lambda spot: (every, spot[0])),
            (1, None, 0, lambda spot: (every, 1 - spot[0])),
        ]
        shape = self.part.shape[:1] + (2,) + self.part.shape[1:]
        self.part = assemble(plan, [own_bit(self.stage - 1)], [self.part, self.came], [shape])[0]
        self.part = self.part.reshape((shape[0], -1) + shape[3:])
        return [self.part]

    def start_last(self):
        self.start_pos()
        self.turned = flip_core(self.part)

    def finish_last(self, tokens, turned_tokens):
        (self.turned,) = gate([self.turned], turned_tokens)
        (self.came,) = gate([self.came], tokens)
        return Pieces([self.part, self.came, self.turned, flip_core(self.came)])


def narrow_kernel(core_ref, weight_ref, *out_refs):
    first = core_ref[0] == 0
    slabs = out_refs[0].shape[0] // 2
    for k, out_ref in enumerate(out_refs):
        for n in range(slabs):
            columns = slice((k * slabs + n) * SLAB, (k * slabs + n + 1) * SLAB)
            left, right = weight_ref[0, :, columns].astype(low), weight_ref[1, :, columns].astype(low)
            out_ref[n] = jnp.where(first, left, right)
            out_ref[slabs + n] = jnp.where(first, right, left)


def narrow(weight, groups, tokens):
    _, owned, hidden = weight.shape
    slabs = hidden // SLAB // groups
    inside = pl.BlockSpec(memory_space=pltpu.VMEM)
    return launch(
        narrow_kernel,
        tokens,
        in_specs=[pl.BlockSpec(memory_space=pltpu.SMEM), inside],
        out_specs=[inside] * groups,
        out_shape=[shaped((2 * slabs, owned, SLAB), low)] * groups,
        cost_estimate=cost(1, 12 * slabs * groups * owned * SLAB),
        name="narrow",
    )(core_index().reshape(1), weight)


class Passing:
    def __init__(self, own, backward, direct):
        self.backward = backward
        came = flip_core(own.astype(low)).astype(wide)
        self.outside = jnp.where(core_index() == (0 if backward else 1), came, 0.0)
        self.total = own + came
        self.bits = powers(lax.axis_size("seq") // 2)
        if direct:
            both = self.total.astype(low)
            self.came = [flip(both, "seq", 2 * j) for j in range(1, lax.axis_size("seq") // 2)]

    def finish(self, tokens):
        total = self.outside
        for j, came in enumerate(gate(self.came, tokens), 1):
            earlier = (pos_index() ^ j) < pos_index()
            total = total + jnp.where(earlier != self.backward, came.astype(wide), 0.0)
        return total

    def hop(self, tokens):
        bit, *self.bits = self.bits
        (came,) = gate([flip(self.total.astype(low), "seq", 2 * bit)], tokens)
        came = came.astype(wide)
        earlier = (pos_index() ^ bit) < pos_index()
        self.outside = self.outside + jnp.where(earlier != self.backward, came, 0.0)
        self.total = self.total + came
        return self.outside


def body(
    images,
    cotangent,
    attention_weight,
    feedforward_weight,
    norm_vectors,
    attention_moment,
    feedforward_moment,
    norm_moment,
    attention_second,
    feedforward_second,
    norm_second,
    attention_average,
    feedforward_average,
    norm_average,
):
    count, span, width = images.shape
    tokens = count * span
    owned = attention_weight.shape[1]
    slabs = feedforward_weight.shape[2] // SLAB
    stages = pos_bits()
    half = slabs // 2
    every = slice(None)

    x, e = images.reshape(tokens, width), cotangent.reshape(tokens, width)
    low_weights = jnp.pad(attention_weight.astype(low), ((0, 0), (0, 0), (0, 128)))
    vectors = jnp.pad(norm_vectors.astype(low).T, ((0, 0), (width, 124)))
    query_weight, key_weight, value_weight, out_weight = low_weights
    kinds = jnp.stack([key_weight, query_weight]), jnp.stack([value_weight + vectors, out_weight])
    first_core = core_index() == 0
    one = Gather(jnp.where(first_core, *kinds), jnp.where(first_core, *kinds[::-1]))
    one.start_slices(True)
    et = turn(e, count, span)
    (one,) = one.finish_slices([et])
    one.start_pos()
    feeds = narrow(feedforward_weight, 2, [one.part])
    marks = [feeds[0]]
    feeds = [lax.all_gather(part, "img", axis=1, tiled=True) for part in feeds]
    for _ in range(stages - 2):
        one.finish_pos(marks)
        one.start_pos()
    one.finish_pos(marks)
    one.start_last()
    pieces = one.finish_last([one.part], [one.part])
    two = Gather.exchange(feeds[0])
    two.start_pos([one.came])
    vec = pieces.second(slice(width, width + 4)).astype(wide).T
    fk, v, a1, a1t, state, wk, wv = project(x, vec, pieces, count, span, [two.part])
    a1t_other = flip_core(a1t)
    prior = Passing(state, False, False)
    for _ in range(stages - 2):
        two.finish_pos([state])
        two.start_pos()
    two.finish_pos([state])
    two.start_last()
    fq, wq, wo = query(a1, pieces, [prior.outside, two.part])
    marks = [prior.hop([fq]), two.turned, a1t_other]
    num, den = attend(fq, fk, v, count, span, marks)
    while prior.bits:
        prior.hop([num])
    prior = prior.outside
    three = Gather.exchange(feeds[1], [num])
    three.start_pos()
    mixed, rden, resid, a2, a2t, mixed_t = mix(x, vec, wo, fq, num, den, prior, count, span, [three.part])
    a2t, mixed_t = turned_whole(a2t), turned_whole(mixed_t)
    lt = jnp.where(first_core, a2t, et)
    lt_other = flip_core(jnp.where(first_core, et, a2t))
    mixed_t_other = flip_core(mixed_t)
    first_pieces = two.finish_last([resid], [fq])
    marks = [resid]
    for _ in range(stages - 2):
        three.finish_pos(marks)
        three.start_pos()
    three.finish_pos(marks)
    three.start_last()
    marks = [three.part, three.turned]

    early = feed(first_pieces, a2, e, None, marks)
    early_other = flip_core(early[3])
    second_pieces = three.finish_last([early[0]], [early[0]])
    late = feed(second_pieces, a2, e, early[:2], [lt_other, mixed_t_other])
    late_other = flip_core(late[3])
    firsts, seconds, outs, inner = [Chain()], [Chain()], [Chain()], [Chain(3)]
    marks = weigh(firsts[0], lt, lt_other, early[2][None], early_other[None], [late[0]])
    output, dres, branch, branch_send, dn, w, dstate, sums_second = turn_back(
        late[0], late[1], resid, e, vec, wo, mixed, rden, fq, count, span, marks + [late_other]
    )
    later = Passing(dstate, True, False)
    marks = [dstate, later.outside]
    for _ in range(stages - 1):
        marks = marks + advance(firsts, [dstate])
    marks = weigh(seconds[0], lt, lt_other, late[2][None], late_other[None], marks)
    passed = later.hop([seconds[0].kept])
    firsts_last = Last(firsts, [seconds[0].kept])
    parts = [attend_back(0, fq, fk, v, dn, w, prior, span, marks + firsts_last.sends + [passed])]
    branch_other = flip_core(gate([branch_send], [parts[0][0]])[0])
    settled = firsts_last.sends
    marks = weigh(outs[0], mixed_t, mixed_t_other, branch[None], branch_other[None], settled)
    for _ in range(stages - 1):
        marks = marks + advance(seconds, [parts[0][0]])
    for image in range(1, count):
        parts.append(attend_back(image, fq, fk, v, dn, w, prior, span, marks))
    for _ in range(stages - 1):
        marks = advance(outs, [parts[-1][0]])
    marks = marks + seconds[0].came + firsts_last.settle(slice(0, None), [parts[-1][0]])
    while later.bits:
        later.hop([parts[-1][0]])
    later = later.outside
    kept, sent = finish(parts, fk, v, later, count, span, marks)
    local_squares = firsts_last.squares()
    came = flip_core(sent)
    seconds_last = Last(seconds + outs, [kept])
    marks = seconds_last.sends + [firsts_last.sums]
    grads_in = [enter(0, kept, sent, (wq, wk, wv), x, dres, vec, span, marks)]
    marks = seconds_last.settle(slice(0, 2), [grads_in[0][1]])
    marks = weigh(inner[0], a1t, a1t_other, kept, came, marks)
    for image in range(1, count):
        grads_in.append(enter(image, kept, sent, (wq, wk, wv), x, dres, vec, span, marks))
    seconds_last.settle(slice(2, None), [grads_in[-1][1]])
    local_squares = local_squares + seconds_last.squares()
    input_grad = jnp.stack([part[0] for part in grads_in])
    sums = sum(part[1] for part in grads_in)
    vector_grad = jnp.concatenate([sums[:2], sums_second[:2]], axis=0)
    hops = slow_hops()
    for axis, bit in hops[:2]:
        vector_grad = vector_grad + flip(vector_grad, axis, bit)
    marks = [seconds_last.sums, vector_grad]
    for _ in range(stages - 1):
        marks = advance(inner, marks)
    (vector_grad,) = gate([vector_grad], marks)
    for axis, bit in hops[2:]:
        vector_grad = vector_grad + flip(vector_grad, axis, bit)
    device = lax.axis_index("seq") * lax.axis_size("img") + lax.axis_index("img")
    vector_shard = lax.dynamic_slice_in_dim(vector_grad, device * owned, owned, 1)
    inner_last = Last(inner, [seconds_last.sums])
    local_squares = local_squares + jnp.sum(vector_shard * vector_shard)
    local_squares = local_squares + inner_last.squares()
    grad_norm = jnp.sqrt(sum_all(jnp.full((8, 128), local_squares))[0, 0])
    (early_shard,) = firsts_last.finish()
    late_shard, out_shard = seconds_last.finish()
    inner_shard = jnp.concatenate([part for pair in inner_last.finish() for part in pair], axis=2)
    attn_shard = jnp.concatenate([inner_shard, jnp.concatenate(out_shard, axis=2)], axis=0)
    feed_shard = jnp.concatenate([jnp.concatenate(pair, axis=2) for pair in zip(early_shard, late_shard)], axis=0)
    factor = clip_bound / jnp.maximum(grad_norm, clip_bound)
    attn_new = adam_update(
        attention_weight, attention_moment, attention_second, attention_average, attn_shard, factor, learn_rate
    )
    feed_new = adam_update(
        feedforward_weight, feedforward_moment, feedforward_second, feedforward_average, feed_shard, factor, learn_rate
    )
    norm_new = adam_update(norm_vectors, norm_moment, norm_second, norm_average, vector_shard, factor, norm_rate)
    output = output.reshape(images.shape)
    input_grad = input_grad.reshape(images.shape)
    return (output, input_grad, grad_norm) + attn_new + feed_new + norm_new


def solution(mesh):
    tokens = P("img", "seq", None)
    rows = P(None, ("seq", "img"), None)
    vectors = P(None, ("seq", "img"))
    group = (rows, rows, vectors)
    return jax.shard_map(
        body,
        mesh=mesh,
        in_specs=(tokens, tokens) + group * 4,
        out_specs=(tokens, tokens, P()) + (rows,) * 8 + (vectors,) * 4,
        check_vma=False,
    )
```

```python
import functools

import jax
import jax.numpy as jnp
import numpy as np
from jax import lax
from jax.experimental import pallas as pl
from jax.experimental.pallas import tpu as pltpu
from jax.sharding import PartitionSpec as P

HEADS = 16
HEAD_DIM = 64
STEP = 10

beta_first = 0.9
beta_second = 0.95
learn_rate = 0.02
norm_rate = 0.2
weight_decay = 0.1
average_decay = 0.75
clip_bound = 1.0
eps_norm = 1e-05
eps_adam = 1e-08

PAIR = 2 * HEAD_DIM
STATE_ROWS = HEAD_DIM + 16
SLAB = 1024
FEED_TILE = 1024
GROUP = 256

low = jnp.bfloat16
wide = jnp.float32


def params(megabytes=56):
    return pltpu.CompilerParams(vmem_limit_bytes=megabytes * 1024 * 1024)


def cost(products, elements):
    return pl.CostEstimate(flops=2 * products, bytes_accessed=elements, transcendentals=0)


def launch(kernel, tokens, in_specs, megabytes=56, **keys):
    known, extra = len(in_specs), len(tokens)

    def run(*refs):
        kernel(*refs[:known], *refs[known + extra :])

    call = pl.pallas_call(
        run, in_specs=list(in_specs) + [pl.BlockSpec(memory_space=pl.ANY)] * extra, compiler_params=params(megabytes), **keys
    )
    return lambda *args: call(*args, *tokens)


def launch_at(kernel, spot, tokens, grid, in_specs, out_specs, megabytes=56, scratch_shapes=(), **keys):
    known, extra = len(in_specs), len(tokens)

    def run(spot_ref, *refs):
        kernel(spot_ref, *refs[:known], *refs[known + extra :])

    call = pl.pallas_call(
        run,
        grid_spec=pltpu.PrefetchScalarGridSpec(
            num_scalar_prefetch=1,
            grid=grid,
            in_specs=list(in_specs) + [pl.BlockSpec(memory_space=pl.ANY)] * extra,
            out_specs=out_specs,
            scratch_shapes=scratch_shapes,
        ),
        compiler_params=params(megabytes),
        **keys,
    )
    return lambda *args: call(spot.reshape(-1).astype(jnp.int32), *args, *tokens)


def reversed_bits(value, count):
    return sum(((value >> k) & 1) << (count - 1 - k) for k in range(count))


def join(target_ref, bits, spot_ref, own_ref, came_ref, own_other_ref, came_other_ref):
    core, high, lowest = spot_ref[0], spot_ref[1], spot_ref[2]
    runs = 1 << (bits - 1)
    rows = target_ref.shape[1] // (2 * runs)
    for run in range(runs):
        source = slice(run * rows, (run + 1) * rows)
        turned = reversed_bits(run, bits)
        for place in range(2):
            first = (high ^ place) * runs + run
            second = turned + (lowest ^ place)
            for ref, slot in (((own_ref, came_ref)[place], core), ((own_other_ref, came_other_ref)[place], 1 - core)):
                at = jnp.where(slot == 0, first, second)
                target_ref[slot, pl.ds(pl.multiple_of(at * rows, rows), rows), :] = ref[source, :]


class Pieces:
    def __init__(self, arrays):
        self.arrays = [array.reshape(array.shape[0], -1, array.shape[-1]) for array in arrays]
        place = pos_index()
        self.bits = pos_bits()
        self.spot = jnp.stack([core_index(), place >> (self.bits - 1), place & 1])

    def blocks(self, columns, place):
        rows = self.arrays[0].shape[1]
        return [pl.BlockSpec((None, rows, columns), place)] * 4

    def second(self, columns):
        mine, others = (
            [part[0, :, columns].reshape(1 << (self.bits - 1), 1, -1, columns.stop - columns.start) for part in pair]
            for pair in (self.arrays[:2], self.arrays[2:])
        )
        own, came = (jnp.where(core_index() == 1, left, right) for left, right in zip(mine, others))
        straight, turned = jnp.concatenate([own, came], axis=1), jnp.concatenate([came, own], axis=1)
        runs = jnp.where(self.spot[2] == 0, straight, turned)
        order = [reversed_bits(run, self.bits - 1) for run in range(1 << (self.bits - 1))]
        return jnp.stack([runs[run] for run in order]).reshape(-1, columns.stop - columns.start)


def shaped(shape, kind):
    return jax.ShapeDtypeStruct(shape, kind)


def whole(shape):
    return pl.BlockSpec(shape, lambda *_: (0,) * len(shape))


def mm(left, right):
    return lax.dot_general(left, right, (((1,), (0,)), ((), ())), preferred_element_type=wide)


def mt(left, right):
    return lax.dot_general(left, right, (((1,), (1,)), ((), ())), preferred_element_type=wide)


def tm(left, right):
    return lax.dot_general(left, right, (((0,), (0,)), ((), ())), preferred_element_type=wide)


def pair_mm(first, second):
    if first[0].shape[1] % 128:
        return mm(*first) + mm(*second)
    return mm(jnp.concatenate([first[0], second[0]], axis=1), jnp.concatenate([first[1], second[1]], axis=0))


def causal_mask(span, below):
    rows = lax.broadcasted_iota(jnp.int32, (span, span), 0)
    columns = lax.broadcasted_iota(jnp.int32, (span, span), 1)
    return (rows >= columns if below else rows <= columns).astype(wide).astype(low)


def first_head(rows):
    return lax.broadcasted_iota(jnp.int32, (rows, PAIR), 1) < HEAD_DIM


def fold_state(product):
    return jnp.where(first_head(HEAD_DIM), product[:HEAD_DIM], product[HEAD_DIM:])


def unfold_state(folded):
    own = first_head(HEAD_DIM)
    zero = jnp.zeros_like(folded)
    return jnp.concatenate([jnp.where(own, folded, zero), jnp.where(own, zero, folded)], axis=0)


def unfold_total(row):
    tall = jnp.broadcast_to(row, (PAIR, PAIR))
    lanes = lax.broadcasted_iota(jnp.int32, (PAIR, PAIR), 1) < HEAD_DIM
    rows = lax.broadcasted_iota(jnp.int32, (PAIR, PAIR), 0) < HEAD_DIM
    return jnp.where(lanes == rows, tall, jnp.zeros_like(tall))


def split_low(values):
    high = values.astype(low)
    return high, (values - high.astype(wide)).astype(low)


def normalised(values):
    centre = jnp.mean(values, axis=-1, keepdims=True)
    centred = values - centre
    spread = jnp.mean(centred * centred, axis=-1, keepdims=True)
    scale = lax.rsqrt(spread + eps_norm)
    return centred * scale, scale


def feature(raw):
    return jnp.where(raw > 0, raw + 1.0, jnp.exp(jnp.minimum(raw, 0.0))).astype(low)


def project_kernel(images, span, bits, spot_ref, x_ref, vec_ref, *refs):
    fk_ref, v_ref, fq_ref, a_ref, at_ref, state_ref, wk_ref, wv_ref, wq_ref, wo_ref, joined_ref = refs[8:]

    @pl.when(pl.program_id(0) == 0)
    def _():
        gain, shift = vec_ref[0:1, :], vec_ref[1:2, :]
        step = span // 3
        for start in range(0, images * span, step):
            rows = slice(start, start + step)
            unit, _ = normalised(x_ref[rows, :].astype(wide))
            a_ref[rows, :] = (unit * gain + shift).astype(low)
        at_ref[...] = a_ref[...].T

    join(joined_ref, bits, spot_ref, *refs[:4])
    keys, values = joined_ref[0], joined_ref[1]
    wk_ref[...] = keys
    wv_ref[...] = values
    fk_ref[...] = feature(mm(a_ref[...], keys))
    v_ref[...] = mm(a_ref[...], values).astype(low)
    join(joined_ref, bits, spot_ref, *refs[4:8])
    wq_ref[...] = joined_ref[0]
    wo_ref[...] = joined_ref[1]
    fq_ref[...] = feature(mm(a_ref[...], joined_ref[0]))
    ones = jnp.ones((16, span), low)
    for image in range(images):
        rows = slice(image * span, (image + 1) * span)
        for pair in range(GROUP // PAIR):
            lanes = slice(pair * PAIR, (pair + 1) * PAIR)
            key, value = fk_ref[rows, lanes], v_ref[rows, lanes]
            state_ref[image, pair, :HEAD_DIM, :] = fold_state(tm(value, key))
            state_ref[image, pair, HEAD_DIM:, :] = mm(ones, key)


def project(x, vec, pieces, images, span, tokens=()):
    count, width = x.shape
    pairs = GROUP // PAIR
    column = pl.BlockSpec((count, GROUP), lambda g, spot: (0, g))
    weight = pl.BlockSpec((width, GROUP), lambda g, spot: (0, g))
    return launch_at(
        functools.partial(project_kernel, images, span, pieces.bits),
        pieces.spot,
        tokens,
        grid=(width // GROUP,),
        in_specs=[whole((count, width)), whole(vec.shape)]
        + pieces.blocks(GROUP, lambda g, spot: (0, 0, g))
        + pieces.blocks(GROUP, lambda g, spot: (1, 0, g)),
        out_specs=[
            column,
            column,
            column,
            whole((count, width)),
            whole((width, count)),
            pl.BlockSpec((images, pairs, STATE_ROWS, PAIR), lambda g, spot: (0, g, 0, 0)),
            weight,
            weight,
            weight,
            weight,
        ],
        out_shape=[
            shaped((count, width), low),
            shaped((count, width), low),
            shaped((count, width), low),
            shaped((count, width), low),
            shaped((width, count), low),
            shaped((images, width // PAIR, STATE_ROWS, PAIR), wide),
            shaped((width, width), low),
            shaped((width, width), low),
            shaped((width, width), low),
            shaped((width, width), low),
        ],
        scratch_shapes=[pltpu.VMEM((2, width, GROUP), low)],
        cost_estimate=cost(3 * count * width * width, 8 * width * width + 12 * count * width),
        name="project",
    )(x, vec, *pieces.arrays, *pieces.arrays)


def turn_kernel(x_ref, out_ref):
    out_ref[...] = x_ref[...].T


def turn(x, images, span, tokens=()):
    count, width = x.shape
    return turned_whole(
        launch(
            turn_kernel,
            tokens,
            grid=(images,),
            in_specs=[pl.BlockSpec((span, width), lambda b: (b, 0))],
            out_specs=turned_block(width, span),
            out_shape=turned_shape(images, width, span),
            cost_estimate=cost(1, 4 * count * width),
                name="turn",
        )(x)
    )


def attend_kernel(span, fq_ref, fk_ref, v_ref, num_ref, den_ref):
    own = first_head(span)
    causal = causal_mask(span, True)
    one = jnp.ones((span, PAIR), low)
    zero = jnp.zeros((span, PAIR), low)
    for pair in range(GROUP // PAIR):
        lanes = slice(pair * PAIR, (pair + 1) * PAIR)
        query, key, value = fq_ref[:, lanes], fk_ref[:, lanes], v_ref[:, lanes]
        products = []
        for mask in (own, jnp.logical_not(own)):
            scores = mt(jnp.where(mask, query, zero), key).astype(low) * causal
            right = jnp.concatenate([jnp.where(mask, value, zero), jnp.where(mask, one, zero)], axis=1)
            products.append((scores, right))
        total = pair_mm(*products)
        num_ref[:, lanes] = total[:, :PAIR]
        den_ref[:, lanes] = total[:, PAIR:]


def attend(fq, fk, v, images, span, tokens=()):
    rows, width = fq.shape
    block = pl.BlockSpec((span, GROUP), lambda b, p: (b, p))
    return launch(
        functools.partial(attend_kernel, span),
        tokens,
        grid=(images, width // GROUP),
        in_specs=[block] * 3,
        out_specs=[block] * 2,
        out_shape=[shaped((rows, width), wide)] * 2,
        cost_estimate=cost(16 * rows * span * width, 14 * rows * width),
        name="attend",
    )(fq, fk, v)


def turned_block(width, span):
    if span % 128:
        return pl.BlockSpec((None, width, span), lambda b: (b, 0, 0))
    return pl.BlockSpec((width, span), lambda b: (0, b))


def turned_shape(images, width, span):
    return shaped((images, width, span) if span % 128 else (width, images * span), low)


def turned_whole(array):
    if array.ndim == 2:
        return array
    return jnp.swapaxes(array, 0, 1).reshape(array.shape[1], -1)


def mix_kernel(x_ref, vec_ref, wo_ref, fq_ref, num_ref, den_ref, prior_ref, mixed_ref, rden_ref, resid_ref, a_ref, at_ref, mt_ref):
    width = x_ref.shape[1]
    for pair in range(width // PAIR):
        lanes = slice(pair * PAIR, (pair + 1) * PAIR)
        folded = prior_ref[0, pair]
        matrix = jnp.concatenate(
            [unfold_state(folded[:HEAD_DIM]), unfold_total(folded[HEAD_DIM : HEAD_DIM + 1])], axis=0
        )
        high, rest = split_low(matrix)
        query = fq_ref[:, lanes]
        both = mt(jnp.concatenate([query, query], axis=1), jnp.concatenate([high, rest], axis=1))
        scale = 1.0 / (den_ref[:, lanes] + both[:, PAIR:])
        rden_ref[:, lanes] = scale
        mixed_ref[:, lanes] = ((num_ref[:, lanes] + both[:, :PAIR]) * scale).astype(low)
    resid = x_ref[...].astype(wide) + mm(mixed_ref[...], wo_ref[...])
    resid_ref[...] = resid
    unit, _ = normalised(resid)
    normed = (unit * vec_ref[2:3, :] + vec_ref[3:4, :]).astype(low)
    a_ref[...] = normed
    at_ref[...] = normed.T
    mt_ref[...] = mixed_ref[...].T


def mix(x, vec, wo, fq, num, den, prior, images, span, tokens=()):
    rows_, width = x.shape
    rows = pl.BlockSpec((span, width), lambda b: (b, 0))
    return launch(
        mix_kernel,
        tokens,
        grid=(images,),
        in_specs=[
            rows,
            whole(vec.shape),
            whole(wo.shape),
            rows,
            rows,
            rows,
            pl.BlockSpec((1,) + prior.shape[1:], lambda b: (b, 0, 0, 0)),
        ],
        out_specs=[rows, rows, rows, rows, turned_block(width, span), turned_block(width, span)],
        out_shape=[
            shaped((rows_, width), low),
            shaped((rows_, width), wide),
            shaped((rows_, width), wide),
            shaped((rows_, width), low),
            turned_shape(images, width, span),
            turned_shape(images, width, span),
        ],
        cost_estimate=cost(4 * rows_ * width * width, 24 * rows_ * width + 2 * width * width),
        name="mix",
    )(x, vec, wo, fq, num, den, prior)


gelu_scale = 0.7978845608028654
gelu_cubic = 0.044715


def feed_kernel(fresh, bits, spot_ref, *refs):
    a_ref, e_ref = refs[:2]
    out_ref, da_ref, kept_ref, sent_ref, joined_ref = refs[-5:]
    join(joined_ref, bits, spot_ref, *refs[2:6])

    @pl.when(pl.program_id(0) == 0)
    def _():
        if fresh:
            out_ref[...] = jnp.zeros_like(out_ref)
            da_ref[...] = jnp.zeros_like(da_ref)
        else:
            out_ref[...] = refs[6][...]
            da_ref[...] = refs[7][...]

    up, down = joined_ref[0], joined_ref[1]
    upper = mm(a_ref[...], up)
    grad = mm(e_ref[...], down)
    square = upper * upper
    bend = jnp.tanh(gelu_scale * upper * (1.0 + gelu_cubic * square))
    gate = 0.5 + 0.5 * bend
    hidden = (upper * gate).astype(low)
    slope = gate + 0.5 * upper * (1.0 - bend * bend) * (gelu_scale * (1.0 + 3.0 * gelu_cubic * square))
    dupper = (grad * slope).astype(low)
    out_ref[...] += mt(hidden, down)
    da_ref[...] += mt(dupper, up)
    first = spot_ref[0] == 0
    kept_ref[...] = jnp.where(first, dupper, hidden)
    sent_ref[...] = jnp.where(first, hidden, dupper)


def feed(pieces, a, e, carried, tokens=()):
    rows, width = a.shape
    slabs = pieces.arrays[0].shape[0]
    tiles = SLAB // FEED_TILE
    grads = pl.BlockSpec((rows, FEED_TILE), lambda g, spot: (0, g))
    full = whole((rows, width))
    fresh = carried is None
    return launch_at(
        functools.partial(feed_kernel, fresh, pieces.bits),
        pieces.spot,
        tokens,
        grid=(slabs * tiles,),
        in_specs=[full, full]
        + pieces.blocks(FEED_TILE, lambda g, spot: (g // tiles, 0, g % tiles))
        + ([] if fresh else [full, full]),
        out_specs=[full, full, grads, grads],
        out_shape=[shaped((rows, width), wide)] * 2 + [shaped((rows, slabs * SLAB), low)] * 2,
        scratch_shapes=[pltpu.VMEM((2, width, FEED_TILE), low)],
        cost_estimate=cost(4 * rows * width * slabs * SLAB, 4 * (width + rows) * slabs * SLAB + 20 * rows * width),
        name="feed",
    )(a, e, *pieces.arrays, *(() if fresh else carried))


def weigh_kernel(count, spot_ref, lt_ref, lt_other_ref, x_ref, x_other_ref, kept_ref, sent_ref):
    rows = kept_ref.shape[1]
    for k in range(2):
        places = [pl.ds(pl.multiple_of(spot_ref[k * count + n] * rows, rows), rows) for n in range(count)]
        left, other = (jnp.concatenate([ref[place, :] for place in places], axis=0) for ref in (lt_ref, lt_other_ref))
        product = (mm(left, x_ref[...]) + mm(other, x_other_ref[...])).astype(low)
        (sent_ref if k else kept_ref)[...] = product.reshape(count, rows, -1)


def weigh(chain, lt, lt_other, x, x_other, tokens=()):
    lead, rows, columns = x.shape
    width = lt.shape[0]
    keeps, sends = chain.table()
    count = keeps.shape[0]
    tile = min(FEED_TILE, columns)
    full = whole((width, rows))
    column = pl.BlockSpec((None, rows, tile), lambda n, g, spot: (n, 0, g))
    result = pl.BlockSpec((None, count, width // (2 * count), tile), lambda n, g, spot: (n, 0, 0, g))
    chain.take(
        launch_at(
            functools.partial(weigh_kernel, count),
            jnp.concatenate([keeps, sends]),
            tokens,
            grid=(lead, columns // tile),
            in_specs=[full, full, column, column],
            out_specs=[result, result],
            out_shape=[shaped((lead, count, width // (2 * count), columns), low)] * 2,
            cost_estimate=cost(2 * lead * rows * width * columns, 4 * lead * (rows + width) * columns + 4 * rows * width),
            name="weigh",
        )(lt, lt_other, x, x_other)
    )
    chain.start()
    return chain.sends


def turn_back_kernel(core_ref, x_out_ref, da_ref, resid_ref, e_ref, vec_ref, wo_ref, mixed_ref, rden_ref, fq_ref,
                     out_ref, dres_ref, kept_ref, sent_ref, dn_ref, w_ref, state_ref, sums_ref):
    width = da_ref.shape[1]
    resid = resid_ref[...]
    out_ref[...] = (resid + x_out_ref[...]).astype(low)
    unit, scale = normalised(resid)
    da = da_ref[...]

    @pl.when(pl.program_id(0) == 0)
    def _():
        sums_ref[...] = jnp.zeros_like(sums_ref)

    sums_ref[0:1, :] += jnp.sum(da * unit, axis=0, keepdims=True)
    sums_ref[1:2, :] += jnp.sum(da, axis=0, keepdims=True)
    p = da * vec_ref[2:3, :]
    back = p - jnp.mean(p, axis=-1, keepdims=True) - unit * jnp.mean(p * unit, axis=-1, keepdims=True)
    dres = e_ref[...].astype(wide) + scale * back
    dres_ref[...] = dres
    branch = dres.astype(low)
    left, right = branch[:, : width // 2], branch[:, width // 2 :]
    first = core_ref[0] == 0
    kept_ref[...] = jnp.where(first, left, right)
    sent_ref[...] = jnp.where(first, right, left)
    dmixed = mt(branch, wo_ref[...]).astype(low).astype(wide)
    dnumer = dmixed * rden_ref[...]
    dn_ref[...] = dnumer.astype(low)
    w_ref[...] = (-dnumer * mixed_ref[...].astype(wide)).astype(low)
    for pair in range(width // PAIR):
        lanes = slice(pair * PAIR, (pair + 1) * PAIR)
        query = fq_ref[:, lanes]
        state_ref[0, pair, :HEAD_DIM, :] = fold_state(tm(dn_ref[:, lanes], query))
        total = jnp.sum(fold_state(tm(w_ref[:, lanes], query)), axis=0, keepdims=True)
        state_ref[0, pair, HEAD_DIM:, :] = jnp.broadcast_to(total, (STATE_ROWS - HEAD_DIM, PAIR))


def turn_back(x_out, da, resid, e, vec, wo, mixed, rden, fq, images, span, tokens=()):
    rows_, width = da.shape
    rows = pl.BlockSpec((span, width), lambda b, core: (b, 0))
    state = (images, width // PAIR, STATE_ROWS, PAIR)
    half = pl.BlockSpec((span, width // 2), lambda b, core: (b, 0))
    return launch_at(
        turn_back_kernel,
        core_index(),
        tokens,
        grid=(images,),
        in_specs=[rows, rows, rows, rows, whole(vec.shape), whole(wo.shape), rows, rows, rows],
        out_specs=[rows, rows, half, half, rows, rows] + [pl.BlockSpec((1,) + state[1:], lambda b, core: (b, 0, 0, 0)), whole((8, width))],
        out_shape=[
            shaped((rows_, width), low),
            shaped((rows_, width), wide),
            shaped((rows_, width // 2), low),
            shaped((rows_, width // 2), low),
            shaped((rows_, width), low),
            shaped((rows_, width), low),
            shaped(state, wide),
            shaped((8, width), wide),
        ],
        cost_estimate=cost(5 * rows_ * width * width, 30 * rows_ * width),
        name="turn_back",
    )(x_out, da, resid, e, vec, wo, mixed, rden, fq)


def attend_back_kernel(span, fq_ref, fk_ref, v_ref, dn_ref, w_ref, prior_ref, dq_ref, dfk_ref, dv_ref):
    own = first_head(span)
    own_twice = jnp.concatenate([own, own], axis=1)
    below, above = causal_mask(span, True), causal_mask(span, False)
    one = jnp.ones((span, PAIR), low)
    zero = jnp.zeros((span, PAIR), low)
    zero_twice = jnp.zeros((span, 2 * PAIR), low)
    for pair in range(GROUP // PAIR):
        lanes = slice(pair * PAIR, (pair + 1) * PAIR)
        query, key, value = fq_ref[:, lanes], fk_ref[:, lanes], v_ref[:, lanes]
        grads = jnp.concatenate([dn_ref[:, lanes], w_ref[:, lanes]], axis=1)
        extended = jnp.concatenate([value, one], axis=1)
        folded = prior_ref[0, pair]
        matrix = jnp.concatenate(
            [unfold_state(folded[:HEAD_DIM]), unfold_total(folded[HEAD_DIM : HEAD_DIM + 1])], axis=0
        )
        high, rest = split_low(matrix)
        dfq = mm(jnp.concatenate([grads, grads], axis=1), jnp.concatenate([high, rest], axis=0))
        to_query, to_key, to_value = [], [], []
        for mask, both in ((own, own_twice), (jnp.logical_not(own), jnp.logical_not(own_twice))):
            head_grads = jnp.where(both, grads, zero_twice)
            head_query = jnp.where(mask, query, zero)
            head_key = jnp.where(mask, key, zero)
            to_query.append((mt(head_grads, extended).astype(low) * below, head_key))
            to_key.append((mt(extended, head_grads).astype(low) * above, head_query))
            to_value.append((mt(head_key, query).astype(low) * above, head_grads[:, :PAIR]))
        dfq = dfq + pair_mm(*to_query)
        dq_ref[:, lanes] = (dfq * jnp.minimum(query.astype(wide), 1.0)).astype(low)
        dfk_ref[:, lanes] = pair_mm(*to_key)
        dv_ref[:, lanes] = pair_mm(*to_value)


def attend_back(image, fq, fk, v, dn, w, prior, span, tokens=()):
    width = fq.shape[1]
    block = pl.BlockSpec((span, GROUP), lambda p: (image, p))
    column = pl.BlockSpec((span, GROUP), lambda p: (0, p))
    return launch(
        functools.partial(attend_back_kernel, span),
        tokens,
        grid=(width // GROUP,),
        in_specs=[block] * 5 + [pl.BlockSpec((1, GROUP // PAIR) + prior.shape[2:], lambda p: (image, p, 0, 0))],
        out_specs=[column] * 3,
        out_shape=[shaped((span, width), low), shaped((span, width), wide), shaped((span, width), wide)],
        cost_estimate=cost(32 * span * span * width, 24 * span * width),
        name="attend_back",
    )(fq, fk, v, dn, w, prior)


def finish_kernel(images, span, core_ref, *refs):
    fk_ref, v_ref, later_ref, kept_ref, sent_ref = refs[3 * images :]

    def run(out_ref):
        for image in range(images):
            rows = slice(image * span, (image + 1) * span)
            dq_ref, dfk_ref, dvl_ref = refs[3 * image : 3 * image + 3]
            out_ref[0, rows, :] = dq_ref[...]
            for pair in range(GROUP // PAIR):
                lanes = slice(pair * PAIR, (pair + 1) * PAIR)
                folded = later_ref[image, pair]
                high, rest = split_low(unfold_state(folded[:HEAD_DIM]))
                key, value = fk_ref[rows, lanes], v_ref[rows, lanes]
                dfk = dfk_ref[:, lanes] + folded[HEAD_DIM : HEAD_DIM + 1]
                dfk = dfk + mm(jnp.concatenate([value, value], axis=1), jnp.concatenate([high, rest], axis=0))
                dv = dvl_ref[:, lanes] + mt(
                    jnp.concatenate([key, key], axis=1), jnp.concatenate([high, rest], axis=1)
                )
                out_ref[1, rows, lanes] = (dfk * jnp.minimum(key.astype(wide), 1.0)).astype(low)
                out_ref[2, rows, lanes] = dv.astype(low)

    @pl.when(pl.program_id(0) < pl.num_programs(0) // 2)
    def _():
        run(kept_ref)

    @pl.when(pl.program_id(0) >= pl.num_programs(0) // 2)
    def _():
        run(sent_ref)


def finish(parts, fk, v, later, images, span, tokens=()):
    rows, width = fk.shape
    groups = width // GROUP // 2

    def column(g, core):
        return ((g // groups) ^ core[0]) * groups + g % groups

    block = pl.BlockSpec((rows, GROUP), lambda g, core: (0, column(g, core)))
    part = pl.BlockSpec((span, GROUP), lambda g, core: (0, column(g, core)))
    state = pl.BlockSpec((images, GROUP // PAIR) + later.shape[2:], lambda g, core: (0, column(g, core), 0, 0))
    return launch_at(
        functools.partial(finish_kernel, images, span),
        core_index(),
        tokens,
        grid=(2 * groups,),
        in_specs=[part] * (3 * images) + [block] * 2 + [state],
        out_specs=[
            pl.BlockSpec((3, rows, GROUP), lambda g, core: (0, 0, jnp.minimum(g, groups - 1))),
            pl.BlockSpec((3, rows, GROUP), lambda g, core: (0, 0, jnp.maximum(g - groups, 0))),
        ],
        out_shape=[shaped((3, rows, width // 2), low)] * 2,
        cost_estimate=cost(rows * width * 512, 24 * rows * width),
        name="finish",
    )(*[array for image in parts for array in image], fk, v, later)


def enter_kernel(core_ref, kept_ref, sent_ref, *refs):
    weights = refs[:3]
    x_ref, dres_ref, vec_ref, grad_ref, sums_ref = refs[3:]
    half = x_ref.shape[1] // 2
    da = None
    for k, weight in enumerate(weights):
        for ref, side in ((kept_ref, core_ref[0]), (sent_ref, 1 - core_ref[0])):
            part = mt(ref[k], weight[:, pl.ds(pl.multiple_of(side * half, half), half)])
            da = part if da is None else da + part
    unit, scale = normalised(x_ref[...].astype(wide))
    sums_ref[0:1, :] = jnp.sum(da * unit, axis=0, keepdims=True)
    sums_ref[1:2, :] = jnp.sum(da, axis=0, keepdims=True)
    sums_ref[2:, :] = jnp.zeros_like(sums_ref[2:, :])
    p = da * vec_ref[0:1, :]
    back = p - jnp.mean(p, axis=-1, keepdims=True) - unit * jnp.mean(p * unit, axis=-1, keepdims=True)
    grad_ref[...] = (dres_ref[...] + scale * back).astype(low)


def enter(image, kept, sent, weights, x, dres, vec, span, tokens=()):
    width = x.shape[1]
    rows = pl.BlockSpec((span, width), lambda g, core: (image, 0))
    part = pl.BlockSpec((3, span, width // 2), lambda g, core: (0, image, 0))
    return launch_at(
        enter_kernel,
        core_index(),
        tokens,
        grid=(1,),
        in_specs=[part] * 2 + [whole((width, width))] * 3 + [rows, rows, whole(vec.shape)],
        out_specs=[whole((span, width)), whole((8, width))],
        out_shape=[shaped((span, width), low), shaped((8, width), wide)],
        cost_estimate=cost(3 * span * width * width, 14 * span * width + 6 * width * width),
        name="enter",
    )(kept, sent, *weights, x, dres, vec)


def adam_update(master, moment, second, average, gradient, factor, rate):
    clipped = gradient * factor
    moment = beta_first * moment + (1.0 - beta_first) * clipped
    second = beta_second * second + (1.0 - beta_second) * clipped * clipped
    first_hat = moment / (1.0 - beta_first**STEP)
    second_hat = second / (1.0 - beta_second**STEP)
    master = master - rate * (first_hat / (jnp.sqrt(second_hat) + eps_adam) + weight_decay * master)
    average = average_decay * average + (1.0 - average_decay) * master
    return (master, moment, second, average)


def powers(count):
    return [1 << k for k in range(count.bit_length() - 1)]


def core_index():
    return lax.axis_index("seq") % 2


def pos_index():
    return lax.axis_index("seq") // 2


def pos_bits():
    return (lax.axis_size("seq") // 2).bit_length() - 1


def flip(array, axis, bit):
    return lax.ppermute(array, axis, [(i, i ^ bit) for i in range(lax.axis_size(axis))])


def flip_core(array):
    return flip(array, "seq", 1)


def flip_pos(array, stage):
    bits = pos_bits()
    pairs = [(i, i ^ (2 << (stage if i % 2 == 0 else bits - 1 - stage))) for i in range(lax.axis_size("seq"))]
    return lax.ppermute(array, "seq", pairs)


def own_bit(stage):
    bits = pos_bits()
    return jnp.where(core_index() == 0, pos_index() >> stage, pos_index() >> (bits - 1 - stage)) & 1


def halves(shape, dim):
    index = np.arange(int(np.prod(shape))).reshape(shape)
    return np.stack([index.take(side, axis=dim).ravel() for side in range(2)])


def fold_kernel(chains, spot_ref, *refs):
    ins, outs = refs[: 4 * chains], refs[4 * chains :]
    for k in range(2 * chains):
        value = ins[2 * k][...].astype(wide) + ins[2 * k + 1][...].astype(wide)
        outs[k][...] = value.astype(outs[k].dtype)


def fold(cuts, tokens=()):
    count = cuts[0][2].shape[0]
    steps = max(1, min(2, min(kept.shape[-1] for kept, *_ in cuts) // 256))
    in_specs, out_specs, out_shape, arrays, moved = [], [], [], [], 0
    for k, (kept, came, keeps, sends) in enumerate(cuts):
        lead, _, rows, columns = kept.shape
        block = (lead, 1, rows, columns // steps)
        for side in range(2):
            at = 2 * k * count + side * count
            spec = pl.BlockSpec(block, lambda g, c, spot, at=at: (0, spot[at + g], 0, c))
            in_specs += [spec, spec]
            arrays += [kept, came]
            out_specs.append(pl.BlockSpec(block, lambda g, c, spot: (0, g, 0, c)))
            out_shape.append(shaped((lead, count, rows, columns), low if side else wide))
        moved += 8 * kept.size
    results = launch_at(
        functools.partial(fold_kernel, len(cuts)),
        jnp.concatenate([part for _, _, keeps, sends in cuts for part in (keeps, sends)]),
        tokens,
        grid=(count, steps),
        in_specs=in_specs,
        out_specs=out_specs,
        out_shape=out_shape,
        cost_estimate=cost(1, moved),
        name="fold",
    )(*arrays)
    return [results[2 * k : 2 * k + 2] for k in range(len(cuts))]


class Chain:
    def __init__(self, lead=1):
        self.lead = lead
        self.stage = -1
        self.left = [list(range(pos_bits()))[::-1]] * 2

    def start(self):
        self.came = [flip_pos(self.sends[0], self.stage)]

    def table(self):
        self.stage += 1
        tables = []
        for kind in range(2):
            bit = self.stage if kind == 0 else pos_bits() - 1 - self.stage
            left = self.left[kind]
            tables.append(halves((2,) * len(left), left.index(bit)))
            self.left[kind] = [other for other in left if other != bit]
        table = jnp.where(core_index() == 0, *[jnp.asarray(part, jnp.int32) for part in tables])
        own = own_bit(self.stage)
        return table[own], table[1 - own]

    def cut(self):
        return (self.kept, self.came[0], *self.table())

    def take(self, parts):
        self.kept, self.sends = parts[0], [parts[1]]


def advance(chains, tokens=()):
    parts = fold([chain.cut() for chain in chains], tokens)
    for chain, part in zip(chains, parts):
        chain.take(part)
        chain.start()
    return [array for chain in chains for array in chain.sends]


def last_kernel(ways, pre, pieces, spot_ref, *refs):
    ins, outs = refs[: 2 * pieces], refs[2 * pieces :]
    at = 0
    for k in range(pieces):
        columns = ins[2 * k].shape[-1]
        for j in range(ways):
            place = spot_ref[0] ^ j
            for n in range(pre):
                value = ins[2 * k][n, place].astype(wide) + ins[2 * k + 1][n, place].astype(wide)
                outs[j][n, :, at : at + columns] = value.astype(outs[j].dtype)
        at += columns


class Last:
    def __init__(self, chains, tokens=(), slowly=False):
        slices = lax.axis_size("img")
        ways = 2 if slowly else slices
        self.lead = chains[0].lead
        pre = self.lead * 2 * slices // ways
        arrays = []
        for chain in chains:
            for array in (chain.kept, chain.came[0]):
                arrays.append(array.reshape(pre, ways, -1, array.shape[-1]))
        self.widths = [array.shape[-1] for array in arrays[::2]]
        inside = pl.BlockSpec(memory_space=pltpu.VMEM)
        parts = launch(
            functools.partial(last_kernel, ways, pre, len(chains)),
            tokens,
            in_specs=[pl.BlockSpec(memory_space=pltpu.SMEM)] + [inside] * len(arrays),
            out_specs=[inside] * ways,
            out_shape=[shaped((pre, arrays[0].shape[2], sum(self.widths)), low if j else wide) for j in range(ways)],
            cost_estimate=cost(1, 4 * sum(array.size for array in arrays)),
                name="last",
        )((lax.axis_index("img") % ways).reshape(1), *arrays)
        self.kept, self.sends = parts[0], list(parts[1:])
        self.hops = list(range(1, ways))
        self.left = powers(slices)[1:][::-1] if slowly else []
        self.start()

    def start(self):
        self.came = [flip(array, "img", hop) for array, hop in zip(self.sends, self.hops)]

    def cut(self):
        bit = self.left[-1]
        entries = self.kept.reshape((1, -1) + self.kept.shape[-2:])
        dims = (2 * self.lead,) + (2,) * len(self.left)
        table = jnp.asarray(halves(dims, len(dims) - 1), jnp.int32)
        own = (lax.axis_index("img") // bit) % 2
        self.left = self.left[:-1]
        self.hops = [bit]
        return (entries, self.came[0].reshape(entries.shape), table[own], table[1 - own])

    def take(self, parts):
        self.kept, self.sends = parts[0][0], [parts[1][0]]

    def total(self):
        while self.left:
            advance([self])
        total = self.kept
        for came in self.came:
            total = total + came.astype(wide)
        return total

    def settle(self, stretch, tokens):
        self.came[stretch] = gate(self.came[stretch], tokens)
        return self.came[stretch]

    def squares(self):
        self.sums = self.total()
        return jnp.sum(self.sums * self.sums)

    def finish(self):
        core = core_index()
        total = self.sums.reshape((self.lead, 2) + self.sums.shape[-2:])
        own = lax.dynamic_index_in_dim(total, core, 1, False)
        came = flip_core(lax.dynamic_index_in_dim(total, 1 - core, 1, False))
        first, second = jnp.where(core == 0, own, came), jnp.where(core == 0, came, own)
        at, found = 0, []
        for columns in self.widths:
            found.append((first[..., at : at + columns], second[..., at : at + columns]))
            at += columns
        return found


def slow_hops():
    return [(axis, bit) for axis in ("seq", "img") for bit in powers(lax.axis_size(axis))]


def sum_all(array):
    rounds = [("img", range(1, lax.axis_size("img"))), ("seq", range(2, lax.axis_size("seq"), 2)), ("seq", [1])]
    for axis, hops in rounds:
        came = [flip(array, axis, hop) for hop in hops]
        for other in came:
            array = array + other
    return array


def assemble_kernel(plan, spot_ref, *refs):
    outs = sorted({out for _, _, out, _ in plan})
    count = len(refs) - 1 - len(outs)
    sems = refs[-1]
    copies = []
    for k, (piece, cut, out, where) in enumerate(plan):
        source = refs[piece].at[cut] if cut is not None else refs[piece]
        target = refs[count + out].at[where(spot_ref)]
        copies.append(pltpu.make_async_copy(source, target, sems.at[k]))
    for copy in copies:
        copy.start()
    for copy in copies:
        copy.wait()


def assemble(plan, spots, pieces, shapes, tokens=()):
    anywhere = pl.BlockSpec(memory_space=pl.ANY)
    return launch(
        functools.partial(assemble_kernel, plan),
        tokens,
        in_specs=[pl.BlockSpec(memory_space=pltpu.SMEM)] + [anywhere] * len(pieces),
        out_specs=[pl.BlockSpec(memory_space=pltpu.VMEM)] * len(shapes),
        out_shape=[shaped(shape, low) for shape in shapes],
        scratch_shapes=[pltpu.SemaphoreType.DMA((len(plan),))],
        cost_estimate=cost(1, 2 * sum(2 * piece.size for piece in pieces)),
        name="assemble",
    )(jnp.stack(spots).astype(jnp.int32), *pieces)


def gate_kernel(*refs):
    pass


def gate(arrays, tokens):
    anywhere = pl.BlockSpec(memory_space=pl.ANY)
    return launch(
        gate_kernel,
        tokens,
        in_specs=[anywhere] * len(arrays),
        out_specs=[anywhere] * len(arrays),
        out_shape=[shaped(array.shape, array.dtype) for array in arrays],
        input_output_aliases={k: k for k in range(len(arrays))},
        cost_estimate=cost(1, 1),
        name="gate",
    )(*arrays)


class Gather:
    def __init__(self, own, other):
        self.own, self.other = own, other
        self.stage = 0

    def pair(self):
        came = flip_core(self.other)
        pairs = [jnp.stack([self.own, came], axis=1), jnp.stack([came, self.own], axis=1)]
        return jnp.where(core_index() == 0, *pairs)

    @staticmethod
    def exchange(both, tokens=()):
        if tokens:
            (both,) = gate([both], tokens)
        own, other = jnp.split(both, 2)
        every = slice(None)
        plan = [(0, None, 0, lambda spot: (every, spot[0])), (1, None, 0, lambda spot: (every, 1 - spot[0]))]
        k, rows, columns = own.shape
        found = Gather(None, None)
        found.part = assemble(plan, [core_index()], [own, flip_core(other)], [(k, 2, rows, columns)])[0]
        found.part = found.part.reshape(k, 1, 2 * rows, columns)
        return found

    def start_slices(self, hops=False):
        self.pieces = [self.pair()]
        for j in range(1, lax.axis_size("img")):
            bit = j & -j if hops else j
            self.pieces.append(flip(self.pieces[j - bit], "img", bit))

    def finish_slices(self, tokens=(), groups=1):
        slices = len(self.pieces)
        if tokens:
            self.pieces = self.pieces[:1] + list(gate(self.pieces[1:], tokens))
        every = slice(None)
        k, _, rows, columns = self.pieces[0].shape
        k = k // groups
        plan = [
            (j, slice(n * k, (n + 1) * k), n, lambda spot, j=j: (every, every, spot[0] ^ j))
            for n in range(groups)
            for j in range(slices)
        ]
        shape = (k, 2, slices, rows, columns)
        parts = assemble(plan, [lax.axis_index("img")], self.pieces, [shape] * groups)
        found = []
        for part in parts:
            found.append(Gather(None, None))
            found[-1].part = part.reshape(k, 1, 2 * slices * rows, columns)
        return found

    def start_pos(self, tokens=()):
        if tokens:
            (self.part,) = gate([self.part], tokens)
        self.came = flip_pos(self.part, self.stage)
        self.stage += 1

    def finish_pos(self, tokens=()):
        every = slice(None)
        if tokens:
            (self.came,) = gate([self.came], tokens)
        plan = [
            (0, None, 0, lambda spot: (every, spot[0])),
            (1, None, 0, lambda spot: (every, 1 - spot[0])),
        ]
        shape = self.part.shape[:1] + (2,) + self.part.shape[1:]
        self.part = assemble(plan, [own_bit(self.stage - 1)], [self.part, self.came], [shape])[0]
        self.part = self.part.reshape((shape[0], -1) + shape[3:])
        return [self.part]

    def start_last(self):
        self.start_pos()
        self.turned = flip_core(self.part)

    def finish_last(self, tokens, turned_tokens):
        (self.turned,) = gate([self.turned], turned_tokens)
        (self.came,) = gate([self.came], tokens)
        return Pieces([self.part, self.came, self.turned, flip_core(self.came)])


def narrow_kernel(core_ref, weight_ref, *out_refs):
    first = core_ref[0] == 0
    slabs = out_refs[0].shape[0] // 2
    for k, out_ref in enumerate(out_refs):
        for n in range(slabs):
            columns = slice((k * slabs + n) * SLAB, (k * slabs + n + 1) * SLAB)
            left, right = weight_ref[0, :, columns].astype(low), weight_ref[1, :, columns].astype(low)
            out_ref[n] = jnp.where(first, left, right)
            out_ref[slabs + n] = jnp.where(first, right, left)


def narrow(weight, groups, tokens):
    _, owned, hidden = weight.shape
    slabs = hidden // SLAB // groups
    inside = pl.BlockSpec(memory_space=pltpu.VMEM)
    return launch(
        narrow_kernel,
        tokens,
        in_specs=[pl.BlockSpec(memory_space=pltpu.SMEM), inside],
        out_specs=[inside] * groups,
        out_shape=[shaped((2 * slabs, owned, SLAB), low)] * groups,
        cost_estimate=cost(1, 12 * slabs * groups * owned * SLAB),
        name="narrow",
    )(core_index().reshape(1), weight)


class Passing:
    def __init__(self, own, backward, direct):
        self.backward = backward
        came = flip_core(own.astype(low)).astype(wide)
        self.outside = jnp.where(core_index() == (0 if backward else 1), came, 0.0)
        self.total = own + came
        self.bits = powers(lax.axis_size("seq") // 2)
        if direct:
            both = self.total.astype(low)
            self.came = [flip(both, "seq", 2 * j) for j in range(1, lax.axis_size("seq") // 2)]

    def finish(self, tokens):
        total = self.outside
        for j, came in enumerate(gate(self.came, tokens), 1):
            earlier = (pos_index() ^ j) < pos_index()
            total = total + jnp.where(earlier != self.backward, came.astype(wide), 0.0)
        return total

    def hop(self, tokens):
        bit, *self.bits = self.bits
        (came,) = gate([flip(self.total.astype(low), "seq", 2 * bit)], tokens)
        came = came.astype(wide)
        earlier = (pos_index() ^ bit) < pos_index()
        self.outside = self.outside + jnp.where(earlier != self.backward, came, 0.0)
        self.total = self.total + came
        return self.outside


def body(
    images,
    cotangent,
    attention_weight,
    feedforward_weight,
    norm_vectors,
    attention_moment,
    feedforward_moment,
    norm_moment,
    attention_second,
    feedforward_second,
    norm_second,
    attention_average,
    feedforward_average,
    norm_average,
):
    count, span, width = images.shape
    tokens = count * span
    owned = attention_weight.shape[1]
    slabs = feedforward_weight.shape[2] // SLAB
    stages = pos_bits()
    half = slabs // 2
    every = slice(None)

    x, e = images.reshape(tokens, width), cotangent.reshape(tokens, width)
    low_weights = jnp.pad(attention_weight.astype(low), ((0, 0), (0, 0), (0, 128)))
    vectors = jnp.pad(norm_vectors.astype(low).T, ((0, 0), (width, 124)))
    query_weight, key_weight, value_weight, out_weight = low_weights
    kinds = jnp.stack([key_weight, query_weight]), jnp.stack([value_weight + vectors, out_weight])
    first_core = core_index() == 0
    one = Gather(jnp.where(first_core, *kinds), jnp.where(first_core, *kinds[::-1]))
    one.start_slices(True)
    et = turn(e, count, span)
    (one,) = one.finish_slices([et])
    one.start_pos()
    feeds = narrow(feedforward_weight, 2, [one.part])
    marks = [feeds[0]]
    feeds = [lax.all_gather(part, "img", axis=1, tiled=True) for part in feeds]
    for _ in range(stages - 2):
        one.finish_pos(marks)
        one.start_pos()
    one.finish_pos(marks)
    one.start_last()
    pieces = one.finish_last([one.part], [one.part])
    two = Gather.exchange(feeds[0])
    two.start_pos([one.came])
    vec = pieces.second(slice(width, width + 4)).astype(wide).T
    fk, v, fq, a1, a1t, state, wk, wv, wq, wo = project(x, vec, pieces, count, span, [two.part])
    a1t_other = flip_core(a1t)
    prior = Passing(state, False, False)
    for _ in range(stages - 2):
        two.finish_pos([state])
        two.start_pos()
    two.finish_pos([state])
    two.start_last()
    marks = [two.part, two.turned, prior.outside, a1t_other]
    num, den = attend(fq, fk, v, count, span, marks)
    while prior.bits:
        prior.hop([num])
    prior = prior.outside
    three = Gather.exchange(feeds[1], [num])
    three.start_pos()
    mixed, rden, resid, a2, a2t, mixed_t = mix(x, vec, wo, fq, num, den, prior, count, span, [three.part])
    a2t, mixed_t = turned_whole(a2t), turned_whole(mixed_t)
    lt = jnp.where(first_core, a2t, et)
    lt_other = flip_core(jnp.where(first_core, et, a2t))
    mixed_t_other = flip_core(mixed_t)
    first_pieces = two.finish_last([resid], [fq])
    marks = [resid]
    for _ in range(stages - 2):
        three.finish_pos(marks)
        three.start_pos()
    three.finish_pos(marks)
    three.start_last()
    marks = [three.part, three.turned]

    early = feed(first_pieces, a2, e, None, marks)
    early_other = flip_core(early[3])
    second_pieces = three.finish_last([early[0]], [early[0]])
    late = feed(second_pieces, a2, e, early[:2], [lt_other, mixed_t_other])
    late_other = flip_core(late[3])
    firsts, seconds, outs, inner = [Chain()], [Chain()], [Chain()], [Chain(3)]
    marks = weigh(firsts[0], lt, lt_other, early[2][None], early_other[None], [late[0]])
    output, dres, branch, branch_send, dn, w, dstate, sums_second = turn_back(
        late[0], late[1], resid, e, vec, wo, mixed, rden, fq, count, span, marks + [late_other]
    )
    later = Passing(dstate, True, False)
    marks = [dstate, later.outside]
    for _ in range(stages - 1):
        marks = marks + advance(firsts, [dstate])
    marks = weigh(seconds[0], lt, lt_other, late[2][None], late_other[None], marks)
    passed = later.hop([seconds[0].kept])
    firsts_last = Last(firsts, [seconds[0].kept])
    parts = [attend_back(0, fq, fk, v, dn, w, prior, span, marks + firsts_last.sends + [passed])]
    branch_other = flip_core(gate([branch_send], [parts[0][0]])[0])
    settled = firsts_last.sends
    marks = weigh(outs[0], mixed_t, mixed_t_other, branch[None], branch_other[None], settled)
    for _ in range(stages - 1):
        marks = marks + advance(seconds, [parts[0][0]])
    for image in range(1, count):
        parts.append(attend_back(image, fq, fk, v, dn, w, prior, span, marks))
    for _ in range(stages - 1):
        marks = advance(outs, [parts[-1][0]])
    marks = marks + seconds[0].came + firsts_last.settle(slice(0, None), [parts[-1][0]])
    while later.bits:
        later.hop([parts[-1][0]])
    later = later.outside
    kept, sent = finish(parts, fk, v, later, count, span, marks)
    local_squares = firsts_last.squares()
    came = flip_core(sent)
    seconds_last = Last(seconds + outs, [kept])
    marks = seconds_last.sends + [firsts_last.sums]
    grads_in = [enter(0, kept, sent, (wq, wk, wv), x, dres, vec, span, marks)]
    marks = seconds_last.settle(slice(0, 2), [grads_in[0][1]])
    marks = weigh(inner[0], a1t, a1t_other, kept, came, marks)
    for image in range(1, count):
        grads_in.append(enter(image, kept, sent, (wq, wk, wv), x, dres, vec, span, marks))
    seconds_last.settle(slice(2, None), [grads_in[-1][1]])
    local_squares = local_squares + seconds_last.squares()
    input_grad = jnp.stack([part[0] for part in grads_in])
    sums = sum(part[1] for part in grads_in)
    vector_grad = jnp.concatenate([sums[:2], sums_second[:2]], axis=0)
    hops = slow_hops()
    for axis, bit in hops[:2]:
        vector_grad = vector_grad + flip(vector_grad, axis, bit)
    marks = [seconds_last.sums, vector_grad]
    for _ in range(stages - 1):
        marks = advance(inner, marks)
    (vector_grad,) = gate([vector_grad], marks)
    for axis, bit in hops[2:]:
        vector_grad = vector_grad + flip(vector_grad, axis, bit)
    device = lax.axis_index("seq") * lax.axis_size("img") + lax.axis_index("img")
    vector_shard = lax.dynamic_slice_in_dim(vector_grad, device * owned, owned, 1)
    inner_last = Last(inner, [seconds_last.sums])
    local_squares = local_squares + jnp.sum(vector_shard * vector_shard)
    local_squares = local_squares + inner_last.squares()
    grad_norm = jnp.sqrt(sum_all(jnp.full((8, 128), local_squares))[0, 0])
    (early_shard,) = firsts_last.finish()
    late_shard, out_shard = seconds_last.finish()
    inner_shard = jnp.concatenate([part for pair in inner_last.finish() for part in pair], axis=2)
    attn_shard = jnp.concatenate([inner_shard, jnp.concatenate(out_shard, axis=2)], axis=0)
    feed_shard = jnp.concatenate([jnp.concatenate(pair, axis=2) for pair in zip(early_shard, late_shard)], axis=0)
    factor = clip_bound / jnp.maximum(grad_norm, clip_bound)
    attn_new = adam_update(
        attention_weight, attention_moment, attention_second, attention_average, attn_shard, factor, learn_rate
    )
    feed_new = adam_update(
        feedforward_weight, feedforward_moment, feedforward_second, feedforward_average, feed_shard, factor, learn_rate
    )
    norm_new = adam_update(norm_vectors, norm_moment, norm_second, norm_average, vector_shard, factor, norm_rate)
    output = output.reshape(images.shape)
    input_grad = input_grad.reshape(images.shape)
    return (output, input_grad, grad_norm) + attn_new + feed_new + norm_new


def solution(mesh):
    tokens = P("img", "seq", None)
    rows = P(None, ("seq", "img"), None)
    vectors = P(None, ("seq", "img"))
    group = (rows, rows, vectors)
    return jax.shard_map(
        body,
        mesh=mesh,
        in_specs=(tokens, tokens) + group * 4,
        out_specs=(tokens, tokens, P()) + (rows,) * 8 + (vectors,) * 4,
        check_vma=False,
    )
```

```python
import functools

import jax
import jax.numpy as jnp
import numpy as np
from jax import lax
from jax.experimental import pallas as pl
from jax.experimental.pallas import tpu as pltpu
from jax.sharding import PartitionSpec as P

HEADS = 16
HEAD_DIM = 64
STEP = 10

beta_first = 0.9
beta_second = 0.95
learn_rate = 0.02
norm_rate = 0.2
weight_decay = 0.1
average_decay = 0.75
clip_bound = 1.0
eps_norm = 1e-05
eps_adam = 1e-08

PAIR = 2 * HEAD_DIM
STATE_ROWS = HEAD_DIM + 16
SLAB = 1024
FEED_TILE = 1024
GROUP = 256

low = jnp.bfloat16
wide = jnp.float32


def params(megabytes=56):
    return pltpu.CompilerParams(vmem_limit_bytes=megabytes * 1024 * 1024)


def cost(products, elements):
    return pl.CostEstimate(flops=2 * products, bytes_accessed=elements, transcendentals=0)


def launch(kernel, tokens, in_specs, megabytes=56, **keys):
    known, extra = len(in_specs), len(tokens)

    def run(*refs):
        kernel(*refs[:known], *refs[known + extra :])

    call = pl.pallas_call(
        run, in_specs=list(in_specs) + [pl.BlockSpec(memory_space=pl.ANY)] * extra, compiler_params=params(megabytes), **keys
    )
    return lambda *args: call(*args, *tokens)


def launch_at(kernel, spot, tokens, grid, in_specs, out_specs, megabytes=56, scratch_shapes=(), **keys):
    known, extra = len(in_specs), len(tokens)

    def run(spot_ref, *refs):
        kernel(spot_ref, *refs[:known], *refs[known + extra :])

    call = pl.pallas_call(
        run,
        grid_spec=pltpu.PrefetchScalarGridSpec(
            num_scalar_prefetch=1,
            grid=grid,
            in_specs=list(in_specs) + [pl.BlockSpec(memory_space=pl.ANY)] * extra,
            out_specs=out_specs,
            scratch_shapes=scratch_shapes,
        ),
        compiler_params=params(megabytes),
        **keys,
    )
    return lambda *args: call(spot.reshape(-1).astype(jnp.int32), *args, *tokens)


def reversed_bits(value, count):
    return sum(((value >> k) & 1) << (count - 1 - k) for k in range(count))


def join(target_ref, bits, spot_ref, own_ref, came_ref, own_other_ref, came_other_ref):
    core, high, lowest = spot_ref[0], spot_ref[1], spot_ref[2]
    runs = 1 << (bits - 1)
    rows = target_ref.shape[1] // (2 * runs)
    for run in range(runs):
        source = slice(run * rows, (run + 1) * rows)
        turned = reversed_bits(run, bits)
        for place in range(2):
            first = (high ^ place) * runs + run
            second = turned + (lowest ^ place)
            for ref, slot in (((own_ref, came_ref)[place], core), ((own_other_ref, came_other_ref)[place], 1 - core)):
                at = jnp.where(slot == 0, first, second)
                target_ref[slot, pl.ds(pl.multiple_of(at * rows, rows), rows), :] = ref[source, :]


class Pieces:
    def __init__(self, arrays):
        self.arrays = [array.reshape(array.shape[0], -1, array.shape[-1]) for array in arrays]
        place = pos_index()
        self.bits = pos_bits()
        self.spot = jnp.stack([core_index(), place >> (self.bits - 1), place & 1])

    def blocks(self, columns, place):
        rows = self.arrays[0].shape[1]
        return [pl.BlockSpec((None, rows, columns), place)] * 4

    def second(self, columns):
        mine, others = (
            [part[0, :, columns].reshape(1 << (self.bits - 1), 1, -1, columns.stop - columns.start) for part in pair]
            for pair in (self.arrays[:2], self.arrays[2:])
        )
        own, came = (jnp.where(core_index() == 1, left, right) for left, right in zip(mine, others))
        straight, turned = jnp.concatenate([own, came], axis=1), jnp.concatenate([came, own], axis=1)
        runs = jnp.where(self.spot[2] == 0, straight, turned)
        order = [reversed_bits(run, self.bits - 1) for run in range(1 << (self.bits - 1))]
        return jnp.stack([runs[run] for run in order]).reshape(-1, columns.stop - columns.start)


def shaped(shape, kind):
    return jax.ShapeDtypeStruct(shape, kind)


def whole(shape):
    return pl.BlockSpec(shape, lambda *_: (0,) * len(shape))


def mm(left, right):
    return lax.dot_general(left, right, (((1,), (0,)), ((), ())), preferred_element_type=wide)


def mt(left, right):
    return lax.dot_general(left, right, (((1,), (1,)), ((), ())), preferred_element_type=wide)


def tm(left, right):
    return lax.dot_general(left, right, (((0,), (0,)), ((), ())), preferred_element_type=wide)


def pair_mm(first, second):
    if first[0].shape[1] % 128:
        return mm(*first) + mm(*second)
    return mm(jnp.concatenate([first[0], second[0]], axis=1), jnp.concatenate([first[1], second[1]], axis=0))


def causal_mask(span, below):
    rows = lax.broadcasted_iota(jnp.int32, (span, span), 0)
    columns = lax.broadcasted_iota(jnp.int32, (span, span), 1)
    return (rows >= columns if below else rows <= columns).astype(wide).astype(low)


def first_head(rows):
    return lax.broadcasted_iota(jnp.int32, (rows, PAIR), 1) < HEAD_DIM


def fold_state(product):
    return jnp.where(first_head(HEAD_DIM), product[:HEAD_DIM], product[HEAD_DIM:])


def unfold_state(folded):
    own = first_head(HEAD_DIM)
    zero = jnp.zeros_like(folded)
    return jnp.concatenate([jnp.where(own, folded, zero), jnp.where(own, zero, folded)], axis=0)


def unfold_total(row):
    tall = jnp.broadcast_to(row, (PAIR, PAIR))
    lanes = lax.broadcasted_iota(jnp.int32, (PAIR, PAIR), 1) < HEAD_DIM
    rows = lax.broadcasted_iota(jnp.int32, (PAIR, PAIR), 0) < HEAD_DIM
    return jnp.where(lanes == rows, tall, jnp.zeros_like(tall))


def split_low(values):
    high = values.astype(low)
    return high, (values - high.astype(wide)).astype(low)


def normalised(values):
    centre = jnp.mean(values, axis=-1, keepdims=True)
    centred = values - centre
    spread = jnp.mean(centred * centred, axis=-1, keepdims=True)
    scale = lax.rsqrt(spread + eps_norm)
    return centred * scale, scale


def feature(raw):
    return jnp.where(raw > 0, raw + 1.0, jnp.exp(jnp.minimum(raw, 0.0))).astype(low)


def project_kernel(images, span, bits, spot_ref, x_ref, vec_ref, *refs):
    fk_ref, v_ref, a_ref, at_ref, state_ref, wk_ref, wv_ref, joined_ref = refs[4:]

    @pl.when(pl.program_id(0) == 0)
    def _():
        gain, shift = vec_ref[0:1, :], vec_ref[1:2, :]
        step = span // 3
        for start in range(0, images * span, step):
            rows = slice(start, start + step)
            unit, _ = normalised(x_ref[rows, :].astype(wide))
            a_ref[rows, :] = (unit * gain + shift).astype(low)
        at_ref[...] = a_ref[...].T

    join(joined_ref, bits, spot_ref, *refs[:4])
    keys, values = joined_ref[0], joined_ref[1]
    wk_ref[...] = keys
    wv_ref[...] = values
    fk_ref[...] = feature(mm(a_ref[...], keys))
    v_ref[...] = mm(a_ref[...], values).astype(low)
    ones = jnp.ones((16, span), low)
    for image in range(images):
        rows = slice(image * span, (image + 1) * span)
        for pair in range(GROUP // PAIR):
            lanes = slice(pair * PAIR, (pair + 1) * PAIR)
            key, value = fk_ref[rows, lanes], v_ref[rows, lanes]
            state_ref[image, pair, :HEAD_DIM, :] = fold_state(tm(value, key))
            state_ref[image, pair, HEAD_DIM:, :] = mm(ones, key)


def project(x, vec, pieces, images, span, tokens=()):
    count, width = x.shape
    pairs = GROUP // PAIR
    column = pl.BlockSpec((count, GROUP), lambda g, spot: (0, g))
    weight = pl.BlockSpec((width, GROUP), lambda g, spot: (0, g))
    return launch_at(
        functools.partial(project_kernel, images, span, pieces.bits),
        pieces.spot,
        tokens,
        grid=(width // GROUP,),
        in_specs=[whole((count, width)), whole(vec.shape)] + pieces.blocks(GROUP, lambda g, spot: (0, 0, g)),
        out_specs=[
            column,
            column,
            whole((count, width)),
            whole((width, count)),
            pl.BlockSpec((images, pairs, STATE_ROWS, PAIR), lambda g, spot: (0, g, 0, 0)),
            weight,
            weight,
        ],
        out_shape=[
            shaped((count, width), low),
            shaped((count, width), low),
            shaped((count, width), low),
            shaped((width, count), low),
            shaped((images, width // PAIR, STATE_ROWS, PAIR), wide),
            shaped((width, width), low),
            shaped((width, width), low),
        ],
        scratch_shapes=[pltpu.VMEM((2, width, GROUP), low)],
        cost_estimate=cost(2 * count * width * width, 8 * width * width + 12 * count * width),
        name="project",
    )(x, vec, *pieces.arrays)


def query_kernel(bits, spot_ref, a_ref, *refs):
    fq_ref, wq_ref, wo_ref, joined_ref = refs[4:]
    join(joined_ref, bits, spot_ref, *refs[:4])
    wq_ref[...] = joined_ref[0]
    wo_ref[...] = joined_ref[1]
    fq_ref[...] = feature(mm(a_ref[...], joined_ref[0]))


def query(a, pieces, tokens=()):
    count, width = a.shape
    weight = pl.BlockSpec((width, GROUP), lambda g, spot: (0, g))
    return launch_at(
        functools.partial(query_kernel, pieces.bits),
        pieces.spot,
        tokens,
        grid=(width // GROUP,),
        in_specs=[whole((count, width))] + pieces.blocks(GROUP, lambda g, spot: (1, 0, g)),
        out_specs=[pl.BlockSpec((count, GROUP), lambda g, spot: (0, g)), weight, weight],
        out_shape=[shaped((count, width), low)] + [shaped((width, width), low)] * 2,
        scratch_shapes=[pltpu.VMEM((2, width, GROUP), low)],
        cost_estimate=cost(count * width * width, 6 * width * width + 4 * count * width),
        name="query",
    )(a, *pieces.arrays)


def turn_kernel(x_ref, out_ref):
    out_ref[...] = x_ref[...].T


def turn(x, images, span, tokens=()):
    count, width = x.shape
    return turned_whole(
        launch(
            turn_kernel,
            tokens,
            grid=(images,),
            in_specs=[pl.BlockSpec((span, width), lambda b: (b, 0))],
            out_specs=turned_block(width, span),
            out_shape=turned_shape(images, width, span),
            cost_estimate=cost(1, 4 * count * width),
                name="turn",
        )(x)
    )


def attend_kernel(span, fq_ref, fk_ref, v_ref, num_ref, den_ref):
    own = first_head(span)
    causal = causal_mask(span, True)
    one = jnp.ones((span, PAIR), low)
    zero = jnp.zeros((span, PAIR), low)
    for pair in range(GROUP // PAIR):
        lanes = slice(pair * PAIR, (pair + 1) * PAIR)
        query, key, value = fq_ref[:, lanes], fk_ref[:, lanes], v_ref[:, lanes]
        products = []
        for mask in (own, jnp.logical_not(own)):
            scores = mt(jnp.where(mask, query, zero), key).astype(low) * causal
            right = jnp.concatenate([jnp.where(mask, value, zero), jnp.where(mask, one, zero)], axis=1)
            products.append((scores, right))
        total = pair_mm(*products)
        num_ref[:, lanes] = total[:, :PAIR]
        den_ref[:, lanes] = total[:, PAIR:]


def attend(fq, fk, v, images, span, tokens=()):
    rows, width = fq.shape
    block = pl.BlockSpec((span, GROUP), lambda b, p: (b, p))
    return launch(
        functools.partial(attend_kernel, span),
        tokens,
        grid=(images, width // GROUP),
        in_specs=[block] * 3,
        out_specs=[block] * 2,
        out_shape=[shaped((rows, width), wide)] * 2,
        cost_estimate=cost(16 * rows * span * width, 14 * rows * width),
        name="attend",
    )(fq, fk, v)


def turned_block(width, span):
    if span % 128:
        return pl.BlockSpec((None, width, span), lambda b: (b, 0, 0))
    return pl.BlockSpec((width, span), lambda b: (0, b))


def turned_shape(images, width, span):
    return shaped((images, width, span) if span % 128 else (width, images * span), low)


def turned_whole(array):
    if array.ndim == 2:
        return array
    return jnp.swapaxes(array, 0, 1).reshape(array.shape[1], -1)


def mix_kernel(x_ref, vec_ref, wo_ref, fq_ref, num_ref, den_ref, prior_ref, mixed_ref, rden_ref, resid_ref, a_ref, at_ref, mt_ref):
    width = x_ref.shape[1]
    for pair in range(width // PAIR):
        lanes = slice(pair * PAIR, (pair + 1) * PAIR)
        folded = prior_ref[0, pair]
        matrix = jnp.concatenate(
            [unfold_state(folded[:HEAD_DIM]), unfold_total(folded[HEAD_DIM : HEAD_DIM + 1])], axis=0
        )
        high, rest = split_low(matrix)
        query = fq_ref[:, lanes]
        both = mt(jnp.concatenate([query, query], axis=1), jnp.concatenate([high, rest], axis=1))
        scale = 1.0 / (den_ref[:, lanes] + both[:, PAIR:])
        rden_ref[:, lanes] = scale
        mixed_ref[:, lanes] = ((num_ref[:, lanes] + both[:, :PAIR]) * scale).astype(low)
    resid = x_ref[...].astype(wide) + mm(mixed_ref[...], wo_ref[...])
    resid_ref[...] = resid
    unit, _ = normalised(resid)
    normed = (unit * vec_ref[2:3, :] + vec_ref[3:4, :]).astype(low)
    a_ref[...] = normed
    at_ref[...] = normed.T
    mt_ref[...] = mixed_ref[...].T


def mix(x, vec, wo, fq, num, den, prior, images, span, tokens=()):
    rows_, width = x.shape
    rows = pl.BlockSpec((span, width), lambda b: (b, 0))
    return launch(
        mix_kernel,
        tokens,
        grid=(images,),
        in_specs=[
            rows,
            whole(vec.shape),
            whole(wo.shape),
            rows,
            rows,
            rows,
            pl.BlockSpec((1,) + prior.shape[1:], lambda b: (b, 0, 0, 0)),
        ],
        out_specs=[rows, rows, rows, rows, turned_block(width, span), turned_block(width, span)],
        out_shape=[
            shaped((rows_, width), low),
            shaped((rows_, width), wide),
            shaped((rows_, width), wide),
            shaped((rows_, width), low),
            turned_shape(images, width, span),
            turned_shape(images, width, span),
        ],
        cost_estimate=cost(4 * rows_ * width * width, 24 * rows_ * width + 2 * width * width),
        name="mix",
    )(x, vec, wo, fq, num, den, prior)


gelu_scale = 0.7978845608028654
gelu_cubic = 0.044715


def feed_kernel(fresh, bits, spot_ref, *refs):
    a_ref, e_ref = refs[:2]
    out_ref, da_ref, kept_ref, sent_ref, joined_ref = refs[-5:]
    join(joined_ref, bits, spot_ref, *refs[2:6])

    @pl.when(pl.program_id(0) == 0)
    def _():
        if fresh:
            out_ref[...] = jnp.zeros_like(out_ref)
            da_ref[...] = jnp.zeros_like(da_ref)
        else:
            out_ref[...] = refs[6][...]
            da_ref[...] = refs[7][...]

    up, down = joined_ref[0], joined_ref[1]
    upper = mm(a_ref[...], up)
    grad = mm(e_ref[...], down)
    square = upper * upper
    bend = jnp.tanh(gelu_scale * upper * (1.0 + gelu_cubic * square))
    gate = 0.5 + 0.5 * bend
    hidden = (upper * gate).astype(low)
    slope = gate + 0.5 * upper * (1.0 - bend * bend) * (gelu_scale * (1.0 + 3.0 * gelu_cubic * square))
    dupper = (grad * slope).astype(low)
    out_ref[...] += mt(hidden, down)
    da_ref[...] += mt(dupper, up)
    first = spot_ref[0] == 0
    kept_ref[...] = jnp.where(first, dupper, hidden)
    sent_ref[...] = jnp.where(first, hidden, dupper)


def feed(pieces, a, e, carried, tokens=()):
    rows, width = a.shape
    slabs = pieces.arrays[0].shape[0]
    tiles = SLAB // FEED_TILE
    grads = pl.BlockSpec((rows, FEED_TILE), lambda g, spot: (0, g))
    full = whole((rows, width))
    fresh = carried is None
    return launch_at(
        functools.partial(feed_kernel, fresh, pieces.bits),
        pieces.spot,
        tokens,
        grid=(slabs * tiles,),
        in_specs=[full, full]
        + pieces.blocks(FEED_TILE, lambda g, spot: (g // tiles, 0, g % tiles))
        + ([] if fresh else [full, full]),
        out_specs=[full, full, grads, grads],
        out_shape=[shaped((rows, width), wide)] * 2 + [shaped((rows, slabs * SLAB), low)] * 2,
        scratch_shapes=[pltpu.VMEM((2, width, FEED_TILE), low)],
        cost_estimate=cost(4 * rows * width * slabs * SLAB, 4 * (width + rows) * slabs * SLAB + 20 * rows * width),
        name="feed",
    )(a, e, *pieces.arrays, *(() if fresh else carried))


def weigh_kernel(count, spot_ref, lt_ref, lt_other_ref, x_ref, x_other_ref, kept_ref, sent_ref):
    rows = kept_ref.shape[1]
    for k in range(2):
        places = [pl.ds(pl.multiple_of(spot_ref[k * count + n] * rows, rows), rows) for n in range(count)]
        left, other = (jnp.concatenate([ref[place, :] for place in places], axis=0) for ref in (lt_ref, lt_other_ref))
        product = (mm(left, x_ref[...]) + mm(other, x_other_ref[...])).astype(low)
        (sent_ref if k else kept_ref)[...] = product.reshape(count, rows, -1)


def weigh(chain, lt, lt_other, x, x_other, tokens=()):
    lead, rows, columns = x.shape
    width = lt.shape[0]
    keeps, sends = chain.table()
    count = keeps.shape[0]
    tile = min(FEED_TILE, columns)
    full = whole((width, rows))
    column = pl.BlockSpec((None, rows, tile), lambda n, g, spot: (n, 0, g))
    result = pl.BlockSpec((None, count, width // (2 * count), tile), lambda n, g, spot: (n, 0, 0, g))
    chain.take(
        launch_at(
            functools.partial(weigh_kernel, count),
            jnp.concatenate([keeps, sends]),
            tokens,
            grid=(lead, columns // tile),
            in_specs=[full, full, column, column],
            out_specs=[result, result],
            out_shape=[shaped((lead, count, width // (2 * count), columns), low)] * 2,
            cost_estimate=cost(2 * lead * rows * width * columns, 4 * lead * (rows + width) * columns + 4 * rows * width),
            name="weigh",
        )(lt, lt_other, x, x_other)
    )
    chain.start()
    return chain.sends


def turn_back_kernel(core_ref, x_out_ref, da_ref, resid_ref, e_ref, vec_ref, wo_ref, mixed_ref, rden_ref, fq_ref,
                     out_ref, dres_ref, kept_ref, sent_ref, dn_ref, w_ref, state_ref, sums_ref):
    width = da_ref.shape[1]
    resid = resid_ref[...]
    out_ref[...] = (resid + x_out_ref[...]).astype(low)
    unit, scale = normalised(resid)
    da = da_ref[...]

    @pl.when(pl.program_id(0) == 0)
    def _():
        sums_ref[...] = jnp.zeros_like(sums_ref)

    sums_ref[0:1, :] += jnp.sum(da * unit, axis=0, keepdims=True)
    sums_ref[1:2, :] += jnp.sum(da, axis=0, keepdims=True)
    p = da * vec_ref[2:3, :]
    back = p - jnp.mean(p, axis=-1, keepdims=True) - unit * jnp.mean(p * unit, axis=-1, keepdims=True)
    dres = e_ref[...].astype(wide) + scale * back
    dres_ref[...] = dres
    branch = dres.astype(low)
    left, right = branch[:, : width // 2], branch[:, width // 2 :]
    first = core_ref[0] == 0
    kept_ref[...] = jnp.where(first, left, right)
    sent_ref[...] = jnp.where(first, right, left)
    dmixed = mt(branch, wo_ref[...]).astype(low).astype(wide)
    dnumer = dmixed * rden_ref[...]
    dn_ref[...] = dnumer.astype(low)
    w_ref[...] = (-dnumer * mixed_ref[...].astype(wide)).astype(low)
    for pair in range(width // PAIR):
        lanes = slice(pair * PAIR, (pair + 1) * PAIR)
        query = fq_ref[:, lanes]
        state_ref[0, pair, :HEAD_DIM, :] = fold_state(tm(dn_ref[:, lanes], query))
        total = jnp.sum(fold_state(tm(w_ref[:, lanes], query)), axis=0, keepdims=True)
        state_ref[0, pair, HEAD_DIM:, :] = jnp.broadcast_to(total, (STATE_ROWS - HEAD_DIM, PAIR))


def turn_back(x_out, da, resid, e, vec, wo, mixed, rden, fq, images, span, tokens=()):
    rows_, width = da.shape
    rows = pl.BlockSpec((span, width), lambda b, core: (b, 0))
    state = (images, width // PAIR, STATE_ROWS, PAIR)
    half = pl.BlockSpec((span, width // 2), lambda b, core: (b, 0))
    return launch_at(
        turn_back_kernel,
        core_index(),
        tokens,
        grid=(images,),
        in_specs=[rows, rows, rows, rows, whole(vec.shape), whole(wo.shape), rows, rows, rows],
        out_specs=[rows, rows, half, half, rows, rows] + [pl.BlockSpec((1,) + state[1:], lambda b, core: (b, 0, 0, 0)), whole((8, width))],
        out_shape=[
            shaped((rows_, width), low),
            shaped((rows_, width), wide),
            shaped((rows_, width // 2), low),
            shaped((rows_, width // 2), low),
            shaped((rows_, width), low),
            shaped((rows_, width), low),
            shaped(state, wide),
            shaped((8, width), wide),
        ],
        cost_estimate=cost(5 * rows_ * width * width, 30 * rows_ * width),
        name="turn_back",
    )(x_out, da, resid, e, vec, wo, mixed, rden, fq)


def attend_back_kernel(span, fq_ref, fk_ref, v_ref, dn_ref, w_ref, prior_ref, dq_ref, dfk_ref, dv_ref):
    own = first_head(span)
    own_twice = jnp.concatenate([own, own], axis=1)
    below, above = causal_mask(span, True), causal_mask(span, False)
    one = jnp.ones((span, PAIR), low)
    zero = jnp.zeros((span, PAIR), low)
    zero_twice = jnp.zeros((span, 2 * PAIR), low)
    for pair in range(GROUP // PAIR):
        lanes = slice(pair * PAIR, (pair + 1) * PAIR)
        query, key, value = fq_ref[:, lanes], fk_ref[:, lanes], v_ref[:, lanes]
        grads = jnp.concatenate([dn_ref[:, lanes], w_ref[:, lanes]], axis=1)
        extended = jnp.concatenate([value, one], axis=1)
        folded = prior_ref[0, pair]
        matrix = jnp.concatenate(
            [unfold_state(folded[:HEAD_DIM]), unfold_total(folded[HEAD_DIM : HEAD_DIM + 1])], axis=0
        )
        high, rest = split_low(matrix)
        dfq = mm(jnp.concatenate([grads, grads], axis=1), jnp.concatenate([high, rest], axis=0))
        to_query, to_key, to_value = [], [], []
        for mask, both in ((own, own_twice), (jnp.logical_not(own), jnp.logical_not(own_twice))):
            head_grads = jnp.where(both, grads, zero_twice)
            head_query = jnp.where(mask, query, zero)
            head_key = jnp.where(mask, key, zero)
            to_query.append((mt(head_grads, extended).astype(low) * below, head_key))
            to_key.append((mt(extended, head_grads).astype(low) * above, head_query))
            to_value.append((mt(head_key, query).astype(low) * above, head_grads[:, :PAIR]))
        dfq = dfq + pair_mm(*to_query)
        dq_ref[:, lanes] = (dfq * jnp.minimum(query.astype(wide), 1.0)).astype(low)
        dfk_ref[:, lanes] = pair_mm(*to_key)
        dv_ref[:, lanes] = pair_mm(*to_value)


def attend_back(image, fq, fk, v, dn, w, prior, span, tokens=()):
    width = fq.shape[1]
    block = pl.BlockSpec((span, GROUP), lambda p: (image, p))
    column = pl.BlockSpec((span, GROUP), lambda p: (0, p))
    return launch(
        functools.partial(attend_back_kernel, span),
        tokens,
        grid=(width // GROUP,),
        in_specs=[block] * 5 + [pl.BlockSpec((1, GROUP // PAIR) + prior.shape[2:], lambda p: (image, p, 0, 0))],
        out_specs=[column] * 3,
        out_shape=[shaped((span, width), low), shaped((span, width), wide), shaped((span, width), wide)],
        cost_estimate=cost(32 * span * span * width, 24 * span * width),
        name="attend_back",
    )(fq, fk, v, dn, w, prior)


def finish_kernel(images, span, core_ref, *refs):
    fk_ref, v_ref, later_ref, kept_ref, sent_ref = refs[3 * images :]

    def run(out_ref):
        for image in range(images):
            rows = slice(image * span, (image + 1) * span)
            dq_ref, dfk_ref, dvl_ref = refs[3 * image : 3 * image + 3]
            out_ref[0, rows, :] = dq_ref[...]
            for pair in range(GROUP // PAIR):
                lanes = slice(pair * PAIR, (pair + 1) * PAIR)
                folded = later_ref[image, pair]
                high, rest = split_low(unfold_state(folded[:HEAD_DIM]))
                key, value = fk_ref[rows, lanes], v_ref[rows, lanes]
                dfk = dfk_ref[:, lanes] + folded[HEAD_DIM : HEAD_DIM + 1]
                dfk = dfk + mm(jnp.concatenate([value, value], axis=1), jnp.concatenate([high, rest], axis=0))
                dv = dvl_ref[:, lanes] + mt(
                    jnp.concatenate([key, key], axis=1), jnp.concatenate([high, rest], axis=1)
                )
                out_ref[1, rows, lanes] = (dfk * jnp.minimum(key.astype(wide), 1.0)).astype(low)
                out_ref[2, rows, lanes] = dv.astype(low)

    @pl.when(pl.program_id(0) < pl.num_programs(0) // 2)
    def _():
        run(kept_ref)

    @pl.when(pl.program_id(0) >= pl.num_programs(0) // 2)
    def _():
        run(sent_ref)


def finish(parts, fk, v, later, images, span, tokens=()):
    rows, width = fk.shape
    groups = width // GROUP // 2

    def column(g, core):
        return ((g // groups) ^ core[0]) * groups + g % groups

    block = pl.BlockSpec((rows, GROUP), lambda g, core: (0, column(g, core)))
    part = pl.BlockSpec((span, GROUP), lambda g, core: (0, column(g, core)))
    state = pl.BlockSpec((images, GROUP // PAIR) + later.shape[2:], lambda g, core: (0, column(g, core), 0, 0))
    return launch_at(
        functools.partial(finish_kernel, images, span),
        core_index(),
        tokens,
        grid=(2 * groups,),
        in_specs=[part] * (3 * images) + [block] * 2 + [state],
        out_specs=[
            pl.BlockSpec((3, rows, GROUP), lambda g, core: (0, 0, jnp.minimum(g, groups - 1))),
            pl.BlockSpec((3, rows, GROUP), lambda g, core: (0, 0, jnp.maximum(g - groups, 0))),
        ],
        out_shape=[shaped((3, rows, width // 2), low)] * 2,
        cost_estimate=cost(rows * width * 512, 24 * rows * width),
        name="finish",
    )(*[array for image in parts for array in image], fk, v, later)


def enter_kernel(core_ref, kept_ref, sent_ref, *refs):
    weights = refs[:3]
    x_ref, dres_ref, vec_ref, grad_ref, sums_ref = refs[3:]
    half = x_ref.shape[1] // 2
    da = None
    for k, weight in enumerate(weights):
        for ref, side in ((kept_ref, core_ref[0]), (sent_ref, 1 - core_ref[0])):
            part = mt(ref[k], weight[:, pl.ds(pl.multiple_of(side * half, half), half)])
            da = part if da is None else da + part
    unit, scale = normalised(x_ref[...].astype(wide))
    sums_ref[0:1, :] = jnp.sum(da * unit, axis=0, keepdims=True)
    sums_ref[1:2, :] = jnp.sum(da, axis=0, keepdims=True)
    sums_ref[2:, :] = jnp.zeros_like(sums_ref[2:, :])
    p = da * vec_ref[0:1, :]
    back = p - jnp.mean(p, axis=-1, keepdims=True) - unit * jnp.mean(p * unit, axis=-1, keepdims=True)
    grad_ref[...] = (dres_ref[...] + scale * back).astype(low)


def enter(image, kept, sent, weights, x, dres, vec, span, tokens=()):
    width = x.shape[1]
    rows = pl.BlockSpec((span, width), lambda g, core: (image, 0))
    part = pl.BlockSpec((3, span, width // 2), lambda g, core: (0, image, 0))
    return launch_at(
        enter_kernel,
        core_index(),
        tokens,
        grid=(1,),
        in_specs=[part] * 2 + [whole((width, width))] * 3 + [rows, rows, whole(vec.shape)],
        out_specs=[whole((span, width)), whole((8, width))],
        out_shape=[shaped((span, width), low), shaped((8, width), wide)],
        cost_estimate=cost(3 * span * width * width, 14 * span * width + 6 * width * width),
        name="enter",
    )(kept, sent, *weights, x, dres, vec)


def adam_update(master, moment, second, average, gradient, factor, rate):
    clipped = gradient * factor
    moment = beta_first * moment + (1.0 - beta_first) * clipped
    second = beta_second * second + (1.0 - beta_second) * clipped * clipped
    first_hat = moment / (1.0 - beta_first**STEP)
    second_hat = second / (1.0 - beta_second**STEP)
    master = master - rate * (first_hat / (jnp.sqrt(second_hat) + eps_adam) + weight_decay * master)
    average = average_decay * average + (1.0 - average_decay) * master
    return (master, moment, second, average)


def powers(count):
    return [1 << k for k in range(count.bit_length() - 1)]


def core_index():
    return lax.axis_index("seq") % 2


def pos_index():
    return lax.axis_index("seq") // 2


def pos_bits():
    return (lax.axis_size("seq") // 2).bit_length() - 1


def flip(array, axis, bit):
    return lax.ppermute(array, axis, [(i, i ^ bit) for i in range(lax.axis_size(axis))])


def flip_core(array):
    return flip(array, "seq", 1)


def flip_pos(array, stage):
    bits = pos_bits()
    pairs = [(i, i ^ (2 << (stage if i % 2 == 0 else bits - 1 - stage))) for i in range(lax.axis_size("seq"))]
    return lax.ppermute(array, "seq", pairs)


def own_bit(stage):
    bits = pos_bits()
    return jnp.where(core_index() == 0, pos_index() >> stage, pos_index() >> (bits - 1 - stage)) & 1


def halves(shape, dim):
    index = np.arange(int(np.prod(shape))).reshape(shape)
    return np.stack([index.take(side, axis=dim).ravel() for side in range(2)])


def fold_kernel(chains, spot_ref, *refs):
    ins, outs = refs[: 4 * chains], refs[4 * chains :]
    for k in range(2 * chains):
        value = ins[2 * k][...].astype(wide) + ins[2 * k + 1][...].astype(wide)
        outs[k][...] = value.astype(outs[k].dtype)


def fold(cuts, tokens=()):
    count = cuts[0][2].shape[0]
    steps = max(1, min(2, min(kept.shape[-1] for kept, *_ in cuts) // 256))
    in_specs, out_specs, out_shape, arrays, moved = [], [], [], [], 0
    for k, (kept, came, keeps, sends) in enumerate(cuts):
        lead, _, rows, columns = kept.shape
        block = (lead, 1, rows, columns // steps)
        for side in range(2):
            at = 2 * k * count + side * count
            spec = pl.BlockSpec(block, lambda g, c, spot, at=at: (0, spot[at + g], 0, c))
            in_specs += [spec, spec]
            arrays += [kept, came]
            out_specs.append(pl.BlockSpec(block, lambda g, c, spot: (0, g, 0, c)))
            out_shape.append(shaped((lead, count, rows, columns), low if side else wide))
        moved += 8 * kept.size
    results = launch_at(
        functools.partial(fold_kernel, len(cuts)),
        jnp.concatenate([part for _, _, keeps, sends in cuts for part in (keeps, sends)]),
        tokens,
        grid=(count, steps),
        in_specs=in_specs,
        out_specs=out_specs,
        out_shape=out_shape,
        cost_estimate=cost(1, moved),
        name="fold",
    )(*arrays)
    return [results[2 * k : 2 * k + 2] for k in range(len(cuts))]


class Chain:
    def __init__(self, lead=1):
        self.lead = lead
        self.stage = -1
        self.left = [list(range(pos_bits()))[::-1]] * 2

    def start(self):
        self.came = [flip_pos(self.sends[0], self.stage)]

    def table(self):
        self.stage += 1
        tables = []
        for kind in range(2):
            bit = self.stage if kind == 0 else pos_bits() - 1 - self.stage
            left = self.left[kind]
            tables.append(halves((2,) * len(left), left.index(bit)))
            self.left[kind] = [other for other in left if other != bit]
        table = jnp.where(core_index() == 0, *[jnp.asarray(part, jnp.int32) for part in tables])
        own = own_bit(self.stage)
        return table[own], table[1 - own]

    def cut(self):
        return (self.kept, self.came[0], *self.table())

    def take(self, parts):
        self.kept, self.sends = parts[0], [parts[1]]


def advance(chains, tokens=()):
    parts = fold([chain.cut() for chain in chains], tokens)
    for chain, part in zip(chains, parts):
        chain.take(part)
        chain.start()
    return [array for chain in chains for array in chain.sends]


def last_kernel(ways, pre, pieces, spot_ref, *refs):
    ins, outs = refs[: 2 * pieces], refs[2 * pieces :]
    at = 0
    for k in range(pieces):
        columns = ins[2 * k].shape[-1]
        for j in range(ways):
            place = spot_ref[0] ^ j
            for n in range(pre):
                value = ins[2 * k][n, place].astype(wide) + ins[2 * k + 1][n, place].astype(wide)
                outs[j][n, :, at : at + columns] = value.astype(outs[j].dtype)
        at += columns


class Last:
    def __init__(self, chains, tokens=(), slowly=False):
        slices = lax.axis_size("img")
        ways = 2 if slowly else slices
        self.lead = chains[0].lead
        pre = self.lead * 2 * slices // ways
        arrays = []
        for chain in chains:
            for array in (chain.kept, chain.came[0]):
                arrays.append(array.reshape(pre, ways, -1, array.shape[-1]))
        self.widths = [array.shape[-1] for array in arrays[::2]]
        inside = pl.BlockSpec(memory_space=pltpu.VMEM)
        parts = launch(
            functools.partial(last_kernel, ways, pre, len(chains)),
            tokens,
            in_specs=[pl.BlockSpec(memory_space=pltpu.SMEM)] + [inside] * len(arrays),
            out_specs=[inside] * ways,
            out_shape=[shaped((pre, arrays[0].shape[2], sum(self.widths)), low if j else wide) for j in range(ways)],
            cost_estimate=cost(1, 4 * sum(array.size for array in arrays)),
                name="last",
        )((lax.axis_index("img") % ways).reshape(1), *arrays)
        self.kept, self.sends = parts[0], list(parts[1:])
        self.hops = list(range(1, ways))
        self.left = powers(slices)[1:][::-1] if slowly else []
        self.start()

    def start(self):
        self.came = [flip(array, "img", hop) for array, hop in zip(self.sends, self.hops)]

    def cut(self):
        bit = self.left[-1]
        entries = self.kept.reshape((1, -1) + self.kept.shape[-2:])
        dims = (2 * self.lead,) + (2,) * len(self.left)
        table = jnp.asarray(halves(dims, len(dims) - 1), jnp.int32)
        own = (lax.axis_index("img") // bit) % 2
        self.left = self.left[:-1]
        self.hops = [bit]
        return (entries, self.came[0].reshape(entries.shape), table[own], table[1 - own])

    def take(self, parts):
        self.kept, self.sends = parts[0][0], [parts[1][0]]

    def total(self):
        while self.left:
            advance([self])
        total = self.kept
        for came in self.came:
            total = total + came.astype(wide)
        return total

    def settle(self, stretch, tokens):
        self.came[stretch] = gate(self.came[stretch], tokens)
        return self.came[stretch]

    def squares(self):
        self.sums = self.total()
        return jnp.sum(self.sums * self.sums)

    def finish(self):
        core = core_index()
        total = self.sums.reshape((self.lead, 2) + self.sums.shape[-2:])
        own = lax.dynamic_index_in_dim(total, core, 1, False)
        came = flip_core(lax.dynamic_index_in_dim(total, 1 - core, 1, False))
        first, second = jnp.where(core == 0, own, came), jnp.where(core == 0, came, own)
        at, found = 0, []
        for columns in self.widths:
            found.append((first[..., at : at + columns], second[..., at : at + columns]))
            at += columns
        return found


def slow_hops():
    return [(axis, bit) for axis in ("seq", "img") for bit in powers(lax.axis_size(axis))]


def sum_all(array):
    rounds = [("img", range(1, lax.axis_size("img"))), ("seq", range(2, lax.axis_size("seq"), 2)), ("seq", [1])]
    for axis, hops in rounds:
        came = [flip(array, axis, hop) for hop in hops]
        for other in came:
            array = array + other
    return array


def assemble_kernel(plan, spot_ref, *refs):
    outs = sorted({out for _, _, out, _ in plan})
    count = len(refs) - 1 - len(outs)
    sems = refs[-1]
    copies = []
    for k, (piece, cut, out, where) in enumerate(plan):
        source = refs[piece].at[cut] if cut is not None else refs[piece]
        target = refs[count + out].at[where(spot_ref)]
        copies.append(pltpu.make_async_copy(source, target, sems.at[k]))
    for copy in copies:
        copy.start()
    for copy in copies:
        copy.wait()


def assemble(plan, spots, pieces, shapes, tokens=()):
    anywhere = pl.BlockSpec(memory_space=pl.ANY)
    return launch(
        functools.partial(assemble_kernel, plan),
        tokens,
        in_specs=[pl.BlockSpec(memory_space=pltpu.SMEM)] + [anywhere] * len(pieces),
        out_specs=[pl.BlockSpec(memory_space=pltpu.VMEM)] * len(shapes),
        out_shape=[shaped(shape, low) for shape in shapes],
        scratch_shapes=[pltpu.SemaphoreType.DMA((len(plan),))],
        cost_estimate=cost(1, 2 * sum(2 * piece.size for piece in pieces)),
        name="assemble",
    )(jnp.stack(spots).astype(jnp.int32), *pieces)


def gate_kernel(*refs):
    pass


def gate(arrays, tokens):
    anywhere = pl.BlockSpec(memory_space=pl.ANY)
    return launch(
        gate_kernel,
        tokens,
        in_specs=[anywhere] * len(arrays),
        out_specs=[anywhere] * len(arrays),
        out_shape=[shaped(array.shape, array.dtype) for array in arrays],
        input_output_aliases={k: k for k in range(len(arrays))},
        cost_estimate=cost(1, 1),
        name="gate",
    )(*arrays)


class Gather:
    def __init__(self, own, other):
        self.own, self.other = own, other
        self.stage = 0

    def pair(self):
        came = flip_core(self.other)
        pairs = [jnp.stack([self.own, came], axis=1), jnp.stack([came, self.own], axis=1)]
        return jnp.where(core_index() == 0, *pairs)

    @staticmethod
    def exchange(both, tokens=()):
        if tokens:
            (both,) = gate([both], tokens)
        own, other = jnp.split(both, 2)
        every = slice(None)
        plan = [(0, None, 0, lambda spot: (every, spot[0])), (1, None, 0, lambda spot: (every, 1 - spot[0]))]
        k, rows, columns = own.shape
        found = Gather(None, None)
        found.part = assemble(plan, [core_index()], [own, flip_core(other)], [(k, 2, rows, columns)])[0]
        found.part = found.part.reshape(k, 1, 2 * rows, columns)
        return found

    def start_slices(self, hops=False):
        self.pieces = [self.pair()]
        for j in range(1, lax.axis_size("img")):
            bit = j & -j if hops else j
            self.pieces.append(flip(self.pieces[j - bit], "img", bit))

    def finish_slices(self, tokens=(), groups=1):
        slices = len(self.pieces)
        if tokens:
            self.pieces = self.pieces[:1] + list(gate(self.pieces[1:], tokens))
        every = slice(None)
        k, _, rows, columns = self.pieces[0].shape
        k = k // groups
        plan = [
            (j, slice(n * k, (n + 1) * k), n, lambda spot, j=j: (every, every, spot[0] ^ j))
            for n in range(groups)
            for j in range(slices)
        ]
        shape = (k, 2, slices, rows, columns)
        parts = assemble(plan, [lax.axis_index("img")], self.pieces, [shape] * groups)
        found = []
        for part in parts:
            found.append(Gather(None, None))
            found[-1].part = part.reshape(k, 1, 2 * slices * rows, columns)
        return found

    def start_pos(self, tokens=()):
        if tokens:
            (self.part,) = gate([self.part], tokens)
        self.came = flip_pos(self.part, self.stage)
        self.stage += 1

    def finish_pos(self, tokens=()):
        every = slice(None)
        if tokens:
            (self.came,) = gate([self.came], tokens)
        plan = [
            (0, None, 0, lambda spot: (every, spot[0])),
            (1, None, 0, lambda spot: (every, 1 - spot[0])),
        ]
        shape = self.part.shape[:1] + (2,) + self.part.shape[1:]
        self.part = assemble(plan, [own_bit(self.stage - 1)], [self.part, self.came], [shape])[0]
        self.part = self.part.reshape((shape[0], -1) + shape[3:])
        return [self.part]

    def start_last(self):
        self.start_pos()
        self.turned = flip_core(self.part)

    def finish_last(self, tokens, turned_tokens):
        (self.turned,) = gate([self.turned], turned_tokens)
        (self.came,) = gate([self.came], tokens)
        return Pieces([self.part, self.came, self.turned, flip_core(self.came)])


def narrow_kernel(core_ref, weight_ref, *out_refs):
    first = core_ref[0] == 0
    slabs = out_refs[0].shape[0] // 2
    for k, out_ref in enumerate(out_refs):
        for n in range(slabs):
            columns = slice((k * slabs + n) * SLAB, (k * slabs + n + 1) * SLAB)
            left, right = weight_ref[0, :, columns].astype(low), weight_ref[1, :, columns].astype(low)
            out_ref[n] = jnp.where(first, left, right)
            out_ref[slabs + n] = jnp.where(first, right, left)


def narrow(weight, groups, tokens):
    _, owned, hidden = weight.shape
    slabs = hidden // SLAB // groups
    inside = pl.BlockSpec(memory_space=pltpu.VMEM)
    return launch(
        narrow_kernel,
        tokens,
        in_specs=[pl.BlockSpec(memory_space=pltpu.SMEM), inside],
        out_specs=[inside] * groups,
        out_shape=[shaped((2 * slabs, owned, SLAB), low)] * groups,
        cost_estimate=cost(1, 12 * slabs * groups * owned * SLAB),
        name="narrow",
    )(core_index().reshape(1), weight)


class Passing:
    def __init__(self, own, backward, direct):
        self.backward = backward
        came = flip_core(own.astype(low)).astype(wide)
        self.outside = jnp.where(core_index() == (0 if backward else 1), came, 0.0)
        self.total = own + came
        self.bits = powers(lax.axis_size("seq") // 2)
        if direct:
            both = self.total.astype(low)
            self.came = [flip(both, "seq", 2 * j) for j in range(1, lax.axis_size("seq") // 2)]

    def finish(self, tokens):
        total = self.outside
        for j, came in enumerate(gate(self.came, tokens), 1):
            earlier = (pos_index() ^ j) < pos_index()
            total = total + jnp.where(earlier != self.backward, came.astype(wide), 0.0)
        return total

    def hop(self, tokens):
        bit, *self.bits = self.bits
        (came,) = gate([flip(self.total.astype(low), "seq", 2 * bit)], tokens)
        came = came.astype(wide)
        earlier = (pos_index() ^ bit) < pos_index()
        self.outside = self.outside + jnp.where(earlier != self.backward, came, 0.0)
        self.total = self.total + came
        return self.outside


def body(
    images,
    cotangent,
    attention_weight,
    feedforward_weight,
    norm_vectors,
    attention_moment,
    feedforward_moment,
    norm_moment,
    attention_second,
    feedforward_second,
    norm_second,
    attention_average,
    feedforward_average,
    norm_average,
):
    count, span, width = images.shape
    tokens = count * span
    owned = attention_weight.shape[1]
    slabs = feedforward_weight.shape[2] // SLAB
    stages = pos_bits()
    half = slabs // 2
    every = slice(None)

    x, e = images.reshape(tokens, width), cotangent.reshape(tokens, width)
    low_weights = jnp.pad(attention_weight.astype(low), ((0, 0), (0, 0), (0, 128)))
    vectors = jnp.pad(norm_vectors.astype(low).T, ((0, 0), (width, 124)))
    query_weight, key_weight, value_weight, out_weight = low_weights
    kinds = jnp.stack([key_weight, query_weight]), jnp.stack([value_weight + vectors, out_weight])
    first_core = core_index() == 0
    one = Gather(jnp.where(first_core, *kinds), jnp.where(first_core, *kinds[::-1]))
    one.start_slices(True)
    et = turn(e, count, span)
    (one,) = one.finish_slices([et])
    one.start_pos()
    feeds = narrow(feedforward_weight, 2, [one.part])
    marks = [feeds[0]]
    feeds = [lax.all_gather(part, "img", axis=1, tiled=True) for part in feeds]
    for _ in range(stages - 2):
        one.finish_pos(marks)
        one.start_pos()
    one.finish_pos(marks)
    one.start_last()
    pieces = one.finish_last([one.part], [one.part])
    two = Gather.exchange(feeds[0])
    two.start_pos([one.came])
    vec = pieces.second(slice(width, width + 4)).astype(wide).T
    fk, v, a1, a1t, state, wk, wv = project(x, vec, pieces, count, span, [two.part])
    a1t_other = flip_core(a1t)
    prior = Passing(state, False, False)
    for _ in range(stages - 2):
        two.finish_pos([state])
        two.start_pos()
    two.finish_pos([state])
    two.start_last()
    fq, wq, wo = query(a1, pieces, [prior.outside, two.part])
    marks = [prior.hop([fq]), two.turned, a1t_other]
    num, den = attend(fq, fk, v, count, span, marks)
    while prior.bits:
        prior.hop([num])
    prior = prior.outside
    three = Gather.exchange(feeds[1], [num])
    three.start_pos()
    mixed, rden, resid, a2, a2t, mixed_t = mix(x, vec, wo, fq, num, den, prior, count, span, [three.part])
    a2t, mixed_t = turned_whole(a2t), turned_whole(mixed_t)
    lt = jnp.where(first_core, a2t, et)
    lt_other = flip_core(jnp.where(first_core, et, a2t))
    mixed_t_other = flip_core(mixed_t)
    first_pieces = two.finish_last([resid], [fq])
    marks = [resid]
    for _ in range(stages - 2):
        three.finish_pos(marks)
        three.start_pos()
    three.finish_pos(marks)
    three.start_last()
    marks = [three.part, three.turned]

    early = feed(first_pieces, a2, e, None, marks)
    early_other = flip_core(early[3])
    second_pieces = three.finish_last([early[0]], [early[0]])
    late = feed(second_pieces, a2, e, early[:2], [lt_other, mixed_t_other])
    late_other = flip_core(late[3])
    firsts, seconds, outs, inner = [Chain()], [Chain()], [Chain()], [Chain(3)]
    marks = weigh(firsts[0], lt, lt_other, early[2][None], early_other[None], [late[0]])
    output, dres, branch, branch_send, dn, w, dstate, sums_second = turn_back(
        late[0], late[1], resid, e, vec, wo, mixed, rden, fq, count, span, marks + [late_other]
    )
    later = Passing(dstate, True, False)
    branch_other = flip_core(branch_send)
    marks = weigh(outs[0], mixed_t, mixed_t_other, branch[None], branch_other[None], [dstate, later.outside])
    for _ in range(stages - 1):
        marks = marks + advance(firsts, [outs[0].kept])
    marks = weigh(seconds[0], lt, lt_other, late[2][None], late_other[None], marks)
    firsts_last = Last(firsts, [seconds[0].kept])
    parts = [attend_back(0, fq, fk, v, dn, w, prior, span, marks + firsts_last.sends)]
    marks = [later.hop([parts[0][0]])]
    for _ in range(stages - 1):
        marks = marks + advance(seconds + outs, [parts[0][0]])
    for image in range(1, count):
        parts.append(attend_back(image, fq, fk, v, dn, w, prior, span, marks))
    marks = seconds[0].came + outs[0].came + firsts_last.settle(slice(0, None), [parts[-1][0]])
    while later.bits:
        later.hop([parts[-1][0]])
    later = later.outside
    kept, sent = finish(parts, fk, v, later, count, span, marks)
    local_squares = firsts_last.squares()
    came = flip_core(sent)
    seconds_last = Last(seconds + outs, [kept])
    marks = seconds_last.sends + [firsts_last.sums]
    grads_in = [enter(0, kept, sent, (wq, wk, wv), x, dres, vec, span, marks)]
    marks = seconds_last.settle(slice(0, 2), [grads_in[0][1]])
    marks = weigh(inner[0], a1t, a1t_other, kept, came, marks)
    for image in range(1, count):
        grads_in.append(enter(image, kept, sent, (wq, wk, wv), x, dres, vec, span, marks))
    seconds_last.settle(slice(2, None), [grads_in[-1][1]])
    local_squares = local_squares + seconds_last.squares()
    input_grad = jnp.stack([part[0] for part in grads_in])
    sums = sum(part[1] for part in grads_in)
    vector_grad = jnp.concatenate([sums[:2], sums_second[:2]], axis=0)
    hops = slow_hops()
    for axis, bit in hops[:2]:
        vector_grad = vector_grad + flip(vector_grad, axis, bit)
    marks = [seconds_last.sums, vector_grad]
    for _ in range(stages - 1):
        marks = advance(inner, marks)
    (vector_grad,) = gate([vector_grad], marks)
    for axis, bit in hops[2:]:
        vector_grad = vector_grad + flip(vector_grad, axis, bit)
    device = lax.axis_index("seq") * lax.axis_size("img") + lax.axis_index("img")
    vector_shard = lax.dynamic_slice_in_dim(vector_grad, device * owned, owned, 1)
    inner_last = Last(inner, [seconds_last.sums])
    local_squares = local_squares + jnp.sum(vector_shard * vector_shard)
    local_squares = local_squares + inner_last.squares()
    grad_norm = jnp.sqrt(sum_all(jnp.full((8, 128), local_squares))[0, 0])
    (early_shard,) = firsts_last.finish()
    late_shard, out_shard = seconds_last.finish()
    inner_shard = jnp.concatenate([part for pair in inner_last.finish() for part in pair], axis=2)
    attn_shard = jnp.concatenate([inner_shard, jnp.concatenate(out_shard, axis=2)], axis=0)
    feed_shard = jnp.concatenate([jnp.concatenate(pair, axis=2) for pair in zip(early_shard, late_shard)], axis=0)
    factor = clip_bound / jnp.maximum(grad_norm, clip_bound)
    attn_new = adam_update(
        attention_weight, attention_moment, attention_second, attention_average, attn_shard, factor, learn_rate
    )
    feed_new = adam_update(
        feedforward_weight, feedforward_moment, feedforward_second, feedforward_average, feed_shard, factor, learn_rate
    )
    norm_new = adam_update(norm_vectors, norm_moment, norm_second, norm_average, vector_shard, factor, norm_rate)
    output = output.reshape(images.shape)
    input_grad = input_grad.reshape(images.shape)
    return (output, input_grad, grad_norm) + attn_new + feed_new + norm_new


def solution(mesh):
    tokens = P("img", "seq", None)
    rows = P(None, ("seq", "img"), None)
    vectors = P(None, ("seq", "img"))
    group = (rows, rows, vectors)
    return jax.shard_map(
        body,
        mesh=mesh,
        in_specs=(tokens, tokens) + group * 4,
        out_specs=(tokens, tokens, P()) + (rows,) * 8 + (vectors,) * 4,
        check_vma=False,
    )
```
